32 devices in a mesh: ctx: 8 (over z, x), wsh: 4 (over y, core).
Axes of the slice: x: 2, y: 2, z: 4, core: 2. Of those that a mesh axis runs over, the one named last changes fastest.
Arguments:
- inputs: bfloat16 [2, 4, 2048, 1024], P(None, 'wsh', 'ctx'), may hold values from -6 to 6
- cotangent: bfloat16 [2, 4, 2048, 1024], P(None, 'wsh', 'ctx'), may hold values from -6 to 6
- lengths: int32 [2, 4, 4], P(None, 'wsh'), may hold values from 0 to 2048, as said below
- norm1_gain: float32 [1024], replicated, may hold values from 0.5 to 1.5
- in_weight: bfloat16 [1024, 3328], P('wsh'), may hold values from -0.1875 to 0.1875
- dt_weight: bfloat16 [1024, 24], P('wsh'), may hold values from -0.1875 to 0.1875
- conv_weight: float32 [4, 1792], replicated, may hold values from -3 to 3
- conv_bias: float32 [1792], replicated, may hold values from -3 to 3
- dt_bias: float32 [24], replicated, may hold values from -2 to 0
- decay_rate: float32 [24], replicated, may hold values from 0.00012207031 to 0.1
- skip_gain: float32 [24], replicated, may hold values from 0.5 to 1.5
- mamba_gain: float32 [1536], replicated, may hold values from 0.5 to 1.5
- out_weight: bfloat16 [1536, 1024], P('wsh'), may hold values from -0.15625 to 0.15625
- q_weight: bfloat16 [1024, 512], P('wsh'), may hold values from -0.1875 to 0.1875
- kv_weight: bfloat16 [1024, 256], P('wsh'), may hold values from -0.1875 to 0.1875
- o_weight: bfloat16 [512, 1024], P('wsh'), may hold values from -1 to 1
- norm2_gain: float32 [1024], replicated, may hold values from 0.5 to 1.5
- gu_weight: bfloat16 [1024, 4096], P('wsh'), may hold values from -0.1875 to 0.1875
- down_weight: bfloat16 [2048, 1024], P('wsh'), may hold values from -0.125 to 0.125
Outputs:
- layer_out: bfloat16 [2, 4, 2048, 1024], P(None, 'wsh', 'ctx')
- input_grad: bfloat16 [2, 4, 2048, 1024], P(None, 'wsh', 'ctx')
- grad_norm1_gain: float32 [1024], replicated
- grad_in_weight: float32 [1024, 3328], P('wsh')
- grad_dt_weight: float32 [1024, 24], P('wsh')
- grad_conv_weight: float32 [4, 1792], replicated
- grad_conv_bias: float32 [1792], replicated
- grad_dt_bias: float32 [24], replicated
- grad_decay_rate: float32 [24], replicated
- grad_skip_gain: float32 [24], replicated
- grad_mamba_gain: float32 [1536], replicated
- grad_out_weight: float32 [1536, 1024], P('wsh')
- grad_q_weight: float32 [1024, 512], P('wsh')
- grad_kv_weight: float32 [1024, 256], P('wsh')
- grad_o_weight: float32 [512, 1024], P('wsh')
- grad_norm2_gain: float32 [1024], replicated
- grad_gu_weight: float32 [1024, 4096], P('wsh')
- grad_down_weight: float32 [2048, 1024], P('wsh')
The draws below stay inside these ranges and needn't reach their ends.
Inputs may be any that keep to these rules, and one draw needn't show every extreme that they name: Each row (micro-batch, group) lists the stream's sequence lengths in order; they sum to 2048, zeros stand only at the end, every nonzero length is at least min(1024, 2048), and in each group one micro-batch holds a single sequence of 2048 tokens.
All inputs are finite; a program needn't handle non-finite values.
Results may differ from the reference program's by a relative error of at most 0.02.
Values may be sent and summed in bfloat16 or wider, within the bound.
A program may use at most 320 MiB of HBM per device.

```python
import math
import jax
import jax.numpy as jnp
from jax import lax

D = 1024
FF = 2048
MHEADS = 24
MDIM = 64
STATE = 128
CONV = 4
QHEADS = 8
KVHEADS = 2
HDIM = 64
TOK_MB = 256
MB = 2
NSEQ = 4
MINSEQ = 1024
GTOK = 2048
GROUPS = 4
DSSM = 1536
CHANS = 1792
INW = 3328
QW = 512
KVW = 256


def draw_lengths(key, part):
    key = jax.random.fold_in(key, 3)
    pieces = max(1, min(NSEQ, GTOK // MINSEQ))
    spare_rows = GTOK - pieces * MINSEQ
    cut_key, pick_key = jax.random.split(key)
    cut_points = jnp.sort(jax.random.randint(cut_key, (MB, GROUPS, pieces - 1), 0, max(spare_rows, 0) + 1), axis=-1).astype(jnp.int32)
    edge_points = jnp.concatenate([jnp.zeros((MB, GROUPS, 1), jnp.int32), cut_points, jnp.full((MB, GROUPS, 1), spare_rows, jnp.int32)], axis=-1)
    ragged = MINSEQ + edge_points[..., 1:] - edge_points[..., :-1]
    ragged = jnp.concatenate([ragged, jnp.zeros((MB, GROUPS, NSEQ - pieces), jnp.int32)], axis=-1)
    single = jnp.concatenate([jnp.full((1,), GTOK, jnp.int32), jnp.zeros((NSEQ - 1,), jnp.int32)])
    chosen = jax.random.randint(pick_key, (GROUPS,), 0, MB)
    whole_mask = jnp.arange(MB)[:, None] == chosen[None, :]
    return jnp.where(whole_mask[..., None], single[None, None, :], ragged).astype(jnp.int32)


def level_of(stream_key, extent, shards, smallest, high):
    gain = 1.0
    for dim, parts in shards:
        steps = jax.random.uniform(jax.random.fold_in(jax.random.fold_in(stream_key, 6), dim), (parts,), jnp.float32, smallest / len(shards), high / len(shards))
        gain = gain * jnp.repeat(jnp.exp(steps), extent[dim] // parts).reshape((-1,) + (1,) * (len(extent) - 1 - dim))
    return gain


def gaussian(own_key, shape, scale, reach, shards=(), held_as=jnp.bfloat16):
    loudness = level_of(own_key, shape, shards, -0.22, 0.18) if shards else 1.0
    result = jax.random.normal(own_key, shape, jnp.float32) * scale * loudness
    return jnp.minimum(jnp.maximum(result, -reach), reach).astype(held_as)


def setup_inputs(seed: int = 0) -> dict:
    arg_keys = jax.random.split(jax.random.key(seed), 20)
    inputs = gaussian(arg_keys[0], (MB, GROUPS, GTOK, D), 1.0, 6.0, ((1, 4), (2, 8)))
    cotangent = gaussian(arg_keys[1], (MB, GROUPS, GTOK, D), 1.0, 6.0, ((1, 4), (2, 8)))
    lengths = draw_lengths(jax.random.fold_in(arg_keys[19], 71), 0)
    norm1_gain = jnp.clip(1.0 + 0.1 * jax.random.normal(arg_keys[3], (D,), jnp.float32), 0.5, 1.5)
    in_weight = gaussian(arg_keys[4], (D, INW), D ** -0.5, 0.1875, ((0, 4),))
    dt_weight = gaussian(arg_keys[5], (D, MHEADS), D ** -0.5, 0.1875, ((0, 4),))
    conv_weight = gaussian(arg_keys[6], (CONV, CHANS), 0.5, 3.0, (), jnp.float32)
    conv_bias = gaussian(arg_keys[7], (CHANS,), 0.5, 3.0, (), jnp.float32)
    dt_bias = jnp.clip(jax.random.uniform(arg_keys[8], (MHEADS,), jnp.float32, -2.0, 0.0), -2.0, 0.0)
    decay_rate = jnp.clip(jnp.exp(jax.random.uniform(arg_keys[9], (MHEADS,), jnp.float32, math.log(0.00012207031), math.log(0.1))), 0.00012207031, 0.1)
    skip_gain = jnp.clip(jax.random.uniform(arg_keys[10], (MHEADS,), jnp.float32, 0.5, 1.5), 0.5, 1.5)
    mamba_gain = jnp.clip(1.0 + 0.1 * jax.random.normal(arg_keys[11], (DSSM,), jnp.float32), 0.5, 1.5)
    out_weight = gaussian(arg_keys[12], (DSSM, D), DSSM ** -0.5, 0.15625, ((0, 4),))
    q_weight = gaussian(arg_keys[13], (D, QW), D ** -0.5, 0.1875, ((0, 4),))
    kv_weight = gaussian(arg_keys[14], (D, KVW), D ** -0.5, 0.1875, ((0, 4),))
    o_weight = gaussian(arg_keys[15], (QW, D), (QW // 16) ** -0.5, 1.0, ((0, 4),))
    norm2_gain = jnp.clip(1.0 + 0.1 * jax.random.normal(arg_keys[16], (D,), jnp.float32), 0.5, 1.5)
    gu_weight = gaussian(arg_keys[17], (D, 2 * FF), D ** -0.5, 0.1875, ((0, 4),))
    down_weight = gaussian(arg_keys[18], (FF, D), FF ** -0.5, 0.125, ((0, 4),))
    return {"inputs": inputs, "cotangent": cotangent, "lengths": lengths, "norm1_gain": norm1_gain, "in_weight": in_weight, "dt_weight": dt_weight, "conv_weight": conv_weight, "conv_bias": conv_bias, "dt_bias": dt_bias, "decay_rate": decay_rate, "skip_gain": skip_gain, "mamba_gain": mamba_gain, "out_weight": out_weight, "q_weight": q_weight, "kv_weight": kv_weight, "o_weight": o_weight, "norm2_gain": norm2_gain, "gu_weight": gu_weight, "down_weight": down_weight}


NORM_EPS = 1e-05
PRECISE = lax.Precision.HIGHEST
MASKED_SCORE = -1e+30

@jax.custom_vjp
def low(v):
    return lax.optimization_barrier(v.astype(jnp.bfloat16)).astype(jnp.float32)

@jax.custom_vjp
def low_back(v):
    return v

def low_keep(v):
    return (low(v), None)

def low_pass(kept, grad):
    return (grad,)

def back_keep(v):
    return (v, None)

def back_low(kept, grad):
    return (low(grad),)
low.defvjp(low_keep, low_pass)
low_back.defvjp(back_keep, back_low)

def matmul(left, right):
    return jnp.dot(left, right, precision=PRECISE, preferred_element_type=jnp.float32)

def rms_scale(features, gain_row):
    return features * lax.rsqrt(lax.optimization_barrier(jnp.mean(features * features, axis=-1, keepdims=True)) + NORM_EPS) * gain_row

def seq_starts(lengths_row, positions):
    end_points = jnp.cumsum(lengths_row, dtype=jnp.int32)
    begins = end_points - lengths_row
    picked = jnp.where(begins[None, :] <= positions[:, None], begins[None, :], 0)
    return lax.optimization_barrier(jnp.max(picked, axis=1)).astype(jnp.int32)

def conv_apply(extended, weight, bias_row, positions, starts):
    row_count = positions.shape[0]
    tap_count = weight.shape[0]
    conv_sum = jnp.zeros((row_count, weight.shape[1]), jnp.float32) + bias_row
    for tap_index in range(tap_count):
        valid_rows = (positions - (tap_count - 1) + tap_index >= starts).astype(jnp.float32)
        conv_sum = conv_sum + weight[tap_index] * extended[tap_index:tap_index + row_count] * valid_rows[:, None]
    return conv_sum

def decay_sums(step_sizes, decay_rates):
    return jnp.cumsum(-step_sizes * decay_rates[None, :], axis=0)

def ssd_output(inner_x, b_rows, c_rows, step_sizes, decay_rates, skip_gains, state_in, positions, starts, first_pos):
    log_decay = decay_sums(step_sizes, decay_rates)
    allowed = (positions[None, :] <= positions[:, None]) & (positions[None, :] >= starts[:, None])
    log_gaps = log_decay.T[:, :, None] - log_decay.T[:, None, :]
    decays = jnp.where(allowed[None], jnp.exp(jnp.where(allowed[None], log_gaps, 0.0)), 0.0)
    inner_prod = jnp.dot(c_rows, b_rows.T, precision=PRECISE)
    scaled = inner_x * step_sizes[:, :, None]
    local_part = jnp.einsum('hij,jhp->ihp', decays * inner_prod[None], scaled, precision=PRECISE)
    carried = (starts < first_pos).astype(jnp.float32)
    incoming = jnp.einsum('in,hpn->ihp', c_rows, state_in, precision=PRECISE)
    return local_part + jnp.exp(log_decay)[:, :, None] * carried[:, None, None] * incoming + skip_gains[None, :, None] * inner_x

def ssd_state(inner_x, b_rows, step_sizes, decay_rates, positions, starts, first_pos):
    log_decay = decay_sums(step_sizes, decay_rates)
    keep_rows = (positions >= starts[-1]).astype(jnp.float32)
    factors = jnp.exp(log_decay[-1][None, :] - log_decay) * step_sizes * keep_rows[:, None]
    fresh_state = jnp.einsum('jh,jhp,jn->hpn', factors, inner_x, b_rows, precision=PRECISE)
    decay_total = jnp.exp(log_decay[-1]) * (starts[-1] < first_pos).astype(jnp.float32)
    return (decay_total, fresh_state)

def mamba_scan(inner_x, b_rows, c_rows, step_sizes, decay_rates, skip_gains, positions, starts):
    length = inner_x.shape[0]
    pieces = length // TOK_MB

    def one_span(state_in, span_parts):
        inner_s, b_s, c_s, dt_s, pos_s, start_s = span_parts
        first_pos = pos_s[0]
        out_rows = ssd_output(inner_s, b_s, c_s, dt_s, decay_rates, skip_gains, state_in, pos_s, start_s, first_pos)
        decay_total, fresh_state = ssd_state(inner_s, b_s, dt_s, decay_rates, pos_s, start_s, first_pos)
        return (state_in * decay_total[:, None, None] + fresh_state, out_rows)

    def reshape_span(array_in):
        return array_in.reshape((pieces, TOK_MB) + array_in.shape[1:])
    state_zero = jnp.zeros((MHEADS, MDIM, STATE), jnp.float32)
    spans = tuple((reshape_span(array_in) for array_in in (inner_x, b_rows, c_rows, step_sizes, positions, starts)))
    state_end, outputs = lax.scan(jax.checkpoint(one_span), state_zero, spans)
    return outputs.reshape(length, MHEADS, MDIM)

def attention(queries, kv_rows, positions, starts):
    length = queries.shape[0]
    block_rows = min(512, length)
    groups = QHEADS // KVHEADS
    score_scale = HDIM ** (-0.5)
    key_rows = kv_rows[:, :KVHEADS * HDIM].reshape(length, KVHEADS, HDIM)
    value_rows = kv_rows[:, KVHEADS * HDIM:].reshape(length, KVHEADS, HDIM)

    def one_block(pieces):
        q_block, pos_block, start_block = pieces
        q_heads = q_block.reshape(block_rows, KVHEADS, groups, HDIM)
        scores = low_back(jnp.einsum('rghd,kgd->ghrk', q_heads, key_rows, precision=PRECISE) * score_scale)
        allowed = (positions[None, :] <= pos_block[:, None]) & (positions[None, :] >= start_block[:, None])
        scores = jnp.where(allowed[None, None], scores, MASKED_SCORE)
        prob_rows = low(jax.nn.softmax(scores, axis=-1))
        mixed_heads = jnp.einsum('ghrk,kgd->rghd', prob_rows, value_rows, precision=PRECISE)
        return mixed_heads.reshape(block_rows, QHEADS * HDIM)
    blocks = length // block_rows
    outcome = lax.map(jax.checkpoint(one_block), (queries.reshape(blocks, block_rows, QHEADS * HDIM), positions.reshape(blocks, block_rows), starts.reshape(blocks, block_rows)))
    return low(low_back(outcome.reshape(length, QHEADS * HDIM)))

def layer_forward(params, features, positions, starts):
    norm1_gain, in_weight, dt_weight, conv_weight, conv_bias, dt_bias, decay_rate, skip_gain, mamba_gain, out_weight, q_weight, kv_weight, o_weight, norm2_gain, gu_weight, down_weight = params
    normed = low(rms_scale(features, norm1_gain))
    projected = low_back(matmul(normed, in_weight))
    gate_z = projected[:, :DSSM]
    conv_in = projected[:, DSSM:]
    dt_raw = low_back(matmul(normed, dt_weight))
    step_sizes = jax.nn.softplus(dt_raw + dt_bias)
    padded = jnp.concatenate([jnp.zeros((CONV - 1, CHANS), jnp.float32), conv_in], axis=0)
    activated = jax.nn.silu(conv_apply(padded, conv_weight, conv_bias, positions, starts))
    inner_x = activated[:, :DSSM].reshape(-1, MHEADS, MDIM)
    b_rows = activated[:, DSSM:DSSM + STATE]
    c_rows = activated[:, DSSM + STATE:]
    scanned = mamba_scan(inner_x, b_rows, c_rows, step_sizes, decay_rate, skip_gain, positions, starts)
    mixed_rows = low(rms_scale(scanned.reshape(-1, DSSM) * jax.nn.silu(gate_z), mamba_gain))
    mamba_out = low_back(matmul(mixed_rows, out_weight))
    queries = low(low_back(matmul(normed, q_weight)))
    kv_rows = low(low_back(matmul(normed, kv_weight)))
    attended = attention(queries, kv_rows, positions, starts)
    attn_out = low_back(matmul(attended, o_weight))
    middle = features + mamba_out + attn_out
    normed_two = low(rms_scale(middle, norm2_gain))
    gate_up = low_back(matmul(normed_two, gu_weight))
    hidden = low(jax.nn.silu(gate_up[:, :FF]) * gate_up[:, FF:])
    return middle + low_back(matmul(hidden, down_weight))

def reference(inputs, cotangent, lengths, norm1_gain, in_weight, dt_weight, conv_weight, conv_bias, dt_bias, decay_rate, skip_gain, mamba_gain, out_weight, q_weight, kv_weight, o_weight, norm2_gain, gu_weight, down_weight):
    params = tuple((tensor.astype(jnp.float32) for tensor in (norm1_gain, in_weight, dt_weight, conv_weight, conv_bias, dt_bias, decay_rate, skip_gain, mamba_gain, out_weight, q_weight, kv_weight, o_weight, norm2_gain, gu_weight, down_weight)))
    positions = jnp.arange(GTOK, dtype=jnp.int32)
    streams = MB * GROUPS

    def one_stream(whole_sums, pieces):
        feat_rows, cot_rows, lengths_row = pieces
        starts = seq_starts(lengths_row, positions)

        def run_layer(param_tuple, rows_in):
            return layer_forward(param_tuple, rows_in, positions, starts)
        out_rows, pull_back = jax.vjp(run_layer, params, feat_rows.astype(jnp.float32))
        grad_params, grad_feat = pull_back(cot_rows.astype(jnp.float32))
        whole_sums = jax.tree.map(jnp.add, whole_sums, grad_params)
        return (whole_sums, (out_rows.astype(jnp.bfloat16), grad_feat.astype(jnp.bfloat16)))
    sums_zero = tuple((jnp.zeros(tensor.shape, jnp.float32) for tensor in params))
    whole_sums, (layer_rows, grad_rows) = lax.scan(one_stream, sums_zero, (inputs.reshape(streams, GTOK, D), cotangent.reshape(streams, GTOK, D), lengths.reshape(streams, NSEQ)))
    g_norm1, g_in, g_dt, g_conv_w, g_conv_b, g_dt_bias, g_decay, g_skip, g_mamba, g_out, g_query, g_kv, g_o, g_norm2, g_gu, g_down = whole_sums
    layer_out = layer_rows.reshape(MB, GROUPS, GTOK, D)
    input_grad = grad_rows.reshape(MB, GROUPS, GTOK, D)
    return (layer_out, input_grad, g_norm1, g_in, g_dt, g_conv_w, g_conv_b, g_dt_bias, g_decay, g_skip, g_mamba, g_out, g_query, g_kv, g_o, g_norm2, g_gu, g_down)
```

```python
import functools

import jax
import jax.numpy as jnp
from jax import lax
from jax.experimental import pallas as pl
from jax.experimental.pallas import tpu as pltpu
from jax.sharding import PartitionSpec as P

FF = 2048
MHEADS = 24
MDIM = 64
STATE = 128
QHEADS = 8
KVHEADS = 2
HDIM = 64
DSSM = 1536
HGROUP = 8
NGROUP = MHEADS // HGROUP
GWIDTH = HGROUP * MDIM
PAIR = 2 * MDIM

NORM_EPS = 1e-05
PRECISE = lax.Precision.HIGHEST
MASKED_SCORE = -1e30
MIB = 2**20
F32 = jnp.float32
BF16 = jnp.bfloat16


def dot_as(left, right, left_dim, right_dim):
    return lax.dot_general(
        left, right, (((left_dim,), (right_dim,)), ((), ())), preferred_element_type=F32
    )


def mat(left, right):
    return dot_as(left, right, 1, 0)


def mat_left_t(left, right):
    return dot_as(left, right, 0, 0)


def mat_right_t(left, right):
    return dot_as(left, right, 1, 1)


def inv_rms(rows):
    return lax.rsqrt(jnp.mean(rows * rows, axis=-1, keepdims=True) + NORM_EPS)


def rms_pull(rows, scale, gain, grad):
    scaled = rows * scale
    grad_gain = jnp.sum(grad * scaled, axis=0)
    through = grad * gain
    inner = jnp.mean(through * scaled, axis=-1, keepdims=True)
    return scale * (through - scaled * inner), grad_gain


def seq_starts(lengths_row, positions):
    begins = jnp.cumsum(lengths_row, dtype=jnp.int32) - lengths_row
    picked = jnp.where(begins[None, :] <= positions[:, None], begins[None, :], 0)
    return jnp.max(picked, axis=1)


def head_lanes(rows):
    return lax.broadcasted_iota(jnp.int32, (rows, PAIR), 1) < MDIM


def masked_products(b_low, c_low, rel_start):
    rows = b_low.shape[0]
    at_row = lax.broadcasted_iota(jnp.int32, (rows, rows), 0)
    at_col = lax.broadcasted_iota(jnp.int32, (rows, rows), 1)
    allowed = (at_col <= at_row) & (at_col >= rel_start)
    return allowed, jnp.where(allowed, mat_right_t(c_low, b_low), 0.0)


def pair_columns(first_half, columns, head):
    return jnp.where(first_half, columns[:, head : head + 1], columns[:, head + 1 : head + 2])


def ssd_forward_kernel(
    x_ref, b_ref, c_ref, step_ref, decay_ref, decay_t_ref, start_ref, state_ref, skip_ref, y_ref
):
    rows = x_ref.shape[1]
    b_low = b_ref[0].astype(BF16)
    c_low = c_ref[0].astype(BF16)
    rel_start = start_ref[0]
    _, products = masked_products(b_low, c_low, rel_start)
    incoming = mat_right_t(c_low, state_ref[0].astype(BF16))
    first_half = head_lanes(rows)
    steps = step_ref[0, 0]
    decay = decay_ref[0, 0]
    reach = jnp.where(rel_start < 0, jnp.exp(decay), 0.0)
    for head in range(0, HGROUP, 2):
        lanes = slice(head * MDIM, head * MDIM + PAIR)
        x_pair = x_ref[0, :, lanes]
        scaled = (x_pair * pair_columns(first_half, steps, head)).astype(BF16)
        parts = []
        for one in (head, head + 1):
            gaps = decay[:, one : one + 1] - decay_t_ref[0, 0, one : one + 1, :]
            weights = (jnp.exp(jnp.minimum(gaps, 0.0)) * products).astype(BF16)
            parts.append(mat(weights, scaled))
        y_ref[0, :, lanes] = (
            jnp.where(first_half, parts[0], parts[1])
            + pair_columns(first_half, reach, head) * incoming[:, lanes]
            + skip_ref[:, lanes] * x_pair
        )


def ssd_backward_kernel(
    x_ref,
    b_ref,
    c_ref,
    step_ref,
    decay_ref,
    decay_t_ref,
    start_ref,
    state_ref,
    skip_ref,
    y_ref,
    dy_ref,
    later_ref,
    keep_ref,
    dx_ref,
    db_ref,
    dc_ref,
    row_ref,
    u_ref,
    v_ref,
    dskip_ref,
    one_sum,
    two_sum,
    three_sum,
    mixed_y,
    mixed_x,
):
    rows = x_ref.shape[1]
    b_low = b_ref[0].astype(BF16)
    c_low = c_ref[0].astype(BF16)
    rel_start = start_ref[0]
    allowed, products = masked_products(b_low, c_low, rel_start)
    state_low = state_ref[0].astype(BF16)
    later_low = later_ref[0].astype(BF16)
    spread = mat_right_t(b_low, later_low)
    first_half = head_lanes(rows)
    steps = step_ref[0, 0]
    decay = decay_ref[0, 0]
    reach = jnp.where(rel_start < 0, jnp.exp(decay), 0.0)
    to_end = jnp.exp(decay[rows - 1 : rows, :] - decay) * steps * keep_ref[0]
    product_grad = jnp.zeros((rows, rows), F32)
    for head in range(0, HGROUP, 2):
        lanes = slice(head * MDIM, head * MDIM + PAIR)
        x_pair = x_ref[0, :, lanes]
        dy_pair = dy_ref[0, :, lanes]
        step_pair = pair_columns(first_half, steps, head)
        scaled = (x_pair * step_pair).astype(BF16)
        dy_low = dy_pair.astype(BF16)
        parts = []
        for one in (head, head + 1):
            gaps = decay[:, one : one + 1] - decay_t_ref[0, 0, one : one + 1, :]
            decays = jnp.exp(jnp.minimum(gaps, 0.0))
            mine = first_half if one == head else ~first_half
            dy_mine = jnp.where(mine, dy_pair, 0.0).astype(BF16)
            weight_grad = mat_right_t(dy_mine, scaled)
            product_grad = product_grad + weight_grad * decays
            parts.append(mat_left_t((decays * products).astype(BF16), dy_low))
        dz_pair = jnp.where(first_half, parts[0], parts[1])
        skip_pair = skip_ref[:, lanes]
        end_pair = pair_columns(first_half, to_end, head)
        spread_pair = spread[:, lanes]
        dx_ref[0, :, lanes] = skip_pair * dy_pair + step_pair * dz_pair + end_pair * spread_pair
        one_sum[:, lanes] = dy_pair * (y_ref[0, :, lanes] - skip_pair * x_pair)
        two_sum[:, lanes] = x_pair * dz_pair
        three_sum[:, lanes] = x_pair * spread_pair
        mixed_y[:, lanes] = (dy_pair * pair_columns(first_half, reach, head)).astype(BF16)
        mixed_x[:, lanes] = (x_pair * end_pair).astype(BF16)
        dskip_ref[0, 0, :, lanes] = jnp.sum(dy_pair * x_pair, axis=0, keepdims=True)
    grad_low = jnp.where(allowed, product_grad, 0.0).astype(BF16)
    dc = mat(grad_low, b_low) + mat(mixed_y[...], state_low)
    db = mat_left_t(grad_low, c_low) + mat(mixed_x[...], later_low)
    group = pl.program_id(1)

    @pl.when(group == 0)
    def _():
        dc_ref[0] = dc
        db_ref[0] = db

    @pl.when(group > 0)
    def _():
        dc_ref[0] += dc
        db_ref[0] += db

    owner = lax.broadcasted_iota(jnp.int32, (GWIDTH, 128), 0) // MDIM
    picks = (owner == lax.broadcasted_iota(jnp.int32, (GWIDTH, 128), 1)).astype(F32)
    for source, target in ((one_sum, row_ref), (two_sum, u_ref), (three_sum, v_ref)):
        sums = lax.dot_general(
            source[...],
            picks,
            (((1,), (0,)), ((), ())),
            precision=PRECISE,
            preferred_element_type=F32,
        )
        target[0, 0] = sums[:, :HGROUP]


def ssd_specs(rows):
    wide = pl.BlockSpec((1, rows, GWIDTH), lambda b, g: (b, 0, g))
    narrow = pl.BlockSpec((1, rows, STATE), lambda b, g: (b, 0, 0))
    heads = pl.BlockSpec((1, 1, rows, HGROUP), lambda b, g: (b, g, 0, 0))
    heads_t = pl.BlockSpec((1, 1, HGROUP, rows), lambda b, g: (b, g, 0, 0))
    column = pl.BlockSpec((1, rows, 1), lambda b, g: (b, 0, 0))
    state = pl.BlockSpec((1, GWIDTH, STATE), lambda b, g: (b, g, 0))
    skip = pl.BlockSpec((1, GWIDTH), lambda b, g: (0, g))
    return wide, narrow, heads, heads_t, column, state, skip


def ssd_forward(inner, b_rows, c_rows, steps, decay, decay_t, rel_start, state_in, skip_row):
    count, rows, _ = inner.shape
    wide, narrow, heads, heads_t, column, state, skip = ssd_specs(rows)
    return pl.pallas_call(
        ssd_forward_kernel,
        grid=(count, NGROUP),
        in_specs=[wide, narrow, narrow, heads, heads, heads_t, column, state, skip],
        out_specs=wide,
        out_shape=jax.ShapeDtypeStruct(inner.shape, F32),
        compiler_params=pltpu.CompilerParams(vmem_limit_bytes=40 * MIB),
        cost_estimate=pl.CostEstimate(
            flops=count * MHEADS * rows * rows * 400, bytes_accessed=8 * MIB, transcendentals=0
        ),
        name="ssd_forward",
    )(inner, b_rows, c_rows, steps, decay, decay_t, rel_start, state_in, skip_row)


def ssd_backward(
    inner,
    b_rows,
    c_rows,
    steps,
    decay,
    decay_t,
    rel_start,
    state_in,
    skip_row,
    scanned,
    grad_scanned,
    later,
    keep,
):
    count, rows, _ = inner.shape
    wide, narrow, heads, heads_t, column, state, skip = ssd_specs(rows)
    head_shape = jax.ShapeDtypeStruct((count, NGROUP, rows, HGROUP), F32)
    return pl.pallas_call(
        ssd_backward_kernel,
        grid=(count, NGROUP),
        in_specs=[
            wide,
            narrow,
            narrow,
            heads,
            heads,
            heads_t,
            column,
            state,
            skip,
            wide,
            wide,
            state,
            column,
        ],
        out_specs=[
            wide,
            narrow,
            narrow,
            heads,
            heads,
            heads,
            pl.BlockSpec((1, 1, 1, GWIDTH), lambda b, g: (b, g, 0, 0)),
        ],
        out_shape=[
            jax.ShapeDtypeStruct(inner.shape, F32),
            jax.ShapeDtypeStruct(b_rows.shape, F32),
            jax.ShapeDtypeStruct(b_rows.shape, F32),
            head_shape,
            head_shape,
            head_shape,
            jax.ShapeDtypeStruct((count, NGROUP, 1, GWIDTH), F32),
        ],
        scratch_shapes=[pltpu.VMEM((rows, GWIDTH), F32)] * 3
        + [pltpu.VMEM((rows, GWIDTH), BF16)] * 2,
        compiler_params=pltpu.CompilerParams(vmem_limit_bytes=40 * MIB),
        cost_estimate=pl.CostEstimate(
            flops=count * MHEADS * rows * rows * 1000, bytes_accessed=16 * MIB, transcendentals=0
        ),
        name="ssd_backward",
    )(
        inner,
        b_rows,
        c_rows,
        steps,
        decay,
        decay_t,
        rel_start,
        state_in,
        skip_row,
        scanned,
        grad_scanned,
        later,
        keep,
    )


def spread_heads(source_ref, target, factor):
    width = source_ref.shape[1]
    target[...] = jnp.zeros(target.shape, target.dtype)
    for head in range(QHEADS):
        group = head // (QHEADS // KVHEADS)
        value = source_ref[head * HDIM : (head + 1) * HDIM, :]
        target[group * HDIM : (group + 1) * HDIM, head * width : (head + 1) * width] = (
            value * factor if factor != 1.0 else value
        )


def attend_allowed(block, first_pos, starts, width):
    key_pos = block * width + lax.broadcasted_iota(jnp.int32, (width, width), 0)
    query_pos = first_pos + lax.broadcasted_iota(jnp.int32, (width, width), 1)
    return (key_pos <= query_pos) & (key_pos >= starts)


def attend_forward_kernel(bounds, start_ref, q_ref, kv_ref, out_ref, log_ref, q_wide, top, total, acc):
    width = q_ref.shape[1]
    batch = pl.program_id(0)
    spread_heads(q_ref, q_wide, HDIM**-0.5)
    top[...] = jnp.full(top.shape, MASKED_SCORE, F32)
    total[...] = jnp.zeros(total.shape, F32)
    acc[...] = jnp.zeros(acc.shape, F32)
    last = bounds[pl.num_programs(0)]
    first_pos = (last - 1) * width

    def one_block(block, carry):
        kv_rows = kv_ref[bounds[pl.num_programs(0) + 1 + block], 0]
        keys = kv_rows[:, : KVHEADS * HDIM]
        values_t = kv_rows[:, KVHEADS * HDIM :].T
        allowed = attend_allowed(block, first_pos, start_ref[0], width)
        for head in range(QHEADS):
            group = head // (QHEADS // KVHEADS)
            scores = mat(keys, q_wide[:, head * width : (head + 1) * width])
            scores = jnp.where(allowed, scores, MASKED_SCORE)
            old = top[head : head + 1, :]
            new = jnp.maximum(old, jnp.max(scores, axis=0, keepdims=True))
            terms = jnp.exp(scores - new)
            shrink = jnp.exp(old - new)
            top[head : head + 1, :] = new
            total[head : head + 1, :] = total[head : head + 1, :] * shrink + jnp.sum(
                terms, axis=0, keepdims=True
            )
            acc[head] = acc[head] * shrink + mat(
                values_t[group * HDIM : (group + 1) * HDIM, :], terms.astype(BF16)
            )
        return carry

    lax.fori_loop(bounds[batch], last, one_block, 0)
    for head in range(QHEADS):
        out_ref[head * HDIM : (head + 1) * HDIM, :] = (
            acc[head] / total[head : head + 1, :]
        ).astype(BF16)
    log_ref[0] = top[...] + jnp.log(total[...])


def attend_forward(bounds, starts, queries_t, key_table):
    blocks, count, width, kv_width = key_table.shape
    column = pl.BlockSpec((QHEADS * HDIM, width), lambda b, s: (0, b))
    logs = pl.BlockSpec((1, QHEADS, width), lambda b, s: (b, 0, 0))
    return pl.pallas_call(
        attend_forward_kernel,
        grid_spec=pltpu.PrefetchScalarGridSpec(
            num_scalar_prefetch=1,
            grid=(count,),
            in_specs=[
                pl.BlockSpec((1, 1, width), lambda b, s: (b, 0, 0)),
                column,
                pl.BlockSpec((blocks, 1, width, kv_width), lambda b, s: (0, b, 0, 0)),
            ],
            out_specs=[column, logs],
            scratch_shapes=[
                pltpu.VMEM((KVHEADS * HDIM, QHEADS * width), BF16),
                pltpu.VMEM((QHEADS, width), F32),
                pltpu.VMEM((QHEADS, width), F32),
                pltpu.VMEM((QHEADS, HDIM, width), F32),
            ],
        ),
        out_shape=[
            jax.ShapeDtypeStruct(queries_t.shape, BF16),
            jax.ShapeDtypeStruct((count, QHEADS, width), F32),
        ],
        compiler_params=pltpu.CompilerParams(vmem_limit_bytes=40 * MIB),
        cost_estimate=pl.CostEstimate(
            flops=count * blocks * width * width * 8 * 1000,
            bytes_accessed=4 * MIB,
            transcendentals=0,
        ),
        name="attend_forward",
    )(bounds, starts, queries_t, key_table)


def attend_backward_kernel(
    bounds,
    start_ref,
    q_ref,
    kv_ref,
    out_ref,
    grad_ref,
    log_ref,
    dq_ref,
    dkv_ref,
    q_wide,
    g_wide,
    q_tall,
    g_tall,
    delta,
    acc,
):
    width = q_ref.shape[1]
    kv_width = KVHEADS * HDIM
    batch = pl.program_id(0)
    spread_heads(q_ref, q_wide, HDIM**-0.5)
    spread_heads(grad_ref, g_wide, 1.0)
    acc[...] = jnp.zeros(acc.shape, F32)
    dkv_ref[...] = jnp.zeros(dkv_ref.shape, BF16)
    for head in range(QHEADS):
        columns = slice(head * width, (head + 1) * width)
        q_tall[columns, :] = q_wide[:, columns].T
        g_tall[columns, :] = g_wide[:, columns].T
        span = slice(head * HDIM, (head + 1) * HDIM)
        delta[head : head + 1, :] = jnp.sum(
            out_ref[span, :].astype(F32) * grad_ref[span, :].astype(F32), axis=0, keepdims=True
        )
    last = bounds[pl.num_programs(0)]
    first_pos = (last - 1) * width

    def one_block(block, carry):
        place = bounds[pl.num_programs(0) + 1 + block]
        kv_rows = kv_ref[place, 0]
        keys = kv_rows[:, :kv_width]
        values = kv_rows[:, kv_width:]
        keys_t = keys.T
        allowed = attend_allowed(block, first_pos, start_ref[0], width)
        dk = jnp.zeros((width, kv_width), F32)
        dv = jnp.zeros((width, kv_width), F32)
        for head in range(QHEADS):
            group = head // (QHEADS // KVHEADS)
            columns = slice(head * width, (head + 1) * width)
            scores = mat(keys, q_wide[:, columns])
            shifted = jnp.where(allowed, scores - log_ref[0, head : head + 1, :], MASKED_SCORE)
            probs = jnp.exp(shifted)
            grad_probs = mat(values, g_wide[:, columns])
            grad_scores = (probs * (grad_probs - delta[head : head + 1, :])).astype(BF16)
            dk = dk + mat(grad_scores, q_tall[columns, :])
            dv = dv + mat(probs.astype(BF16), g_tall[columns, :])
            acc[head] += mat(keys_t[group * HDIM : (group + 1) * HDIM, :], grad_scores)
        dkv_ref[place, 0] = jnp.concatenate([dk, dv], axis=1).astype(BF16)
        return carry

    lax.fori_loop(bounds[batch], last, one_block, 0)
    for head in range(QHEADS):
        dq_ref[head * HDIM : (head + 1) * HDIM, :] = (acc[head] * HDIM**-0.5).astype(BF16)


def attend_backward(bounds, starts, queries_t, key_table, out_t, grad_t, logs):
    blocks, count, width, kv_width = key_table.shape
    column = pl.BlockSpec((QHEADS * HDIM, width), lambda b, s: (0, b))
    table = pl.BlockSpec((blocks, 1, width, kv_width), lambda b, s: (0, b, 0, 0))
    wide = pltpu.VMEM((KVHEADS * HDIM, QHEADS * width), BF16)
    tall = pltpu.VMEM((QHEADS * width, KVHEADS * HDIM), BF16)
    return pl.pallas_call(
        attend_backward_kernel,
        grid_spec=pltpu.PrefetchScalarGridSpec(
            num_scalar_prefetch=1,
            grid=(count,),
            in_specs=[
                pl.BlockSpec((1, 1, width), lambda b, s: (b, 0, 0)),
                column,
                table,
                column,
                column,
                pl.BlockSpec((1, QHEADS, width), lambda b, s: (b, 0, 0)),
            ],
            out_specs=[column, table],
            scratch_shapes=[
                wide,
                wide,
                tall,
                tall,
                pltpu.VMEM((QHEADS, width), F32),
                pltpu.VMEM((QHEADS, HDIM, width), F32),
            ],
        ),
        out_shape=[
            jax.ShapeDtypeStruct(queries_t.shape, BF16),
            jax.ShapeDtypeStruct(key_table.shape, BF16),
        ],
        compiler_params=pltpu.CompilerParams(vmem_limit_bytes=48 * MIB),
        cost_estimate=pl.CostEstimate(
            flops=count * blocks * width * width * 8 * 2000,
            bytes_accessed=8 * MIB,
            transcendentals=0,
        ),
        name="attend_backward",
    )(bounds, starts, queries_t, key_table, out_t, grad_t, logs)


def passed_along(block, axis, distance):
    devices = range(lax.axis_size(axis))
    route = [(i - distance, i) for i in devices if i - distance in devices]
    return lax.ppermute(block, axis, route)


def swapped(block, axis, bit):
    return lax.ppermute(block, axis, [(i, i ^ bit) for i in range(lax.axis_size(axis))])


def bits_of(axis):
    return [1 << k for k in range(lax.axis_size(axis).bit_length() - 1)]


def gathered_near(shard):
    half = jnp.concatenate([shard, swapped(shard, "wsh", 2)], axis=0)
    return jnp.concatenate([half, swapped(half, "wsh", 1)], axis=0)


def near_order(array, axis):
    here = lax.axis_index("wsh")
    block = array.shape[axis] // 4
    return jnp.concatenate(
        [
            lax.dynamic_slice_in_dim(array, (here ^ step) * block, block, axis)
            for step in (0, 2, 1, 3)
        ],
        axis=axis,
    )


def natural_order(array, axis):
    here = lax.axis_index("wsh")
    block = array.shape[axis] // 4
    places = []
    for index in range(4):
        step = here ^ index
        place = jnp.where(step == 1, 2, jnp.where(step == 2, 1, step))
        places.append(lax.dynamic_slice_in_dim(array, place * block, block, axis))
    return jnp.concatenate(places, axis=axis)


def reduced_over_wsh(send, keep):
    came = swapped(send.astype(BF16), "wsh", 1)
    both = keep + came.astype(F32)
    block = both.shape[0] // 2
    crossed = swapped(both[block:].astype(BF16), "wsh", 2)
    return both[:block] + crossed.astype(F32)


def pick_half(array, upper):
    half = array.shape[0] // 2
    return lax.dynamic_slice_in_dim(array, upper * half, half, 0)


def joined(mine, other, upper):
    return jnp.where(
        upper == 1,
        jnp.concatenate([other, mine], axis=0),
        jnp.concatenate([mine, other], axis=0),
    )


def summed_over_ctx(part):
    here = lax.axis_index("ctx")
    bits = bits_of("ctx")
    for bit in bits:
        upper = (here // bit) % 2
        came = swapped(pick_half(part, 1 - upper).astype(BF16), "ctx", bit)
        part = pick_half(part, upper) + came.astype(F32)
    part = part.astype(BF16)
    for bit in bits[::-1]:
        part = joined(part, swapped(part, "ctx", bit), (here // bit) % 2)
    return part.astype(F32)


def summed_everywhere(vector):
    for axis in ("wsh", "ctx"):
        for bit in bits_of(axis):
            vector = vector + swapped(vector, axis, bit)
    return vector


def table_gather(rows):
    table = rows[None]
    for bit in bits_of("ctx")[::-1]:
        table = jnp.concatenate([table, swapped(table, "ctx", bit)], axis=0)
    return table


def table_places(here, count):
    bits = count.bit_length() - 1
    apart = jnp.arange(count, dtype=jnp.int32) ^ here
    return sum(((apart >> bit) & 1) << (bits - 1 - bit) for bit in range(bits))


def table_scatter(table):
    for bit in bits_of("ctx"):
        half = table.shape[0] // 2
        table = (
            table[:half].astype(F32) + swapped(table[half:], "ctx", bit).astype(F32)
        ).astype(BF16)
    return table[0]


def widened_rows(factor):
    return jnp.repeat(factor, MDIM, axis=1)[..., None]


def chain_scan(total, state, forward):
    here = lax.axis_index("ctx")
    bits = bits_of("ctx")
    reached = jnp.zeros_like(state)
    reach = jnp.ones_like(total)
    for bit in bits:
        late = ((here // bit) % 2 == 1) == forward
        other_total = swapped(total, "ctx", bit)
        other = swapped(state.astype(BF16), "ctx", bit).astype(F32)
        reached = jnp.where(late, reached + widened_rows(reach) * other, reached)
        reach = jnp.where(late, reach * other_total, reach)
        state = jnp.where(
            late,
            widened_rows(total) * other + state,
            widened_rows(other_total) * state + other,
        )
        total = total * other_total
    return reached


def local(
    inputs,
    cotangent,
    lengths,
    norm1_gain,
    in_weight,
    dt_weight,
    conv_weight,
    conv_bias,
    dt_bias,
    decay_rate,
    skip_gain,
    mamba_gain,
    out_weight,
    q_weight,
    kv_weight,
    o_weight,
    norm2_gain,
    gu_weight,
    down_weight,
):
    count, _, rows, features = inputs.shape
    here = lax.axis_index("ctx")
    ctx_count = lax.axis_size("ctx")
    tokens = count * rows
    first_pos = here * rows
    own_pos = first_pos + jnp.arange(rows, dtype=jnp.int32)
    starts = jax.vmap(lambda row: seq_starts(row, own_pos))(lengths[:, 0])
    rel_start = starts - first_pos
    taps = conv_weight.shape[0]

    full_kv, full_in, full_dt, full_q, full_out, full_o, full_gu, full_down = [
        gathered_near(shard)
        for shard in (
            kv_weight,
            in_weight,
            dt_weight,
            q_weight,
            out_weight,
            o_weight,
            gu_weight,
            down_weight,
        )
    ]

    x = inputs.reshape(tokens, features).astype(F32)
    scale_one = inv_rms(x)
    normed = near_order((x * scale_one * norm1_gain).astype(BF16), 1)
    kv_rows = mat(normed, full_kv).astype(BF16)
    key_table = table_gather(kv_rows.reshape(count, rows, -1))
    projected = mat(normed, full_in)
    gate_z = projected[:, :DSSM]
    conv_rows = projected[:, DSSM:].reshape(count, rows, -1)
    dt_raw = mat(normed, full_dt) + dt_bias
    steps = jax.nn.softplus(dt_raw).reshape(count, rows, MHEADS)
    edge = passed_along(conv_rows[:, rows - taps + 1 :], "ctx", 1)
    extended = jnp.concatenate([edge, conv_rows], axis=1)
    valid = [
        (own_pos[None] - (taps - 1) + tap >= starts).astype(F32)[..., None] for tap in range(taps)
    ]
    conv_sum = jnp.zeros_like(conv_rows) + conv_bias
    for tap in range(taps):
        conv_sum = conv_sum + conv_weight[tap] * extended[:, tap : tap + rows] * valid[tap]
    conv_gate = jax.nn.sigmoid(conv_sum)
    activated = conv_sum * conv_gate
    inner = activated[..., :DSSM]
    b_rows = activated[..., DSSM : DSSM + STATE]
    c_rows = activated[..., DSSM + STATE :]

    lower = (own_pos[:, None] >= own_pos[None, :]).astype(F32)
    drop = -steps * decay_rate
    decay = jnp.einsum("ik,bkh->bih", lower, drop, precision=PRECISE)
    end = decay[:, -1:]
    keep = (own_pos[None] >= starts[:, -1:]).astype(F32)[..., None]
    to_end = jnp.exp(end - decay) * keep
    reach = jnp.where(rel_start[..., None] < 0, jnp.exp(decay), 0.0)
    carried = (starts[:, -1:] < first_pos).astype(F32)
    total = jnp.exp(end[:, 0]) * carried

    def grouped(columns):
        return columns.reshape(count, rows, NGROUP, HGROUP).transpose(0, 2, 1, 3)

    def ungrouped(columns):
        return columns.transpose(0, 2, 1, 3).reshape(count, rows, MHEADS)

    def widened(columns):
        return jnp.repeat(columns, MDIM, axis=-1)

    def outer(left, right):
        return jnp.einsum(
            "bti,btn->bin", left.astype(BF16), right.astype(BF16), preferred_element_type=F32
        )

    fresh = outer(inner * widened(to_end * steps), b_rows)
    state_in = chain_scan(total, fresh, True)

    queries_t = dot_as(full_q, normed, 0, 1).astype(BF16)
    bounds = jnp.concatenate(
        [starts[:, 0] // rows, jnp.full((1,), here + 1, jnp.int32), table_places(here, ctx_count)]
    )
    starts_row = starts[:, None, :]
    attended_t, logs = attend_forward(bounds, starts_row, queries_t, key_table)

    steps_g = grouped(steps)
    decay_g = grouped(decay)
    decay_t = decay_g.transpose(0, 1, 3, 2)
    skip_row = widened(skip_gain)[None]
    rel_column = rel_start[..., None]
    scanned = ssd_forward(
        inner, b_rows, c_rows, steps_g, decay_g, decay_t, rel_column, state_in, skip_row
    )
    flat = scanned.reshape(tokens, DSSM)
    gate_sig = jax.nn.sigmoid(gate_z)
    gated = flat * gate_z * gate_sig
    scale_m = inv_rms(gated)
    mixed = near_order((gated * scale_m * mamba_gain).astype(BF16), 1)
    attended_near = near_order(attended_t, 0)
    middle = x + mat(mixed, full_out) + mat_left_t(attended_near, full_o)
    scale_two = inv_rms(middle)
    normed_two = near_order((middle * scale_two * norm2_gain).astype(BF16), 1)
    gate_up = mat(normed_two, full_gu)
    gate_part = gate_up[:, :FF]
    up_part = gate_up[:, FF:]
    sig = jax.nn.sigmoid(gate_part)
    hidden = near_order((gate_part * sig * up_part).astype(BF16), 1)
    layer_out = (middle + mat(hidden, full_down)).astype(BF16)

    grad_top = cotangent.reshape(tokens, features)
    half = hidden.shape[1] // 2
    down_shard = reduced_over_wsh(
        mat_left_t(hidden[:, half:], grad_top), mat_left_t(hidden[:, :half], grad_top)
    )
    grad_hidden = natural_order(mat_right_t(grad_top, full_down), 1)
    grad_gate = grad_hidden * up_part * sig * (1.0 + gate_part * (1.0 - sig))
    grad_up = grad_hidden * gate_part * sig
    grad_gu_rows = jnp.concatenate([grad_gate, grad_up], axis=1).astype(BF16)
    half = normed_two.shape[1] // 2
    gu_shard = reduced_over_wsh(
        mat_left_t(normed_two[:, half:], grad_gu_rows),
        mat_left_t(normed_two[:, :half], grad_gu_rows),
    )
    grad_two, grad_norm2 = rms_pull(
        middle, scale_two, norm2_gain, natural_order(mat_right_t(grad_gu_rows, full_gu), 1)
    )
    grad_middle = grad_top.astype(F32) + grad_two
    branch = grad_middle.astype(BF16)
    half = attended_near.shape[0] // 2
    o_shard = reduced_over_wsh(mat(attended_near[half:], branch), mat(attended_near[:half], branch))
    grad_attended_t = natural_order(dot_as(full_o, branch, 1, 1).astype(BF16), 0)
    half = mixed.shape[1] // 2
    out_shard = reduced_over_wsh(
        mat_left_t(mixed[:, half:], branch), mat_left_t(mixed[:, :half], branch)
    )
    grad_mixed = natural_order(mat_right_t(branch, full_out), 1)
    grad_gated, grad_mamba = rms_pull(gated, scale_m, mamba_gain, grad_mixed)
    grad_gate_z = grad_gated * flat * gate_sig * (1.0 + gate_z * (1.0 - gate_sig))
    grad_scanned = (grad_gated * gate_z * gate_sig).reshape(count, rows, DSSM)
    grad_state = outer(grad_scanned * widened(reach), c_rows)
    later = chain_scan(total, grad_state, False)

    dq_t, dkv_table = attend_backward(
        bounds, starts_row, queries_t, key_table, attended_t, grad_attended_t, logs
    )
    grad_kv_rows = table_scatter(dkv_table).reshape(tokens, -1)
    dx, db, dc, row_dot, u_dot, v_dot, dskip = ssd_backward(
        inner,
        b_rows,
        c_rows,
        steps_g,
        decay_g,
        decay_t,
        rel_column,
        state_in,
        skip_row,
        scanned,
        grad_scanned,
        later,
        keep,
    )
    row_dot, u_dot, v_dot = ungrouped(row_dot), ungrouped(u_dot), ungrouped(v_dot)
    to_last = v_dot * to_end * steps
    grad_total = jnp.sum((later * state_in).reshape(count, MHEADS, MDIM * STATE), axis=-1) * total
    grad_decay = row_dot - u_dot * steps - to_last
    grad_drop = (
        jnp.einsum("ki,bkh->bih", lower, grad_decay, precision=PRECISE)
        + (jnp.sum(to_last, axis=1) + grad_total)[:, None]
    )
    grad_rate = jnp.sum(-steps * grad_drop, axis=(0, 1))
    grad_steps = u_dot + v_dot * to_end - decay_rate * grad_drop
    grad_dt_raw = grad_steps.reshape(tokens, MHEADS) * jax.nn.sigmoid(dt_raw)
    grad_dt_bias = jnp.sum(grad_dt_raw, axis=0)
    dt_low = grad_dt_raw.astype(BF16)
    grad_skip = jnp.sum(dskip.reshape(count, MHEADS, MDIM), axis=(0, 2))

    grad_act = jnp.concatenate([dx, db, dc], axis=-1)
    grad_conv = grad_act * conv_gate * (1.0 + conv_sum * (1.0 - conv_gate))
    grad_conv_b = jnp.sum(grad_conv, axis=(0, 1))
    grad_conv_w = jnp.stack(
        [
            jnp.sum(grad_conv * extended[:, tap : tap + rows] * valid[tap], axis=(0, 1))
            for tap in range(taps)
        ]
    )
    grad_extended = jnp.zeros_like(extended)
    for tap in range(taps):
        grad_extended = grad_extended + jnp.pad(
            conv_weight[tap] * grad_conv * valid[tap], ((0, 0), (tap, taps - 1 - tap), (0, 0))
        )
    edge_back = passed_along(grad_extended[:, : taps - 1], "ctx", -1)
    grad_conv_rows = grad_extended[:, taps - 1 :] + jnp.pad(
        edge_back, ((0, 0), (rows - taps + 1, 0), (0, 0))
    )
    grad_proj = jnp.concatenate(
        [grad_gate_z, grad_conv_rows.reshape(tokens, -1)], axis=1
    ).astype(BF16)
    half = features // 2

    def shard_sum(grad, dim):
        return reduced_over_wsh(
            dot_as(normed[:, half:], grad, 0, dim), dot_as(normed[:, :half], grad, 0, dim)
        )

    q_shard = shard_sum(dq_t, 1)
    kv_shard = shard_sum(grad_kv_rows, 0)
    dt_shard = shard_sum(dt_low, 0)
    in_shard = shard_sum(grad_proj, 0)
    grad_normed = (
        dot_as(dq_t, full_q, 0, 1)
        + mat_right_t(grad_kv_rows, full_kv)
        + mat_right_t(grad_proj, full_in)
        + mat_right_t(dt_low, full_dt)
    )
    grad_normed = natural_order(grad_normed, 1)
    grad_one, grad_norm1 = rms_pull(x, scale_one, norm1_gain, grad_normed)
    input_grad = (grad_middle + grad_one).astype(BF16)

    totals_w = [
        summed_over_ctx(shard)
        for shard in (in_shard, dt_shard, out_shard, q_shard, kv_shard, o_shard, gu_shard, down_shard)
    ]
    pieces = (
        grad_norm1,
        grad_conv_w,
        grad_conv_b,
        grad_dt_bias,
        grad_rate,
        grad_skip,
        grad_mamba,
        grad_norm2,
    )
    packed = jnp.concatenate([piece.reshape(-1) for piece in pieces])
    packed = jnp.pad(packed, (0, -packed.size % 1024)).reshape(-1, 128)
    packed = summed_everywhere(packed).reshape(-1)
    small = []
    place = 0
    for piece in pieces:
        small.append(packed[place : place + piece.size].reshape(piece.shape))
        place += piece.size
    shape = (count, 1, rows, features)
    return (
        layer_out.reshape(shape),
        input_grad.reshape(shape),
        small[0],
        totals_w[0],
        totals_w[1],
        small[1],
        small[2],
        small[3],
        small[4],
        small[5],
        small[6],
        totals_w[2],
        totals_w[3],
        totals_w[4],
        totals_w[5],
        small[7],
        totals_w[6],
        totals_w[7],
    )


def solution(mesh):
    stream = P(None, "wsh", "ctx", None)
    shard = P("wsh", None)
    in_specs = (
        stream,
        stream,
        P(None, "wsh", None),
        P(),
        shard,
        shard,
        P(),
        P(),
        P(),
        P(),
        P(),
        P(),
        shard,
        shard,
        shard,
        shard,
        P(),
        shard,
        shard,
    )
    out_specs = (
        stream,
        stream,
        P(),
        shard,
        shard,
        P(),
        P(),
        P(),
        P(),
        P(),
        P(),
        shard,
        shard,
        shard,
        shard,
        P(),
        shard,
        shard,
    )
    return jax.shard_map(local, mesh=mesh, in_specs=in_specs, out_specs=out_specs, check_vma=False)
```

```python
import functools

import jax
import jax.numpy as jnp
from jax import lax
from jax.experimental import pallas as pl
from jax.experimental.pallas import tpu as pltpu
from jax.sharding import PartitionSpec as P

FF = 2048
MHEADS = 24
MDIM = 64
STATE = 128
QHEADS = 8
KVHEADS = 2
HDIM = 64
DSSM = 1536
HGROUP = 8
NGROUP = MHEADS // HGROUP
GWIDTH = HGROUP * MDIM
PAIR = 2 * MDIM

NORM_EPS = 1e-05
PRECISE = lax.Precision.HIGHEST
MASKED_SCORE = -1e30
MIB = 2**20
F32 = jnp.float32
BF16 = jnp.bfloat16


def dot_as(left, right, left_dim, right_dim):
    return lax.dot_general(
        left, right, (((left_dim,), (right_dim,)), ((), ())), preferred_element_type=F32
    )


def mat(left, right):
    return dot_as(left, right, 1, 0)


def mat_left_t(left, right):
    return dot_as(left, right, 0, 0)


def mat_right_t(left, right):
    return dot_as(left, right, 1, 1)


def inv_rms(rows):
    return lax.rsqrt(jnp.mean(rows * rows, axis=-1, keepdims=True) + NORM_EPS)


def rms_pull(rows, scale, gain, grad):
    scaled = rows * scale
    grad_gain = jnp.sum(grad * scaled, axis=0)
    through = grad * gain
    inner = jnp.mean(through * scaled, axis=-1, keepdims=True)
    return scale * (through - scaled * inner), grad_gain


def seq_starts(lengths_row, positions):
    begins = jnp.cumsum(lengths_row, dtype=jnp.int32) - lengths_row
    picked = jnp.where(begins[None, :] <= positions[:, None], begins[None, :], 0)
    return jnp.max(picked, axis=1)


def head_lanes(rows):
    return lax.broadcasted_iota(jnp.int32, (rows, PAIR), 1) < MDIM


def masked_products(b_low, c_low, rel_start):
    rows = b_low.shape[0]
    at_row = lax.broadcasted_iota(jnp.int32, (rows, rows), 0)
    at_col = lax.broadcasted_iota(jnp.int32, (rows, rows), 1)
    allowed = (at_col <= at_row) & (at_col >= rel_start)
    return allowed, jnp.where(allowed, mat_right_t(c_low, b_low), 0.0)


def pair_columns(first_half, columns, head):
    return jnp.where(first_half, columns[:, head : head + 1], columns[:, head + 1 : head + 2])


def ssd_forward_kernel(
    x_ref, b_ref, c_ref, step_ref, decay_ref, decay_t_ref, start_ref, state_ref, skip_ref, y_ref
):
    rows = x_ref.shape[1]
    b_low = b_ref[0].astype(BF16)
    c_low = c_ref[0].astype(BF16)
    rel_start = start_ref[0]
    _, products = masked_products(b_low, c_low, rel_start)
    incoming = mat_right_t(c_low, state_ref[0].astype(BF16))
    first_half = head_lanes(rows)
    steps = step_ref[0, 0]
    decay = decay_ref[0, 0]
    reach = jnp.where(rel_start < 0, jnp.exp(decay), 0.0)
    for head in range(0, HGROUP, 2):
        lanes = slice(head * MDIM, head * MDIM + PAIR)
        x_pair = x_ref[0, :, lanes]
        scaled = (x_pair * pair_columns(first_half, steps, head)).astype(BF16)
        parts = []
        for one in (head, head + 1):
            gaps = decay[:, one : one + 1] - decay_t_ref[0, 0, one : one + 1, :]
            weights = (jnp.exp(jnp.minimum(gaps, 0.0)) * products).astype(BF16)
            parts.append(mat(weights, scaled))
        y_ref[0, :, lanes] = (
            jnp.where(first_half, parts[0], parts[1])
            + pair_columns(first_half, reach, head) * incoming[:, lanes]
            + skip_ref[:, lanes] * x_pair
        )


def ssd_backward_kernel(
    x_ref,
    b_ref,
    c_ref,
    step_ref,
    decay_ref,
    decay_t_ref,
    start_ref,
    state_ref,
    skip_ref,
    y_ref,
    dy_ref,
    later_ref,
    keep_ref,
    dx_ref,
    db_ref,
    dc_ref,
    row_ref,
    u_ref,
    v_ref,
    dskip_ref,
    one_sum,
    two_sum,
    three_sum,
    mixed_y,
    mixed_x,
):
    rows = x_ref.shape[1]
    b_low = b_ref[0].astype(BF16)
    c_low = c_ref[0].astype(BF16)
    rel_start = start_ref[0]
    allowed, products = masked_products(b_low, c_low, rel_start)
    state_low = state_ref[0].astype(BF16)
    later_low = later_ref[0].astype(BF16)
    spread = mat_right_t(b_low, later_low)
    first_half = head_lanes(rows)
    steps = step_ref[0, 0]
    decay = decay_ref[0, 0]
    reach = jnp.where(rel_start < 0, jnp.exp(decay), 0.0)
    to_end = jnp.exp(decay[rows - 1 : rows, :] - decay) * steps * keep_ref[0]
    product_grad = jnp.zeros((rows, rows), F32)
    for head in range(0, HGROUP, 2):
        lanes = slice(head * MDIM, head * MDIM + PAIR)
        x_pair = x_ref[0, :, lanes]
        dy_pair = dy_ref[0, :, lanes]
        step_pair = pair_columns(first_half, steps, head)
        scaled = (x_pair * step_pair).astype(BF16)
        dy_low = dy_pair.astype(BF16)
        parts = []
        for one in (head, head + 1):
            gaps = decay[:, one : one + 1] - decay_t_ref[0, 0, one : one + 1, :]
            decays = jnp.exp(jnp.minimum(gaps, 0.0))
            mine = first_half if one == head else ~first_half
            dy_mine = jnp.where(mine, dy_pair, 0.0).astype(BF16)
            weight_grad = mat_right_t(dy_mine, scaled)
            product_grad = product_grad + weight_grad * decays
            parts.append(mat_left_t((decays * products).astype(BF16), dy_low))
        dz_pair = jnp.where(first_half, parts[0], parts[1])
        skip_pair = skip_ref[:, lanes]
        end_pair = pair_columns(first_half, to_end, head)
        spread_pair = spread[:, lanes]
        dx_ref[0, :, lanes] = skip_pair * dy_pair + step_pair * dz_pair + end_pair * spread_pair
        one_sum[:, lanes] = dy_pair * (y_ref[0, :, lanes] - skip_pair * x_pair)
        two_sum[:, lanes] = x_pair * dz_pair
        three_sum[:, lanes] = x_pair * spread_pair
        mixed_y[:, lanes] = (dy_pair * pair_columns(first_half, reach, head)).astype(BF16)
        mixed_x[:, lanes] = (x_pair * end_pair).astype(BF16)
        dskip_ref[0, 0, :, lanes] = jnp.sum(dy_pair * x_pair, axis=0, keepdims=True)
    grad_low = jnp.where(allowed, product_grad, 0.0).astype(BF16)
    dc = mat(grad_low, b_low) + mat(mixed_y[...], state_low)
    db = mat_left_t(grad_low, c_low) + mat(mixed_x[...], later_low)
    group = pl.program_id(1)

    @pl.when(group == 0)
    def _():
        dc_ref[0] = dc
        db_ref[0] = db

    @pl.when(group > 0)
    def _():
        dc_ref[0] += dc
        db_ref[0] += db

    owner = lax.broadcasted_iota(jnp.int32, (GWIDTH, 128), 0) // MDIM
    picks = (owner == lax.broadcasted_iota(jnp.int32, (GWIDTH, 128), 1)).astype(F32)
    for source, target in ((one_sum, row_ref), (two_sum, u_ref), (three_sum, v_ref)):
        sums = lax.dot_general(
            source[...],
            picks,
            (((1,), (0,)), ((), ())),
            precision=PRECISE,
            preferred_element_type=F32,
        )
        target[0, 0] = sums[:, :HGROUP]


def ssd_specs(rows):
    wide = pl.BlockSpec((1, rows, GWIDTH), lambda b, g: (b, 0, g))
    narrow = pl.BlockSpec((1, rows, STATE), lambda b, g: (b, 0, 0))
    heads = pl.BlockSpec((1, 1, rows, HGROUP), lambda b, g: (b, g, 0, 0))
    heads_t = pl.BlockSpec((1, 1, HGROUP, rows), lambda b, g: (b, g, 0, 0))
    column = pl.BlockSpec((1, rows, 1), lambda b, g: (b, 0, 0))
    state = pl.BlockSpec((1, GWIDTH, STATE), lambda b, g: (b, g, 0))
    skip = pl.BlockSpec((1, GWIDTH), lambda b, g: (0, g))
    return wide, narrow, heads, heads_t, column, state, skip


def ssd_forward(inner, b_rows, c_rows, steps, decay, decay_t, rel_start, state_in, skip_row):
    count, rows, _ = inner.shape
    wide, narrow, heads, heads_t, column, state, skip = ssd_specs(rows)
    return pl.pallas_call(
        ssd_forward_kernel,
        grid=(count, NGROUP),
        in_specs=[wide, narrow, narrow, heads, heads, heads_t, column, state, skip],
        out_specs=wide,
        out_shape=jax.ShapeDtypeStruct(inner.shape, F32),
        compiler_params=pltpu.CompilerParams(vmem_limit_bytes=40 * MIB),
        cost_estimate=pl.CostEstimate(
            flops=count * MHEADS * rows * rows * 400, bytes_accessed=8 * MIB, transcendentals=0
        ),
        name="ssd_forward",
    )(inner, b_rows, c_rows, steps, decay, decay_t, rel_start, state_in, skip_row)


def ssd_backward(
    inner,
    b_rows,
    c_rows,
    steps,
    decay,
    decay_t,
    rel_start,
    state_in,
    skip_row,
    scanned,
    grad_scanned,
    later,
    keep,
):
    count, rows, _ = inner.shape
    wide, narrow, heads, heads_t, column, state, skip = ssd_specs(rows)
    head_shape = jax.ShapeDtypeStruct((count, NGROUP, rows, HGROUP), F32)
    return pl.pallas_call(
        ssd_backward_kernel,
        grid=(count, NGROUP),
        in_specs=[
            wide,
            narrow,
            narrow,
            heads,
            heads,
            heads_t,
            column,
            state,
            skip,
            wide,
            wide,
            state,
            column,
        ],
        out_specs=[
            wide,
            narrow,
            narrow,
            heads,
            heads,
            heads,
            pl.BlockSpec((1, 1, 1, GWIDTH), lambda b, g: (b, g, 0, 0)),
        ],
        out_shape=[
            jax.ShapeDtypeStruct(inner.shape, F32),
            jax.ShapeDtypeStruct(b_rows.shape, F32),
            jax.ShapeDtypeStruct(b_rows.shape, F32),
            head_shape,
            head_shape,
            head_shape,
            jax.ShapeDtypeStruct((count, NGROUP, 1, GWIDTH), F32),
        ],
        scratch_shapes=[pltpu.VMEM((rows, GWIDTH), F32)] * 3
        + [pltpu.VMEM((rows, GWIDTH), BF16)] * 2,
        compiler_params=pltpu.CompilerParams(vmem_limit_bytes=40 * MIB),
        cost_estimate=pl.CostEstimate(
            flops=count * MHEADS * rows * rows * 1000, bytes_accessed=16 * MIB, transcendentals=0
        ),
        name="ssd_backward",
    )(
        inner,
        b_rows,
        c_rows,
        steps,
        decay,
        decay_t,
        rel_start,
        state_in,
        skip_row,
        scanned,
        grad_scanned,
        later,
        keep,
    )


def spread_heads(source_ref, target, factor):
    width = source_ref.shape[1]
    target[...] = jnp.zeros(target.shape, target.dtype)
    for head in range(QHEADS):
        group = head // (QHEADS // KVHEADS)
        value = source_ref[head * HDIM : (head + 1) * HDIM, :]
        target[group * HDIM : (group + 1) * HDIM, head * width : (head + 1) * width] = (
            value * factor if factor != 1.0 else value
        )


def attend_allowed(block, first_pos, starts, width):
    key_pos = block * width + lax.broadcasted_iota(jnp.int32, (width, width), 0)
    query_pos = first_pos + lax.broadcasted_iota(jnp.int32, (width, width), 1)
    return (key_pos <= query_pos) & (key_pos >= starts)


def attend_forward_kernel(bounds, start_ref, q_ref, kv_ref, out_ref, log_ref, q_wide, top, total, acc):
    width = q_ref.shape[1]
    batch = pl.program_id(0)
    spread_heads(q_ref, q_wide, HDIM**-0.5)
    top[...] = jnp.full(top.shape, MASKED_SCORE, F32)
    total[...] = jnp.zeros(total.shape, F32)
    acc[...] = jnp.zeros(acc.shape, F32)
    last = bounds[pl.num_programs(0)]
    first_pos = (last - 1) * width

    def one_block(block, carry):
        kv_rows = kv_ref[bounds[pl.num_programs(0) + 1 + block], 0]
        keys = kv_rows[:, : KVHEADS * HDIM]
        values_t = kv_rows[:, KVHEADS * HDIM :].T
        allowed = attend_allowed(block, first_pos, start_ref[0], width)
        for head in range(QHEADS):
            group = head // (QHEADS // KVHEADS)
            scores = mat(keys, q_wide[:, head * width : (head + 1) * width])
            scores = jnp.where(allowed, scores, MASKED_SCORE)
            old = top[head : head + 1, :]
            new = jnp.maximum(old, jnp.max(scores, axis=0, keepdims=True))
            terms = jnp.exp(scores - new)
            shrink = jnp.exp(old - new)
            top[head : head + 1, :] = new
            total[head : head + 1, :] = total[head : head + 1, :] * shrink + jnp.sum(
                terms, axis=0, keepdims=True
            )
            acc[head] = acc[head] * shrink + mat(
                values_t[group * HDIM : (group + 1) * HDIM, :], terms.astype(BF16)
            )
        return carry

    lax.fori_loop(bounds[batch], last, one_block, 0)
    for head in range(QHEADS):
        out_ref[head * HDIM : (head + 1) * HDIM, :] = (
            acc[head] / total[head : head + 1, :]
        ).astype(BF16)
    log_ref[0] = top[...] + jnp.log(total[...])


def attend_forward(bounds, starts, queries_t, key_table):
    blocks, count, width, kv_width = key_table.shape
    column = pl.BlockSpec((QHEADS * HDIM, width), lambda b, s: (0, b))
    logs = pl.BlockSpec((1, QHEADS, width), lambda b, s: (b, 0, 0))
    return pl.pallas_call(
        attend_forward_kernel,
        grid_spec=pltpu.PrefetchScalarGridSpec(
            num_scalar_prefetch=1,
            grid=(count,),
            in_specs=[
                pl.BlockSpec((1, 1, width), lambda b, s: (b, 0, 0)),
                column,
                pl.BlockSpec((blocks, 1, width, kv_width), lambda b, s: (0, b, 0, 0)),
            ],
            out_specs=[column, logs],
            scratch_shapes=[
                pltpu.VMEM((KVHEADS * HDIM, QHEADS * width), BF16),
                pltpu.VMEM((QHEADS, width), F32),
                pltpu.VMEM((QHEADS, width), F32),
                pltpu.VMEM((QHEADS, HDIM, width), F32),
            ],
        ),
        out_shape=[
            jax.ShapeDtypeStruct(queries_t.shape, BF16),
            jax.ShapeDtypeStruct((count, QHEADS, width), F32),
        ],
        compiler_params=pltpu.CompilerParams(vmem_limit_bytes=40 * MIB),
        cost_estimate=pl.CostEstimate(
            flops=count * blocks * width * width * 8 * 1000,
            bytes_accessed=4 * MIB,
            transcendentals=0,
        ),
        name="attend_forward",
    )(bounds, starts, queries_t, key_table)


def attend_backward_kernel(
    bounds,
    start_ref,
    q_ref,
    kv_ref,
    out_ref,
    grad_ref,
    log_ref,
    dq_ref,
    dkv_ref,
    q_wide,
    g_wide,
    q_tall,
    g_tall,
    delta,
    acc,
):
    width = q_ref.shape[1]
    kv_width = KVHEADS * HDIM
    batch = pl.program_id(0)
    spread_heads(q_ref, q_wide, HDIM**-0.5)
    spread_heads(grad_ref, g_wide, 1.0)
    acc[...] = jnp.zeros(acc.shape, F32)
    dkv_ref[...] = jnp.zeros(dkv_ref.shape, BF16)
    for head in range(QHEADS):
        columns = slice(head * width, (head + 1) * width)
        q_tall[columns, :] = q_wide[:, columns].T
        g_tall[columns, :] = g_wide[:, columns].T
        span = slice(head * HDIM, (head + 1) * HDIM)
        delta[head : head + 1, :] = jnp.sum(
            out_ref[span, :].astype(F32) * grad_ref[span, :].astype(F32), axis=0, keepdims=True
        )
    last = bounds[pl.num_programs(0)]
    first_pos = (last - 1) * width

    def one_block(block, carry):
        place = bounds[pl.num_programs(0) + 1 + block]
        kv_rows = kv_ref[place, 0]
        keys = kv_rows[:, :kv_width]
        values = kv_rows[:, kv_width:]
        keys_t = keys.T
        allowed = attend_allowed(block, first_pos, start_ref[0], width)
        dk = jnp.zeros((width, kv_width), F32)
        dv = jnp.zeros((width, kv_width), F32)
        for head in range(QHEADS):
            group = head // (QHEADS // KVHEADS)
            columns = slice(head * width, (head + 1) * width)
            scores = mat(keys, q_wide[:, columns])
            shifted = jnp.where(allowed, scores - log_ref[0, head : head + 1, :], MASKED_SCORE)
            probs = jnp.exp(shifted)
            grad_probs = mat(values, g_wide[:, columns])
            grad_scores = (probs * (grad_probs - delta[head : head + 1, :])).astype(BF16)
            dk = dk + mat(grad_scores, q_tall[columns, :])
            dv = dv + mat(probs.astype(BF16), g_tall[columns, :])
            acc[head] += mat(keys_t[group * HDIM : (group + 1) * HDIM, :], grad_scores)
        dkv_ref[place, 0] = jnp.concatenate([dk, dv], axis=1).astype(BF16)
        return carry

    lax.fori_loop(bounds[batch], last, one_block, 0)
    for head in range(QHEADS):
        dq_ref[head * HDIM : (head + 1) * HDIM, :] = (acc[head] * HDIM**-0.5).astype(BF16)


def attend_backward(bounds, starts, queries_t, key_table, out_t, grad_t, logs):
    blocks, count, width, kv_width = key_table.shape
    column = pl.BlockSpec((QHEADS * HDIM, width), lambda b, s: (0, b))
    table = pl.BlockSpec((blocks, 1, width, kv_width), lambda b, s: (0, b, 0, 0))
    wide = pltpu.VMEM((KVHEADS * HDIM, QHEADS * width), BF16)
    tall = pltpu.VMEM((QHEADS * width, KVHEADS * HDIM), BF16)
    return pl.pallas_call(
        attend_backward_kernel,
        grid_spec=pltpu.PrefetchScalarGridSpec(
            num_scalar_prefetch=1,
            grid=(count,),
            in_specs=[
                pl.BlockSpec((1, 1, width), lambda b, s: (b, 0, 0)),
                column,
                table,
                column,
                column,
                pl.BlockSpec((1, QHEADS, width), lambda b, s: (b, 0, 0)),
            ],
            out_specs=[column, table],
            scratch_shapes=[
                wide,
                wide,
                tall,
                tall,
                pltpu.VMEM((QHEADS, width), F32),
                pltpu.VMEM((QHEADS, HDIM, width), F32),
            ],
        ),
        out_shape=[
            jax.ShapeDtypeStruct(queries_t.shape, BF16),
            jax.ShapeDtypeStruct(key_table.shape, BF16),
        ],
        compiler_params=pltpu.CompilerParams(vmem_limit_bytes=48 * MIB),
        cost_estimate=pl.CostEstimate(
            flops=count * blocks * width * width * 8 * 2000,
            bytes_accessed=8 * MIB,
            transcendentals=0,
        ),
        name="attend_backward",
    )(bounds, starts, queries_t, key_table, out_t, grad_t, logs)


NEAR = (0, 2, 1, 3)


def near_at(step, size):
    return pl.ds(pl.multiple_of((lax.axis_index("wsh") ^ step) * size, 128), size)


def project_kernel(x_ref, *refs):
    *weights, out_ref = refs
    size = weights[0].shape[0]
    total = None
    for step, weight in zip(NEAR, weights):
        part = mat(x_ref[:, near_at(step, size)], weight[...])
        total = part if total is None else total + part
    out_ref[...] = total


def project(x, weights, tile):
    tokens, depth = x.shape
    size, columns = weights[0].shape
    return pl.pallas_call(
        project_kernel,
        grid=(columns // tile,),
        in_specs=[pl.BlockSpec((tokens, depth), lambda i: (0, 0))]
        + [pl.BlockSpec((size, tile), lambda i: (0, i))] * 4,
        out_specs=pl.BlockSpec((tokens, tile), lambda i: (0, i)),
        out_shape=jax.ShapeDtypeStruct((tokens, columns), F32),
        compiler_params=pltpu.CompilerParams(vmem_limit_bytes=40 * MIB),
        cost_estimate=pl.CostEstimate(
            flops=2 * tokens * depth * columns,
            bytes_accessed=2 * depth * columns + 4 * tokens * columns,
            transcendentals=0,
        ),
        name="project",
    )(x, *weights)


def unproject_kernel(base_ref, grad_ref, *refs):
    *weights, out_ref = refs
    size = weights[0].shape[0]

    @pl.when(pl.program_id(0) == 0)
    def _():
        out_ref[...] = base_ref[...]

    for step, weight in zip(NEAR, weights):
        out_ref[:, near_at(step, size)] += mat_right_t(grad_ref[...], weight[...])


def unproject(base, grad, weights, tile):
    tokens, columns = grad.shape
    size = weights[0].shape[0]
    whole = pl.BlockSpec((tokens, 4 * size), lambda i: (0, 0))
    return pl.pallas_call(
        unproject_kernel,
        grid=(columns // tile,),
        in_specs=[whole, pl.BlockSpec((tokens, tile), lambda i: (0, i))]
        + [pl.BlockSpec((size, tile), lambda i: (0, i))] * 4,
        out_specs=whole,
        out_shape=jax.ShapeDtypeStruct((tokens, 4 * size), F32),
        compiler_params=pltpu.CompilerParams(vmem_limit_bytes=40 * MIB),
        cost_estimate=pl.CostEstimate(
            flops=8 * tokens * size * columns,
            bytes_accessed=8 * size * columns + 2 * tokens * columns,
            transcendentals=0,
        ),
        name="unproject",
    )(base, grad, *weights)


def out_proj_kernel(x_ref, mixed_ref, heads_ref, gain_ref, *refs):
    *weights, middle_ref, normed_ref = refs
    wide = mixed_ref.shape[1] // 4
    narrow = heads_ref.shape[0] // 4
    middle_ref[...] = x_ref[...].astype(F32)
    for step, weight in zip(NEAR, weights):
        middle_ref[...] += mat(mixed_ref[:, near_at(step, wide)], weight[:wide]) + mat_left_t(
            heads_ref[near_at(step, narrow), :], weight[wide:]
        )
    middle = middle_ref[...]
    normed_ref[...] = (middle * inv_rms(middle) * gain_ref[...]).astype(BF16)


def out_project(x, mixed, heads_t, gain, weights):
    vmem = pl.BlockSpec(memory_space=pltpu.VMEM)
    return pl.pallas_call(
        out_proj_kernel,
        in_specs=[vmem] * 8,
        out_specs=[vmem, vmem],
        out_shape=[jax.ShapeDtypeStruct(x.shape, F32), jax.ShapeDtypeStruct(x.shape, BF16)],
        compiler_params=pltpu.CompilerParams(vmem_limit_bytes=40 * MIB),
        cost_estimate=pl.CostEstimate(
            flops=2 * x.size * 2048, bytes_accessed=12 * MIB, transcendentals=0
        ),
        name="out_project",
    )(x, mixed, heads_t, gain[None], *weights)


def out_back_kernel(branch_ref, *refs):
    *weights, mixed_ref, heads_ref = refs
    wide = mixed_ref.shape[1] // 4
    narrow = heads_ref.shape[0] // 4
    for step, weight in zip(NEAR, weights):
        mixed_ref[:, near_at(step, wide)] = mat_right_t(branch_ref[...], weight[:wide])
        heads_ref[near_at(step, narrow), :] = mat_right_t(weight[wide:], branch_ref[...]).astype(
            BF16
        )


def out_unproject(branch, weights, mixed_width, heads_width):
    vmem = pl.BlockSpec(memory_space=pltpu.VMEM)
    tokens = branch.shape[0]
    return pl.pallas_call(
        out_back_kernel,
        in_specs=[vmem] * 5,
        out_specs=[vmem, vmem],
        out_shape=[
            jax.ShapeDtypeStruct((tokens, mixed_width), F32),
            jax.ShapeDtypeStruct((heads_width, tokens), BF16),
        ],
        compiler_params=pltpu.CompilerParams(vmem_limit_bytes=40 * MIB),
        cost_estimate=pl.CostEstimate(
            flops=2 * branch.size * 2048, bytes_accessed=12 * MIB, transcendentals=0
        ),
        name="out_unproject",
    )(branch, *weights)


FF_TILE = 256


def mlp_kernel(
    place_ref, normed_ref, top_ref, middle_ref, gain_ref, *refs
):
    gates, ups, downs = refs[0:4], refs[4:8], refs[8:12]
    layer_ref, grad_ref, branch_ref, gain_grad_ref, hidden_ref, pair_ref = refs[12:18]
    down_tile, out_sum, back_sum = refs[18:]
    step_at = pl.program_id(0)
    per_piece = pl.num_programs(0) // 4
    size = gates[0].shape[0]
    for piece in range(4):

        @pl.when(step_at // per_piece == piece)
        def _():
            down_tile[...] = downs[piece][...]

    gate = up = None
    for step, gate_ref, up_ref in zip(NEAR, gates, ups):
        rows = normed_ref[:, near_at(step, size)]
        gate_part, up_part = mat(rows, gate_ref[...]), mat(rows, up_ref[...])
        gate = gate_part if gate is None else gate + gate_part
        up = up_part if up is None else up + up_part
    sig = 1.0 / (1.0 + jnp.exp(-gate))
    silu = gate * sig
    hidden = (silu * up).astype(BF16)
    hidden_ref[...] = hidden
    grad_hidden = mat_right_t(top_ref[...], down_tile[...])
    grad_gate = (grad_hidden * up * (sig + silu * (1.0 - sig))).astype(BF16)
    grad_up = (grad_hidden * silu).astype(BF16)
    pair_ref[0] = grad_gate
    pair_ref[1] = grad_up

    @pl.when(step_at == 0)
    def _():
        out_sum[...] = jnp.zeros(out_sum.shape, F32)
        back_sum[...] = jnp.zeros(back_sum.shape, F32)

    out_sum[...] += mat(hidden, down_tile[...])
    for step, gate_ref, up_ref in zip(NEAR, gates, ups):
        back_sum[:, near_at(step, size)] += mat_right_t(grad_gate, gate_ref[...]) + mat_right_t(
            grad_up, up_ref[...]
        )

    @pl.when(step_at == pl.num_programs(0) - 1)
    def _():
        middle = middle_ref[...]
        layer_ref[...] = (middle + out_sum[...]).astype(BF16)
        grad_rows, grad_gain = rms_pull(middle, inv_rms(middle), gain_ref[...], back_sum[...])
        grad = top_ref[...].astype(F32) + grad_rows
        grad_ref[...] = grad
        branch_ref[...] = grad.astype(BF16)
        gain_grad_ref[...] = grad_gain[None]


def mlp_both(place, normed, top, middle, gain, gu_weights, down_weights):
    tokens, features = middle.shape
    size, columns = gu_weights[0].shape
    width = columns // 2
    steps = width // FF_TILE
    per_piece = steps // 4

    def natural(i, p):
        piece = i // per_piece
        near = (piece % 2) * 2 + piece // 2
        return (near ^ p[0]) * per_piece + i % per_piece

    whole = pl.BlockSpec((tokens, features), lambda i, p: (0, 0))
    gain_spec = pl.BlockSpec((1, features), lambda i, p: (0, 0))

    def down_spec(piece):
        return pl.BlockSpec(
            (FF_TILE, features),
            lambda i, p: (jnp.clip(i - piece * per_piece, 0, per_piece - 1), 0),
        )

    return pl.pallas_call(
        mlp_kernel,
        grid_spec=pltpu.PrefetchScalarGridSpec(
            num_scalar_prefetch=1,
            grid=(steps,),
            in_specs=[whole, whole, whole, gain_spec]
            + [pl.BlockSpec((size, FF_TILE), lambda i, p: (0, natural(i, p)))] * 4
            + [pl.BlockSpec((size, FF_TILE), lambda i, p: (0, natural(i, p) + steps))] * 4
            + [down_spec(piece) for piece in range(4)],
            out_specs=[
                whole,
                whole,
                whole,
                gain_spec,
                pl.BlockSpec((tokens, FF_TILE), lambda i, p: (0, natural(i, p))),
                pl.BlockSpec((2, tokens, FF_TILE), lambda i, p: (0, 0, natural(i, p))),
            ],
            scratch_shapes=[
                pltpu.VMEM((FF_TILE, features), BF16),
                pltpu.VMEM((tokens, features), F32),
                pltpu.VMEM((tokens, features), F32),
            ],
        ),
        out_shape=[
            jax.ShapeDtypeStruct((tokens, features), BF16),
            jax.ShapeDtypeStruct((tokens, features), F32),
            jax.ShapeDtypeStruct((tokens, features), BF16),
            jax.ShapeDtypeStruct((1, features), F32),
            jax.ShapeDtypeStruct((tokens, width), BF16),
            jax.ShapeDtypeStruct((2, tokens, width), BF16),
        ],
        compiler_params=pltpu.CompilerParams(vmem_limit_bytes=48 * MIB),
        cost_estimate=pl.CostEstimate(
            flops=12 * tokens * features * width, bytes_accessed=30 * MIB, transcendentals=0
        ),
        name="mlp_both",
    )(
        place,
        normed,
        top,
        middle,
        gain[None],
        *gu_weights,
        *gu_weights,
        *down_weights,
    )


def passed_along(block, axis, distance):
    devices = range(lax.axis_size(axis))
    route = [(i - distance, i) for i in devices if i - distance in devices]
    return lax.ppermute(block, axis, route)


def swapped(block, axis, bit):
    return lax.ppermute(block, axis, [(i, i ^ bit) for i in range(lax.axis_size(axis))])


def bits_of(axis):
    return [1 << k for k in range(lax.axis_size(axis).bit_length() - 1)]


def after(value, earlier):
    return lax.optimization_barrier((value, earlier))[0]


def gathered_near(shard, earlier=None):
    if earlier is not None:
        shard = after(shard, earlier)
    across = swapped(shard, "wsh", 2)
    return [shard, across, swapped(shard, "wsh", 1), swapped(across, "wsh", 1)]


def table_gather(rows):
    table = rows[None]
    for bit in bits_of("ctx")[::-1]:
        table = jnp.concatenate([table, swapped(table, "ctx", bit)], axis=0)
    return table


def table_places(here, count):
    bits = count.bit_length() - 1
    apart = jnp.arange(count, dtype=jnp.int32) ^ here
    return sum(((apart >> bit) & 1) << (bits - 1 - bit) for bit in range(bits))


def table_scatter(table):
    for bit in bits_of("ctx"):
        half = table.shape[0] // 2
        table = (
            table[:half].astype(F32) + swapped(table[half:], "ctx", bit).astype(F32)
        ).astype(BF16)
    return table[0]


def widened_rows(factor):
    return jnp.repeat(factor, MDIM, axis=1)[..., None]


def chain_scan(total, state, forward):
    here = lax.axis_index("ctx")
    bits = bits_of("ctx")
    reached = jnp.zeros_like(state)
    reach = jnp.ones_like(total)
    for bit in bits:
        late = ((here // bit) % 2 == 1) == forward
        other_total = swapped(total, "ctx", bit)
        other = swapped(state.astype(BF16), "ctx", bit).astype(F32)
        reached = jnp.where(late, reached + widened_rows(reach) * other, reached)
        reach = jnp.where(late, reach * other_total, reach)
        state = jnp.where(
            late,
            widened_rows(total) * other + state,
            widened_rows(other_total) * state + other,
        )
        total = total * other_total
    return reached


TILE_ROWS = 256
TILE_COLS = 512


def ctx_bits(count):
    return [1 << k for k in range(count.bit_length() - 1)]


def partner_wsh(step):
    return (lax.axis_index("ctx"), lax.axis_index("wsh") ^ step)


def partner_ctx(step):
    return (lax.axis_index("ctx") ^ step, lax.axis_index("wsh"))


def remote(source, target, send, recv, device):
    return pltpu.make_async_remote_copy(
        src_ref=source,
        dst_ref=target,
        send_sem=send,
        recv_sem=recv,
        device_id=device,
        device_id_type=pl.DeviceIdType.MESH,
    )


def grads_kernel(
    count,
    split,
    early_units,
    late_units,
    gu_units,
    one_ref,
    two_ref,
    mix_ref,
    hid_ref,
    early_ref,
    late_ref,
    pair_ref,
    branch_ref,
    top_ref,
    small_ref,
    early_out,
    late_out,
    gu_out,
    mix_out,
    down_out,
    small_out,
    core_out,
    work,
    y_in,
    ctx_in,
    final,
    small_in,
    core_sems,
    y_sems,
    rs_sems,
    ag_sems,
    small_sems,
    out_sems,
):
    bits = ctx_bits(count)
    here = lax.axis_index("ctx")
    units = work.shape[0]
    rows = work.shape[2]
    width = work.shape[3]
    wsh_steps = (1, 2)
    barrier = pltpu.get_barrier_semaphore()
    partners = [partner_wsh(step) for step in wsh_steps] + [partner_ctx(bit) for bit in bits]
    for device in partners:
        pl.semaphore_signal(
            barrier, inc=1, device_id=device, device_id_type=pl.DeviceIdType.MESH
        )
    pl.semaphore_wait(barrier, len(partners))

    sizes = [rows >> (k + 1) for k in range(len(bits))]
    starts = []
    others = []
    base = 0
    for bit, size in zip(bits, sizes):
        upper = (here // bit) % 2
        others.append(base + (1 - upper) * size)
        base = base + upper * size
        starts.append(base)

    def span(start, size):
        return pl.ds(pl.multiple_of(start, 16), size)

    def core_copy(u):
        return remote(
            core_out.at[u % 2],
            work.at[u],
            core_sems.at[0, u],
            core_sems.at[1, u],
            partner_wsh(1),
        )

    def y_copy(u):
        return remote(work.at[u, 1], y_in.at[u], y_sems.at[0, u], y_sems.at[1, u], partner_wsh(2))

    recv_base = [rows - (rows >> k) for k in range(len(bits))]

    def rs_copy(u, k):
        return remote(
            work.at[u, 0, span(others[k], sizes[k])],
            ctx_in.at[u, pl.ds(recv_base[k], sizes[k])],
            rs_sems.at[0, k, u],
            rs_sems.at[1, k, u],
            partner_ctx(bits[k]),
        )

    def ag_copy(u, k):
        return remote(
            final.at[u, span(starts[k], sizes[k])],
            final.at[u, span(starts[k], sizes[k])],
            ag_sems.at[0, k, u],
            ag_sems.at[1, k, u],
            partner_ctx(bits[k]),
        )

    limits = []
    first_unit = 0
    for size in (early_units, late_units, gu_units, 4, 4):
        limits.append((first_unit, first_unit + size))
        first_unit += size
    outs = (early_out, late_out, gu_out, mix_out, down_out)

    def by_part(u, action):
        for part, (low, high) in enumerate(limits):
            pl.when((u >= low) & (u < high))(functools.partial(action, part, u - low))

    def each_out(u, act):
        def one(part, v):
            tall = part >= 3
            for i in range(split):
                row = (v // 2) * TILE_ROWS if tall else 0
                column = ((v % 2) if tall else v) * TILE_COLS + i * width
                copy = pltpu.make_async_copy(
                    final.at[u, pl.ds(i * TILE_ROWS, TILE_ROWS)],
                    outs[part].at[
                        pl.ds(pl.multiple_of(row, TILE_ROWS), TILE_ROWS),
                        pl.ds(pl.multiple_of(column, 128), width),
                    ],
                    out_sems.at[u, i],
                )
                act(copy)

        by_part(u, one)

    def columns_at(v):
        return pl.ds(pl.multiple_of(v * TILE_COLS, 128), TILE_COLS)

    wide = mix_ref.shape[0] * 3 // 16
    narrow = mix_ref.shape[0] // 16

    def pieces(u, first, put):
        steps = NEAR[2 * first : 2 * first + 2]

        def one(part, v):
            for place, step in enumerate(steps):
                if part < 2:
                    left = one_ref[:, near_at(step, TILE_ROWS)]
                    value = mat_left_t(left, (early_ref, late_ref)[part][:, columns_at(v)])
                elif part == 2:
                    left = two_ref[:, near_at(step, TILE_ROWS)]
                    half = gu_units // 2
                    value = mat_left_t(left, pair_ref[v // half, :, columns_at(v % half)])
                elif part == 3:
                    right = branch_ref[:, columns_at(v % 2)]
                    other = lax.axis_index("wsh") ^ step
                    begin = pl.multiple_of(other * wide, 128)

                    @pl.when(v < 2)
                    def _():
                        put(place, mat(mix_ref[pl.ds(begin, TILE_ROWS), :], right))

                    @pl.when(v >= 2)
                    def _():
                        tail = mat(
                            mix_ref[pl.ds(begin + TILE_ROWS, wide - TILE_ROWS), :], right
                        )
                        heads_at = pl.multiple_of(4 * wide + other * narrow, 128)
                        heads = mat(mix_ref[pl.ds(heads_at, narrow), :], right)
                        put(place, jnp.concatenate([tail, heads], axis=0))

                    continue
                else:
                    block = hid_ref.shape[1] // 4
                    start = (lax.axis_index("wsh") ^ step) * block + (v // 2) * TILE_ROWS
                    left = hid_ref[:, pl.ds(pl.multiple_of(start, 128), TILE_ROWS)]
                    value = mat_left_t(left, top_ref[:, columns_at(v % 2)])
                put(place, value)

        by_part(u, one)

    def chunked(value):
        return [
            (slice(i * TILE_ROWS, (i + 1) * TILE_ROWS), value[:, i * width : (i + 1) * width])
            for i in range(split)
        ]

    def begin(u):
        def put(place, value):
            for where, part in chunked(value):
                core_out[u % 2, place, where] = part.astype(BF16)

        pieces(u, 1, put)
        core_copy(u).start()

    def after_core(u):
        core_copy(u).wait()

        def put(place, value):
            for where, part in chunked(value):
                work[u, place, where] = (work[u, place, where].astype(F32) + part).astype(BF16)

        pieces(u, 0, put)
        y_copy(u).start()

    def after_y(u):
        y_copy(u).wait()
        work[u, 0] = (work[u, 0].astype(F32) + y_in[u].astype(F32)).astype(BF16)
        rs_copy(u, 0).start()

    def after_rs(u, k):
        rs_copy(u, k).wait()
        mine = span(starts[k], sizes[k])
        total = work[u, 0, mine].astype(F32) + ctx_in[
            u, pl.ds(recv_base[k], sizes[k])
        ].astype(F32)
        if k + 1 < len(bits):
            work[u, 0, mine] = total.astype(BF16)
            rs_copy(u, k + 1).start()
        else:
            final[u, mine] = total.astype(BF16)
            ag_copy(u, k).start()

    def after_ag(u, k):
        ag_copy(u, k).wait()
        if k > 0:
            ag_copy(u, k - 1).start()
        else:
            each_out(u, lambda copy: copy.start())

    stages = [(0, begin), (1, after_core), (3, after_y)]
    delay = 3
    for k in range(len(bits)):
        delay += 1
        stages.append((delay, functools.partial(after_rs, k=k)))
    for k in range(len(bits) - 1, -1, -1):
        delay += 1
        stages.append((delay, functools.partial(after_ag, k=k)))

    small_out[...] = small_ref[...]
    hops = partners

    def small_copy(k):
        return remote(
            small_in.at[k, 0], small_in.at[k, 1], small_sems.at[0, k], small_sems.at[1, k], hops[k]
        )

    def small_step(k):
        if k > 0:
            small_copy(k - 1).wait()
            small_out[...] += small_in[k - 1, 1]
        if k < len(hops):
            small_in[k, 0] = small_out[...]
            small_copy(k).start()

    def one_step(t, carry):
        for k in range(len(hops) + 1):
            pl.when(t == 2 * k + 1)(functools.partial(small_step, k))
        for offset, stage in stages[::-1]:
            u = t - offset
            pl.when((u >= 0) & (u < units))(functools.partial(stage, u))
        return carry

    lax.fori_loop(0, units + delay, one_step, 0)

    def finish(u, carry):
        each_out(u, lambda copy: copy.wait())
        return carry

    lax.fori_loop(0, units, finish, 0)


def reduce_grads(
    count, early_width, one, two, mix_t, hidden, early, late, pair, branch, top, small
):
    bits = ctx_bits(count)
    hops = len(bits) + 2
    split = max(1, 16 * count // TILE_ROWS)
    early_units = early_width // TILE_COLS
    late_units = late.shape[1] // TILE_COLS
    gu_units = 2 * pair.shape[2] // TILE_COLS
    units = early_units + late_units + gu_units + 8
    rows, width = TILE_ROWS * split, TILE_COLS // split
    dma = pltpu.SemaphoreType.DMA
    vmem = pl.BlockSpec(memory_space=pltpu.VMEM)
    hbm = pl.BlockSpec(memory_space=pl.ANY)
    return pl.pallas_call(
        functools.partial(grads_kernel, count, split, early_units, late_units, gu_units),
        in_specs=[vmem] * 10,
        out_specs=[hbm] * 5 + [vmem],
        out_shape=[
            jax.ShapeDtypeStruct((TILE_ROWS, early_units * TILE_COLS), BF16),
            jax.ShapeDtypeStruct((TILE_ROWS, late_units * TILE_COLS), BF16),
            jax.ShapeDtypeStruct((TILE_ROWS, gu_units * TILE_COLS), BF16),
            jax.ShapeDtypeStruct((2 * TILE_ROWS, 2 * TILE_COLS), BF16),
            jax.ShapeDtypeStruct((2 * TILE_ROWS, 2 * TILE_COLS), BF16),
            jax.ShapeDtypeStruct(small.shape, F32),
        ],
        scratch_shapes=[
            pltpu.VMEM((2, 2, rows, width), BF16),
            pltpu.VMEM((units, 2, rows, width), BF16),
            pltpu.VMEM((units, rows, width), BF16),
            pltpu.VMEM((units, rows, width), BF16),
            pltpu.VMEM((units, rows, width), BF16),
            pltpu.VMEM((hops, 2) + small.shape, F32),
            dma((2, units)),
            dma((2, units)),
            dma((2, len(bits), units)),
            dma((2, len(bits), units)),
            dma((2, hops)),
            dma((units, split)),
        ],
        compiler_params=pltpu.CompilerParams(
            collective_id=1, has_side_effects=True, vmem_limit_bytes=62 * MIB
        ),
        cost_estimate=pl.CostEstimate(
            flops=13_000_000_000, bytes_accessed=30 * MIB, transcendentals=0
        ),
        name="reduce_grads",
    )(one, two, mix_t, hidden, early, late, pair, branch, top, small)


def local(
    inputs,
    cotangent,
    lengths,
    norm1_gain,
    in_weight,
    dt_weight,
    conv_weight,
    conv_bias,
    dt_bias,
    decay_rate,
    skip_gain,
    mamba_gain,
    out_weight,
    q_weight,
    kv_weight,
    o_weight,
    norm2_gain,
    gu_weight,
    down_weight,
):
    count, _, rows, features = inputs.shape
    here = lax.axis_index("ctx")
    ctx_count = lax.axis_size("ctx")
    tokens = count * rows
    first_pos = here * rows
    own_pos = first_pos + jnp.arange(rows, dtype=jnp.int32)
    starts = jax.vmap(lambda row: seq_starts(row, own_pos))(lengths[:, 0])
    rel_start = starts - first_pos
    taps = conv_weight.shape[0]

    features_in = in_weight.shape[1]
    early_shard = jnp.concatenate(
        [
            kv_weight,
            in_weight[:, DSSM:],
            jnp.pad(dt_weight, ((0, 0), (0, 256 - dt_weight.shape[1]))),
        ],
        axis=1,
    )
    early = gathered_near(early_shard)
    late_shard = jnp.concatenate([in_weight[:, :DSSM], q_weight], axis=1)
    late = gathered_near(late_shard, early[1])
    outs = gathered_near(jnp.concatenate([out_weight, o_weight], axis=0), late[1])
    gu_full = gathered_near(gu_weight, outs[1])
    down_full = gathered_near(down_weight, gu_full[1])
    kv_width = kv_weight.shape[1]
    conv_width = features_in - DSSM

    x = inputs.reshape(tokens, features).astype(F32)
    scale_one = inv_rms(x)
    normed = (x * scale_one * norm1_gain).astype(BF16)
    early_rows = project(normed, early, 768)
    kv_rows = early_rows[:, :kv_width].astype(BF16)
    key_table = table_gather(kv_rows.reshape(count, rows, -1))
    conv_rows = early_rows[:, kv_width : kv_width + conv_width].reshape(count, rows, -1)
    dt_raw = early_rows[:, kv_width + conv_width :][:, :MHEADS] + dt_bias
    steps = jax.nn.softplus(dt_raw).reshape(count, rows, MHEADS)
    edge = passed_along(conv_rows[:, rows - taps + 1 :], "ctx", 1)
    extended = jnp.concatenate([edge, conv_rows], axis=1)
    valid = [
        (own_pos[None] - (taps - 1) + tap >= starts).astype(F32)[..., None] for tap in range(taps)
    ]
    conv_sum = jnp.zeros_like(conv_rows) + conv_bias
    for tap in range(taps):
        conv_sum = conv_sum + conv_weight[tap] * extended[:, tap : tap + rows] * valid[tap]
    conv_gate = jax.nn.sigmoid(conv_sum)
    activated = conv_sum * conv_gate
    inner = activated[..., :DSSM]
    b_rows = activated[..., DSSM : DSSM + STATE]
    c_rows = activated[..., DSSM + STATE :]

    lower = (own_pos[:, None] >= own_pos[None, :]).astype(F32)
    drop = -steps * decay_rate
    decay = jnp.einsum("ik,bkh->bih", lower, drop, precision=PRECISE)
    end = decay[:, -1:]
    keep = (own_pos[None] >= starts[:, -1:]).astype(F32)[..., None]
    to_end = jnp.exp(end - decay) * keep
    reach = jnp.where(rel_start[..., None] < 0, jnp.exp(decay), 0.0)
    carried = (starts[:, -1:] < first_pos).astype(F32)
    total = jnp.exp(end[:, 0]) * carried

    def grouped(columns):
        return columns.reshape(count, rows, NGROUP, HGROUP).transpose(0, 2, 1, 3)

    def ungrouped(columns):
        return columns.transpose(0, 2, 1, 3).reshape(count, rows, MHEADS)

    def widened(columns):
        return jnp.repeat(columns, MDIM, axis=-1)

    def outer(left, right):
        return jnp.einsum(
            "bti,btn->bin", left.astype(BF16), right.astype(BF16), preferred_element_type=F32
        )

    fresh = outer(inner * widened(to_end * steps), b_rows)
    state_in = chain_scan(total, fresh, True)

    late_rows = project(normed, late, 1024)
    gate_z = late_rows[:, :DSSM]
    queries_t = late_rows[:, DSSM:].astype(BF16).T
    bounds = jnp.concatenate(
        [starts[:, 0] // rows, jnp.full((1,), here + 1, jnp.int32), table_places(here, ctx_count)]
    )
    starts_row = starts[:, None, :]
    attended_t, logs = attend_forward(bounds, starts_row, queries_t, key_table)

    steps_g = grouped(steps)
    decay_g = grouped(decay)
    decay_t = decay_g.transpose(0, 1, 3, 2)
    skip_row = widened(skip_gain)[None]
    rel_column = rel_start[..., None]
    scanned = ssd_forward(
        inner, b_rows, c_rows, steps_g, decay_g, decay_t, rel_column, state_in, skip_row
    )
    flat = scanned.reshape(tokens, DSSM)
    gate_sig = jax.nn.sigmoid(gate_z)
    gated = flat * gate_z * gate_sig
    scale_m = inv_rms(gated)
    mixed = (gated * scale_m * mamba_gain).astype(BF16)
    middle, normed_two = out_project(
        inputs.reshape(tokens, features), mixed, attended_t, norm2_gain, outs
    )
    grad_top = cotangent.reshape(tokens, features)
    layer_out, grad_middle, branch, grad_norm2, hidden, grad_pair = mlp_both(
        lax.axis_index("wsh").astype(jnp.int32)[None],
        normed_two,
        grad_top,
        middle,
        norm2_gain,
        gu_full,
        down_full,
    )
    grad_mixed, grad_attended_t = out_unproject(branch, outs, DSSM, QHEADS * HDIM)
    grad_gated, grad_mamba = rms_pull(gated, scale_m, mamba_gain, grad_mixed)
    grad_gate_z = grad_gated * flat * gate_sig * (1.0 + gate_z * (1.0 - gate_sig))
    grad_scanned = (grad_gated * gate_z * gate_sig).reshape(count, rows, DSSM)
    grad_state = outer(grad_scanned * widened(reach), c_rows)
    later = chain_scan(total, grad_state, False)

    dq_t, dkv_table = attend_backward(
        bounds, starts_row, queries_t, key_table, attended_t, grad_attended_t, logs
    )
    dq_rows = dq_t.T
    grad_kv_rows = table_scatter(dkv_table).reshape(tokens, -1)
    dx, db, dc, row_dot, u_dot, v_dot, dskip = ssd_backward(
        inner,
        b_rows,
        c_rows,
        steps_g,
        decay_g,
        decay_t,
        rel_column,
        state_in,
        skip_row,
        scanned,
        grad_scanned,
        later,
        keep,
    )
    row_dot, u_dot, v_dot = ungrouped(row_dot), ungrouped(u_dot), ungrouped(v_dot)
    to_last = v_dot * to_end * steps
    grad_total = jnp.sum((later * state_in).reshape(count, MHEADS, MDIM * STATE), axis=-1) * total
    grad_decay = row_dot - u_dot * steps - to_last
    grad_drop = (
        jnp.einsum("ki,bkh->bih", lower, grad_decay, precision=PRECISE)
        + (jnp.sum(to_last, axis=1) + grad_total)[:, None]
    )
    grad_rate = jnp.sum(-steps * grad_drop, axis=(0, 1))
    grad_steps = u_dot + v_dot * to_end - decay_rate * grad_drop
    grad_dt_raw = grad_steps.reshape(tokens, MHEADS) * jax.nn.sigmoid(dt_raw)
    grad_dt_bias = jnp.sum(grad_dt_raw, axis=0)
    dt_low = grad_dt_raw.astype(BF16)
    grad_skip = jnp.sum(dskip.reshape(count, MHEADS, MDIM), axis=(0, 2))

    grad_act = jnp.concatenate([dx, db, dc], axis=-1)
    grad_conv = grad_act * conv_gate * (1.0 + conv_sum * (1.0 - conv_gate))
    grad_conv_b = jnp.sum(grad_conv, axis=(0, 1))
    grad_conv_w = jnp.stack(
        [
            jnp.sum(grad_conv * extended[:, tap : tap + rows] * valid[tap], axis=(0, 1))
            for tap in range(taps)
        ]
    )
    grad_extended = jnp.zeros_like(extended)
    for tap in range(taps):
        grad_extended = grad_extended + jnp.pad(
            conv_weight[tap] * grad_conv * valid[tap], ((0, 0), (tap, taps - 1 - tap), (0, 0))
        )
    edge_back = passed_along(grad_extended[:, : taps - 1], "ctx", -1)
    grad_conv_rows = grad_extended[:, taps - 1 :] + jnp.pad(
        edge_back, ((0, 0), (rows - taps + 1, 0), (0, 0))
    )
    grad_late = jnp.concatenate([grad_gate_z.astype(BF16), dq_rows], axis=1)
    grad_early = jnp.concatenate(
        [
            grad_kv_rows,
            grad_conv_rows.reshape(tokens, -1).astype(BF16),
            jnp.pad(dt_low, ((0, 0), (0, 256 - MHEADS))),
        ],
        axis=1,
    )
    grad_dt_w = mat_left_t(normed, dt_low)
    grad_normed = unproject(jnp.zeros((tokens, features), F32), grad_late, late, 1024)
    grad_normed = unproject(grad_normed, grad_early, early, 768)
    grad_one, grad_norm1 = rms_pull(x, scale_one, norm1_gain, grad_normed)
    input_grad = (grad_middle + grad_one).astype(BF16)

    pieces = (
        grad_norm1,
        grad_conv_w,
        grad_conv_b,
        grad_dt_bias,
        grad_rate,
        grad_skip,
        grad_mamba,
        grad_norm2[0],
        grad_dt_w,
    )
    packed = jnp.concatenate([piece.reshape(-1) for piece in pieces])
    packed = jnp.pad(packed, (0, -packed.size % 1024)).reshape(-1, 128)
    mix_t = jnp.concatenate([mixed.T, attended_t], axis=0)
    early_sum, late_sum, gu_sum, mix_sum, down_sum, packed = reduce_grads(
        ctx_count,
        kv_width + conv_width,
        normed,
        normed_two,
        mix_t,
        hidden,
        grad_early,
        grad_late,
        grad_pair,
        branch,
        grad_top,
        packed,
    )
    packed = packed.reshape(-1)
    split_row = out_weight.shape[0]
    totals_w = [
        part.astype(F32)
        for part in (
            jnp.concatenate([late_sum[:, :DSSM], early_sum[:, kv_width:]], axis=1),
            mix_sum[:split_row],
            late_sum[:, DSSM:],
            early_sum[:, :kv_width],
            mix_sum[split_row:],
            gu_sum,
            down_sum,
        )
    ]
    small = []
    place = 0
    for piece in pieces:
        small.append(packed[place : place + piece.size].reshape(piece.shape))
        place += piece.size
    dt_rows = dt_weight.shape[0]
    dt_sum = lax.dynamic_slice_in_dim(small[8], lax.axis_index("wsh") * dt_rows, dt_rows, 0)
    shape = (count, 1, rows, features)
    return (
        layer_out.reshape(shape),
        input_grad.reshape(shape),
        small[0],
        totals_w[0],
        dt_sum,
        small[1],
        small[2],
        small[3],
        small[4],
        small[5],
        small[6],
        totals_w[1],
        totals_w[2],
        totals_w[3],
        totals_w[4],
        small[7],
        totals_w[5],
        totals_w[6],
    )


def solution(mesh):
    stream = P(None, "wsh", "ctx", None)
    shard = P("wsh", None)
    in_specs = (
        stream,
        stream,
        P(None, "wsh", None),
        P(),
        shard,
        shard,
        P(),
        P(),
        P(),
        P(),
        P(),
        P(),
        shard,
        shard,
        shard,
        shard,
        P(),
        shard,
        shard,
    )
    out_specs = (
        stream,
        stream,
        P(),
        shard,
        shard,
        P(),
        P(),
        P(),
        P(),
        P(),
        P(),
        shard,
        shard,
        shard,
        shard,
        P(),
        shard,
        shard,
    )
    return jax.shard_map(local, mesh=mesh, in_specs=in_specs, out_specs=out_specs, check_vma=False)
```

```python
import functools

import jax
import jax.numpy as jnp
from jax import lax
from jax.experimental import pallas as pl
from jax.experimental.pallas import tpu as pltpu
from jax.sharding import PartitionSpec as P

FF = 2048
MHEADS = 24
MDIM = 64
STATE = 128
QHEADS = 8
KVHEADS = 2
HDIM = 64
DSSM = 1536
HGROUP = 8
NGROUP = MHEADS // HGROUP
GWIDTH = HGROUP * MDIM
PAIR = 2 * MDIM

NORM_EPS = 1e-05
PRECISE = lax.Precision.HIGHEST
MASKED_SCORE = -1e30
MIB = 2**20
F32 = jnp.float32
BF16 = jnp.bfloat16


def dot_as(left, right, left_dim, right_dim):
    return lax.dot_general(
        left, right, (((left_dim,), (right_dim,)), ((), ())), preferred_element_type=F32
    )


def mat(left, right):
    return dot_as(left, right, 1, 0)


def mat_left_t(left, right):
    return dot_as(left, right, 0, 0)


def mat_right_t(left, right):
    return dot_as(left, right, 1, 1)


def inv_rms(rows):
    return lax.rsqrt(jnp.mean(rows * rows, axis=-1, keepdims=True) + NORM_EPS)


def rms_pull(rows, scale, gain, grad):
    scaled = rows * scale
    grad_gain = jnp.sum(grad * scaled, axis=0)
    through = grad * gain
    inner = jnp.mean(through * scaled, axis=-1, keepdims=True)
    return scale * (through - scaled * inner), grad_gain


def seq_starts(lengths_row, positions):
    begins = jnp.cumsum(lengths_row, dtype=jnp.int32) - lengths_row
    picked = jnp.where(begins[None, :] <= positions[:, None], begins[None, :], 0)
    return jnp.max(picked, axis=1)


def head_lanes(rows):
    return lax.broadcasted_iota(jnp.int32, (rows, PAIR), 1) < MDIM


def masked_products(b_low, c_low, rel_start):
    rows = b_low.shape[0]
    at_row = lax.broadcasted_iota(jnp.int32, (rows, rows), 0)
    at_col = lax.broadcasted_iota(jnp.int32, (rows, rows), 1)
    allowed = (at_col <= at_row) & (at_col >= rel_start)
    return allowed, jnp.where(allowed, mat_right_t(c_low, b_low), 0.0)


def pair_columns(first_half, columns, head):
    return jnp.where(first_half, columns[:, head : head + 1], columns[:, head + 1 : head + 2])


def exact(left, right, left_dim, right_dim):
    return lax.dot_general(
        left,
        right,
        (((left_dim,), (right_dim,)), ((), ())),
        precision=PRECISE,
        preferred_element_type=F32,
    )


def lower_ones(rows):
    at_row = lax.broadcasted_iota(jnp.int32, (rows, rows), 0)
    at_col = lax.broadcasted_iota(jnp.int32, (rows, rows), 1)
    return (at_row >= at_col).astype(F32)


def sigmoid(value):
    return 1.0 / (1.0 + jnp.exp(-value))


def softplus(value):
    return jnp.maximum(value, 0.0) + jnp.log1p(jnp.exp(-jnp.abs(value)))


def scaled_rows(target, source_ref, factors):
    first_half = head_lanes(source_ref.shape[0])
    for head in range(0, MHEADS, 2):
        lanes = slice(head * MDIM, head * MDIM + PAIR)
        target[:, lanes] = (
            source_ref[:, lanes] * pair_columns(first_half, factors, head)
        ).astype(BF16)


def ssd_state_kernel(
    act_ref,
    dt_ref,
    bias_ref,
    rate_ref,
    start_ref,
    step_ref,
    decay_ref,
    decay_t_ref,
    end_ref,
    total_ref,
    state_ref,
    scaled,
):
    rows = act_ref.shape[0]
    steps = softplus(dt_ref[:, :128] + bias_ref[...])
    decay = exact(lower_ones(rows), -steps * rate_ref[...], 1, 0)
    rel_start = start_ref[...]
    last_start = rel_start[rows - 1 : rows, :]
    kept = lax.broadcasted_iota(jnp.int32, (rows, 1), 0) >= last_start
    end = decay[rows - 1 : rows, :]
    to_end = jnp.where(kept, jnp.exp(end - decay), 0.0)
    step_ref[...] = steps
    decay_ref[...] = decay
    decay_t_ref[0] = decay.T
    end_ref[...] = to_end
    total_ref[0] = jnp.broadcast_to(jnp.where(last_start < 0, jnp.exp(end), 0.0), (8, 128))
    scaled_rows(scaled, act_ref, to_end * steps)
    state_ref[0] = mat_left_t(scaled[...], act_ref[:, DSSM : DSSM + STATE].astype(BF16))


def row_spec(rows, width, place=0):
    return pl.BlockSpec((rows, width), lambda b: (b, place))


def ssd_state(count, act, dt_rows, bias, rate, rel_start):
    rows = act.shape[0] // count
    lanes = pl.BlockSpec((1, 128), lambda b: (0, 0))
    heads = jax.ShapeDtypeStruct((count * rows, 128), F32)
    return pl.pallas_call(
        ssd_state_kernel,
        grid=(count,),
        in_specs=[
            row_spec(rows, act.shape[1]),
            row_spec(rows, dt_rows.shape[1]),
            lanes,
            lanes,
            row_spec(rows, 1),
        ],
        out_specs=[
            row_spec(rows, 128),
            row_spec(rows, 128),
            pl.BlockSpec((1, 128, rows), lambda b: (b, 0, 0)),
            row_spec(rows, 128),
            pl.BlockSpec((1, 8, 128), lambda b: (b, 0, 0)),
            pl.BlockSpec((1, DSSM, STATE), lambda b: (b, 0, 0)),
        ],
        out_shape=[
            heads,
            heads,
            jax.ShapeDtypeStruct((count, 128, rows), F32),
            heads,
            jax.ShapeDtypeStruct((count, 8, 128), F32),
            jax.ShapeDtypeStruct((count, DSSM, STATE), F32),
        ],
        scratch_shapes=[pltpu.VMEM((rows, DSSM), BF16)],
        compiler_params=pltpu.CompilerParams(vmem_limit_bytes=40 * MIB),
        cost_estimate=pl.CostEstimate(
            flops=1_000_000_000, bytes_accessed=8 * MIB, transcendentals=0
        ),
        name="ssd_state",
    )(act, dt_rows, bias, rate, rel_start)


def state_grad_kernel(dy_ref, c_ref, decay_ref, start_ref, out_ref, scaled):
    reach = jnp.where(start_ref[...] < 0, jnp.exp(decay_ref[...]), 0.0)
    scaled_rows(scaled, dy_ref, reach)
    out_ref[0] = mat_left_t(scaled[...], c_ref[...].astype(BF16))


def state_grad(count, dy, act, decay, rel_start):
    rows = act.shape[0] // count
    return pl.pallas_call(
        state_grad_kernel,
        grid=(count,),
        in_specs=[
            row_spec(rows, DSSM),
            row_spec(rows, STATE, DSSM // STATE + 1),
            row_spec(rows, 128),
            row_spec(rows, 1),
        ],
        out_specs=pl.BlockSpec((1, DSSM, STATE), lambda b: (b, 0, 0)),
        out_shape=jax.ShapeDtypeStruct((count, DSSM, STATE), F32),
        scratch_shapes=[pltpu.VMEM((rows, DSSM), BF16)],
        compiler_params=pltpu.CompilerParams(vmem_limit_bytes=40 * MIB),
        cost_estimate=pl.CostEstimate(
            flops=1_000_000_000, bytes_accessed=8 * MIB, transcendentals=0
        ),
        name="state_grad",
    )(dy, act, decay, rel_start)


def group_heads(ref):
    return pltpu.roll(ref[...], (128 - HGROUP * pl.program_id(1)) % 128, 1)


def group_rows(decay_t_ref):
    return decay_t_ref[0, pl.ds(pl.multiple_of(HGROUP * pl.program_id(1), HGROUP), HGROUP), :]


def ssd_forward_kernel(
    x_ref, b_ref, c_ref, step_ref, decay_ref, decay_t_ref, start_ref, state_ref, skip_ref, y_ref
):
    rows = x_ref.shape[0]
    b_low = b_ref[...].astype(BF16)
    c_low = c_ref[...].astype(BF16)
    rel_start = start_ref[...]
    _, products = masked_products(b_low, c_low, rel_start)
    incoming = mat_right_t(c_low, state_ref[0].astype(BF16))
    first_half = head_lanes(rows)
    steps = group_heads(step_ref)
    decay = group_heads(decay_ref)
    decay_t = group_rows(decay_t_ref)
    reach = jnp.where(rel_start < 0, jnp.exp(decay), 0.0)
    for head in range(0, HGROUP, 2):
        lanes = slice(head * MDIM, head * MDIM + PAIR)
        x_pair = x_ref[:, lanes]
        scaled = (x_pair * pair_columns(first_half, steps, head)).astype(BF16)
        parts = []
        for one in (head, head + 1):
            gaps = decay[:, one : one + 1] - decay_t[one : one + 1, :]
            weights = (jnp.exp(jnp.minimum(gaps, 0.0)) * products).astype(BF16)
            parts.append(mat(weights, scaled))
        y_ref[:, lanes] = (
            jnp.where(first_half, parts[0], parts[1])
            + pair_columns(first_half, reach, head) * incoming[:, lanes]
            + skip_ref[:, lanes] * x_pair
        )


def ssd_backward_kernel(
    x_ref,
    b_ref,
    c_ref,
    step_ref,
    decay_ref,
    decay_t_ref,
    start_ref,
    state_ref,
    skip_ref,
    y_ref,
    dy_ref,
    later_ref,
    end_ref,
    total_ref,
    dt_ref,
    bias_ref,
    rate_ref,
    dx_ref,
    db_ref,
    dc_ref,
    dt_grad_ref,
    small_ref,
    one_sum,
    two_sum,
    three_sum,
    mixed_y,
    mixed_x,
    head_sums,
    row_sums,
):
    rows = x_ref.shape[0]
    b_low = b_ref[...].astype(BF16)
    c_low = c_ref[...].astype(BF16)
    rel_start = start_ref[...]
    allowed, products = masked_products(b_low, c_low, rel_start)
    state_low = state_ref[0].astype(BF16)
    later_low = later_ref[0].astype(BF16)
    spread = mat_right_t(b_low, later_low)
    first_half = head_lanes(rows)
    steps = group_heads(step_ref)
    decay = group_heads(decay_ref)
    decay_t = group_rows(decay_t_ref)
    reach = jnp.where(rel_start < 0, jnp.exp(decay), 0.0)
    to_end = group_heads(end_ref) * steps
    product_grad = jnp.zeros((rows, rows), F32)
    skip_parts = []
    for head in range(0, HGROUP, 2):
        lanes = slice(head * MDIM, head * MDIM + PAIR)
        x_pair = x_ref[:, lanes]
        dy_pair = dy_ref[:, lanes]
        step_pair = pair_columns(first_half, steps, head)
        scaled = (x_pair * step_pair).astype(BF16)
        dy_low = dy_pair.astype(BF16)
        parts = []
        for one in (head, head + 1):
            gaps = decay[:, one : one + 1] - decay_t[one : one + 1, :]
            decays = jnp.exp(jnp.minimum(gaps, 0.0))
            mine = first_half if one == head else ~first_half
            dy_mine = jnp.where(mine, dy_pair, 0.0).astype(BF16)
            weight_grad = mat_right_t(dy_mine, scaled)
            product_grad = product_grad + weight_grad * decays
            parts.append(mat_left_t((decays * products).astype(BF16), dy_low))
        dz_pair = jnp.where(first_half, parts[0], parts[1])
        skip_pair = skip_ref[:, lanes]
        end_pair = pair_columns(first_half, to_end, head)
        spread_pair = spread[:, lanes]
        dx_ref[:, lanes] = skip_pair * dy_pair + step_pair * dz_pair + end_pair * spread_pair
        one_sum[:, lanes] = dy_pair * (y_ref[:, lanes] - skip_pair * x_pair)
        two_sum[:, lanes] = x_pair * dz_pair
        three_sum[:, lanes] = x_pair * spread_pair
        mixed_y[:, lanes] = (dy_pair * pair_columns(first_half, reach, head)).astype(BF16)
        mixed_x[:, lanes] = (x_pair * end_pair).astype(BF16)
        skip_parts.append(jnp.sum(dy_pair * x_pair, axis=0, keepdims=True))
    grad_low = jnp.where(allowed, product_grad, 0.0).astype(BF16)
    dc = mat(grad_low, b_low) + mat(mixed_y[...], state_low)
    db = mat_left_t(grad_low, c_low) + mat(mixed_x[...], later_low)
    group = pl.program_id(1)

    @pl.when(group == 0)
    def _():
        dc_ref[...] = jnp.zeros(dc_ref.shape, F32)
        db_ref[...] = jnp.zeros(db_ref.shape, F32)
        head_sums[...] = jnp.zeros(head_sums.shape, F32)
        row_sums[...] = jnp.zeros(row_sums.shape, F32)

    dc_ref[...] += dc
    db_ref[...] += db
    owner = lax.broadcasted_iota(jnp.int32, (GWIDTH, 128), 0) // MDIM + group * HGROUP
    picks = (owner == lax.broadcasted_iota(jnp.int32, (GWIDTH, 128), 1)).astype(F32)
    for place, source in enumerate((one_sum, two_sum, three_sum)):
        head_sums[place] += exact(source[...], picks, 1, 0)
    skips = jnp.broadcast_to(jnp.concatenate(skip_parts, axis=1), (8, GWIDTH))
    row_sums[0] += exact(skips, picks, 1, 0)
    meets = exact(
        jnp.ones((8, STATE), F32), later_ref[0].astype(F32) * state_ref[0].astype(F32), 1, 1
    )
    row_sums[1] += exact(meets, picks, 1, 0)

    @pl.when(group == pl.num_programs(1) - 1)
    def _():
        all_steps = step_ref[...]
        all_end = end_ref[...]
        rate = rate_ref[...]
        row_dot, u_dot, v_dot = head_sums[0], head_sums[1], head_sums[2]
        to_last = v_dot * all_end * all_steps
        grad_decay = row_dot - u_dot * all_steps - to_last
        at_end = jnp.sum(to_last, axis=0, keepdims=True) + row_sums[1, :1] * total_ref[0, :1]
        grad_drop = exact(lower_ones(rows), grad_decay, 0, 0) + at_end
        grad_steps = u_dot + v_dot * all_end - rate * grad_drop
        grad_dt = grad_steps * sigmoid(dt_ref[:, :128] + bias_ref[...])
        dt_grad_ref[:, :128] = grad_dt.astype(BF16)
        dt_grad_ref[:, 128:] = jnp.zeros((rows, dt_grad_ref.shape[1] - 128), BF16)
        small_ref[0, 0:1] = jnp.sum(grad_dt, axis=0, keepdims=True)
        small_ref[0, 1:2] = jnp.sum(-all_steps * grad_drop, axis=0, keepdims=True)
        small_ref[0, 2:8] = row_sums[0, :6]


def ssd_specs(rows):
    wide = pl.BlockSpec((rows, GWIDTH), lambda b, g: (b, g))
    b_spec = pl.BlockSpec((rows, STATE), lambda b, g: (b, DSSM // STATE))
    c_spec = pl.BlockSpec((rows, STATE), lambda b, g: (b, DSSM // STATE + 1))
    heads = pl.BlockSpec((rows, 128), lambda b, g: (b, 0))
    heads_t = pl.BlockSpec((1, 128, rows), lambda b, g: (b, 0, 0))
    column = pl.BlockSpec((rows, 1), lambda b, g: (b, 0))
    state = pl.BlockSpec((1, GWIDTH, STATE), lambda b, g: (b, g, 0))
    skip = pl.BlockSpec((1, GWIDTH), lambda b, g: (0, g))
    return [wide, b_spec, c_spec, heads, heads, heads_t, column, state, skip]


def ssd_forward(count, act, steps, decay, decay_t, rel_start, state_in, skip_row):
    rows = act.shape[0] // count
    specs = ssd_specs(rows)
    return pl.pallas_call(
        ssd_forward_kernel,
        grid=(count, NGROUP),
        in_specs=specs,
        out_specs=specs[0],
        out_shape=jax.ShapeDtypeStruct((count * rows, DSSM), F32),
        compiler_params=pltpu.CompilerParams(vmem_limit_bytes=40 * MIB),
        cost_estimate=pl.CostEstimate(
            flops=count * MHEADS * rows * rows * 400, bytes_accessed=8 * MIB, transcendentals=0
        ),
        name="ssd_forward",
    )(act, act, act, steps, decay, decay_t, rel_start, state_in, skip_row)


def ssd_backward(
    count,
    act,
    steps,
    decay,
    decay_t,
    rel_start,
    state_in,
    skip_row,
    scanned,
    grad_scanned,
    later,
    to_end,
    total,
    dt_rows,
    bias,
    rate,
):
    rows = act.shape[0] // count
    specs = ssd_specs(rows)
    wide, heads, state = specs[0], specs[3], specs[7]
    row = pl.BlockSpec((1, 128), lambda b, g: (0, 0))
    packed = pl.BlockSpec((1, 8, 128), lambda b, g: (b, 0, 0))
    narrow = pl.BlockSpec((rows, STATE), lambda b, g: (b, 0))
    dt_spec = pl.BlockSpec((rows, dt_rows.shape[1]), lambda b, g: (b, 0))
    tokens = count * rows
    return pl.pallas_call(
        ssd_backward_kernel,
        grid=(count, NGROUP),
        in_specs=specs + [wide, wide, state, heads, packed, dt_spec, row, row],
        out_specs=[wide, narrow, narrow, dt_spec, packed],
        out_shape=[
            jax.ShapeDtypeStruct((tokens, DSSM), F32),
            jax.ShapeDtypeStruct((tokens, STATE), F32),
            jax.ShapeDtypeStruct((tokens, STATE), F32),
            jax.ShapeDtypeStruct(dt_rows.shape, BF16),
            jax.ShapeDtypeStruct((count, 8, 128), F32),
        ],
        scratch_shapes=[pltpu.VMEM((rows, GWIDTH), F32)] * 3
        + [pltpu.VMEM((rows, GWIDTH), BF16)] * 2
        + [pltpu.VMEM((3, rows, 128), F32), pltpu.VMEM((2, 8, 128), F32)],
        compiler_params=pltpu.CompilerParams(vmem_limit_bytes=40 * MIB),
        cost_estimate=pl.CostEstimate(
            flops=count * MHEADS * rows * rows * 1000, bytes_accessed=16 * MIB, transcendentals=0
        ),
        name="ssd_backward",
    )(
        act,
        act,
        act,
        steps,
        decay,
        decay_t,
        rel_start,
        state_in,
        skip_row,
        scanned,
        grad_scanned,
        later,
        to_end,
        total,
        dt_rows,
        bias,
        rate,
    )


def spread_heads(source_ref, target, factor):
    width = source_ref.shape[1]
    target[...] = jnp.zeros(target.shape, target.dtype)
    for head in range(QHEADS):
        group = head // (QHEADS // KVHEADS)
        value = source_ref[head * HDIM : (head + 1) * HDIM, :]
        target[group * HDIM : (group + 1) * HDIM, head * width : (head + 1) * width] = (
            value * factor if factor != 1.0 else value
        )


def attend_allowed(block, first_pos, starts, width):
    key_pos = block * width + lax.broadcasted_iota(jnp.int32, (width, width), 0)
    query_pos = first_pos + lax.broadcasted_iota(jnp.int32, (width, width), 1)
    return (key_pos <= query_pos) & (key_pos >= starts)


NEAR = (0, 2, 1, 3)
TILE_ROWS = 256
TILE_COLS = 512


def near_at(step, size):
    return pl.ds(pl.multiple_of((lax.axis_index("wsh") ^ step) * size, 128), size)


def project_kernel(x_ref, *refs):
    *weights, out_ref = refs
    size = weights[0].shape[0]
    total = None
    for step, weight in zip(NEAR, weights):
        part = mat(x_ref[:, near_at(step, size)], weight[...])
        total = part if total is None else total + part
    out_ref[...] = total.astype(out_ref.dtype)


def project(x, weights, tile, kind=F32):
    tokens, depth = x.shape
    size, columns = weights[0].shape
    return pl.pallas_call(
        project_kernel,
        grid=(columns // tile,),
        in_specs=[pl.BlockSpec((tokens, depth), lambda i: (0, 0))]
        + [pl.BlockSpec((size, tile), lambda i: (0, i))] * 4,
        out_specs=pl.BlockSpec((tokens, tile), lambda i: (0, i)),
        out_shape=jax.ShapeDtypeStruct((tokens, columns), kind),
        compiler_params=pltpu.CompilerParams(vmem_limit_bytes=40 * MIB),
        cost_estimate=pl.CostEstimate(
            flops=2 * tokens * depth * columns,
            bytes_accessed=2 * depth * columns + 4 * tokens * columns,
            transcendentals=0,
        ),
        name="project",
    )(x, *weights)


def unproject_kernel(base_ref, grad_ref, *refs):
    *weights, out_ref = refs
    size = weights[0].shape[0]

    @pl.when(pl.program_id(0) == 0)
    def _():
        out_ref[...] = base_ref[...]

    for step, weight in zip(NEAR, weights):
        out_ref[:, near_at(step, size)] += mat_right_t(grad_ref[...], weight[...])


def unproject(base, grad, weights, tile):
    tokens, columns = grad.shape
    size = weights[0].shape[0]
    whole = pl.BlockSpec((tokens, 4 * size), lambda i: (0, 0))
    return pl.pallas_call(
        unproject_kernel,
        grid=(columns // tile,),
        in_specs=[whole, pl.BlockSpec((tokens, tile), lambda i: (0, i))]
        + [pl.BlockSpec((size, tile), lambda i: (0, i))] * 4,
        out_specs=whole,
        out_shape=jax.ShapeDtypeStruct((tokens, 4 * size), F32),
        compiler_params=pltpu.CompilerParams(vmem_limit_bytes=40 * MIB),
        cost_estimate=pl.CostEstimate(
            flops=8 * tokens * size * columns,
            bytes_accessed=8 * size * columns + 2 * tokens * columns,
            transcendentals=0,
        ),
        name="unproject",
    )(base, grad, *weights)


def out_proj_kernel(x_ref, mixed_ref, heads_ref, gain_ref, *refs):
    *weights, middle_ref, normed_ref = refs
    wide = mixed_ref.shape[1] // 4
    narrow = heads_ref.shape[0] // 4
    middle_ref[...] = x_ref[...].astype(F32)
    for step, weight in zip(NEAR, weights):
        middle_ref[...] += mat(mixed_ref[:, near_at(step, wide)], weight[:wide]) + mat_left_t(
            heads_ref[near_at(step, narrow), :], weight[wide:]
        )
    middle = middle_ref[...]
    normed_ref[...] = (middle * inv_rms(middle) * gain_ref[...]).astype(BF16)


def out_project(x, mixed, heads_t, gain, weights):
    vmem = pl.BlockSpec(memory_space=pltpu.VMEM)
    return pl.pallas_call(
        out_proj_kernel,
        in_specs=[vmem] * 8,
        out_specs=[vmem, vmem],
        out_shape=[jax.ShapeDtypeStruct(x.shape, F32), jax.ShapeDtypeStruct(x.shape, BF16)],
        compiler_params=pltpu.CompilerParams(vmem_limit_bytes=40 * MIB),
        cost_estimate=pl.CostEstimate(
            flops=2 * x.size * 2048, bytes_accessed=12 * MIB, transcendentals=0
        ),
        name="out_project",
    )(x, mixed, heads_t, gain[None], *weights)


def out_back_kernel(branch_ref, *refs):
    *weights, mixed_ref, heads_ref = refs
    wide = mixed_ref.shape[1] // 4
    narrow = heads_ref.shape[0] // 4
    for step, weight in zip(NEAR, weights):
        mixed_ref[:, near_at(step, wide)] = mat_right_t(branch_ref[...], weight[:wide])
        heads_ref[near_at(step, narrow), :] = mat_right_t(weight[wide:], branch_ref[...]).astype(
            BF16
        )


def out_unproject(branch, weights, mixed_width, heads_width):
    vmem = pl.BlockSpec(memory_space=pltpu.VMEM)
    tokens = branch.shape[0]
    return pl.pallas_call(
        out_back_kernel,
        in_specs=[vmem] * 5,
        out_specs=[vmem, vmem],
        out_shape=[
            jax.ShapeDtypeStruct((tokens, mixed_width), F32),
            jax.ShapeDtypeStruct((heads_width, tokens), BF16),
        ],
        compiler_params=pltpu.CompilerParams(vmem_limit_bytes=40 * MIB),
        cost_estimate=pl.CostEstimate(
            flops=2 * branch.size * 2048, bytes_accessed=12 * MIB, transcendentals=0
        ),
        name="out_unproject",
    )(branch, *weights)


FF_TILE = 512


def mlp_kernel(
    place_ref, normed_ref, top_ref, middle_ref, gain_ref, *refs
):
    gates, ups, downs = refs[0:4], refs[4:8], refs[8:12]
    layer_ref, grad_ref, branch_ref, gain_grad_ref, hidden_ref, pair_ref = refs[12:18]
    down_tile, out_sum, back_sum = refs[18:]
    step_at = pl.program_id(0)
    per_piece = pl.num_programs(0) // 4
    size = gates[0].shape[0]
    for piece in range(4):

        @pl.when(step_at // per_piece == piece)
        def _():
            down_tile[...] = downs[piece][...]

    gate = up = None
    for step, gate_ref, up_ref in zip(NEAR, gates, ups):
        rows = normed_ref[:, near_at(step, size)]
        gate_part, up_part = mat(rows, gate_ref[...]), mat(rows, up_ref[...])
        gate = gate_part if gate is None else gate + gate_part
        up = up_part if up is None else up + up_part
    sig = 1.0 / (1.0 + jnp.exp(-gate))
    silu = gate * sig
    hidden = (silu * up).astype(BF16)
    hidden_ref[...] = hidden
    grad_hidden = mat_right_t(top_ref[...], down_tile[...])
    grad_gate = (grad_hidden * up * (sig + silu * (1.0 - sig))).astype(BF16)
    grad_up = (grad_hidden * silu).astype(BF16)
    pair_ref[0] = grad_gate
    pair_ref[1] = grad_up

    @pl.when(step_at == 0)
    def _():
        out_sum[...] = jnp.zeros(out_sum.shape, F32)
        back_sum[...] = jnp.zeros(back_sum.shape, F32)

    out_sum[...] += mat(hidden, down_tile[...])
    for step, gate_ref, up_ref in zip(NEAR, gates, ups):
        back_sum[:, near_at(step, size)] += mat_right_t(grad_gate, gate_ref[...]) + mat_right_t(
            grad_up, up_ref[...]
        )

    @pl.when(step_at == pl.num_programs(0) - 1)
    def _():
        middle = middle_ref[...]
        layer_ref[...] = (middle + out_sum[...]).astype(BF16)
        grad_rows, grad_gain = rms_pull(middle, inv_rms(middle), gain_ref[...], back_sum[...])
        grad = top_ref[...].astype(F32) + grad_rows
        grad_ref[...] = grad
        branch_ref[...] = grad.astype(BF16)
        gain_grad_ref[...] = grad_gain[None]


def mlp_both(place, normed, top, middle, gain, gu_weights, down_weights):
    tokens, features = middle.shape
    size, columns = gu_weights[0].shape
    width = columns // 2
    steps = width // FF_TILE
    per_piece = steps // 4

    def natural(i, p):
        piece = i // per_piece
        near = (piece % 2) * 2 + piece // 2
        return (near ^ p[0]) * per_piece + i % per_piece

    whole = pl.BlockSpec((tokens, features), lambda i, p: (0, 0))
    gain_spec = pl.BlockSpec((1, features), lambda i, p: (0, 0))

    def down_spec(piece):
        return pl.BlockSpec(
            (FF_TILE, features),
            lambda i, p: (jnp.clip(i - piece * per_piece, 0, per_piece - 1), 0),
        )

    return pl.pallas_call(
        mlp_kernel,
        grid_spec=pltpu.PrefetchScalarGridSpec(
            num_scalar_prefetch=1,
            grid=(steps,),
            in_specs=[whole, whole, whole, gain_spec]
            + [pl.BlockSpec((size, FF_TILE), lambda i, p: (0, natural(i, p)))] * 4
            + [pl.BlockSpec((size, FF_TILE), lambda i, p: (0, natural(i, p) + steps))] * 4
            + [down_spec(piece) for piece in range(4)],
            out_specs=[
                whole,
                whole,
                whole,
                gain_spec,
                pl.BlockSpec((tokens, FF_TILE), lambda i, p: (0, natural(i, p))),
                pl.BlockSpec((2, tokens, FF_TILE), lambda i, p: (0, 0, natural(i, p))),
            ],
            scratch_shapes=[
                pltpu.VMEM((FF_TILE, features), BF16),
                pltpu.VMEM((tokens, features), F32),
                pltpu.VMEM((tokens, features), F32),
            ],
        ),
        out_shape=[
            jax.ShapeDtypeStruct((tokens, features), BF16),
            jax.ShapeDtypeStruct((tokens, features), F32),
            jax.ShapeDtypeStruct((tokens, features), BF16),
            jax.ShapeDtypeStruct((1, features), F32),
            jax.ShapeDtypeStruct((tokens, width), BF16),
            jax.ShapeDtypeStruct((2, tokens, width), BF16),
        ],
        compiler_params=pltpu.CompilerParams(vmem_limit_bytes=56 * MIB),
        cost_estimate=pl.CostEstimate(
            flops=12 * tokens * features * width, bytes_accessed=30 * MIB, transcendentals=0
        ),
        name="mlp_both",
    )(
        place,
        normed,
        top,
        middle,
        gain[None],
        *gu_weights,
        *gu_weights,
        *down_weights,
    )


EDGE = 8
EARLY_TILE = 256


def conv_inputs(edge_rows, own_rows):
    return jnp.concatenate([edge_rows, own_rows], axis=0)


def conv_valid(rel_start, tap, taps):
    rows = rel_start.shape[0]
    place = lax.broadcasted_iota(jnp.int32, (rows, 1), 0)
    return place - (taps - 1) + tap >= rel_start


def conv_sums(extended, weights, bias, rel_start):
    taps = weights.shape[0]
    rows = rel_start.shape[0]
    shifted = []
    total = None
    for tap in range(taps):
        begin = EDGE - (taps - 1) + tap
        part = jnp.where(
            conv_valid(rel_start, tap, taps), extended[begin : begin + rows], 0.0
        )
        shifted.append(part)
        term = weights[tap : tap + 1] * part
        total = bias + term if total is None else total + term
    return total, shifted


def early_kernel(
    count, x_ref, edge_ref, start_ref, weight_ref, bias_ref, *refs
):
    *blocks, conv_ref, edge_out, act_ref, dt_ref = refs
    size = blocks[0].shape[0]
    tile = pl.program_id(0)
    last = pl.num_programs(0) - 1

    def product(source):
        total = None
        for step, block in zip(NEAR, blocks):
            part = mat(source[:, near_at(step, size)], block[...])
            total = part if total is None else total + part
        return total

    value = product(x_ref)

    @pl.when(tile == last)
    def _():
        dt_ref[...] = value

    @pl.when(tile < last)
    def _():
        conv_ref[...] = value
        edge = product(edge_ref)
        edge_out[...] = edge
        rows = value.shape[0] // count
        for b in range(count):
            span = slice(b * rows, (b + 1) * rows)
            extended = conv_inputs(edge[b * EDGE : (b + 1) * EDGE], value[span])
            total, _ = conv_sums(extended, weight_ref[...], bias_ref[...], start_ref[span])
            act_ref[span] = total * sigmoid(total)


def conv_tile_spec(rows, count, begin=0):
    return pl.BlockSpec((rows, EARLY_TILE), lambda i: (0, jnp.clip(i - begin, 0, count - 1)))


def project_early(count, x, edge_x, rel_start, conv_weight, conv_bias, blocks):
    tokens, depth = x.shape
    size, columns = blocks[0].shape
    channels = conv_weight.shape[1]
    tiles = columns // EARLY_TILE
    conv_tiles = channels // EARLY_TILE

    def whole(array):
        return pl.BlockSpec(array.shape, lambda i: (0, 0))

    tile_shape = pl.BlockSpec((tokens, EARLY_TILE), lambda i: (0, 0))
    return pl.pallas_call(
        functools.partial(early_kernel, count),
        grid=(tiles,),
        in_specs=[
            whole(x),
            whole(edge_x),
            whole(rel_start),
            conv_tile_spec(conv_weight.shape[0], conv_tiles),
            conv_tile_spec(1, conv_tiles),
        ]
        + [pl.BlockSpec((size, EARLY_TILE), lambda i: (0, i))] * 4,
        out_specs=[
            conv_tile_spec(tokens, conv_tiles),
            conv_tile_spec(edge_x.shape[0], conv_tiles),
            conv_tile_spec(tokens, conv_tiles),
            tile_shape,
        ],
        out_shape=[
            jax.ShapeDtypeStruct((tokens, channels), F32),
            jax.ShapeDtypeStruct((edge_x.shape[0], channels), F32),
            jax.ShapeDtypeStruct((tokens, channels), F32),
            jax.ShapeDtypeStruct((tokens, EARLY_TILE), F32),
        ],
        compiler_params=pltpu.CompilerParams(vmem_limit_bytes=40 * MIB),
        cost_estimate=pl.CostEstimate(
            flops=2 * tokens * depth * columns, bytes_accessed=16 * MIB, transcendentals=0
        ),
        name="project_early",
    )(x, edge_x, rel_start, conv_weight, conv_bias[None], *blocks)


def conv_back(extended, weights, bias, rel_start, grad_act):
    total, shifted = conv_sums(extended, weights, bias, rel_start)
    gate = sigmoid(total)
    return grad_act * gate * (1.0 + total * (1.0 - gate)), shifted


def edge_grad_kernel(
    dx_ref, db_ref, dc_ref, conv_ref, edge_ref, start_ref, weight_ref, bias_ref, out_ref
):
    taps = weight_ref.shape[0]
    grad_act = jnp.concatenate([dx_ref[...], db_ref[...], dc_ref[...]], axis=1)
    extended = conv_inputs(edge_ref[...], conv_ref[...])
    grad, _ = conv_back(extended, weight_ref[...], bias_ref[...], start_ref[...], grad_act)
    total = jnp.zeros(grad.shape, F32)
    for tap in range(taps):
        part = jnp.where(
            conv_valid(start_ref[...], tap, taps), grad * weight_ref[tap : tap + 1], 0.0
        )
        padded = jnp.concatenate([jnp.zeros(part.shape, F32), part], axis=0)
        total = total + padded[taps - 1 - tap : taps - 1 - tap + EDGE]
    out_ref[...] = total


def edge_grads(count, dx, db, dc, conv_rows, edge_rows, rel_start, conv_weight, conv_bias):
    rows = dx.shape[0] // count
    steps = rows // EDGE

    def first(array):
        return pl.BlockSpec((EDGE, array.shape[1]), lambda b: (b * steps, 0))

    channels = conv_weight.shape[1]
    return pl.pallas_call(
        edge_grad_kernel,
        grid=(count,),
        in_specs=[
            first(dx),
            first(db),
            first(dc),
            first(conv_rows),
            pl.BlockSpec((EDGE, channels), lambda b: (b, 0)),
            first(rel_start),
            pl.BlockSpec(conv_weight.shape, lambda b: (0, 0)),
            pl.BlockSpec((1, channels), lambda b: (0, 0)),
        ],
        out_specs=pl.BlockSpec((EDGE, channels), lambda b: (b, 0)),
        out_shape=jax.ShapeDtypeStruct((count * EDGE, channels), F32),
        compiler_params=pltpu.CompilerParams(vmem_limit_bytes=16 * MIB),
        cost_estimate=pl.CostEstimate(flops=MIB, bytes_accessed=MIB, transcendentals=0),
        name="edge_grads",
    )(dx, db, dc, conv_rows, edge_rows, rel_start, conv_weight, conv_bias[None])


def early_back_kernel(
    count,
    base_ref,
    kv_ref,
    dx_ref,
    db_ref,
    dc_ref,
    conv_ref,
    edge_ref,
    came_ref,
    dt_ref,
    start_ref,
    weight_ref,
    bias_ref,
    x_ref,
    gain_ref,
    middle_ref,
    *refs,
):
    *blocks, grad_ref, conv_grad_ref, input_ref, gain_grad_ref, total = refs
    blocks, kv_blocks = blocks[:4], blocks[4:]
    size = blocks[0].shape[0]
    tile = pl.program_id(0)
    last = pl.num_programs(0) - 1
    taps = weight_ref.shape[0]

    @pl.when(tile == 0)
    def _():
        total[...] = base_ref[...]
        grad_ref[...] = kv_ref[...]
        for step, block in zip(NEAR, kv_blocks):
            total[:, near_at(step, size)] += mat_right_t(kv_ref[...], block[...])

    @pl.when(tile == last)
    def _():
        grad_ref[...] = dt_ref[...]

    @pl.when((tile > 0) & (tile < last))
    def _():
        rows = dx_ref.shape[0] // count
        tail = jnp.concatenate([db_ref[...], dc_ref[...]], axis=1)
        grad_act = jnp.where(tile == last - 1, tail, dx_ref[...])
        sums = [None] * (taps + 1)
        for b in range(count):
            span = slice(b * rows, (b + 1) * rows)
            ends = slice(b * EDGE, (b + 1) * EDGE)
            extended = conv_inputs(edge_ref[ends], conv_ref[span])
            rel_start = start_ref[span]
            grad, shifted = conv_back(
                extended, weight_ref[...], bias_ref[...], rel_start, grad_act[span]
            )
            back = jnp.concatenate(
                [jnp.zeros((rows - EDGE, grad.shape[1]), F32), came_ref[ends]], axis=0
            )
            for tap in range(taps):
                part = jnp.where(
                    conv_valid(rel_start, tap, taps), grad * weight_ref[tap : tap + 1], 0.0
                )
                padded = jnp.concatenate([part, jnp.zeros((EDGE, part.shape[1]), F32)], axis=0)
                back = back + padded[taps - 1 - tap : taps - 1 - tap + rows]
                term = jnp.sum(grad * shifted[tap], axis=0, keepdims=True)
                sums[tap] = term if sums[tap] is None else sums[tap] + term
            term = jnp.sum(grad, axis=0, keepdims=True)
            sums[taps] = term if sums[taps] is None else sums[taps] + term
            grad_ref[span] = back.astype(BF16)
        conv_grad_ref[0 : taps + 1] = jnp.concatenate(sums, axis=0)
        conv_grad_ref[taps + 1 :] = jnp.zeros(
            (conv_grad_ref.shape[0] - taps - 1, grad_act.shape[1]), F32
        )

    @pl.when(tile > 0)
    def _():
        for step, block in zip(NEAR, blocks):
            total[:, near_at(step, size)] += mat_right_t(grad_ref[...], block[...])

    @pl.when(tile == last)
    def _():
        x = x_ref[...].astype(F32)
        grad_rows, grad_gain = rms_pull(x, inv_rms(x), gain_ref[...], total[...])
        input_ref[...] = (middle_ref[...] + grad_rows).astype(BF16)
        gain_grad_ref[...] = grad_gain[None]


def early_back(
    count,
    base,
    grad_kv,
    dx,
    db,
    dc,
    conv_rows,
    edge_rows,
    came,
    dt_grad,
    rel_start,
    conv_weight,
    conv_bias,
    x,
    gain,
    grad_middle,
    blocks,
    kv_blocks,
):
    tokens, depth = base.shape
    size, columns = blocks[0].shape
    channels = conv_weight.shape[1]
    tiles = columns // EARLY_TILE + 1
    conv_tiles = channels // EARLY_TILE

    def whole(array):
        return pl.BlockSpec(array.shape, lambda i: (0, 0))

    return pl.pallas_call(
        functools.partial(early_back_kernel, count),
        grid=(tiles,),
        in_specs=[
            whole(base),
            whole(grad_kv),
            conv_tile_spec(tokens, conv_tiles - 1, 1),
            whole(db),
            whole(dc),
            conv_tile_spec(tokens, conv_tiles, 1),
            conv_tile_spec(edge_rows.shape[0], conv_tiles, 1),
            conv_tile_spec(edge_rows.shape[0], conv_tiles, 1),
            whole(dt_grad),
            whole(rel_start),
            conv_tile_spec(conv_weight.shape[0], conv_tiles, 1),
            conv_tile_spec(1, conv_tiles, 1),
            whole(x),
            pl.BlockSpec((1, depth), lambda i: (0, 0)),
            whole(grad_middle),
        ]
        + [pl.BlockSpec((size, EARLY_TILE), lambda i: (0, jnp.maximum(i - 1, 0)))] * 4
        + [pl.BlockSpec((size, EARLY_TILE), lambda i: (0, 0))] * 4,
        out_specs=[
            pl.BlockSpec((tokens, EARLY_TILE), lambda i: (0, i)),
            conv_tile_spec(8, conv_tiles, 1),
            whole(x),
            pl.BlockSpec((1, depth), lambda i: (0, 0)),
        ],
        out_shape=[
            jax.ShapeDtypeStruct((tokens, columns + EARLY_TILE), BF16),
            jax.ShapeDtypeStruct((8, channels), F32),
            jax.ShapeDtypeStruct(x.shape, BF16),
            jax.ShapeDtypeStruct((1, depth), F32),
        ],
        scratch_shapes=[pltpu.VMEM((tokens, depth), F32)],
        compiler_params=pltpu.CompilerParams(vmem_limit_bytes=48 * MIB),
        cost_estimate=pl.CostEstimate(
            flops=2 * tokens * depth * columns, bytes_accessed=20 * MIB, transcendentals=0
        ),
        name="early_back",
    )(
        base,
        grad_kv,
        dx,
        db,
        dc,
        conv_rows,
        edge_rows,
        came,
        dt_grad,
        rel_start,
        conv_weight,
        conv_bias[None],
        x,
        gain[None],
        grad_middle,
        *blocks,
        *kv_blocks,
    )


def block_grads_kernel(steps, left_ref, right_ref, *refs):
    came = refs[0] if len(refs) == 3 else None
    outs = refs[-2:] if came is not None else refs
    size = left_ref.shape[1] // 4
    for place, step in enumerate(steps):
        value = mat_left_t(left_ref[:, near_at(step, size)], right_ref[0])
        if came is None:
            outs[0][place * size : (place + 1) * size] = value.astype(BF16)
        else:
            value = value + came[place * size : (place + 1) * size].astype(F32)
            outs[place][...] = value.astype(BF16)


def block_grads(left, right, steps, came=None):
    tokens, depth = left.shape
    size = depth // 4
    parts, _, width = right.shape
    per_part = width // TILE_COLS
    columns = parts * width
    tall = pl.BlockSpec((2 * size, TILE_COLS), lambda i: (0, i))
    flat = pl.BlockSpec((size, TILE_COLS), lambda i: (0, i))
    operands = [left, right] + ([] if came is None else [came])
    return pl.pallas_call(
        functools.partial(block_grads_kernel, steps),
        grid=(columns // TILE_COLS,),
        in_specs=[
            pl.BlockSpec((tokens, depth), lambda i: (0, 0)),
            pl.BlockSpec((1, tokens, TILE_COLS), lambda i: (i // per_part, 0, i % per_part)),
        ]
        + ([] if came is None else [tall]),
        out_specs=[tall] if came is None else [flat, flat],
        out_shape=[jax.ShapeDtypeStruct((2 * size, columns), BF16)]
        if came is None
        else [jax.ShapeDtypeStruct((size, columns), BF16)] * 2,
        compiler_params=pltpu.CompilerParams(vmem_limit_bytes=32 * MIB),
        cost_estimate=pl.CostEstimate(
            flops=4 * tokens * size * columns, bytes_accessed=6 * MIB, transcendentals=0
        ),
        name="block_grads",
    )(*operands)


def finish_kernel(
    conv_width, early_ref, late_ref, mix_ref, in_ref, q_ref, kv_ref, out_ref, o_ref
):
    kv_width = kv_ref.shape[1]
    gate = in_ref.shape[1] - conv_width
    in_ref[:, :gate] = late_ref[:, :gate].astype(F32)
    in_ref[:, gate:] = early_ref[:, kv_width:].astype(F32)
    q_ref[...] = late_ref[:, gate:].astype(F32)
    kv_ref[...] = early_ref[:, :kv_width].astype(F32)
    split = out_ref.shape[0]
    out_ref[...] = mix_ref[:split].astype(F32)
    o_ref[...] = mix_ref[split:].astype(F32)


def finish(early, late, mix, shapes, conv_width):
    vmem = pl.BlockSpec(memory_space=pltpu.VMEM)
    return pl.pallas_call(
        functools.partial(finish_kernel, conv_width),
        in_specs=[vmem] * 3,
        out_specs=[vmem] * 5,
        out_shape=[jax.ShapeDtypeStruct(shape, F32) for shape in shapes],
        compiler_params=pltpu.CompilerParams(vmem_limit_bytes=32 * MIB),
        cost_estimate=pl.CostEstimate(flops=MIB, bytes_accessed=10 * MIB, transcendentals=0),
        name="finish",
    )(early, late, mix)


def passed_along(block, axis, distance):
    devices = range(lax.axis_size(axis))
    route = [(i - distance, i) for i in devices if i - distance in devices]
    return lax.ppermute(block, axis, route)


def swapped(block, axis, bit):
    return lax.ppermute(block, axis, [(i, i ^ bit) for i in range(lax.axis_size(axis))])


def bits_of(axis):
    return [1 << k for k in range(lax.axis_size(axis).bit_length() - 1)]


def after(value, earlier):
    return lax.optimization_barrier((value, earlier))[0]


def gathered_near(shard, earlier=None, held=None):
    if earlier is not None:
        shard = after(shard, earlier)
    across = swapped(shard, "wsh", 2)
    if held is not None:
        across = after(across, held)
    return [shard, across, swapped(shard, "wsh", 1), swapped(across, "wsh", 1)]


class Gathering:
    def __init__(self, rows, bits):
        self.table = rows[None]
        self.bits = list(bits)
        self.start()

    def start(self):
        if self.bits:
            self.came = swapped(self.table, "ctx", self.bits.pop(0))
        else:
            self.came = None

    def advance(self, held=None):
        if self.came is not None:
            came = self.came if held is None else after(self.came, held)
            self.table = jnp.concatenate([self.table, came], axis=0)
            self.start()
        return self.table

    def finish(self):
        while self.came is not None:
            self.advance()
        return self.table


class Scattering:
    def __init__(self, table, bits):
        self.table = table
        self.bits = list(bits)
        self.start()

    def start(self):
        if self.bits:
            half = self.table.shape[0] // 2
            self.came = swapped(self.table[half:], "ctx", self.bits.pop(0))
        else:
            self.came = None

    def advance(self, held=None):
        if self.came is not None:
            came = self.came if held is None else after(self.came, held)
            half = self.table.shape[0] // 2
            self.table = (self.table[:half].astype(F32) + came.astype(F32)).astype(BF16)
            self.start()
        return self.table

    def finish(self):
        while self.came is not None:
            self.advance()
        return self.table[0]


def ctx_bits(count):
    return [1 << k for k in range(count.bit_length() - 1)]


def partner_wsh(step):
    return (lax.axis_index("ctx"), lax.axis_index("wsh") ^ step)


def partner_ctx(step):
    return (lax.axis_index("ctx") ^ step, lax.axis_index("wsh"))


def remote(source, target, send, recv, device):
    return pltpu.make_async_remote_copy(
        src_ref=source,
        dst_ref=target,
        send_sem=send,
        recv_sem=recv,
        device_id=device,
        device_id_type=pl.DeviceIdType.MESH,
    )


def grads_kernel(
    count,
    split,
    early_units,
    late_units,
    one_ref,
    mix_ref,
    heads_ref,
    early_ref,
    late_ref,
    branch_ref,
    small_ref,
    early_out,
    late_out,
    mix_out,
    small_out,
    core_out,
    work,
    y_in,
    ctx_in,
    final,
    small_in,
    core_sems,
    y_sems,
    rs_sems,
    ag_sems,
    small_sems,
    out_sems,
):
    bits = ctx_bits(count)
    here = lax.axis_index("ctx")
    units = work.shape[0]
    rows = work.shape[2]
    width = work.shape[3]
    wsh_steps = (1, 2)
    barrier = pltpu.get_barrier_semaphore()
    partners = [partner_wsh(step) for step in wsh_steps] + [partner_ctx(bit) for bit in bits]
    for device in partners:
        pl.semaphore_signal(
            barrier, inc=1, device_id=device, device_id_type=pl.DeviceIdType.MESH
        )
    pl.semaphore_wait(barrier, len(partners))

    sizes = [rows >> (k + 1) for k in range(len(bits))]
    starts = []
    others = []
    base = 0
    for bit, size in zip(bits, sizes):
        upper = (here // bit) % 2
        others.append(base + (1 - upper) * size)
        base = base + upper * size
        starts.append(base)

    def span(start, size):
        return pl.ds(pl.multiple_of(start, 16), size)

    def core_copy(u):
        return remote(
            core_out.at[u % 2],
            work.at[u],
            core_sems.at[0, u],
            core_sems.at[1, u],
            partner_wsh(1),
        )

    def y_copy(u):
        return remote(work.at[u, 1], y_in.at[u], y_sems.at[0, u], y_sems.at[1, u], partner_wsh(2))

    recv_base = [rows - (rows >> k) for k in range(len(bits))]

    def rs_copy(u, k):
        return remote(
            work.at[u, 0, span(others[k], sizes[k])],
            ctx_in.at[u, pl.ds(recv_base[k], sizes[k])],
            rs_sems.at[0, k, u],
            rs_sems.at[1, k, u],
            partner_ctx(bits[k]),
        )

    def ag_copy(u, k):
        return remote(
            final.at[u, span(starts[k], sizes[k])],
            final.at[u, span(starts[k], sizes[k])],
            ag_sems.at[0, k, u],
            ag_sems.at[1, k, u],
            partner_ctx(bits[k]),
        )

    limits = []
    first_unit = 0
    for size in (early_units, late_units, 4):
        limits.append((first_unit, first_unit + size))
        first_unit += size
    outs = (early_out, late_out, mix_out)

    def by_part(u, action):
        for part, (low, high) in enumerate(limits):
            pl.when((u >= low) & (u < high))(functools.partial(action, part, u - low))

    def each_out(u, act):
        def one(part, v):
            tall = part == 2
            for i in range(split):
                row = (v // 2) * TILE_ROWS if tall else 0
                column = ((v % 2) if tall else v) * TILE_COLS + i * width
                copy = pltpu.make_async_copy(
                    final.at[u, pl.ds(i * TILE_ROWS, TILE_ROWS)],
                    outs[part].at[
                        pl.ds(pl.multiple_of(row, TILE_ROWS), TILE_ROWS),
                        pl.ds(pl.multiple_of(column, 128), width),
                    ],
                    out_sems.at[u, i],
                )
                act(copy)

        by_part(u, one)

    def columns_at(v):
        return pl.ds(pl.multiple_of(v * TILE_COLS, 128), TILE_COLS)

    wide = mix_ref.shape[1] // 4
    narrow = heads_ref.shape[0] // 4

    def pieces(u, first, put):
        steps = NEAR[2 * first : 2 * first + 2]

        def one(part, v):
            for place, step in enumerate(steps):
                if part < 2:
                    left = one_ref[:, near_at(step, TILE_ROWS)]
                    value = mat_left_t(left, (early_ref, late_ref)[part][:, columns_at(v)])
                else:
                    right = branch_ref[:, columns_at(v % 2)]
                    other = lax.axis_index("wsh") ^ step
                    begin = pl.multiple_of(other * wide, 128)

                    @pl.when(v < 2)
                    def _():
                        put(place, mat_left_t(mix_ref[:, pl.ds(begin, TILE_ROWS)], right))

                    @pl.when(v >= 2)
                    def _():
                        tail_at = pl.multiple_of(begin + TILE_ROWS, 128)
                        tail = mat_left_t(mix_ref[:, pl.ds(tail_at, wide - TILE_ROWS)], right)
                        heads_at = pl.multiple_of(other * narrow, 128)
                        heads = mat(heads_ref[pl.ds(heads_at, narrow), :], right)
                        put(place, jnp.concatenate([tail, heads], axis=0))

                    continue
                put(place, value)

        by_part(u, one)

    def chunked(value):
        return [
            (slice(i * TILE_ROWS, (i + 1) * TILE_ROWS), value[:, i * width : (i + 1) * width])
            for i in range(split)
        ]

    def begin(u):
        def put(place, value):
            for where, part in chunked(value):
                core_out[u % 2, place, where] = part.astype(BF16)

        pieces(u, 1, put)
        core_copy(u).start()

    def after_core(u):
        core_copy(u).wait()

        def put(place, value):
            for where, part in chunked(value):
                work[u, place, where] = (work[u, place, where].astype(F32) + part).astype(BF16)

        pieces(u, 0, put)
        y_copy(u).start()

    def after_y(u):
        y_copy(u).wait()
        work[u, 0] = (work[u, 0].astype(F32) + y_in[u].astype(F32)).astype(BF16)
        rs_copy(u, 0).start()

    def after_rs(u, k):
        rs_copy(u, k).wait()
        mine = span(starts[k], sizes[k])
        total = work[u, 0, mine].astype(F32) + ctx_in[
            u, pl.ds(recv_base[k], sizes[k])
        ].astype(F32)
        if k + 1 < len(bits):
            work[u, 0, mine] = total.astype(BF16)
            rs_copy(u, k + 1).start()
        else:
            final[u, mine] = total.astype(BF16)
            ag_copy(u, k).start()

    def after_ag(u, k):
        ag_copy(u, k).wait()
        if k > 0:
            ag_copy(u, k - 1).start()
        else:
            each_out(u, lambda copy: copy.start())

    stages = [(0, begin), (1, after_core), (3, after_y)]
    delay = 3
    for k in range(len(bits)):
        delay += 1
        stages.append((delay, functools.partial(after_rs, k=k)))
    for k in range(len(bits) - 1, -1, -1):
        delay += 1
        stages.append((delay, functools.partial(after_ag, k=k)))

    small_out[...] = small_ref[...]
    hops = partners

    def small_copy(k):
        return remote(
            small_in.at[k, 0], small_in.at[k, 1], small_sems.at[0, k], small_sems.at[1, k], hops[k]
        )

    def small_step(k):
        if k > 0:
            small_copy(k - 1).wait()
            small_out[...] += small_in[k - 1, 1]
        if k < len(hops):
            small_in[k, 0] = small_out[...]
            small_copy(k).start()

    def one_step(t, carry):
        for k in range(len(hops) + 1):
            pl.when(t == 2 * k + 1)(functools.partial(small_step, k))
        for offset, stage in stages[::-1]:
            u = t - offset
            pl.when((u >= 0) & (u < units))(functools.partial(stage, u))
        return carry

    lax.fori_loop(0, units + delay, one_step, 0)

    def finish(u, carry):
        each_out(u, lambda copy: copy.wait())
        return carry

    lax.fori_loop(0, units, finish, 0)


def reduce_grads(
    count, early_width, one, mixed, heads_t, early, late, branch, small
):
    bits = ctx_bits(count)
    hops = len(bits) + 2
    split = max(1, 16 * count // TILE_ROWS)
    early_units = early_width // TILE_COLS
    late_units = late.shape[1] // TILE_COLS
    units = early_units + late_units + 4
    rows, width = TILE_ROWS * split, TILE_COLS // split
    dma = pltpu.SemaphoreType.DMA
    vmem = pl.BlockSpec(memory_space=pltpu.VMEM)
    hbm = pl.BlockSpec(memory_space=pl.ANY)
    return pl.pallas_call(
        functools.partial(grads_kernel, count, split, early_units, late_units),
        in_specs=[vmem] * 7,
        out_specs=[hbm] * 3 + [vmem],
        out_shape=[
            jax.ShapeDtypeStruct((TILE_ROWS, early_units * TILE_COLS), BF16),
            jax.ShapeDtypeStruct((TILE_ROWS, late_units * TILE_COLS), BF16),
            jax.ShapeDtypeStruct((2 * TILE_ROWS, 2 * TILE_COLS), BF16),
            jax.ShapeDtypeStruct(small.shape, F32),
        ],
        scratch_shapes=[
            pltpu.VMEM((2, 2, rows, width), BF16),
            pltpu.VMEM((units, 2, rows, width), BF16),
            pltpu.VMEM((units, rows, width), BF16),
            pltpu.VMEM((units, rows, width), BF16),
            pltpu.VMEM((units, rows, width), BF16),
            pltpu.VMEM((hops, 2) + small.shape, F32),
            dma((2, units)),
            dma((2, units)),
            dma((2, len(bits), units)),
            dma((2, len(bits), units)),
            dma((2, hops)),
            dma((units, split)),
        ],
        compiler_params=pltpu.CompilerParams(
            collective_id=1, has_side_effects=True, vmem_limit_bytes=62 * MIB
        ),
        cost_estimate=pl.CostEstimate(
            flops=6_500_000_000, bytes_accessed=30 * MIB, transcendentals=0
        ),
        name="reduce_grads",
    )(one, mixed, heads_t, early, late, branch, small)


def exchange_barrier(devices):
    barrier = pltpu.get_barrier_semaphore()
    for device in devices:
        pl.semaphore_signal(
            barrier, inc=1, device_id=device, device_id_type=pl.DeviceIdType.MESH
        )
    pl.semaphore_wait(barrier, len(devices))


def row_factors(totals, owner):
    rows = owner.shape[0]
    picks = (owner == lax.broadcasted_iota(jnp.int32, (rows, 128), 1)).astype(F32)
    return exact(picks, totals, 1, 1)[:, :1]


class StateExchange:
    def __init__(self, count, forward, state_ref, totals, result, sent, came, back, sems):
        self.count, self.forward = count, forward
        self.state_ref, self.totals, self.result = state_ref, totals, result
        self.sent, self.came, self.back, self.sems = sent, came, back, sems
        self.here = lax.axis_index("ctx")
        self.share = state_ref.shape[1] // count

    def rows_of(self, place):
        return pl.ds(pl.multiple_of(place * self.share, 16), self.share)

    def out_copy(self, k):
        return remote(
            self.sent.at[:, self.rows_of(self.here ^ k)],
            self.came.at[self.here],
            self.sems.at[0, k],
            self.sems.at[1, k],
            partner_ctx(k),
        )

    def in_copy(self, k):
        return remote(
            self.sent.at[:, self.rows_of(self.here ^ k)],
            self.came.at[self.here ^ k],
            self.sems.at[0, k],
            self.sems.at[1, k],
            partner_ctx(k),
        )

    def back_copy(self, k):
        return remote(
            self.back.at[self.here ^ k],
            self.result.at[:, self.rows_of(self.here)],
            self.sems.at[2, k],
            self.sems.at[3, k],
            partner_ctx(k),
        )

    def back_in(self, k):
        return remote(
            self.back.at[self.here ^ k],
            self.result.at[:, self.rows_of(self.here ^ k)],
            self.sems.at[2, k],
            self.sems.at[3, k],
            partner_ctx(k),
        )

    def begin(self):
        self.sent[...] = self.state_ref[...].astype(BF16)
        for k in range(1, self.count):
            self.out_copy(k).start()
        self.came[self.here] = self.state_ref[:, self.rows_of(self.here), :].astype(BF16)

    def middle(self):
        for k in range(1, self.count):
            self.out_copy(k).wait_send()
            self.in_copy(k).wait_recv()
        place = lax.broadcasted_iota(jnp.int32, (self.share, 128), 0) + self.here * self.share
        owner = place // MDIM
        order = range(self.count) if self.forward else range(self.count - 1, -1, -1)
        for b in range(self.state_ref.shape[0]):
            total = jnp.zeros((self.share, STATE), F32)
            for block in order:
                self.back[block, b] = total.astype(BF16)
                factor = row_factors(self.totals[block, b], owner)
                total = factor * total + self.came[block, b].astype(F32)
        for k in range(1, self.count):
            self.back_copy(k).start()
        self.result[:, self.rows_of(self.here), :] = self.back[self.here]

    def end(self):
        for k in range(1, self.count):
            self.back_copy(k).wait_send()
            self.back_in(k).wait_recv()


def mix_forward_kernel(
    count,
    start_ref,
    q_ref,
    near_ref,
    state_ref,
    total_ref,
    out_ref,
    log_ref,
    table_out,
    state_out,
    totals_out,
    q_wide,
    top,
    total,
    acc,
    far,
    totals,
    sent,
    came,
    back,
    result,
    total_sems,
    table_sems,
    state_sems,
):
    here = lax.axis_index("ctx")
    batch = near_ref.shape[1]
    width = near_ref.shape[2]
    half = count // 2
    exchange_barrier([partner_ctx(k) for k in range(1, count)])
    totals[here] = total_ref[...]

    def total_copy(k, place):
        return remote(
            totals.at[here],
            totals.at[place],
            total_sems.at[0, k],
            total_sems.at[1, k],
            partner_ctx(k),
        )

    def table_copy(i):
        return remote(
            near_ref.at[i], far.at[i], table_sems.at[0, i], table_sems.at[1, i], partner_ctx(1)
        )

    for k in range(1, count):
        total_copy(k, here).start()
    states = StateExchange(
        count, True, state_ref, totals, result, sent, came, back, state_sems
    )
    states.begin()
    for i in range(half):
        table_copy(i).start()
    for b in range(batch):
        spread_heads(q_ref.at[:, b * width : (b + 1) * width], q_wide.at[b], HDIM**-0.5)
    top[...] = jnp.full(top.shape, MASKED_SCORE, F32)
    total[...] = jnp.zeros(total.shape, F32)
    acc[...] = jnp.zeros(acc.shape, F32)
    first_pos = here * width

    def attend(b, source, i, block):
        kv_rows = source[i, b]
        keys = kv_rows[:, : KVHEADS * HDIM]
        values_t = kv_rows[:, KVHEADS * HDIM :].T
        allowed = attend_allowed(block, first_pos, start_ref[b][:1], width)
        tops, totals_now = top[b], total[b]
        new_tops, new_totals = [], []
        for head in range(QHEADS):
            group = head // (QHEADS // KVHEADS)
            line = slice(head, head + 1)
            scores = mat(keys, q_wide[b, :, head * width : (head + 1) * width])
            scores = jnp.where(allowed, scores, MASKED_SCORE)
            old = tops[line]
            new = jnp.maximum(old, jnp.max(scores, axis=0, keepdims=True))
            terms = jnp.exp(scores - new)
            shrink = jnp.exp(old - new)
            new_tops.append(new)
            new_totals.append(
                totals_now[line] * shrink + jnp.sum(terms, axis=0, keepdims=True)
            )
            acc[b, head] = acc[b, head] * shrink + mat(
                values_t[group * HDIM : (group + 1) * HDIM, :], terms.astype(BF16)
            )
        top[b] = jnp.concatenate(new_tops, axis=0)
        total[b] = jnp.concatenate(new_totals, axis=0)

    bits = ctx_bits(count)
    high = len(bits) - 1

    def step_of(i):
        return sum(((i // (1 << p)) % 2) * (1 << (high - p)) for p in range(high))

    def pair(source, low):
        def one(i, carry):
            block = here ^ (step_of(i) + low)

            @pl.when(block <= here)
            def _():
                for b in range(batch):
                    attend(b, source, i, block)

            return carry

        lax.fori_loop(0, half, one, 0)

    pair(near_ref, 0)
    for k in range(1, count):
        total_copy(k, here).wait_send()
        total_copy(k, here ^ k).wait_recv()
    states.middle()
    for i in range(half):
        table_copy(i).wait()
    pair(far, 1)
    for b in range(batch):
        for head in range(QHEADS):
            out_ref[head * HDIM : (head + 1) * HDIM, b * width : (b + 1) * width] = (
                acc[b, head] / total[b, head : head + 1, :]
            ).astype(BF16)
        log_ref[b] = top[b] + jnp.log(total[b])
    table_out[:half] = near_ref[...]
    table_out[half:] = far[...]
    totals_out[...] = totals[...]
    states.end()
    state_out[...] = result[...]


def mix_forward(count, starts, queries_t, near, state, total):
    half, batch, width, kv_width = near.shape
    vmem = pl.BlockSpec(memory_space=pltpu.VMEM)
    dma = pltpu.SemaphoreType.DMA
    share = state.shape[1] // count
    low = functools.partial(jax.ShapeDtypeStruct, dtype=BF16)
    wide = functools.partial(jax.ShapeDtypeStruct, dtype=F32)
    return pl.pallas_call(
        functools.partial(mix_forward_kernel, count),
        in_specs=[vmem] * 5,
        out_specs=[vmem] * 5,
        out_shape=[
            low(queries_t.shape),
            wide((batch, QHEADS, width)),
            low((count,) + near.shape[1:]),
            low(state.shape),
            wide((count,) + total.shape),
        ],
        scratch_shapes=[
            pltpu.VMEM((batch, KVHEADS * HDIM, QHEADS * width), BF16),
            pltpu.VMEM((batch, QHEADS, width), F32),
            pltpu.VMEM((batch, QHEADS, width), F32),
            pltpu.VMEM((batch, QHEADS, HDIM, width), F32),
            pltpu.VMEM(near.shape, BF16),
            pltpu.VMEM((count,) + total.shape, F32),
            pltpu.VMEM(state.shape, BF16),
            pltpu.VMEM((count, batch, share, STATE), BF16),
            pltpu.VMEM((count, batch, share, STATE), BF16),
            pltpu.VMEM(state.shape, BF16),
            dma((2, count)),
            dma((2, half)),
            dma((4, count)),
        ],
        compiler_params=pltpu.CompilerParams(
            collective_id=2, has_side_effects=True, vmem_limit_bytes=56 * MIB
        ),
        cost_estimate=pl.CostEstimate(
            flops=batch * count * width * width * 8 * 1000,
            bytes_accessed=4 * MIB,
            transcendentals=0,
        ),
        name="mix_forward",
    )(starts, queries_t, near, state, total)


def mix_backward_kernel(
    count,
    start_ref,
    q_ref,
    table_ref,
    attended_ref,
    grad_ref,
    log_ref,
    state_ref,
    totals_ref,
    dq_ref,
    dkv_ref,
    later_ref,
    q_wide,
    g_wide,
    q_tall,
    g_tall,
    delta,
    acc,
    mine,
    theirs,
    far,
    sent,
    came,
    back,
    result,
    table_sems,
    state_sems,
):
    here = lax.axis_index("ctx")
    batch = table_ref.shape[1]
    width = table_ref.shape[2]
    half = count // 2
    kv_width = KVHEADS * HDIM
    exchange_barrier([partner_ctx(k) for k in range(1, count)])
    states = StateExchange(
        count, False, state_ref, totals_ref, result, sent, came, back, state_sems
    )
    states.begin()
    first_pos = here * width
    acc[...] = jnp.zeros(acc.shape, F32)
    mine[...] = jnp.zeros(mine.shape, BF16)
    theirs[...] = jnp.zeros(theirs.shape, BF16)
    for b in range(batch):
        columns = slice(b * width, (b + 1) * width)
        spread_heads(q_ref.at[:, columns], q_wide.at[b], HDIM**-0.5)
        spread_heads(grad_ref.at[:, columns], g_wide.at[b], 1.0)
        for head in range(QHEADS):
            lanes = slice(head * width, (head + 1) * width)
            q_tall[b, lanes, :] = q_wide[b, :, lanes].T
            g_tall[b, lanes, :] = g_wide[b, :, lanes].T
            span = slice(head * HDIM, (head + 1) * HDIM)
            delta[b, head : head + 1, :] = jnp.sum(
                attended_ref[span, columns].astype(F32) * grad_ref[span, columns].astype(F32),
                axis=0,
                keepdims=True,
            )

    def attend(b, place, block, target, i):
        kv_rows = table_ref[place, b]
        keys = kv_rows[:, :kv_width]
        values = kv_rows[:, kv_width:]
        keys_t = keys.T
        allowed = attend_allowed(block, first_pos, start_ref[b][:1], width)
        logs_now, deltas = log_ref[b], delta[b]
        dk = jnp.zeros((width, kv_width), F32)
        dv = jnp.zeros((width, kv_width), F32)
        for head in range(QHEADS):
            group = head // (QHEADS // KVHEADS)
            lanes = slice(head * width, (head + 1) * width)
            line = slice(head, head + 1)
            scores = mat(keys, q_wide[b, :, lanes])
            shifted = jnp.where(allowed, scores - logs_now[line], MASKED_SCORE)
            probs = jnp.exp(shifted)
            grad_probs = mat(values, g_wide[b, :, lanes])
            grad_scores = (probs * (grad_probs - deltas[line])).astype(BF16)
            dk = dk + mat(grad_scores, q_tall[b, lanes, :])
            dv = dv + mat(probs.astype(BF16), g_tall[b, lanes, :])
            acc[b, head] += mat(keys_t[group * HDIM : (group + 1) * HDIM, :], grad_scores)
        target[i, b] = jnp.concatenate([dk, dv], axis=1).astype(BF16)

    bits = ctx_bits(count)
    high = len(bits) - 1

    def step_of(i):
        return sum(((i // (1 << p)) % 2) * (1 << (high - p)) for p in range(high))

    def pair(target, low):
        def one(i, carry):
            block = here ^ (step_of(i) + low)

            @pl.when(block <= here)
            def _():
                for b in range(batch):
                    attend(b, i + low * half, block, target, i)

            return carry

        lax.fori_loop(0, half, one, 0)

    def table_copy(i):
        return remote(
            theirs.at[i], far.at[i], table_sems.at[0, i], table_sems.at[1, i], partner_ctx(1)
        )

    pair(theirs, 1)
    for i in range(half):
        table_copy(i).start()
    states.middle()
    pair(mine, 0)
    for b in range(batch):
        for head in range(QHEADS):
            dq_ref[head * HDIM : (head + 1) * HDIM, b * width : (b + 1) * width] = (
                acc[b, head] * HDIM**-0.5
            ).astype(BF16)
    for i in range(half):
        table_copy(i).wait()
    dkv_ref[...] = (mine[...].astype(F32) + far[...].astype(F32)).astype(BF16)
    states.end()
    later_ref[...] = result[...]


def mix_backward(count, starts, queries_t, table, attended_t, grad_t, logs, state, totals):
    _, batch, width, kv_width = table.shape
    half = count // 2
    vmem = pl.BlockSpec(memory_space=pltpu.VMEM)
    dma = pltpu.SemaphoreType.DMA
    share = state.shape[1] // count
    low = functools.partial(jax.ShapeDtypeStruct, dtype=BF16)
    near = (half, batch, width, kv_width)
    wide = pltpu.VMEM((batch, KVHEADS * HDIM, QHEADS * width), BF16)
    tall = pltpu.VMEM((batch, QHEADS * width, KVHEADS * HDIM), BF16)
    return pl.pallas_call(
        functools.partial(mix_backward_kernel, count),
        in_specs=[vmem] * 8,
        out_specs=[vmem] * 3,
        out_shape=[low(queries_t.shape), low(near), low(state.shape)],
        scratch_shapes=[
            wide,
            wide,
            tall,
            tall,
            pltpu.VMEM((batch, QHEADS, width), F32),
            pltpu.VMEM((batch, QHEADS, HDIM, width), F32),
            pltpu.VMEM(near, BF16),
            pltpu.VMEM(near, BF16),
            pltpu.VMEM(near, BF16),
            pltpu.VMEM(state.shape, BF16),
            pltpu.VMEM((count, batch, share, STATE), BF16),
            pltpu.VMEM((count, batch, share, STATE), BF16),
            pltpu.VMEM(state.shape, BF16),
            dma((2, half)),
            dma((4, count)),
        ],
        compiler_params=pltpu.CompilerParams(
            collective_id=3, has_side_effects=True, vmem_limit_bytes=56 * MIB
        ),
        cost_estimate=pl.CostEstimate(
            flops=batch * count * width * width * 8 * 2000,
            bytes_accessed=8 * MIB,
            transcendentals=0,
        ),
        name="mix_backward",
    )(starts, queries_t, table, attended_t, grad_t, logs, state, totals)


def local(
    inputs,
    cotangent,
    lengths,
    norm1_gain,
    in_weight,
    dt_weight,
    conv_weight,
    conv_bias,
    dt_bias,
    decay_rate,
    skip_gain,
    mamba_gain,
    out_weight,
    q_weight,
    kv_weight,
    o_weight,
    norm2_gain,
    gu_weight,
    down_weight,
):
    count, _, rows, features = inputs.shape
    here = lax.axis_index("ctx")
    ctx_count = lax.axis_size("ctx")
    tokens = count * rows
    first_pos = here * rows
    own_pos = first_pos + jnp.arange(rows, dtype=jnp.int32)
    starts = jax.vmap(lambda row: seq_starts(row, own_pos))(lengths[:, 0])
    rel_start = (starts - first_pos).reshape(tokens, 1)
    taps = conv_weight.shape[0]
    channels = conv_weight.shape[1]
    kv_width = kv_weight.shape[1]
    x_low = inputs.reshape(tokens, features)
    grad_top = cotangent.reshape(tokens, features)

    kv_near = gathered_near(kv_weight)
    early_shard = jnp.concatenate(
        [
            in_weight[:, DSSM:],
            jnp.pad(dt_weight, ((0, 0), (0, EARLY_TILE - dt_weight.shape[1]))),
        ],
        axis=1,
    )
    edge_x = passed_along(inputs[:, 0, rows - EDGE :], "ctx", 1).reshape(count * EDGE, features)

    def normalized(low):
        wide = low.astype(F32)
        return (wide * inv_rms(wide) * norm1_gain).astype(BF16)

    normed = normalized(x_low)
    edge_normed = normalized(edge_x)
    kv_rows = project(normed, kv_near, kv_width, BF16)
    high_bits = bits_of("ctx")[1:]
    keys = Gathering(kv_rows.reshape(count, rows, -1), high_bits[::-1])
    early = gathered_near(early_shard, kv_near[1])
    late_shard = jnp.concatenate([in_weight[:, :DSSM], q_weight], axis=1)
    late = gathered_near(late_shard, early[1])
    conv_rows, edge_rows, act, dt_rows = project_early(
        count,
        after(normed, kv_rows),
        edge_normed,
        rel_start,
        conv_weight,
        conv_bias,
        early,
    )
    outs_shard = jnp.concatenate([out_weight, o_weight], axis=0)
    outs = gathered_near(outs_shard, (late[1], dt_rows))
    gu_full = gathered_near(gu_weight, (late[1], dt_rows))
    down_full = gathered_near(down_weight, (late[1], dt_rows))

    def head_row(values):
        return jnp.pad(values, (0, 128 - MHEADS))[None]

    bias_row, rate_row = head_row(dt_bias), head_row(decay_rate)
    steps, decay, decay_t, to_end, total, fresh = ssd_state(
        count, act, dt_rows, bias_row, rate_row, rel_start
    )
    late_rows = project(normed, late, 1024)
    gate_z = late_rows[:, :DSSM]
    queries_t = late_rows[:, DSSM:].astype(BF16).T
    starts_row = jnp.broadcast_to(starts[:, None, :], (count, 8, rows))
    attended_t, logs, key_table, state_in, totals = mix_forward(
        ctx_count, starts_row, queries_t, keys.finish(), fresh, total
    )

    skip_row = jnp.repeat(skip_gain, MDIM)[None]
    scanned = ssd_forward(count, act, steps, decay, decay_t, rel_start, state_in, skip_row)
    gate_sig = jax.nn.sigmoid(gate_z)
    gated = scanned * gate_z * gate_sig
    scale_m = inv_rms(gated)
    mixed = (gated * scale_m * mamba_gain).astype(BF16)
    middle, normed_two = out_project(x_low, mixed, attended_t, norm2_gain, outs)

    layer_out, grad_middle, branch, grad_norm2, hidden, grad_pair = mlp_both(
        lax.axis_index("wsh").astype(jnp.int32)[None],
        normed_two,
        grad_top,
        middle,
        norm2_gain,
        gu_full,
        down_full,
    )
    gu_send = block_grads(normed_two, grad_pair, NEAR[2:])[0]
    down_send = block_grads(hidden, grad_top[None], NEAR[2:])[0]
    gu_sent = swapped(gu_send, "wsh", 1)
    down_sent = swapped(down_send, "wsh", 1)
    branch = after(branch, (gu_send, down_send))
    grad_mixed, grad_attended_t = out_unproject(branch, outs, DSSM, QHEADS * HDIM)
    grad_gated, grad_mamba = rms_pull(gated, scale_m, mamba_gain, grad_mixed)
    grad_gate_z = grad_gated * scanned * gate_sig * (1.0 + gate_z * (1.0 - gate_sig))
    grad_scanned = grad_gated * gate_z * gate_sig
    grad_state = state_grad(count, grad_scanned, act, decay, rel_start)
    gu_left, down_left = after((normed_two, hidden), grad_state)
    gu_kept, gu_other = block_grads(gu_left, grad_pair, NEAR[:2], gu_sent)
    down_kept, down_other = block_grads(down_left, grad_top[None], NEAR[:2], down_sent)
    gu_crossed = swapped(gu_other, "wsh", 2)
    down_crossed = swapped(down_other, "wsh", 2)

    grad_attended_t = after(grad_attended_t, (gu_other, down_other))
    dq_t, dkv_near, later = mix_backward(
        ctx_count,
        starts_row,
        queries_t,
        key_table,
        attended_t,
        grad_attended_t,
        logs,
        grad_state,
        totals,
    )
    key_grads = Scattering(dkv_near, high_bits)
    grad_late = jnp.concatenate([grad_gate_z.astype(BF16), dq_t.T], axis=1)
    grad_normed = unproject(jnp.zeros((tokens, features), F32), grad_late, late, 1024)

    def total_of(kept, crossed):
        return (kept.astype(F32) + crossed.astype(F32)).astype(BF16)

    parts = total_of(gu_kept, gu_crossed), total_of(down_kept, down_crossed)
    later = after(later, (key_grads.advance(grad_normed), parts))
    dx, db, dc, dt_grad, small_ssd = ssd_backward(
        count,
        act,
        steps,
        decay,
        decay_t,
        rel_start,
        state_in,
        skip_row,
        scanned,
        grad_scanned,
        later,
        to_end,
        total,
        dt_rows,
        bias_row,
        rate_row,
    )
    edge_back = passed_along(
        edge_grads(count, dx, db, dc, conv_rows, edge_rows, rel_start, conv_weight, conv_bias),
        "ctx",
        -1,
    )
    grad_early, conv_grads, input_grad, grad_norm1 = early_back(
        count,
        grad_normed,
        key_grads.finish().reshape(tokens, -1),
        dx,
        db,
        dc,
        conv_rows,
        edge_rows,
        edge_back,
        dt_grad,
        rel_start,
        conv_weight,
        conv_bias,
        x_low,
        norm1_gain,
        grad_middle,
        early,
        kv_near,
    )
    small_ssd = jnp.sum(small_ssd, axis=0)
    grad_dt_w = mat_left_t(normed, dt_grad[:, :MHEADS])

    gu_sum, down_sum = lax.psum(parts, "ctx")
    pieces = (
        grad_norm1[0],
        conv_grads[:taps],
        conv_grads[taps],
        small_ssd[0, :MHEADS],
        small_ssd[1, :MHEADS],
        small_ssd[2, :MHEADS],
        grad_mamba,
        grad_norm2[0],
        grad_dt_w,
    )
    packed = jnp.concatenate(
        [
            jnp.pad(piece.reshape(-1), (0, -piece.size % 1024)).reshape(-1, 128)
            for piece in pieces
        ],
        axis=0,
    )
    early_sum, late_sum, mix_sum, packed = reduce_grads(
        ctx_count,
        kv_width + channels,
        normed,
        mixed,
        attended_t,
        grad_early,
        grad_late,
        branch,
        packed,
    )
    in_sum, q_sum, kv_sum, out_sum, o_sum = finish(
        early_sum,
        late_sum,
        mix_sum,
        [w.shape for w in (in_weight, q_weight, kv_weight, out_weight, o_weight)],
        channels,
    )
    totals_w = [in_sum, out_sum, q_sum, kv_sum, o_sum, gu_sum.astype(F32), down_sum.astype(F32)]
    small = []
    place = 0
    for piece in pieces:
        lines = -(-piece.size // 1024) * 8
        small.append(packed[place : place + lines].reshape(-1)[: piece.size].reshape(piece.shape))
        place += lines
    dt_size = dt_weight.shape[0]
    dt_sum = lax.dynamic_slice_in_dim(small[8], lax.axis_index("wsh") * dt_size, dt_size, 0)
    shape = (count, 1, rows, features)
    return (
        layer_out.reshape(shape),
        input_grad.reshape(shape),
        small[0],
        totals_w[0],
        dt_sum,
        small[1],
        small[2],
        small[3],
        small[4],
        small[5],
        small[6],
        totals_w[1],
        totals_w[2],
        totals_w[3],
        totals_w[4],
        small[7],
        totals_w[5],
        totals_w[6],
    )


def solution(mesh):
    stream = P(None, "wsh", "ctx", None)
    shard = P("wsh", None)
    in_specs = (
        stream,
        stream,
        P(None, "wsh", None),
        P(),
        shard,
        shard,
        P(),
        P(),
        P(),
        P(),
        P(),
        P(),
        shard,
        shard,
        shard,
        shard,
        P(),
        shard,
        shard,
    )
    out_specs = (
        stream,
        stream,
        P(),
        shard,
        shard,
        P(),
        P(),
        P(),
        P(),
        P(),
        P(),
        shard,
        shard,
        shard,
        shard,
        P(),
        shard,
        shard,
    )
    return jax.shard_map(local, mesh=mesh, in_specs=in_specs, out_specs=out_specs, check_vma=False)
```

```python
import functools

import jax
import jax.numpy as jnp
from jax import lax
from jax.experimental import pallas as pl
from jax.experimental.pallas import tpu as pltpu
from jax.sharding import PartitionSpec as P

FF = 2048
MHEADS = 24
MDIM = 64
STATE = 128
QHEADS = 8
KVHEADS = 2
HDIM = 64
DSSM = 1536
HGROUP = 8
NGROUP = MHEADS // HGROUP
GWIDTH = HGROUP * MDIM
PAIR = 2 * MDIM

NORM_EPS = 1e-05
PRECISE = lax.Precision.HIGHEST
MASKED_SCORE = -1e30
MIB = 2**20
KERNEL_VMEM = 60 * MIB
F32 = jnp.float32
BF16 = jnp.bfloat16


def dot_as(left, right, left_dim, right_dim):
    return lax.dot_general(
        left, right, (((left_dim,), (right_dim,)), ((), ())), preferred_element_type=F32
    )


def mat(left, right):
    return dot_as(left, right, 1, 0)


def mat_left_t(left, right):
    return dot_as(left, right, 0, 0)


def mat_right_t(left, right):
    return dot_as(left, right, 1, 1)


def inv_rms(rows):
    return lax.rsqrt(jnp.mean(rows * rows, axis=-1, keepdims=True) + NORM_EPS)


def rms_pull(rows, scale, gain, grad):
    scaled = rows * scale
    grad_gain = jnp.sum(grad * scaled, axis=0)
    through = grad * gain
    inner = jnp.mean(through * scaled, axis=-1, keepdims=True)
    return scale * (through - scaled * inner), grad_gain


def seq_starts(lengths_row, positions):
    begins = jnp.cumsum(lengths_row, dtype=jnp.int32) - lengths_row
    picked = jnp.where(begins[None, :] <= positions[:, None], begins[None, :], 0)
    return jnp.max(picked, axis=1)


def head_lanes(rows):
    return lax.broadcasted_iota(jnp.int32, (rows, PAIR), 1) < MDIM


def masked_products(b_low, c_low, rel_start):
    rows = b_low.shape[0]
    at_row = lax.broadcasted_iota(jnp.int32, (rows, rows), 0)
    at_col = lax.broadcasted_iota(jnp.int32, (rows, rows), 1)
    allowed = (at_col <= at_row) & (at_col >= rel_start)
    return allowed, jnp.where(allowed, mat_right_t(c_low, b_low), 0.0)


def pair_columns(first_half, columns, head):
    return jnp.where(first_half, columns[:, head : head + 1], columns[:, head + 1 : head + 2])


def exact(left, right, left_dim, right_dim):
    return lax.dot_general(
        left,
        right,
        (((left_dim,), (right_dim,)), ((), ())),
        precision=PRECISE,
        preferred_element_type=F32,
    )


def sums_by(values, picks):
    high = values.astype(BF16)
    low = (values - high.astype(F32)).astype(BF16)
    return mat(high, picks) + mat(low, picks)


def lower_ones(rows):
    at_row = lax.broadcasted_iota(jnp.int32, (rows, rows), 0)
    at_col = lax.broadcasted_iota(jnp.int32, (rows, rows), 1)
    return (at_row >= at_col).astype(F32)


def sigmoid(value):
    return 1.0 / (1.0 + jnp.exp(-value))


def softplus(value):
    return jnp.maximum(value, 0.0) + jnp.log1p(jnp.exp(-jnp.abs(value)))


def scaled_rows(target, source_ref, factors):
    first_half = head_lanes(source_ref.shape[0])
    for head in range(0, MHEADS, 2):
        lanes = slice(head * MDIM, head * MDIM + PAIR)
        target[:, lanes] = (
            source_ref[:, lanes] * pair_columns(first_half, factors, head)
        ).astype(BF16)


def ssd_state_kernel(
    act_ref,
    dt_ref,
    bias_ref,
    rate_ref,
    start_ref,
    step_ref,
    decay_ref,
    decay_t_ref,
    end_ref,
    total_ref,
    state_ref,
    scaled,
):
    rows = act_ref.shape[0]
    steps = softplus(dt_ref[:, :128] + bias_ref[...])
    decay = exact(lower_ones(rows), -steps * rate_ref[...], 1, 0)
    rel_start = start_ref[...]
    last_start = rel_start[rows - 1 : rows, :]
    kept = lax.broadcasted_iota(jnp.int32, (rows, 1), 0) >= last_start
    end = decay[rows - 1 : rows, :]
    to_end = jnp.where(kept, jnp.exp(end - decay), 0.0)
    step_ref[...] = steps
    decay_ref[...] = decay
    decay_t_ref[0] = decay.T
    end_ref[...] = to_end
    total_ref[0] = jnp.broadcast_to(jnp.where(last_start < 0, jnp.exp(end), 0.0), (8, 128))
    scaled_rows(scaled, act_ref, to_end * steps)
    state_ref[0] = mat_left_t(scaled[...], act_ref[:, DSSM : DSSM + STATE].astype(BF16))


def row_spec(rows, width, place=0):
    return pl.BlockSpec((rows, width), lambda b: (b, place))


def ssd_state(count, act, dt_rows, bias, rate, rel_start):
    rows = act.shape[0] // count
    lanes = pl.BlockSpec((1, 128), lambda b: (0, 0))
    heads = jax.ShapeDtypeStruct((count * rows, 128), F32)
    return pl.pallas_call(
        ssd_state_kernel,
        grid=(count,),
        in_specs=[
            row_spec(rows, act.shape[1]),
            row_spec(rows, dt_rows.shape[1]),
            lanes,
            lanes,
            row_spec(rows, 1),
        ],
        out_specs=[
            row_spec(rows, 128),
            row_spec(rows, 128),
            pl.BlockSpec((1, 128, rows), lambda b: (b, 0, 0)),
            row_spec(rows, 128),
            pl.BlockSpec((1, 8, 128), lambda b: (b, 0, 0)),
            pl.BlockSpec((1, DSSM, STATE), lambda b: (b, 0, 0)),
        ],
        out_shape=[
            heads,
            heads,
            jax.ShapeDtypeStruct((count, 128, rows), F32),
            heads,
            jax.ShapeDtypeStruct((count, 8, 128), F32),
            jax.ShapeDtypeStruct((count, DSSM, STATE), F32),
        ],
        scratch_shapes=[pltpu.VMEM((rows, DSSM), BF16)],
        compiler_params=pltpu.CompilerParams(vmem_limit_bytes=KERNEL_VMEM),
        cost_estimate=pl.CostEstimate(
            flops=1_000_000_000, bytes_accessed=8 * MIB, transcendentals=0
        ),
        name="ssd_state",
    )(act, dt_rows, bias, rate, rel_start)


def state_grad_kernel(dy_ref, c_ref, decay_ref, start_ref, out_ref, scaled):
    reach = jnp.where(start_ref[...] < 0, jnp.exp(decay_ref[...]), 0.0)
    scaled_rows(scaled, dy_ref, reach)
    out_ref[0] = mat_left_t(scaled[...], c_ref[...].astype(BF16))


def state_grad(count, dy, act, decay, rel_start):
    rows = act.shape[0] // count
    return pl.pallas_call(
        state_grad_kernel,
        grid=(count,),
        in_specs=[
            row_spec(rows, DSSM),
            row_spec(rows, STATE, DSSM // STATE + 1),
            row_spec(rows, 128),
            row_spec(rows, 1),
        ],
        out_specs=pl.BlockSpec((1, DSSM, STATE), lambda b: (b, 0, 0)),
        out_shape=jax.ShapeDtypeStruct((count, DSSM, STATE), F32),
        scratch_shapes=[pltpu.VMEM((rows, DSSM), BF16)],
        compiler_params=pltpu.CompilerParams(vmem_limit_bytes=KERNEL_VMEM),
        cost_estimate=pl.CostEstimate(
            flops=1_000_000_000, bytes_accessed=8 * MIB, transcendentals=0
        ),
        name="state_grad",
    )(dy, act, decay, rel_start)


def group_heads(ref):
    return pltpu.roll(ref[...], (128 - HGROUP * pl.program_id(1)) % 128, 1)


def group_rows(decay_t_ref):
    return decay_t_ref[0, pl.ds(pl.multiple_of(HGROUP * pl.program_id(1), HGROUP), HGROUP), :]


def ssd_forward_kernel(
    x_ref, b_ref, c_ref, step_ref, decay_ref, decay_t_ref, start_ref, state_ref, skip_ref, y_ref
):
    rows = x_ref.shape[0]
    b_low = b_ref[...].astype(BF16)
    c_low = c_ref[...].astype(BF16)
    rel_start = start_ref[...]
    _, products = masked_products(b_low, c_low, rel_start)
    incoming = mat_right_t(c_low, state_ref[0].astype(BF16))
    first_half = head_lanes(rows)
    steps = group_heads(step_ref)
    decay = group_heads(decay_ref)
    decay_t = group_rows(decay_t_ref)
    reach = jnp.where(rel_start < 0, jnp.exp(decay), 0.0)
    for head in range(0, HGROUP, 2):
        lanes = slice(head * MDIM, head * MDIM + PAIR)
        x_pair = x_ref[:, lanes]
        scaled = (x_pair * pair_columns(first_half, steps, head)).astype(BF16)
        parts = []
        for one in (head, head + 1):
            gaps = decay[:, one : one + 1] - decay_t[one : one + 1, :]
            weights = (jnp.exp(jnp.minimum(gaps, 0.0)) * products).astype(BF16)
            parts.append(mat(weights, scaled))
        y_ref[:, lanes] = (
            jnp.where(first_half, parts[0], parts[1])
            + pair_columns(first_half, reach, head) * incoming[:, lanes]
            + skip_ref[:, lanes] * x_pair
        )


def ssd_backward_kernel(
    x_ref,
    b_ref,
    c_ref,
    step_ref,
    decay_ref,
    decay_t_ref,
    start_ref,
    state_ref,
    skip_ref,
    y_ref,
    dy_ref,
    later_ref,
    end_ref,
    total_ref,
    dt_ref,
    bias_ref,
    rate_ref,
    dx_ref,
    db_ref,
    dc_ref,
    dt_grad_ref,
    small_ref,
    one_sum,
    two_sum,
    three_sum,
    mixed_y,
    mixed_x,
    head_sums,
    row_sums,
):
    rows = x_ref.shape[0]
    b_low = b_ref[...].astype(BF16)
    c_low = c_ref[...].astype(BF16)
    rel_start = start_ref[...]
    allowed, products = masked_products(b_low, c_low, rel_start)
    state_low = state_ref[0].astype(BF16)
    later_low = later_ref[0].astype(BF16)
    spread = mat_right_t(b_low, later_low)
    first_half = head_lanes(rows)
    steps = group_heads(step_ref)
    decay = group_heads(decay_ref)
    decay_t = group_rows(decay_t_ref)
    reach = jnp.where(rel_start < 0, jnp.exp(decay), 0.0)
    to_end = group_heads(end_ref) * steps
    product_grad = jnp.zeros((rows, rows), F32)
    skip_parts = []
    for head in range(0, HGROUP, 2):
        lanes = slice(head * MDIM, head * MDIM + PAIR)
        x_pair = x_ref[:, lanes]
        dy_pair = dy_ref[:, lanes]
        step_pair = pair_columns(first_half, steps, head)
        scaled = (x_pair * step_pair).astype(BF16)
        dy_low = dy_pair.astype(BF16)
        parts = []
        for one in (head, head + 1):
            gaps = decay[:, one : one + 1] - decay_t[one : one + 1, :]
            decays = jnp.exp(jnp.minimum(gaps, 0.0))
            mine = first_half if one == head else ~first_half
            dy_mine = jnp.where(mine, dy_pair, 0.0).astype(BF16)
            weight_grad = mat_right_t(dy_mine, scaled)
            product_grad = product_grad + weight_grad * decays
            parts.append(mat_left_t((decays * products).astype(BF16), dy_low))
        dz_pair = jnp.where(first_half, parts[0], parts[1])
        skip_pair = skip_ref[:, lanes]
        end_pair = pair_columns(first_half, to_end, head)
        spread_pair = spread[:, lanes]
        dx_ref[:, lanes] = skip_pair * dy_pair + step_pair * dz_pair + end_pair * spread_pair
        one_sum[:, lanes] = dy_pair * (y_ref[:, lanes] - skip_pair * x_pair)
        two_sum[:, lanes] = x_pair * dz_pair
        three_sum[:, lanes] = x_pair * spread_pair
        mixed_y[:, lanes] = (dy_pair * pair_columns(first_half, reach, head)).astype(BF16)
        mixed_x[:, lanes] = (x_pair * end_pair).astype(BF16)
        skip_parts.append(jnp.sum(dy_pair * x_pair, axis=0, keepdims=True))
    grad_low = jnp.where(allowed, product_grad, 0.0).astype(BF16)
    dc = mat(grad_low, b_low) + mat(mixed_y[...], state_low)
    db = mat_left_t(grad_low, c_low) + mat(mixed_x[...], later_low)
    group = pl.program_id(1)

    @pl.when(group == 0)
    def _():
        dc_ref[...] = jnp.zeros(dc_ref.shape, F32)
        db_ref[...] = jnp.zeros(db_ref.shape, F32)
        head_sums[...] = jnp.zeros(head_sums.shape, F32)
        row_sums[...] = jnp.zeros(row_sums.shape, F32)

    dc_ref[...] += dc
    db_ref[...] += db
    owner = lax.broadcasted_iota(jnp.int32, (GWIDTH, 128), 0) // MDIM + group * HGROUP
    picks = (owner == lax.broadcasted_iota(jnp.int32, (GWIDTH, 128), 1)).astype(BF16)
    for place, source in enumerate((one_sum, two_sum, three_sum)):
        head_sums[place] += sums_by(source[...], picks)
    skips = jnp.broadcast_to(jnp.concatenate(skip_parts, axis=1), (8, GWIDTH))
    row_sums[0] += sums_by(skips, picks)
    meets = exact(
        jnp.ones((8, STATE), F32), later_ref[0].astype(F32) * state_ref[0].astype(F32), 1, 1
    )
    row_sums[1] += sums_by(meets, picks)

    @pl.when(group == pl.num_programs(1) - 1)
    def _():
        all_steps = step_ref[...]
        all_end = end_ref[...]
        rate = rate_ref[...]
        row_dot, u_dot, v_dot = head_sums[0], head_sums[1], head_sums[2]
        to_last = v_dot * all_end * all_steps
        grad_decay = row_dot - u_dot * all_steps - to_last
        at_end = jnp.sum(to_last, axis=0, keepdims=True) + row_sums[1, :1] * total_ref[0, :1]
        grad_drop = exact(lower_ones(rows), grad_decay, 0, 0) + at_end
        grad_steps = u_dot + v_dot * all_end - rate * grad_drop
        grad_dt = grad_steps * sigmoid(dt_ref[:, :128] + bias_ref[...])
        dt_grad_ref[:, :128] = grad_dt.astype(BF16)
        dt_grad_ref[:, 128:] = jnp.zeros((rows, dt_grad_ref.shape[1] - 128), BF16)
        small_ref[0, 0:1] = jnp.sum(grad_dt, axis=0, keepdims=True)
        small_ref[0, 1:2] = jnp.sum(-all_steps * grad_drop, axis=0, keepdims=True)
        small_ref[0, 2:8] = row_sums[0, :6]


def ssd_specs(rows):
    wide = pl.BlockSpec((rows, GWIDTH), lambda b, g: (b, g))
    b_spec = pl.BlockSpec((rows, STATE), lambda b, g: (b, DSSM // STATE))
    c_spec = pl.BlockSpec((rows, STATE), lambda b, g: (b, DSSM // STATE + 1))
    heads = pl.BlockSpec((rows, 128), lambda b, g: (b, 0))
    heads_t = pl.BlockSpec((1, 128, rows), lambda b, g: (b, 0, 0))
    column = pl.BlockSpec((rows, 1), lambda b, g: (b, 0))
    state = pl.BlockSpec((1, GWIDTH, STATE), lambda b, g: (b, g, 0))
    skip = pl.BlockSpec((1, GWIDTH), lambda b, g: (0, g))
    return [wide, b_spec, c_spec, heads, heads, heads_t, column, state, skip]


def ssd_forward(count, act, steps, decay, decay_t, rel_start, state_in, skip_row):
    rows = act.shape[0] // count
    specs = ssd_specs(rows)
    return pl.pallas_call(
        ssd_forward_kernel,
        grid=(count, NGROUP),
        in_specs=specs,
        out_specs=specs[0],
        out_shape=jax.ShapeDtypeStruct((count * rows, DSSM), F32),
        compiler_params=pltpu.CompilerParams(vmem_limit_bytes=KERNEL_VMEM),
        cost_estimate=pl.CostEstimate(
            flops=count * MHEADS * rows * rows * 400, bytes_accessed=8 * MIB, transcendentals=0
        ),
        name="ssd_forward",
    )(act, act, act, steps, decay, decay_t, rel_start, state_in, skip_row)


def ssd_backward(
    count,
    act,
    steps,
    decay,
    decay_t,
    rel_start,
    state_in,
    skip_row,
    scanned,
    grad_scanned,
    later,
    to_end,
    total,
    dt_rows,
    bias,
    rate,
):
    rows = act.shape[0] // count
    specs = ssd_specs(rows)
    wide, heads, state = specs[0], specs[3], specs[7]
    row = pl.BlockSpec((1, 128), lambda b, g: (0, 0))
    packed = pl.BlockSpec((1, 8, 128), lambda b, g: (b, 0, 0))
    narrow = pl.BlockSpec((rows, STATE), lambda b, g: (b, 0))
    dt_spec = pl.BlockSpec((rows, dt_rows.shape[1]), lambda b, g: (b, 0))
    tokens = count * rows
    return pl.pallas_call(
        ssd_backward_kernel,
        grid=(count, NGROUP),
        in_specs=specs + [wide, wide, state, heads, packed, dt_spec, row, row],
        out_specs=[wide, narrow, narrow, dt_spec, packed],
        out_shape=[
            jax.ShapeDtypeStruct((tokens, DSSM), F32),
            jax.ShapeDtypeStruct((tokens, STATE), F32),
            jax.ShapeDtypeStruct((tokens, STATE), F32),
            jax.ShapeDtypeStruct(dt_rows.shape, BF16),
            jax.ShapeDtypeStruct((count, 8, 128), F32),
        ],
        scratch_shapes=[pltpu.VMEM((rows, GWIDTH), F32)] * 3
        + [pltpu.VMEM((rows, GWIDTH), BF16)] * 2
        + [pltpu.VMEM((3, rows, 128), F32), pltpu.VMEM((2, 8, 128), F32)],
        compiler_params=pltpu.CompilerParams(vmem_limit_bytes=KERNEL_VMEM),
        cost_estimate=pl.CostEstimate(
            flops=count * MHEADS * rows * rows * 1000, bytes_accessed=16 * MIB, transcendentals=0
        ),
        name="ssd_backward",
    )(
        act,
        act,
        act,
        steps,
        decay,
        decay_t,
        rel_start,
        state_in,
        skip_row,
        scanned,
        grad_scanned,
        later,
        to_end,
        total,
        dt_rows,
        bias,
        rate,
    )


def spread_heads(source_ref, target, factor):
    width = source_ref.shape[1]
    target[...] = jnp.zeros(target.shape, target.dtype)
    for head in range(QHEADS):
        group = head // (QHEADS // KVHEADS)
        value = source_ref[head * HDIM : (head + 1) * HDIM, :]
        target[group * HDIM : (group + 1) * HDIM, head * width : (head + 1) * width] = (
            value * factor if factor != 1.0 else value
        )


def attend_allowed(block, first_pos, starts, width):
    key_pos = block * width + lax.broadcasted_iota(jnp.int32, (width, width), 0)
    query_pos = first_pos + lax.broadcasted_iota(jnp.int32, (width, width), 1)
    return (key_pos <= query_pos) & (key_pos >= starts)


NEAR = (0, 2, 1, 3)
TILE_ROWS = 256
TILE_COLS = 512


def near_at(step, size):
    return pl.ds(pl.multiple_of((lax.axis_index("wsh") ^ step) * size, 128), size)


def project_kernel(x_ref, *refs):
    *weights, out_ref = refs
    size = weights[0].shape[0]
    total = None
    for step, weight in zip(NEAR, weights):
        part = mat(x_ref[:, near_at(step, size)], weight[...])
        total = part if total is None else total + part
    out_ref[...] = total.astype(out_ref.dtype)


def project(x, weights, tile, kind=F32):
    tokens, depth = x.shape
    size, columns = weights[0].shape
    return pl.pallas_call(
        project_kernel,
        grid=(columns // tile,),
        in_specs=[pl.BlockSpec((tokens, depth), lambda i: (0, 0))]
        + [pl.BlockSpec((size, tile), lambda i: (0, i))] * 4,
        out_specs=pl.BlockSpec((tokens, tile), lambda i: (0, i)),
        out_shape=jax.ShapeDtypeStruct((tokens, columns), kind),
        compiler_params=pltpu.CompilerParams(vmem_limit_bytes=KERNEL_VMEM),
        cost_estimate=pl.CostEstimate(
            flops=2 * tokens * depth * columns,
            bytes_accessed=2 * depth * columns + 4 * tokens * columns,
            transcendentals=0,
        ),
        name="project",
    )(x, *weights)


def near_specs(own, tile, offset):
    size = own.shape[0]
    return [pl.BlockSpec((size, tile), lambda i: (0, i + offset))] + [
        pl.BlockSpec((None, size, tile), lambda i, place=place: (place, 0, i + offset))
        for place in range(3)
    ]


def unproject_kernel(base_ref, grad_ref, *refs):
    *weights, out_ref = refs
    size = weights[0].shape[0]

    @pl.when(pl.program_id(0) == 0)
    def _():
        out_ref[...] = base_ref[...]

    for step, weight in zip(NEAR, weights):
        out_ref[:, near_at(step, size)] += mat_right_t(grad_ref[...], weight[...])


def unproject(base, grad, weights, tile, specs=None):
    tokens, columns = grad.shape
    size = weights[0].shape[0]
    whole = pl.BlockSpec((tokens, 4 * size), lambda i: (0, 0))
    return pl.pallas_call(
        unproject_kernel,
        grid=(columns // tile,),
        in_specs=[whole, pl.BlockSpec((tokens, tile), lambda i: (0, i))]
        + (specs or [pl.BlockSpec((size, tile), lambda i: (0, i))] * 4),
        out_specs=whole,
        out_shape=jax.ShapeDtypeStruct((tokens, 4 * size), F32),
        compiler_params=pltpu.CompilerParams(vmem_limit_bytes=KERNEL_VMEM),
        cost_estimate=pl.CostEstimate(
            flops=8 * tokens * size * columns,
            bytes_accessed=8 * size * columns + 2 * tokens * columns,
            transcendentals=0,
        ),
        name="unproject",
    )(base, grad, *weights)


def out_proj_kernel(x_ref, mixed_ref, heads_ref, gain_ref, *refs):
    *weights, middle_ref, normed_ref = refs
    wide = mixed_ref.shape[1] // 4
    narrow = heads_ref.shape[0] // 4
    middle_ref[...] = x_ref[...].astype(F32)
    for step, weight in zip(NEAR, weights):
        middle_ref[...] += mat(mixed_ref[:, near_at(step, wide)], weight[:wide]) + mat_left_t(
            heads_ref[near_at(step, narrow), :], weight[wide:]
        )
    middle = middle_ref[...]
    normed_ref[...] = (middle * inv_rms(middle) * gain_ref[...]).astype(BF16)


def out_project(x, mixed, heads_t, gain, weights):
    vmem = pl.BlockSpec(memory_space=pltpu.VMEM)
    return pl.pallas_call(
        out_proj_kernel,
        in_specs=[vmem] * 8,
        out_specs=[vmem, vmem],
        out_shape=[jax.ShapeDtypeStruct(x.shape, F32), jax.ShapeDtypeStruct(x.shape, BF16)],
        compiler_params=pltpu.CompilerParams(vmem_limit_bytes=KERNEL_VMEM),
        cost_estimate=pl.CostEstimate(
            flops=2 * x.size * 2048, bytes_accessed=12 * MIB, transcendentals=0
        ),
        name="out_project",
    )(x, mixed, heads_t, gain[None], *weights)


def out_back_kernel(branch_ref, *refs):
    *weights, mixed_ref, heads_ref = refs
    wide = mixed_ref.shape[1] // 4
    narrow = heads_ref.shape[0] // 4
    for step, weight in zip(NEAR, weights):
        mixed_ref[:, near_at(step, wide)] = mat_right_t(branch_ref[...], weight[:wide])
        heads_ref[near_at(step, narrow), :] = mat_right_t(weight[wide:], branch_ref[...]).astype(
            BF16
        )


def out_unproject(branch, weights, mixed_width, heads_width):
    vmem = pl.BlockSpec(memory_space=pltpu.VMEM)
    tokens = branch.shape[0]
    return pl.pallas_call(
        out_back_kernel,
        in_specs=[vmem] * 5,
        out_specs=[vmem, vmem],
        out_shape=[
            jax.ShapeDtypeStruct((tokens, mixed_width), F32),
            jax.ShapeDtypeStruct((heads_width, tokens), BF16),
        ],
        compiler_params=pltpu.CompilerParams(vmem_limit_bytes=KERNEL_VMEM),
        cost_estimate=pl.CostEstimate(
            flops=2 * branch.size * 2048, bytes_accessed=12 * MIB, transcendentals=0
        ),
        name="out_unproject",
    )(branch, *weights)


FF_TILE = 512


def mlp_kernel(
    place_ref, normed_ref, top_ref, middle_ref, gain_ref, *refs
):
    gates, ups, downs = refs[0:4], refs[4:8], refs[8:12]
    layer_ref, grad_ref, branch_ref, gain_grad_ref, hidden_ref, pair_ref = refs[12:18]
    down_tile, out_sum, back_sum = refs[18:]
    step_at = pl.program_id(0)
    per_piece = pl.num_programs(0) // 4
    size = gates[0].shape[0]
    for piece in range(4):

        @pl.when(step_at // per_piece == piece)
        def _():
            down_tile[...] = downs[piece][...]

    gate = up = None
    for step, gate_ref, up_ref in zip(NEAR, gates, ups):
        rows = normed_ref[:, near_at(step, size)]
        gate_part, up_part = mat(rows, gate_ref[...]), mat(rows, up_ref[...])
        gate = gate_part if gate is None else gate + gate_part
        up = up_part if up is None else up + up_part
    sig = 1.0 / (1.0 + jnp.exp(-gate))
    silu = gate * sig
    hidden = (silu * up).astype(BF16)
    hidden_ref[...] = hidden
    grad_hidden = mat_right_t(top_ref[...], down_tile[...])
    grad_gate = (grad_hidden * up * (sig + silu * (1.0 - sig))).astype(BF16)
    grad_up = (grad_hidden * silu).astype(BF16)
    pair_ref[0] = grad_gate
    pair_ref[1] = grad_up

    @pl.when(step_at == 0)
    def _():
        out_sum[...] = jnp.zeros(out_sum.shape, F32)
        back_sum[...] = jnp.zeros(back_sum.shape, F32)

    out_sum[...] += mat(hidden, down_tile[...])
    for step, gate_ref, up_ref in zip(NEAR, gates, ups):
        back_sum[:, near_at(step, size)] += mat_right_t(grad_gate, gate_ref[...]) + mat_right_t(
            grad_up, up_ref[...]
        )

    @pl.when(step_at == pl.num_programs(0) - 1)
    def _():
        middle = middle_ref[...]
        layer_ref[...] = (middle + out_sum[...]).astype(BF16)
        grad_rows, grad_gain = rms_pull(middle, inv_rms(middle), gain_ref[...], back_sum[...])
        grad = top_ref[...].astype(F32) + grad_rows
        grad_ref[...] = grad
        branch_ref[...] = grad.astype(BF16)
        gain_grad_ref[...] = grad_gain[None]


def mlp_both(place, normed, top, middle, gain, gu_weights, down_weights):
    tokens, features = middle.shape
    size, columns = gu_weights[0].shape
    width = columns // 2
    steps = width // FF_TILE
    per_piece = steps // 4

    def natural(i, p):
        piece = i // per_piece
        near = (piece % 2) * 2 + piece // 2
        return (near ^ p[0]) * per_piece + i % per_piece

    whole = pl.BlockSpec((tokens, features), lambda i, p: (0, 0))
    gain_spec = pl.BlockSpec((1, features), lambda i, p: (0, 0))

    def down_spec(piece):
        return pl.BlockSpec(
            (FF_TILE, features),
            lambda i, p: (jnp.clip(i - piece * per_piece, 0, per_piece - 1), 0),
        )

    return pl.pallas_call(
        mlp_kernel,
        grid_spec=pltpu.PrefetchScalarGridSpec(
            num_scalar_prefetch=1,
            grid=(steps,),
            in_specs=[whole, whole, whole, gain_spec]
            + [pl.BlockSpec((size, FF_TILE), lambda i, p: (0, natural(i, p)))] * 4
            + [pl.BlockSpec((size, FF_TILE), lambda i, p: (0, natural(i, p) + steps))] * 4
            + [down_spec(piece) for piece in range(4)],
            out_specs=[
                whole,
                whole,
                whole,
                gain_spec,
                pl.BlockSpec((tokens, FF_TILE), lambda i, p: (0, natural(i, p))),
                pl.BlockSpec((2, tokens, FF_TILE), lambda i, p: (0, 0, natural(i, p))),
            ],
            scratch_shapes=[
                pltpu.VMEM((FF_TILE, features), BF16),
                pltpu.VMEM((tokens, features), F32),
                pltpu.VMEM((tokens, features), F32),
            ],
        ),
        out_shape=[
            jax.ShapeDtypeStruct((tokens, features), BF16),
            jax.ShapeDtypeStruct((tokens, features), F32),
            jax.ShapeDtypeStruct((tokens, features), BF16),
            jax.ShapeDtypeStruct((1, features), F32),
            jax.ShapeDtypeStruct((tokens, width), BF16),
            jax.ShapeDtypeStruct((2, tokens, width), BF16),
        ],
        compiler_params=pltpu.CompilerParams(vmem_limit_bytes=KERNEL_VMEM),
        cost_estimate=pl.CostEstimate(
            flops=12 * tokens * features * width, bytes_accessed=30 * MIB, transcendentals=0
        ),
        name="mlp_both",
    )(
        place,
        normed,
        top,
        middle,
        gain[None],
        *gu_weights,
        *gu_weights,
        *down_weights,
    )


EDGE = 8
EARLY_TILE = 256


def conv_inputs(edge_rows, own_rows):
    return jnp.concatenate([edge_rows, own_rows], axis=0)


def conv_valid(rel_start, tap, taps):
    rows = rel_start.shape[0]
    place = lax.broadcasted_iota(jnp.int32, (rows, 1), 0)
    return place - (taps - 1) + tap >= rel_start


def conv_sums(extended, weights, bias, rel_start):
    taps = weights.shape[0]
    rows = rel_start.shape[0]
    shifted = []
    total = None
    for tap in range(taps):
        begin = EDGE - (taps - 1) + tap
        part = jnp.where(
            conv_valid(rel_start, tap, taps), extended[begin : begin + rows], 0.0
        )
        shifted.append(part)
        term = weights[tap : tap + 1] * part
        total = bias + term if total is None else total + term
    return total, shifted


def conv_tile_spec(rows, first, last, begin=0):
    return pl.BlockSpec(
        (rows, EARLY_TILE), lambda i: (0, jnp.clip(i - begin + first, first, last))
    )


def conv_back(extended, weights, bias, rel_start, grad_act):
    total, shifted = conv_sums(extended, weights, bias, rel_start)
    gate = sigmoid(total)
    return grad_act * gate * (1.0 + total * (1.0 - gate)), shifted


def edge_grad_kernel(
    dx_ref, db_ref, dc_ref, conv_ref, edge_ref, start_ref, weight_ref, bias_ref, out_ref
):
    taps = weight_ref.shape[0]
    grad_act = jnp.concatenate([dx_ref[...], db_ref[...], dc_ref[...]], axis=1)
    extended = conv_inputs(edge_ref[...], conv_ref[...])
    grad, _ = conv_back(extended, weight_ref[...], bias_ref[...], start_ref[...], grad_act)
    total = jnp.zeros(grad.shape, F32)
    for tap in range(taps):
        part = jnp.where(
            conv_valid(start_ref[...], tap, taps), grad * weight_ref[tap : tap + 1], 0.0
        )
        padded = jnp.concatenate([jnp.zeros(part.shape, F32), part], axis=0)
        total = total + padded[taps - 1 - tap : taps - 1 - tap + EDGE]
    out_ref[...] = total


def edge_grads(count, dx, db, dc, conv_rows, edge_rows, rel_start, conv_weight, conv_bias):
    rows = dx.shape[0] // count
    steps = rows // EDGE

    def first(array):
        return pl.BlockSpec((EDGE, array.shape[1]), lambda b: (b * steps, 0))

    channels = conv_weight.shape[1]
    return pl.pallas_call(
        edge_grad_kernel,
        grid=(count,),
        in_specs=[
            first(dx),
            first(db),
            first(dc),
            first(conv_rows),
            pl.BlockSpec((EDGE, channels), lambda b: (b, 0)),
            first(rel_start),
            pl.BlockSpec(conv_weight.shape, lambda b: (0, 0)),
            pl.BlockSpec((1, channels), lambda b: (0, 0)),
        ],
        out_specs=pl.BlockSpec((EDGE, channels), lambda b: (b, 0)),
        out_shape=jax.ShapeDtypeStruct((count * EDGE, channels), F32),
        compiler_params=pltpu.CompilerParams(vmem_limit_bytes=KERNEL_VMEM),
        cost_estimate=pl.CostEstimate(flops=MIB, bytes_accessed=MIB, transcendentals=0),
        name="edge_grads",
    )(dx, db, dc, conv_rows, edge_rows, rel_start, conv_weight, conv_bias[None])


def early_back_kernel(
    count,
    base_ref,
    kv_ref,
    dx_ref,
    db_ref,
    dc_ref,
    conv_ref,
    edge_ref,
    came_ref,
    dt_ref,
    start_ref,
    weight_ref,
    bias_ref,
    x_ref,
    gain_ref,
    middle_ref,
    *refs,
):
    *blocks, grad_ref, conv_grad_ref, input_ref, gain_grad_ref, total = refs
    size = blocks[0].shape[0]
    tile = pl.program_id(0)
    last = pl.num_programs(0) - 1
    taps = weight_ref.shape[0]

    @pl.when(tile == 0)
    def _():
        total[...] = base_ref[...]
        grad_ref[...] = kv_ref[...]

    @pl.when(tile == last)
    def _():
        grad_ref[...] = dt_ref[...]

    @pl.when((tile > 0) & (tile < last))
    def _():
        rows = dx_ref.shape[0] // count
        tail = jnp.concatenate([db_ref[...], dc_ref[...]], axis=1)
        grad_act = jnp.where(tile == last - 1, tail, dx_ref[...])
        sums = [None] * (taps + 1)
        for b in range(count):
            span = slice(b * rows, (b + 1) * rows)
            ends = slice(b * EDGE, (b + 1) * EDGE)
            extended = conv_inputs(edge_ref[ends], conv_ref[span])
            rel_start = start_ref[span]
            grad, shifted = conv_back(
                extended, weight_ref[...], bias_ref[...], rel_start, grad_act[span]
            )
            back = jnp.concatenate(
                [jnp.zeros((rows - EDGE, grad.shape[1]), F32), came_ref[ends]], axis=0
            )
            for tap in range(taps):
                part = jnp.where(
                    conv_valid(rel_start, tap, taps), grad * weight_ref[tap : tap + 1], 0.0
                )
                padded = jnp.concatenate([part, jnp.zeros((EDGE, part.shape[1]), F32)], axis=0)
                back = back + padded[taps - 1 - tap : taps - 1 - tap + rows]
                term = jnp.sum(grad * shifted[tap], axis=0, keepdims=True)
                sums[tap] = term if sums[tap] is None else sums[tap] + term
            term = jnp.sum(grad, axis=0, keepdims=True)
            sums[taps] = term if sums[taps] is None else sums[taps] + term
            grad_ref[span] = back.astype(BF16)
        conv_grad_ref[0 : taps + 1] = jnp.concatenate(sums, axis=0)
        conv_grad_ref[taps + 1 :] = jnp.zeros(
            (conv_grad_ref.shape[0] - taps - 1, grad_act.shape[1]), F32
        )

    for step, block in zip(NEAR, blocks):
        total[:, near_at(step, size)] += mat_right_t(grad_ref[...], block[...])

    @pl.when(tile == last)
    def _():
        x = x_ref[...].astype(F32)
        grad_rows, grad_gain = rms_pull(x, inv_rms(x), gain_ref[...], total[...])
        input_ref[...] = (middle_ref[...] + grad_rows).astype(BF16)
        gain_grad_ref[...] = grad_gain[None]


def early_back(
    count,
    base,
    grad_kv,
    dx,
    db,
    dc,
    conv_rows,
    edge_rows,
    came,
    dt_grad,
    rel_start,
    conv_weight,
    conv_bias,
    x,
    gain,
    grad_middle,
    own,
    others,
):
    tokens, depth = base.shape
    channels = conv_weight.shape[1]
    tiles = conv_weight.shape[1] // EARLY_TILE + 2
    conv_tiles = channels // EARLY_TILE

    def whole(array):
        return pl.BlockSpec(array.shape, lambda i: (0, 0))

    return pl.pallas_call(
        functools.partial(early_back_kernel, count),
        grid=(tiles,),
        in_specs=[
            whole(base),
            whole(grad_kv),
            conv_tile_spec(tokens, 0, conv_tiles - 2, 1),
            whole(db),
            whole(dc),
            conv_tile_spec(tokens, 0, conv_tiles - 1, 1),
            conv_tile_spec(edge_rows.shape[0], 0, conv_tiles - 1, 1),
            conv_tile_spec(edge_rows.shape[0], 0, conv_tiles - 1, 1),
            whole(dt_grad),
            whole(rel_start),
            conv_tile_spec(conv_weight.shape[0], 0, conv_tiles - 1, 1),
            conv_tile_spec(1, 0, conv_tiles - 1, 1),
            whole(x),
            pl.BlockSpec((1, depth), lambda i: (0, 0)),
            whole(grad_middle),
        ]
        + near_specs(own, EARLY_TILE, DSSM // EARLY_TILE),
        out_specs=[
            pl.BlockSpec((tokens, EARLY_TILE), lambda i: (0, i)),
            conv_tile_spec(8, 0, conv_tiles - 1, 1),
            whole(x),
            pl.BlockSpec((1, depth), lambda i: (0, 0)),
        ],
        out_shape=[
            jax.ShapeDtypeStruct((tokens, tiles * EARLY_TILE), BF16),
            jax.ShapeDtypeStruct((8, channels), F32),
            jax.ShapeDtypeStruct(x.shape, BF16),
            jax.ShapeDtypeStruct((1, depth), F32),
        ],
        scratch_shapes=[pltpu.VMEM((tokens, depth), F32)],
        compiler_params=pltpu.CompilerParams(vmem_limit_bytes=KERNEL_VMEM),
        cost_estimate=pl.CostEstimate(
            flops=2 * tokens * depth * tiles * EARLY_TILE, bytes_accessed=20 * MIB, transcendentals=0
        ),
        name="early_back",
    )(
        base,
        grad_kv,
        dx,
        db,
        dc,
        conv_rows,
        edge_rows,
        came,
        dt_grad,
        rel_start,
        conv_weight,
        conv_bias[None],
        x,
        gain[None],
        grad_middle,
        own,
        others,
        others,
        others,
    )


def block_grads_kernel(steps, left_ref, right_ref, *refs):
    came = refs[0] if len(refs) == 3 else None
    outs = refs[-2:] if came is not None else refs
    size = left_ref.shape[1] // 4
    for place, step in enumerate(steps):
        value = mat_left_t(left_ref[:, near_at(step, size)], right_ref[0])
        if came is None:
            outs[0][place * size : (place + 1) * size] = value.astype(BF16)
        else:
            value = value + came[place * size : (place + 1) * size].astype(F32)
            outs[place][...] = value.astype(BF16)


def block_grads(left, right, steps, came=None):
    tokens, depth = left.shape
    size = depth // 4
    parts, _, width = right.shape
    per_part = width // TILE_COLS
    columns = parts * width
    tall = pl.BlockSpec((2 * size, TILE_COLS), lambda i: (0, i))
    flat = pl.BlockSpec((size, TILE_COLS), lambda i: (0, i))
    operands = [left, right] + ([] if came is None else [came])
    return pl.pallas_call(
        functools.partial(block_grads_kernel, steps),
        grid=(columns // TILE_COLS,),
        in_specs=[
            pl.BlockSpec((tokens, depth), lambda i: (0, 0)),
            pl.BlockSpec((1, tokens, TILE_COLS), lambda i: (i // per_part, 0, i % per_part)),
        ]
        + ([] if came is None else [tall]),
        out_specs=[tall] if came is None else [flat, flat],
        out_shape=[jax.ShapeDtypeStruct((2 * size, columns), BF16)]
        if came is None
        else [jax.ShapeDtypeStruct((size, columns), BF16)] * 2,
        compiler_params=pltpu.CompilerParams(vmem_limit_bytes=KERNEL_VMEM),
        cost_estimate=pl.CostEstimate(
            flops=4 * tokens * size * columns, bytes_accessed=6 * MIB, transcendentals=0
        ),
        name="block_grads",
    )(*operands)


def finish_kernel(
    early_ref, gate_ref, mix_ref, q_low_ref, in_ref, q_ref, kv_ref, out_ref, o_ref
):
    kv_width = kv_ref.shape[1]
    gate = gate_ref.shape[1]
    in_ref[:, :gate] = gate_ref[...].astype(F32)
    in_ref[:, gate:] = early_ref[:, kv_width:].astype(F32)
    q_ref[...] = q_low_ref[...].astype(F32)
    kv_ref[...] = early_ref[:, :kv_width].astype(F32)
    split = out_ref.shape[0]
    out_ref[...] = mix_ref[:split].astype(F32)
    o_ref[...] = mix_ref[split:].astype(F32)


def finish(early, gate, mix, q, shapes):
    vmem = pl.BlockSpec(memory_space=pltpu.VMEM)
    return pl.pallas_call(
        finish_kernel,
        in_specs=[vmem] * 4,
        out_specs=[vmem] * 5,
        out_shape=[jax.ShapeDtypeStruct(shape, F32) for shape in shapes],
        compiler_params=pltpu.CompilerParams(vmem_limit_bytes=KERNEL_VMEM),
        cost_estimate=pl.CostEstimate(flops=MIB, bytes_accessed=10 * MIB, transcendentals=0),
        name="finish",
    )(early, gate, mix, q)


def passed_along(block, axis, distance):
    devices = range(lax.axis_size(axis))
    route = [(i - distance, i) for i in devices if i - distance in devices]
    return lax.ppermute(block, axis, route)


def swapped(block, axis, bit):
    return lax.ppermute(block, axis, [(i, i ^ bit) for i in range(lax.axis_size(axis))])


def bits_of(axis):
    return [1 << k for k in range(lax.axis_size(axis).bit_length() - 1)]


def after(value, earlier):
    return lax.optimization_barrier((value, earlier))[0]


def gathered_near(shard, earlier=None, held=None):
    if earlier is not None:
        shard = after(shard, earlier)
    across = swapped(shard, "wsh", 2)
    if held is not None:
        across = after(across, held)
    return [shard, across, swapped(shard, "wsh", 1), swapped(across, "wsh", 1)]


class Scattering:
    def __init__(self, table, bits):
        self.table = table
        self.bits = list(bits)
        self.start()

    def start(self):
        if self.bits:
            half = self.table.shape[0] // 2
            self.came = swapped(self.table[half:], "ctx", self.bits.pop(0))
        else:
            self.came = None

    def advance(self, held=None):
        if self.came is not None:
            came = self.came if held is None else after(self.came, held)
            half = self.table.shape[0] // 2
            self.table = (self.table[:half].astype(F32) + came.astype(F32)).astype(BF16)
            self.start()
        return self.table

    def finish(self):
        while self.came is not None:
            self.advance()
        return self.table[0]


def ctx_bits(count):
    return [1 << k for k in range(count.bit_length() - 1)]


def partner_wsh(step):
    return (lax.axis_index("ctx"), lax.axis_index("wsh") ^ step)


def partner_ctx(step):
    return (lax.axis_index("ctx") ^ step, lax.axis_index("wsh"))


def remote(source, target, send, recv, device):
    return pltpu.make_async_remote_copy(
        src_ref=source,
        dst_ref=target,
        send_sem=send,
        recv_sem=recv,
        device_id=device,
        device_id_type=pl.DeviceIdType.MESH,
    )


def grads_kernel(
    count,
    split,
    early_units,
    gate_units,
    q_units,
    one_ref,
    mix_ref,
    heads_ref,
    early_ref,
    gate_ref,
    q_ref,
    branch_ref,
    small_ref,
    early_out,
    gate_out,
    q_out,
    mix_out,
    small_out,
    core_out,
    work,
    y_in,
    ctx_in,
    final,
    small_in,
    core_sems,
    y_sems,
    rs_sems,
    ag_sems,
    small_sems,
    out_sems,
):
    bits = ctx_bits(count)
    here = lax.axis_index("ctx")
    units = work.shape[0]
    rows = work.shape[2]
    width = work.shape[3]
    wsh_steps = (1, 2)
    barrier = pltpu.get_barrier_semaphore()
    partners = [partner_wsh(step) for step in wsh_steps] + [partner_ctx(bit) for bit in bits]
    for device in partners:
        pl.semaphore_signal(
            barrier, inc=1, device_id=device, device_id_type=pl.DeviceIdType.MESH
        )
    pl.semaphore_wait(barrier, len(partners))

    sizes = [rows >> (k + 1) for k in range(len(bits))]
    starts = []
    others = []
    base = 0
    for bit, size in zip(bits, sizes):
        upper = (here // bit) % 2
        others.append(base + (1 - upper) * size)
        base = base + upper * size
        starts.append(base)

    def span(start, size):
        return pl.ds(pl.multiple_of(start, 16), size)

    def core_copy(u):
        return remote(
            core_out.at[u % 2],
            work.at[u],
            core_sems.at[0, u],
            core_sems.at[1, u],
            partner_wsh(1),
        )

    def y_copy(u):
        return remote(work.at[u, 1], y_in.at[u], y_sems.at[0, u], y_sems.at[1, u], partner_wsh(2))

    recv_base = [rows - (rows >> k) for k in range(len(bits))]

    def rs_copy(u, k):
        return remote(
            work.at[u, 0, span(others[k], sizes[k])],
            ctx_in.at[u, pl.ds(recv_base[k], sizes[k])],
            rs_sems.at[0, k, u],
            rs_sems.at[1, k, u],
            partner_ctx(bits[k]),
        )

    def ag_copy(u, k):
        return remote(
            final.at[u, span(starts[k], sizes[k])],
            final.at[u, span(starts[k], sizes[k])],
            ag_sems.at[0, k, u],
            ag_sems.at[1, k, u],
            partner_ctx(bits[k]),
        )

    limits = []
    first_unit = 0
    for size in (early_units, gate_units, q_units, 4):
        limits.append((first_unit, first_unit + size))
        first_unit += size
    outs = (early_out, gate_out, q_out, mix_out)

    def by_part(u, action):
        for part, (low, high) in enumerate(limits):
            pl.when((u >= low) & (u < high))(functools.partial(action, part, u - low))

    def each_out(u, act):
        def one(part, v):
            tall = part == 3
            for i in range(split):
                row = (v // 2) * TILE_ROWS if tall else 0
                column = ((v % 2) if tall else v) * TILE_COLS + i * width
                copy = pltpu.make_async_copy(
                    final.at[u, pl.ds(i * TILE_ROWS, TILE_ROWS)],
                    outs[part].at[
                        pl.ds(pl.multiple_of(row, TILE_ROWS), TILE_ROWS),
                        pl.ds(pl.multiple_of(column, 128), width),
                    ],
                    out_sems.at[u, i],
                )
                act(copy)

        by_part(u, one)

    def columns_at(v):
        return pl.ds(pl.multiple_of(v * TILE_COLS, 128), TILE_COLS)

    wide = mix_ref.shape[1] // 4
    narrow = heads_ref.shape[0] // 4

    def pieces(u, first, put):
        steps = NEAR[2 * first : 2 * first + 2]

        def one(part, v):
            for place, step in enumerate(steps):
                if part < 3:
                    left = one_ref[:, near_at(step, TILE_ROWS)]
                    value = mat_left_t(left, (early_ref, gate_ref, q_ref)[part][:, columns_at(v)])
                else:
                    right = branch_ref[:, columns_at(v % 2)]
                    other = lax.axis_index("wsh") ^ step
                    begin = pl.multiple_of(other * wide, 128)

                    @pl.when(v < 2)
                    def _():
                        put(place, mat_left_t(mix_ref[:, pl.ds(begin, TILE_ROWS)], right))

                    @pl.when(v >= 2)
                    def _():
                        tail_at = pl.multiple_of(begin + TILE_ROWS, 128)
                        tail = mat_left_t(mix_ref[:, pl.ds(tail_at, wide - TILE_ROWS)], right)
                        heads_at = pl.multiple_of(other * narrow, 128)
                        heads = mat(heads_ref[pl.ds(heads_at, narrow), :], right)
                        put(place, jnp.concatenate([tail, heads], axis=0))

                    continue
                put(place, value)

        by_part(u, one)

    def chunked(value):
        return [
            (slice(i * TILE_ROWS, (i + 1) * TILE_ROWS), value[:, i * width : (i + 1) * width])
            for i in range(split)
        ]

    def begin(u):
        def put(place, value):
            for where, part in chunked(value):
                core_out[u % 2, place, where] = part.astype(BF16)

        pieces(u, 1, put)
        core_copy(u).start()

    def after_core(u):
        core_copy(u).wait()

        def put(place, value):
            for where, part in chunked(value):
                work[u, place, where] = (work[u, place, where].astype(F32) + part).astype(BF16)

        pieces(u, 0, put)
        y_copy(u).start()

    def after_y(u):
        y_copy(u).wait()
        work[u, 0] = (work[u, 0].astype(F32) + y_in[u].astype(F32)).astype(BF16)
        rs_copy(u, 0).start()

    def after_rs(u, k):
        rs_copy(u, k).wait()
        mine = span(starts[k], sizes[k])
        total = work[u, 0, mine].astype(F32) + ctx_in[
            u, pl.ds(recv_base[k], sizes[k])
        ].astype(F32)
        if k + 1 < len(bits):
            work[u, 0, mine] = total.astype(BF16)
            rs_copy(u, k + 1).start()
        else:
            final[u, mine] = total.astype(BF16)
            ag_copy(u, k).start()

    def after_ag(u, k):
        ag_copy(u, k).wait()
        if k > 0:
            ag_copy(u, k - 1).start()
        else:
            each_out(u, lambda copy: copy.start())

    stages = [(0, begin), (1, after_core), (3, after_y)]
    delay = 3
    for k in range(len(bits)):
        delay += 1
        stages.append((delay, functools.partial(after_rs, k=k)))
    for k in range(len(bits) - 1, -1, -1):
        delay += 1
        stages.append((delay, functools.partial(after_ag, k=k)))

    small_out[...] = small_ref[...]
    hops = partners

    def small_copy(k):
        return remote(
            small_in.at[k, 0], small_in.at[k, 1], small_sems.at[0, k], small_sems.at[1, k], hops[k]
        )

    def small_step(k):
        if k > 0:
            small_copy(k - 1).wait()
            small_out[...] += small_in[k - 1, 1]
        if k < len(hops):
            small_in[k, 0] = small_out[...]
            small_copy(k).start()

    def one_step(t, carry):
        for k in range(len(hops) + 1):
            pl.when(t == 2 * k + 1)(functools.partial(small_step, k))
        for offset, stage in stages[::-1]:
            u = t - offset
            pl.when((u >= 0) & (u < units))(functools.partial(stage, u))
        return carry

    lax.fori_loop(0, units + delay, one_step, 0)

    def finish(u, carry):
        each_out(u, lambda copy: copy.wait())
        return carry

    lax.fori_loop(0, units, finish, 0)


def reduce_grads(
    count, early_width, one, mixed, heads_t, early, gate, q, branch, small
):
    bits = ctx_bits(count)
    hops = len(bits) + 2
    split = max(1, 16 * count // TILE_ROWS)
    early_units = early_width // TILE_COLS
    gate_units = gate.shape[1] // TILE_COLS
    q_units = q.shape[1] // TILE_COLS
    units = early_units + gate_units + q_units + 4
    rows, width = TILE_ROWS * split, TILE_COLS // split
    dma = pltpu.SemaphoreType.DMA
    vmem = pl.BlockSpec(memory_space=pltpu.VMEM)
    hbm = pl.BlockSpec(memory_space=pl.ANY)
    return pl.pallas_call(
        functools.partial(grads_kernel, count, split, early_units, gate_units, q_units),
        in_specs=[vmem] * 8,
        out_specs=[hbm] * 4 + [vmem],
        out_shape=[
            jax.ShapeDtypeStruct((TILE_ROWS, early_units * TILE_COLS), BF16),
            jax.ShapeDtypeStruct((TILE_ROWS, gate_units * TILE_COLS), BF16),
            jax.ShapeDtypeStruct((TILE_ROWS, q_units * TILE_COLS), BF16),
            jax.ShapeDtypeStruct((2 * TILE_ROWS, 2 * TILE_COLS), BF16),
            jax.ShapeDtypeStruct(small.shape, F32),
        ],
        scratch_shapes=[
            pltpu.VMEM((2, 2, rows, width), BF16),
            pltpu.VMEM((units, 2, rows, width), BF16),
            pltpu.VMEM((units, rows, width), BF16),
            pltpu.VMEM((units, rows, width), BF16),
            pltpu.VMEM((units, rows, width), BF16),
            pltpu.VMEM((hops, 2) + small.shape, F32),
            dma((2, units)),
            dma((2, units)),
            dma((2, len(bits), units)),
            dma((2, len(bits), units)),
            dma((2, hops)),
            dma((units, split)),
        ],
        compiler_params=pltpu.CompilerParams(
            collective_id=1, has_side_effects=True, vmem_limit_bytes=KERNEL_VMEM
        ),
        cost_estimate=pl.CostEstimate(
            flops=6_500_000_000, bytes_accessed=30 * MIB, transcendentals=0
        ),
        name="reduce_grads",
    )(one, mixed, heads_t, early, gate, q, branch, small)


def exchange_barrier(devices):
    barrier = pltpu.get_barrier_semaphore()
    for device in devices:
        pl.semaphore_signal(
            barrier, inc=1, device_id=device, device_id_type=pl.DeviceIdType.MESH
        )
    pl.semaphore_wait(barrier, len(devices))


def row_factors(totals, owner):
    rows = owner.shape[0]
    picks = (owner == lax.broadcasted_iota(jnp.int32, (rows, 128), 1)).astype(BF16)
    high = totals.astype(BF16)
    low = (totals - high.astype(F32)).astype(BF16)
    return mat_right_t(picks, high) + mat_right_t(picks, low)


STATE_GROUP = 4


class StateExchange:
    def __init__(self, count, forward, state_ref, totals, result, scratch):
        self.group = min(STATE_GROUP, count)
        self.groups = count // self.group
        self.forward = forward
        self.state_ref, self.totals, self.result = state_ref, totals, result
        (
            self.sent,
            self.came,
            self.before,
            self.back,
            self.whole,
            self.cross,
            self.sems,
            self.cross_sems,
        ) = scratch
        self.place = lax.axis_index("ctx") % self.group
        self.at = lax.axis_index("ctx") // self.group
        self.share = state_ref.shape[1] // self.group

    @staticmethod
    def scratch(count, state):
        group = min(STATE_GROUP, count)
        groups = count // group
        part = (state.shape[0], state.shape[1] // group, STATE)
        return [
            pltpu.VMEM(state.shape, BF16),
            pltpu.VMEM((group,) + part, BF16),
            pltpu.VMEM((group,) + part, F32),
            pltpu.VMEM((group,) + part, BF16),
            pltpu.VMEM(part, BF16),
            pltpu.VMEM((groups,) + part, BF16),
            pltpu.SemaphoreType.DMA((4, group)),
            pltpu.SemaphoreType.DMA((2, groups)),
        ]

    def rows_of(self, place):
        return pl.ds(pl.multiple_of(place * self.share, 16), self.share)

    def deal(self, k, slot):
        return remote(
            self.sent.at[:, self.rows_of(self.place ^ k)],
            self.came.at[slot],
            self.sems.at[0, k],
            self.sems.at[1, k],
            partner_ctx(k),
        )

    def give(self, m, slot):
        return remote(
            self.whole,
            self.cross.at[slot],
            self.cross_sems.at[0, m],
            self.cross_sems.at[1, m],
            partner_ctx(m * self.group),
        )

    def give_back(self, k, slot):
        return remote(
            self.back.at[self.place ^ k],
            self.result.at[:, self.rows_of(slot)],
            self.sems.at[2, k],
            self.sems.at[3, k],
            partner_ctx(k),
        )

    def order(self, count):
        return range(count) if self.forward else range(count - 1, -1, -1)

    def factors(self, blocks):
        part = self.totals[blocks]
        batch = part.shape[1]
        place = lax.broadcasted_iota(jnp.int32, (self.share, 128), 0) + self.place * self.share
        columns = row_factors(part.reshape(-1, 128), place // MDIM)

        def column(block, b):
            at = (block * batch + b) * 8
            return columns[:, at : at + 1]

        return column

    def own_blocks(self):
        return pl.ds(self.at * self.group, self.group)

    def begin(self):
        self.sent[...] = self.state_ref[...].astype(BF16)
        for k in range(1, self.group):
            self.deal(k, self.place).start()
        self.came[self.place] = self.state_ref[:, self.rows_of(self.place), :].astype(BF16)
        self.cross[self.at] = jnp.zeros(self.whole.shape, BF16)

    def middle(self):
        for k in range(1, self.group):
            self.deal(k, self.place).wait_send()
            self.deal(k, self.place ^ k).wait_recv()
        factor_of = self.factors(self.own_blocks())
        for b in range(self.whole.shape[0]):
            total = jnp.zeros((self.share, STATE), F32)
            for j in self.order(self.group):
                self.before[j, b] = total
                total = factor_of(j, b) * total + self.came[j, b].astype(F32)
            self.whole[b] = total.astype(BF16)
        for m in range(1, self.groups):
            self.give(m, self.at).start()

    def carry(self):
        for m in range(1, self.groups):
            self.give(m, self.at).wait_send()
            self.give(m, self.at ^ m).wait_recv()
        factor_of = self.factors(self.own_blocks())
        any_factor = self.factors(slice(None))
        for b in range(self.whole.shape[0]):
            reach = jnp.zeros((self.share, STATE), F32)
            for g in self.order(self.groups):
                decay = None
                for j in range(self.group):
                    one = any_factor(g * self.group + j, b)
                    decay = one if decay is None else decay * one
                earlier = (g < self.at) if self.forward else (g > self.at)
                reach = jnp.where(earlier, decay * reach + self.cross[g, b].astype(F32), reach)
            for j in self.order(self.group):
                self.back[j, b] = (self.before[j, b] + reach).astype(BF16)
                reach = reach * factor_of(j, b)
        for k in range(1, self.group):
            self.give_back(k, self.place).start()
        self.result[:, self.rows_of(self.place), :] = self.back[self.place]

    def end(self):
        for k in range(1, self.group):
            self.give_back(k, self.place).wait_send()
            self.give_back(k, self.place ^ k).wait_recv()


def mix_forward_kernel(
    count,
    start_ref,
    q_ref,
    near_ref,
    state_ref,
    total_ref,
    out_ref,
    log_ref,
    table_out,
    state_out,
    totals_out,
    q_wide,
    top,
    total,
    acc,
    far,
    totals,
    result,
    total_sems,
    table_sems,
    *state_scratch,
):
    here = lax.axis_index("ctx")
    batch = near_ref.shape[1]
    width = near_ref.shape[2]
    half = count // 2
    exchange_barrier([partner_ctx(k) for k in range(1, count)])
    totals[here] = total_ref[...]

    def total_copy(k, place):
        return remote(
            totals.at[here],
            totals.at[place],
            total_sems.at[0, k],
            total_sems.at[1, k],
            partner_ctx(k),
        )

    def table_copy(i):
        return remote(
            near_ref.at[i], far.at[i], table_sems.at[0, i], table_sems.at[1, i], partner_ctx(1)
        )

    for k in range(1, count):
        total_copy(k, here).start()
    states = StateExchange(count, True, state_ref, totals, result, state_scratch)
    states.begin()
    for i in range(half):
        table_copy(i).start()
    for b in range(batch):
        spread_heads(q_ref.at[:, b * width : (b + 1) * width], q_wide.at[b], HDIM**-0.5)
    top[...] = jnp.full(top.shape, MASKED_SCORE, F32)
    total[...] = jnp.zeros(total.shape, F32)
    acc[...] = jnp.zeros(acc.shape, F32)
    first_pos = here * width

    def attend(b, source, i, block):
        kv_rows = source[i, b]
        keys = kv_rows[:, : KVHEADS * HDIM]
        values_t = kv_rows[:, KVHEADS * HDIM :].T
        allowed = attend_allowed(block, first_pos, start_ref[b][:1], width)
        tops, totals_now = top[b], total[b]
        new_tops, new_totals = [], []
        for head in range(QHEADS):
            group = head // (QHEADS // KVHEADS)
            line = slice(head, head + 1)
            scores = mat(keys, q_wide[b, :, head * width : (head + 1) * width])
            scores = jnp.where(allowed, scores, MASKED_SCORE)
            old = tops[line]
            new = jnp.maximum(old, jnp.max(scores, axis=0, keepdims=True))
            terms = jnp.exp(scores - new)
            shrink = jnp.exp(old - new)
            new_tops.append(new)
            new_totals.append(
                totals_now[line] * shrink + jnp.sum(terms, axis=0, keepdims=True)
            )
            acc[b, head] = acc[b, head] * shrink + mat(
                values_t[group * HDIM : (group + 1) * HDIM, :], terms.astype(BF16)
            )
        top[b] = jnp.concatenate(new_tops, axis=0)
        total[b] = jnp.concatenate(new_totals, axis=0)

    bits = ctx_bits(count)
    high = len(bits) - 1

    def step_of(i):
        return sum(((i // (1 << p)) % 2) * (1 << (high - p)) for p in range(high))

    def pair(source, low, begin=0, end=half):
        def one(i, carry):
            block = here ^ (step_of(i) + low)

            @pl.when(block <= here)
            def _():
                for b in range(batch):
                    attend(b, source, i, block)

            return carry

        lax.fori_loop(begin, end, one, 0)

    pair(near_ref, 0, 0, half // 2)
    for k in range(1, count):
        total_copy(k, here).wait_send()
        total_copy(k, here ^ k).wait_recv()
    states.middle()
    pair(near_ref, 0, half // 2)
    states.carry()
    for i in range(half):
        table_copy(i).wait()
    pair(far, 1)
    for b in range(batch):
        for head in range(QHEADS):
            out_ref[head * HDIM : (head + 1) * HDIM, b * width : (b + 1) * width] = (
                acc[b, head] / total[b, head : head + 1, :]
            ).astype(BF16)
        log_ref[b] = top[b] + jnp.log(total[b])
    table_out[:half] = near_ref[...]
    table_out[half:] = far[...]
    totals_out[...] = totals[...]
    states.end()
    state_out[...] = result[...]


def mix_forward(count, starts, queries_t, near, state, total):
    half, batch, width, kv_width = near.shape
    vmem = pl.BlockSpec(memory_space=pltpu.VMEM)
    dma = pltpu.SemaphoreType.DMA
    low = functools.partial(jax.ShapeDtypeStruct, dtype=BF16)
    wide = functools.partial(jax.ShapeDtypeStruct, dtype=F32)
    return pl.pallas_call(
        functools.partial(mix_forward_kernel, count),
        in_specs=[vmem] * 5,
        out_specs=[vmem] * 5,
        out_shape=[
            low(queries_t.shape),
            wide((batch, QHEADS, width)),
            low((count,) + near.shape[1:]),
            low(state.shape),
            wide((count,) + total.shape),
        ],
        scratch_shapes=[
            pltpu.VMEM((batch, KVHEADS * HDIM, QHEADS * width), BF16),
            pltpu.VMEM((batch, QHEADS, width), F32),
            pltpu.VMEM((batch, QHEADS, width), F32),
            pltpu.VMEM((batch, QHEADS, HDIM, width), F32),
            pltpu.VMEM(near.shape, BF16),
            pltpu.VMEM((count,) + total.shape, F32),
            pltpu.VMEM(state.shape, BF16),
            dma((2, count)),
            dma((2, half)),
        ]
        + StateExchange.scratch(count, state),
        compiler_params=pltpu.CompilerParams(
            collective_id=2, has_side_effects=True, vmem_limit_bytes=KERNEL_VMEM
        ),
        cost_estimate=pl.CostEstimate(
            flops=batch * count * width * width * 8 * 1000,
            bytes_accessed=4 * MIB,
            transcendentals=0,
        ),
        name="mix_forward",
    )(starts, queries_t, near, state, total)


def mix_backward_kernel(
    count,
    start_ref,
    q_ref,
    table_ref,
    attended_ref,
    grad_ref,
    log_ref,
    state_ref,
    totals_ref,
    dq_ref,
    dkv_ref,
    later_ref,
    q_wide,
    g_wide,
    q_tall,
    g_tall,
    delta,
    acc,
    mine,
    theirs,
    far,
    result,
    table_sems,
    *state_scratch,
):
    here = lax.axis_index("ctx")
    batch = table_ref.shape[1]
    width = table_ref.shape[2]
    half = count // 2
    kv_width = KVHEADS * HDIM
    exchange_barrier([partner_ctx(k) for k in range(1, count)])
    states = StateExchange(count, False, state_ref, totals_ref, result, state_scratch)
    states.begin()
    first_pos = here * width
    acc[...] = jnp.zeros(acc.shape, F32)
    mine[...] = jnp.zeros(mine.shape, BF16)
    theirs[...] = jnp.zeros(theirs.shape, BF16)
    for b in range(batch):
        columns = slice(b * width, (b + 1) * width)
        spread_heads(q_ref.at[:, columns], q_wide.at[b], HDIM**-0.5)
        spread_heads(grad_ref.at[:, columns], g_wide.at[b], 1.0)
        for head in range(QHEADS):
            lanes = slice(head * width, (head + 1) * width)
            q_tall[b, lanes, :] = q_wide[b, :, lanes].T
            g_tall[b, lanes, :] = g_wide[b, :, lanes].T
            span = slice(head * HDIM, (head + 1) * HDIM)
            delta[b, head : head + 1, :] = jnp.sum(
                attended_ref[span, columns].astype(F32) * grad_ref[span, columns].astype(F32),
                axis=0,
                keepdims=True,
            )

    def attend(b, place, block, target, i):
        kv_rows = table_ref[place, b]
        keys = kv_rows[:, :kv_width]
        values = kv_rows[:, kv_width:]
        keys_t = keys.T
        allowed = attend_allowed(block, first_pos, start_ref[b][:1], width)
        logs_now, deltas = log_ref[b], delta[b]
        dk = jnp.zeros((width, kv_width), F32)
        dv = jnp.zeros((width, kv_width), F32)
        for head in range(QHEADS):
            group = head // (QHEADS // KVHEADS)
            lanes = slice(head * width, (head + 1) * width)
            line = slice(head, head + 1)
            scores = mat(keys, q_wide[b, :, lanes])
            shifted = jnp.where(allowed, scores - logs_now[line], MASKED_SCORE)
            probs = jnp.exp(shifted)
            grad_probs = mat(values, g_wide[b, :, lanes])
            grad_scores = (probs * (grad_probs - deltas[line])).astype(BF16)
            dk = dk + mat(grad_scores, q_tall[b, lanes, :])
            dv = dv + mat(probs.astype(BF16), g_tall[b, lanes, :])
            acc[b, head] += mat(keys_t[group * HDIM : (group + 1) * HDIM, :], grad_scores)
        target[i, b] = jnp.concatenate([dk, dv], axis=1).astype(BF16)

    bits = ctx_bits(count)
    high = len(bits) - 1

    def step_of(i):
        return sum(((i // (1 << p)) % 2) * (1 << (high - p)) for p in range(high))

    def pair(target, low, begin=0, end=half):
        def one(i, carry):
            block = here ^ (step_of(i) + low)

            @pl.when(block <= here)
            def _():
                for b in range(batch):
                    attend(b, i + low * half, block, target, i)

            return carry

        lax.fori_loop(begin, end, one, 0)

    def table_copy(i):
        return remote(
            theirs.at[i], far.at[i], table_sems.at[0, i], table_sems.at[1, i], partner_ctx(1)
        )

    pair(theirs, 1, 0, half // 2)
    states.middle()
    pair(theirs, 1, half // 2)
    for i in range(half):
        table_copy(i).start()
    states.carry()
    pair(mine, 0)
    for b in range(batch):
        for head in range(QHEADS):
            dq_ref[head * HDIM : (head + 1) * HDIM, b * width : (b + 1) * width] = (
                acc[b, head] * HDIM**-0.5
            ).astype(BF16)
    for i in range(half):
        table_copy(i).wait()
    dkv_ref[...] = (mine[...].astype(F32) + far[...].astype(F32)).astype(BF16)
    states.end()
    later_ref[...] = result[...]


def mix_backward(count, starts, queries_t, table, attended_t, grad_t, logs, state, totals):
    _, batch, width, kv_width = table.shape
    half = count // 2
    vmem = pl.BlockSpec(memory_space=pltpu.VMEM)
    dma = pltpu.SemaphoreType.DMA
    low = functools.partial(jax.ShapeDtypeStruct, dtype=BF16)
    near = (half, batch, width, kv_width)
    wide = pltpu.VMEM((batch, KVHEADS * HDIM, QHEADS * width), BF16)
    tall = pltpu.VMEM((batch, QHEADS * width, KVHEADS * HDIM), BF16)
    return pl.pallas_call(
        functools.partial(mix_backward_kernel, count),
        in_specs=[vmem] * 8,
        out_specs=[vmem] * 3,
        out_shape=[low(queries_t.shape), low(near), low(state.shape)],
        scratch_shapes=[
            wide,
            wide,
            tall,
            tall,
            pltpu.VMEM((batch, QHEADS, width), F32),
            pltpu.VMEM((batch, QHEADS, HDIM, width), F32),
            pltpu.VMEM(near, BF16),
            pltpu.VMEM(near, BF16),
            pltpu.VMEM(near, BF16),
            pltpu.VMEM(state.shape, BF16),
            dma((2, half)),
        ]
        + StateExchange.scratch(count, state),
        compiler_params=pltpu.CompilerParams(
            collective_id=3, has_side_effects=True, vmem_limit_bytes=KERNEL_VMEM
        ),
        cost_estimate=pl.CostEstimate(
            flops=batch * count * width * width * 8 * 2000,
            bytes_accessed=8 * MIB,
            transcendentals=0,
        ),
        name="mix_backward",
    )(starts, queries_t, table, attended_t, grad_t, logs, state, totals)


def front_kernel(
    count,
    conv_tiles,
    gate_tiles,
    x_ref,
    gain_ref,
    start_ref,
    own_ref,
    weight_ref,
    bias_ref,
    normed_ref,
    others_ref,
    conv_ref,
    edge_ref,
    act_ref,
    dt_ref,
    q_ref,
    gate_ref,
    table_ref,
    edge_x,
    near,
    table,
    cross_sems,
    core_sems,
    side_sems,
    last_sems,
    table_sems,
    edge_sems,
):
    here = lax.axis_index("ctx")
    batch = table.shape[1]
    rows = table.shape[2]
    size = own_ref.shape[0]
    chunks = own_ref.shape[1] // EARLY_TILE
    half = count // 2
    exchange_barrier(
        [partner_wsh(1), partner_wsh(2)] + [partner_ctx(k) for k in range(1, count)]
    )
    right = (here + 1) % count

    def edge_copy(b):
        return remote(
            x_ref.at[pl.ds((b + 1) * rows - 16, 16)],
            edge_x.at[b],
            edge_sems.at[0, b],
            edge_sems.at[1, b],
            (right, lax.axis_index("wsh")),
        )

    my_half = pl.ds(pl.multiple_of((here % 2) * (size // 2), 16), size // 2)
    other_half = pl.ds(pl.multiple_of((1 - here % 2) * (size // 2), 16), size // 2)

    def tile(place):
        return pl.ds(pl.multiple_of(place * EARLY_TILE, EARLY_TILE), EARLY_TILE)

    def columns(k):
        return tile((k + gate_tiles) % chunks)

    gate_from = chunks - gate_tiles

    def cross_copy(k):
        return remote(
            own_ref.at[my_half, columns(k)],
            near.at[0, my_half, columns(k)],
            cross_sems.at[0, k],
            cross_sems.at[1, k],
            partner_wsh(2),
        )

    def side_copy(k):
        return remote(
            near.at[0, my_half, columns(k)],
            near.at[0, my_half, columns(k)],
            side_sems.at[0, k],
            side_sems.at[1, k],
            partner_ctx(1),
        )

    def side_in(k):
        return remote(
            near.at[0, other_half, columns(k)],
            near.at[0, other_half, columns(k)],
            side_sems.at[0, k],
            side_sems.at[1, k],
            partner_ctx(1),
        )

    def core_copy(k):
        return remote(
            own_ref.at[:, columns(k)],
            near.at[1, :, columns(k)],
            core_sems.at[0, k],
            core_sems.at[1, k],
            partner_wsh(1),
        )

    def last_copy(k):
        return remote(
            near.at[0, :, columns(k)],
            near.at[2, :, columns(k)],
            last_sems.at[0, k],
            last_sems.at[1, k],
            partner_wsh(1),
        )

    bits = ctx_bits(count)
    high = len(bits) - 1

    def step_of(i):
        return sum(((i >> p) & 1) * (1 << (high - p)) for p in range(high))

    def table_copy(i):
        return remote(
            table.at[0],
            table.at[i],
            table_sems.at[0, i],
            table_sems.at[1, i],
            partner_ctx(step_of(i)),
        )

    def send_first(k, carry):
        cross_copy(k).start()
        core_copy(k).start()
        return carry

    lax.fori_loop(0, chunks, send_first, 0)
    for b in range(batch):
        edge_copy(b).start()

    def normalized(low):
        wide = low.astype(F32)
        return (wide * inv_rms(wide) * gain_ref[...]).astype(BF16)

    normed_ref[...] = normalized(x_ref[...])
    for b in range(batch):
        edge_copy(b).wait()
    edge_normed = normalized(
        jnp.concatenate([edge_x[b] for b in range(batch)], axis=0)
    )
    edge_x[...] = edge_normed.reshape(edge_x.shape)

    def product(pick, k):
        total = None
        for place, step in enumerate(NEAR):
            block = own_ref[:, columns(k)] if place == 0 else near[place - 1, :, columns(k)]
            part = mat(pick(near_at(step, size)), block)
            total = part if total is None else total + part
        return total

    def compute(k):
        core_copy(k).wait()
        last_copy(k).wait()
        value = product(lambda at: normed_ref[:, at], k)

        @pl.when(k == 0)
        def _():
            table[0] = value.astype(BF16).reshape(table.shape[1:])
            for i in range(1, half):
                table_copy(i).start()

        @pl.when((k > 0) & (k <= conv_tiles))
        def _():
            place = tile(k - 1)
            conv_ref[:, place] = value
            taps = weight_ref[:, place]
            bias = bias_ref[:, place]
            for b in range(batch):
                edge = product(lambda at, b=b: edge_x[b, :, at], k)[16 - EDGE :]
                edge_ref[b * EDGE : (b + 1) * EDGE, place] = edge
                span = slice(b * rows, (b + 1) * rows)
                total, _ = conv_sums(
                    conv_inputs(edge, value[span]), taps, bias, start_ref[span]
                )
                act_ref[span, place] = total * sigmoid(total)

        @pl.when(k == conv_tiles + 1)
        def _():
            dt_ref[...] = value

        @pl.when((k > conv_tiles + 1) & (k < gate_from))
        def _():
            q_ref[tile(k - conv_tiles - 2), :] = value.T.astype(BF16)

        @pl.when(k >= gate_from)
        def _():
            gate_ref[:, tile(k - gate_from)] = value

    def one_step(t, carry):
        @pl.when(t < chunks)
        def _():
            cross_copy(t).wait()
            side_copy(t).start()

        @pl.when((t >= 1) & (t <= chunks))
        def _():
            side_copy(t - 1).wait_send()
            side_in(t - 1).wait_recv()
            last_copy(t - 1).start()

        pl.when(t >= 2)(functools.partial(compute, t - 2))
        return carry

    lax.fori_loop(0, chunks + 2, one_step, 0)
    others_ref[...] = near[...]
    for i in range(1, half):
        table_copy(i).wait()
    table_ref[...] = table[...]


def front(count, batch, x, gain, rel_start, own, conv_weight, conv_bias, q_width):
    tokens, depth = x.shape
    size, columns = own.shape
    rows = tokens // batch
    channels = conv_weight.shape[1]
    chunks = columns // EARLY_TILE
    half = count // 2
    vmem = pl.BlockSpec(memory_space=pltpu.VMEM)
    dma = pltpu.SemaphoreType.DMA
    low = functools.partial(jax.ShapeDtypeStruct, dtype=BF16)
    wide = functools.partial(jax.ShapeDtypeStruct, dtype=F32)
    table = (half, batch, rows, EARLY_TILE)
    return pl.pallas_call(
        functools.partial(
            front_kernel, count, channels // EARLY_TILE, DSSM // EARLY_TILE
        ),
        in_specs=[vmem] * 6,
        out_specs=[vmem] * 9,
        out_shape=[
            low((tokens, depth)),
            low((3, size, columns)),
            wide((tokens, channels)),
            wide((batch * EDGE, channels)),
            wide((tokens, channels)),
            wide((tokens, EARLY_TILE)),
            low((q_width, tokens)),
            wide((tokens, DSSM)),
            low(table),
        ],
        scratch_shapes=[
            pltpu.VMEM((batch, 16, depth), BF16),
            pltpu.VMEM((3, size, columns), BF16),
            pltpu.VMEM(table, BF16),
            dma((2, chunks)),
            dma((2, chunks)),
            dma((2, chunks)),
            dma((2, chunks)),
            dma((2, half)),
            dma((2, batch)),
        ],
        compiler_params=pltpu.CompilerParams(
            collective_id=4, has_side_effects=True, vmem_limit_bytes=KERNEL_VMEM
        ),
        cost_estimate=pl.CostEstimate(
            flops=2 * tokens * depth * columns, bytes_accessed=20 * MIB, transcendentals=0
        ),
        name="front",
    )(x, gain[None], rel_start, own, conv_weight, conv_bias[None])


def local(
    inputs,
    cotangent,
    lengths,
    norm1_gain,
    in_weight,
    dt_weight,
    conv_weight,
    conv_bias,
    dt_bias,
    decay_rate,
    skip_gain,
    mamba_gain,
    out_weight,
    q_weight,
    kv_weight,
    o_weight,
    norm2_gain,
    gu_weight,
    down_weight,
):
    count, _, rows, features = inputs.shape
    here = lax.axis_index("ctx")
    ctx_count = lax.axis_size("ctx")
    tokens = count * rows
    first_pos = here * rows
    own_pos = first_pos + jnp.arange(rows, dtype=jnp.int32)
    starts = jax.vmap(lambda row: seq_starts(row, own_pos))(lengths[:, 0])
    rel_start = (starts - first_pos).reshape(tokens, 1)
    taps = conv_weight.shape[0]
    channels = conv_weight.shape[1]
    kv_width = kv_weight.shape[1]
    x_low = inputs.reshape(tokens, features)
    grad_top = cotangent.reshape(tokens, features)

    conv_tiles = channels // EARLY_TILE
    gate_tiles = DSSM // EARLY_TILE
    early_shard = jnp.concatenate(
        [
            in_weight[:, :DSSM],
            kv_weight,
            in_weight[:, DSSM:],
            jnp.pad(dt_weight, ((0, 0), (0, EARLY_TILE - dt_weight.shape[1]))),
            q_weight,
        ],
        axis=1,
    )

    normed, early_others, conv_rows, edge_rows, act, dt_rows, queries_t, gate_z, near_table = front(
        ctx_count,
        count,
        x_low,
        norm1_gain,
        rel_start,
        early_shard,
        conv_weight,
        conv_bias,
        q_weight.shape[1],
    )
    high_bits = bits_of("ctx")[1:]
    later_shards = after(
        (
            jnp.concatenate([out_weight, o_weight], axis=0),
            gu_weight,
            down_weight,
        ),
        dt_rows,
    )
    crossing = [swapped(shard, "wsh", 2) for shard in later_shards]

    def head_row(values):
        return jnp.pad(values, (0, 128 - MHEADS))[None]

    bias_row, rate_row = head_row(dt_bias), head_row(decay_rate)
    steps, decay, decay_t, to_end, total, fresh = ssd_state(
        count, act, dt_rows, bias_row, rate_row, rel_start
    )
    starts_row = jnp.broadcast_to(starts[:, None, :], (count, 8, rows))
    attended_t, logs, key_table, state_in, totals = mix_forward(
        ctx_count, starts_row, queries_t, near_table, fresh, total
    )

    def near_blocks(which, held):
        shard, across = later_shards[which], after(crossing[which], held)
        return [shard, across, swapped(shard, "wsh", 1), swapped(across, "wsh", 1)]

    outs = near_blocks(0, attended_t)
    skip_row = jnp.repeat(skip_gain, MDIM)[None]
    scanned = ssd_forward(count, act, steps, decay, decay_t, rel_start, state_in, skip_row)
    gate_sig = jax.nn.sigmoid(gate_z)
    gated = scanned * gate_z * gate_sig
    scale_m = inv_rms(gated)
    mixed = (gated * scale_m * mamba_gain).astype(BF16)
    gu_full, down_full = near_blocks(1, mixed), near_blocks(2, mixed)
    middle, normed_two = out_project(x_low, mixed, attended_t, norm2_gain, outs)

    layer_out, grad_middle, branch, grad_norm2, hidden, grad_pair = mlp_both(
        lax.axis_index("wsh").astype(jnp.int32)[None],
        normed_two,
        grad_top,
        middle,
        norm2_gain,
        gu_full,
        down_full,
    )
    gu_send = block_grads(normed_two, grad_pair, NEAR[2:])[0]
    down_send = block_grads(hidden, grad_top[None], NEAR[2:])[0]
    gu_sent = swapped(gu_send, "wsh", 1)
    down_sent = swapped(down_send, "wsh", 1)
    branch = after(branch, (gu_send, down_send))
    grad_mixed, grad_attended_t = out_unproject(branch, outs, DSSM, QHEADS * HDIM)
    grad_gated, grad_mamba = rms_pull(gated, scale_m, mamba_gain, grad_mixed)
    grad_gate_z = grad_gated * scanned * gate_sig * (1.0 + gate_z * (1.0 - gate_sig))
    grad_scanned = grad_gated * gate_z * gate_sig
    grad_state = state_grad(count, grad_scanned, act, decay, rel_start)
    gu_left, down_left = after((normed_two, hidden), grad_state)
    gu_kept, gu_other = block_grads(gu_left, grad_pair, NEAR[:2], gu_sent)
    down_kept, down_other = block_grads(down_left, grad_top[None], NEAR[:2], down_sent)
    gu_crossed = swapped(gu_other, "wsh", 2)
    down_crossed = swapped(down_other, "wsh", 2)

    grad_attended_t = after(grad_attended_t, (gu_other, down_other))
    dq_t, dkv_near, later = mix_backward(
        ctx_count,
        starts_row,
        queries_t,
        key_table,
        attended_t,
        grad_attended_t,
        logs,
        grad_state,
        totals,
    )
    key_grads = Scattering(dkv_near, high_bits)
    grad_gate_z = grad_gate_z.astype(BF16)
    dq_rows = dq_t.T
    grad_normed = unproject(
        jnp.zeros((tokens, features), F32),
        grad_gate_z,
        [early_shard] + [early_others] * 3,
        768,
        near_specs(early_shard, 768, 0),
    )
    grad_normed = unproject(
        grad_normed,
        dq_rows,
        [early_shard] + [early_others] * 3,
        EARLY_TILE,
        near_specs(early_shard, EARLY_TILE, gate_tiles + conv_tiles + 2),
    )

    def total_of(kept, crossed):
        return (kept.astype(F32) + crossed.astype(F32)).astype(BF16)

    parts = total_of(gu_kept, gu_crossed), total_of(down_kept, down_crossed)
    later = after(later, (key_grads.advance(grad_normed), parts))
    dx, db, dc, dt_grad, small_ssd = ssd_backward(
        count,
        act,
        steps,
        decay,
        decay_t,
        rel_start,
        state_in,
        skip_row,
        scanned,
        grad_scanned,
        later,
        to_end,
        total,
        dt_rows,
        bias_row,
        rate_row,
    )
    key_grads.advance(dx)
    grad_kv_rows = key_grads.finish().reshape(tokens, -1)
    edge_back = passed_along(
        edge_grads(count, dx, db, dc, conv_rows, edge_rows, rel_start, conv_weight, conv_bias),
        "ctx",
        -1,
    )
    grad_early, conv_grads, input_grad, grad_norm1 = early_back(
        count,
        grad_normed,
        grad_kv_rows,
        dx,
        db,
        dc,
        conv_rows,
        edge_rows,
        edge_back,
        dt_grad,
        rel_start,
        conv_weight,
        conv_bias,
        x_low,
        norm1_gain,
        grad_middle,
        early_shard,
        early_others,
    )
    small_ssd = jnp.sum(small_ssd, axis=0)
    grad_dt_w = mat_left_t(normed, dt_grad[:, :MHEADS])

    gu_sum, down_sum = lax.psum(parts, "ctx")
    pieces = (
        grad_norm1[0],
        conv_grads[:taps],
        conv_grads[taps],
        small_ssd[0, :MHEADS],
        small_ssd[1, :MHEADS],
        small_ssd[2, :MHEADS],
        grad_mamba,
        grad_norm2[0],
        grad_dt_w,
    )
    packed = jnp.concatenate(
        [
            jnp.pad(piece.reshape(-1), (0, -piece.size % 1024)).reshape(-1, 128)
            for piece in pieces
        ],
        axis=0,
    )
    early_sum, gate_sum, q_sum, mix_sum, packed = reduce_grads(
        ctx_count,
        kv_width + channels,
        normed,
        mixed,
        attended_t,
        grad_early,
        grad_gate_z,
        dq_rows,
        branch,
        packed,
    )
    in_sum, q_sum, kv_sum, out_sum, o_sum = finish(
        early_sum,
        gate_sum,
        mix_sum,
        q_sum,
        [w.shape for w in (in_weight, q_weight, kv_weight, out_weight, o_weight)],
    )
    totals_w = [in_sum, out_sum, q_sum, kv_sum, o_sum, gu_sum.astype(F32), down_sum.astype(F32)]
    small = []
    place = 0
    for piece in pieces:
        lines = -(-piece.size // 1024) * 8
        small.append(packed[place : place + lines].reshape(-1)[: piece.size].reshape(piece.shape))
        place += lines
    dt_size = dt_weight.shape[0]
    dt_sum = lax.dynamic_slice_in_dim(small[8], lax.axis_index("wsh") * dt_size, dt_size, 0)
    shape = (count, 1, rows, features)
    return (
        layer_out.reshape(shape),
        input_grad.reshape(shape),
        small[0],
        totals_w[0],
        dt_sum,
        small[1],
        small[2],
        small[3],
        small[4],
        small[5],
        small[6],
        totals_w[1],
        totals_w[2],
        totals_w[3],
        totals_w[4],
        small[7],
        totals_w[5],
        totals_w[6],
    )


def solution(mesh):
    stream = P(None, "wsh", "ctx", None)
    shard = P("wsh", None)
    in_specs = (
        stream,
        stream,
        P(None, "wsh", None),
        P(),
        shard,
        shard,
        P(),
        P(),
        P(),
        P(),
        P(),
        P(),
        shard,
        shard,
        shard,
        shard,
        P(),
        shard,
        shard,
    )
    out_specs = (
        stream,
        stream,
        P(),
        shard,
        shard,
        P(),
        P(),
        P(),
        P(),
        P(),
        P(),
        shard,
        shard,
        shard,
        shard,
        P(),
        shard,
        shard,
    )
    return jax.shard_map(local, mesh=mesh, in_specs=in_specs, out_specs=out_specs, check_vma=False)
```

```python
import functools

import jax
import jax.numpy as jnp
from jax import lax
from jax.experimental import pallas as pl
from jax.experimental.pallas import tpu as pltpu
from jax.sharding import PartitionSpec as P

FF = 2048
MHEADS = 24
MDIM = 64
STATE = 128
QHEADS = 8
KVHEADS = 2
HDIM = 64
DSSM = 1536
HGROUP = 8
NGROUP = MHEADS // HGROUP
GWIDTH = HGROUP * MDIM
PAIR = 2 * MDIM

NORM_EPS = 1e-05
PRECISE = lax.Precision.HIGHEST
MASKED_SCORE = -1e30
MIB = 2**20
KERNEL_VMEM = 60 * MIB
F32 = jnp.float32
BF16 = jnp.bfloat16


def dot_as(left, right, left_dim, right_dim):
    return lax.dot_general(
        left, right, (((left_dim,), (right_dim,)), ((), ())), preferred_element_type=F32
    )


def mat(left, right):
    return dot_as(left, right, 1, 0)


def mat_left_t(left, right):
    return dot_as(left, right, 0, 0)


def mat_right_t(left, right):
    return dot_as(left, right, 1, 1)


def inv_rms(rows):
    return lax.rsqrt(jnp.mean(rows * rows, axis=-1, keepdims=True) + NORM_EPS)


def rms_pull(rows, scale, gain, grad):
    scaled = rows * scale
    grad_gain = jnp.sum(grad * scaled, axis=0)
    through = grad * gain
    inner = jnp.mean(through * scaled, axis=-1, keepdims=True)
    return scale * (through - scaled * inner), grad_gain


def seq_starts(lengths_row, positions):
    begins = jnp.cumsum(lengths_row, dtype=jnp.int32) - lengths_row
    picked = jnp.where(begins[None, :] <= positions[:, None], begins[None, :], 0)
    return jnp.max(picked, axis=1)


def head_lanes(rows):
    return lax.broadcasted_iota(jnp.int32, (rows, PAIR), 1) < MDIM


def masked_products(b_low, c_low, rel_start):
    rows = b_low.shape[0]
    at_row = lax.broadcasted_iota(jnp.int32, (rows, rows), 0)
    at_col = lax.broadcasted_iota(jnp.int32, (rows, rows), 1)
    allowed = (at_col <= at_row) & (at_col >= rel_start)
    return allowed, jnp.where(allowed, mat_right_t(c_low, b_low), 0.0)


def pair_columns(first_half, columns, head):
    return jnp.where(first_half, columns[:, head : head + 1], columns[:, head + 1 : head + 2])


def exact(left, right, left_dim, right_dim):
    return lax.dot_general(
        left,
        right,
        (((left_dim,), (right_dim,)), ((), ())),
        precision=PRECISE,
        preferred_element_type=F32,
    )


def sums_by(values, picks):
    high = values.astype(BF16)
    low = (values - high.astype(F32)).astype(BF16)
    return mat(high, picks) + mat(low, picks)


def lower_ones(rows):
    at_row = lax.broadcasted_iota(jnp.int32, (rows, rows), 0)
    at_col = lax.broadcasted_iota(jnp.int32, (rows, rows), 1)
    return (at_row >= at_col).astype(F32)


def sigmoid(value):
    return 1.0 / (1.0 + jnp.exp(-value))


def softplus(value):
    return jnp.maximum(value, 0.0) + jnp.log1p(jnp.exp(-jnp.abs(value)))


def scaled_rows(target, source_ref, factors):
    first_half = head_lanes(source_ref.shape[0])
    for head in range(0, MHEADS, 2):
        lanes = slice(head * MDIM, head * MDIM + PAIR)
        target[:, lanes] = (
            source_ref[:, lanes] * pair_columns(first_half, factors, head)
        ).astype(BF16)


def ssd_state_kernel(
    act_ref,
    dt_ref,
    bias_ref,
    rate_ref,
    start_ref,
    step_ref,
    decay_ref,
    decay_t_ref,
    end_ref,
    total_ref,
    state_ref,
    scaled,
):
    rows = act_ref.shape[0]
    steps = softplus(dt_ref[:, :128] + bias_ref[...])
    decay = exact(lower_ones(rows), -steps * rate_ref[...], 1, 0)
    rel_start = start_ref[...]
    last_start = rel_start[rows - 1 : rows, :]
    kept = lax.broadcasted_iota(jnp.int32, (rows, 1), 0) >= last_start
    end = decay[rows - 1 : rows, :]
    to_end = jnp.where(kept, jnp.exp(end - decay), 0.0)
    step_ref[...] = steps
    decay_ref[...] = decay
    decay_t_ref[0] = decay.T
    end_ref[...] = to_end
    total_ref[0] = jnp.broadcast_to(jnp.where(last_start < 0, jnp.exp(end), 0.0), (8, 128))
    scaled_rows(scaled, act_ref, to_end * steps)
    state_ref[0] = mat_left_t(scaled[...], act_ref[:, DSSM : DSSM + STATE].astype(BF16))


def row_spec(rows, width, place=0):
    return pl.BlockSpec((rows, width), lambda b: (b, place))


def ssd_state(count, act, dt_rows, bias, rate, rel_start):
    rows = act.shape[0] // count
    lanes = pl.BlockSpec((1, 128), lambda b: (0, 0))
    heads = jax.ShapeDtypeStruct((count * rows, 128), F32)
    return pl.pallas_call(
        ssd_state_kernel,
        grid=(count,),
        in_specs=[
            row_spec(rows, act.shape[1]),
            row_spec(rows, dt_rows.shape[1]),
            lanes,
            lanes,
            row_spec(rows, 1),
        ],
        out_specs=[
            row_spec(rows, 128),
            row_spec(rows, 128),
            pl.BlockSpec((1, 128, rows), lambda b: (b, 0, 0)),
            row_spec(rows, 128),
            pl.BlockSpec((1, 8, 128), lambda b: (b, 0, 0)),
            pl.BlockSpec((1, DSSM, STATE), lambda b: (b, 0, 0)),
        ],
        out_shape=[
            heads,
            heads,
            jax.ShapeDtypeStruct((count, 128, rows), F32),
            heads,
            jax.ShapeDtypeStruct((count, 8, 128), F32),
            jax.ShapeDtypeStruct((count, DSSM, STATE), F32),
        ],
        scratch_shapes=[pltpu.VMEM((rows, DSSM), BF16)],
        compiler_params=pltpu.CompilerParams(vmem_limit_bytes=KERNEL_VMEM),
        cost_estimate=pl.CostEstimate(
            flops=1_000_000_000, bytes_accessed=8 * MIB, transcendentals=0
        ),
        name="ssd_state",
    )(act, dt_rows, bias, rate, rel_start)


def state_grad_kernel(dy_ref, c_ref, decay_ref, start_ref, out_ref, scaled):
    reach = jnp.where(start_ref[...] < 0, jnp.exp(decay_ref[...]), 0.0)
    scaled_rows(scaled, dy_ref, reach)
    out_ref[0] = mat_left_t(scaled[...], c_ref[...].astype(BF16))


def state_grad(count, dy, act, decay, rel_start):
    rows = act.shape[0] // count
    return pl.pallas_call(
        state_grad_kernel,
        grid=(count,),
        in_specs=[
            row_spec(rows, DSSM),
            row_spec(rows, STATE, DSSM // STATE + 1),
            row_spec(rows, 128),
            row_spec(rows, 1),
        ],
        out_specs=pl.BlockSpec((1, DSSM, STATE), lambda b: (b, 0, 0)),
        out_shape=jax.ShapeDtypeStruct((count, DSSM, STATE), F32),
        scratch_shapes=[pltpu.VMEM((rows, DSSM), BF16)],
        compiler_params=pltpu.CompilerParams(vmem_limit_bytes=KERNEL_VMEM),
        cost_estimate=pl.CostEstimate(
            flops=1_000_000_000, bytes_accessed=8 * MIB, transcendentals=0
        ),
        name="state_grad",
    )(dy, act, decay, rel_start)


def group_heads(ref):
    return pltpu.roll(ref[...], (128 - HGROUP * pl.program_id(1)) % 128, 1)


def group_rows(decay_t_ref):
    return decay_t_ref[0, pl.ds(pl.multiple_of(HGROUP * pl.program_id(1), HGROUP), HGROUP), :]


def ssd_forward_kernel(
    x_ref, b_ref, c_ref, step_ref, decay_ref, decay_t_ref, start_ref, state_ref, skip_ref, y_ref
):
    rows = x_ref.shape[0]
    b_low = b_ref[...].astype(BF16)
    c_low = c_ref[...].astype(BF16)
    rel_start = start_ref[...]
    _, products = masked_products(b_low, c_low, rel_start)
    incoming = mat_right_t(c_low, state_ref[0].astype(BF16))
    first_half = head_lanes(rows)
    steps = group_heads(step_ref)
    decay = group_heads(decay_ref)
    decay_t = group_rows(decay_t_ref)
    reach = jnp.where(rel_start < 0, jnp.exp(decay), 0.0)
    for head in range(0, HGROUP, 2):
        lanes = slice(head * MDIM, head * MDIM + PAIR)
        x_pair = x_ref[:, lanes]
        scaled = (x_pair * pair_columns(first_half, steps, head)).astype(BF16)
        parts = []
        for one in (head, head + 1):
            gaps = decay[:, one : one + 1] - decay_t[one : one + 1, :]
            weights = (jnp.exp(jnp.minimum(gaps, 0.0)) * products).astype(BF16)
            parts.append(mat(weights, scaled))
        y_ref[:, lanes] = (
            jnp.where(first_half, parts[0], parts[1])
            + pair_columns(first_half, reach, head) * incoming[:, lanes]
            + skip_ref[:, lanes] * x_pair
        )


def ssd_backward_kernel(
    x_ref,
    b_ref,
    c_ref,
    step_ref,
    decay_ref,
    decay_t_ref,
    start_ref,
    state_ref,
    skip_ref,
    y_ref,
    dy_ref,
    later_ref,
    end_ref,
    total_ref,
    dt_ref,
    bias_ref,
    rate_ref,
    dx_ref,
    db_ref,
    dc_ref,
    dt_grad_ref,
    small_ref,
    one_sum,
    two_sum,
    three_sum,
    mixed_y,
    mixed_x,
    head_sums,
    row_sums,
):
    rows = x_ref.shape[0]
    b_low = b_ref[...].astype(BF16)
    c_low = c_ref[...].astype(BF16)
    rel_start = start_ref[...]
    allowed, products = masked_products(b_low, c_low, rel_start)
    state_low = state_ref[0].astype(BF16)
    later_low = later_ref[0].astype(BF16)
    spread = mat_right_t(b_low, later_low)
    first_half = head_lanes(rows)
    steps = group_heads(step_ref)
    decay = group_heads(decay_ref)
    decay_t = group_rows(decay_t_ref)
    reach = jnp.where(rel_start < 0, jnp.exp(decay), 0.0)
    to_end = group_heads(end_ref) * steps
    product_grad = jnp.zeros((rows, rows), F32)
    skip_parts = []
    for head in range(0, HGROUP, 2):
        lanes = slice(head * MDIM, head * MDIM + PAIR)
        x_pair = x_ref[:, lanes]
        dy_pair = dy_ref[:, lanes]
        step_pair = pair_columns(first_half, steps, head)
        scaled = (x_pair * step_pair).astype(BF16)
        dy_low = dy_pair.astype(BF16)
        parts = []
        for one in (head, head + 1):
            gaps = decay[:, one : one + 1] - decay_t[one : one + 1, :]
            decays = jnp.exp(jnp.minimum(gaps, 0.0))
            mine = first_half if one == head else ~first_half
            dy_mine = jnp.where(mine, dy_pair, 0.0).astype(BF16)
            weight_grad = mat_right_t(dy_mine, scaled)
            product_grad = product_grad + weight_grad * decays
            parts.append(mat_left_t((decays * products).astype(BF16), dy_low))
        dz_pair = jnp.where(first_half, parts[0], parts[1])
        skip_pair = skip_ref[:, lanes]
        end_pair = pair_columns(first_half, to_end, head)
        spread_pair = spread[:, lanes]
        dx_ref[:, lanes] = skip_pair * dy_pair + step_pair * dz_pair + end_pair * spread_pair
        one_sum[:, lanes] = dy_pair * (y_ref[:, lanes] - skip_pair * x_pair)
        two_sum[:, lanes] = x_pair * dz_pair
        three_sum[:, lanes] = x_pair * spread_pair
        mixed_y[:, lanes] = (dy_pair * pair_columns(first_half, reach, head)).astype(BF16)
        mixed_x[:, lanes] = (x_pair * end_pair).astype(BF16)
        skip_parts.append(jnp.sum(dy_pair * x_pair, axis=0, keepdims=True))
    grad_low = jnp.where(allowed, product_grad, 0.0).astype(BF16)
    dc = mat(grad_low, b_low) + mat(mixed_y[...], state_low)
    db = mat_left_t(grad_low, c_low) + mat(mixed_x[...], later_low)
    group = pl.program_id(1)

    @pl.when(group == 0)
    def _():
        dc_ref[...] = jnp.zeros(dc_ref.shape, F32)
        db_ref[...] = jnp.zeros(db_ref.shape, F32)
        head_sums[...] = jnp.zeros(head_sums.shape, F32)
        row_sums[...] = jnp.zeros(row_sums.shape, F32)

    dc_ref[...] += dc
    db_ref[...] += db
    owner = lax.broadcasted_iota(jnp.int32, (GWIDTH, 128), 0) // MDIM + group * HGROUP
    picks = (owner == lax.broadcasted_iota(jnp.int32, (GWIDTH, 128), 1)).astype(BF16)
    for place, source in enumerate((one_sum, two_sum, three_sum)):
        head_sums[place] += sums_by(source[...], picks)
    skips = jnp.broadcast_to(jnp.concatenate(skip_parts, axis=1), (8, GWIDTH))
    row_sums[0] += sums_by(skips, picks)
    meets = exact(
        jnp.ones((8, STATE), F32), later_ref[0].astype(F32) * state_ref[0].astype(F32), 1, 1
    )
    row_sums[1] += sums_by(meets, picks)

    @pl.when(group == pl.num_programs(1) - 1)
    def _():
        all_steps = step_ref[...]
        all_end = end_ref[...]
        rate = rate_ref[...]
        row_dot, u_dot, v_dot = head_sums[0], head_sums[1], head_sums[2]
        to_last = v_dot * all_end * all_steps
        grad_decay = row_dot - u_dot * all_steps - to_last
        at_end = jnp.sum(to_last, axis=0, keepdims=True) + row_sums[1, :1] * total_ref[0, :1]
        grad_drop = exact(lower_ones(rows), grad_decay, 0, 0) + at_end
        grad_steps = u_dot + v_dot * all_end - rate * grad_drop
        grad_dt = grad_steps * sigmoid(dt_ref[:, :128] + bias_ref[...])
        dt_grad_ref[:, :128] = grad_dt.astype(BF16)
        dt_grad_ref[:, 128:] = jnp.zeros((rows, dt_grad_ref.shape[1] - 128), BF16)
        small_ref[0, 0:1] = jnp.sum(grad_dt, axis=0, keepdims=True)
        small_ref[0, 1:2] = jnp.sum(-all_steps * grad_drop, axis=0, keepdims=True)
        small_ref[0, 2:8] = row_sums[0, :6]


def ssd_specs(rows):
    wide = pl.BlockSpec((rows, GWIDTH), lambda b, g: (b, g))
    b_spec = pl.BlockSpec((rows, STATE), lambda b, g: (b, DSSM // STATE))
    c_spec = pl.BlockSpec((rows, STATE), lambda b, g: (b, DSSM // STATE + 1))
    heads = pl.BlockSpec((rows, 128), lambda b, g: (b, 0))
    heads_t = pl.BlockSpec((1, 128, rows), lambda b, g: (b, 0, 0))
    column = pl.BlockSpec((rows, 1), lambda b, g: (b, 0))
    state = pl.BlockSpec((1, GWIDTH, STATE), lambda b, g: (b, g, 0))
    skip = pl.BlockSpec((1, GWIDTH), lambda b, g: (0, g))
    return [wide, b_spec, c_spec, heads, heads, heads_t, column, state, skip]


def ssd_forward(count, act, steps, decay, decay_t, rel_start, state_in, skip_row):
    rows = act.shape[0] // count
    specs = ssd_specs(rows)
    return pl.pallas_call(
        ssd_forward_kernel,
        grid=(count, NGROUP),
        in_specs=specs,
        out_specs=specs[0],
        out_shape=jax.ShapeDtypeStruct((count * rows, DSSM), F32),
        compiler_params=pltpu.CompilerParams(vmem_limit_bytes=KERNEL_VMEM),
        cost_estimate=pl.CostEstimate(
            flops=count * MHEADS * rows * rows * 400, bytes_accessed=8 * MIB, transcendentals=0
        ),
        name="ssd_forward",
    )(act, act, act, steps, decay, decay_t, rel_start, state_in, skip_row)


def ssd_backward(
    count,
    act,
    steps,
    decay,
    decay_t,
    rel_start,
    state_in,
    skip_row,
    scanned,
    grad_scanned,
    later,
    to_end,
    total,
    dt_rows,
    bias,
    rate,
):
    rows = act.shape[0] // count
    specs = ssd_specs(rows)
    wide, heads, state = specs[0], specs[3], specs[7]
    row = pl.BlockSpec((1, 128), lambda b, g: (0, 0))
    packed = pl.BlockSpec((1, 8, 128), lambda b, g: (b, 0, 0))
    narrow = pl.BlockSpec((rows, STATE), lambda b, g: (b, 0))
    dt_spec = pl.BlockSpec((rows, dt_rows.shape[1]), lambda b, g: (b, 0))
    tokens = count * rows
    return pl.pallas_call(
        ssd_backward_kernel,
        grid=(count, NGROUP),
        in_specs=specs + [wide, wide, state, heads, packed, dt_spec, row, row],
        out_specs=[wide, narrow, narrow, dt_spec, packed],
        out_shape=[
            jax.ShapeDtypeStruct((tokens, DSSM), F32),
            jax.ShapeDtypeStruct((tokens, STATE), F32),
            jax.ShapeDtypeStruct((tokens, STATE), F32),
            jax.ShapeDtypeStruct(dt_rows.shape, BF16),
            jax.ShapeDtypeStruct((count, 8, 128), F32),
        ],
        scratch_shapes=[pltpu.VMEM((rows, GWIDTH), F32)] * 3
        + [pltpu.VMEM((rows, GWIDTH), BF16)] * 2
        + [pltpu.VMEM((3, rows, 128), F32), pltpu.VMEM((2, 8, 128), F32)],
        compiler_params=pltpu.CompilerParams(vmem_limit_bytes=KERNEL_VMEM),
        cost_estimate=pl.CostEstimate(
            flops=count * MHEADS * rows * rows * 1000, bytes_accessed=16 * MIB, transcendentals=0
        ),
        name="ssd_backward",
    )(
        act,
        act,
        act,
        steps,
        decay,
        decay_t,
        rel_start,
        state_in,
        skip_row,
        scanned,
        grad_scanned,
        later,
        to_end,
        total,
        dt_rows,
        bias,
        rate,
    )


def spread_heads(source_ref, target, factor):
    width = source_ref.shape[1]
    target[...] = jnp.zeros(target.shape, target.dtype)
    for head in range(QHEADS):
        group = head // (QHEADS // KVHEADS)
        value = source_ref[head * HDIM : (head + 1) * HDIM, :]
        target[group * HDIM : (group + 1) * HDIM, head * width : (head + 1) * width] = (
            value * factor if factor != 1.0 else value
        )


def attend_allowed(block, first_pos, starts, width):
    key_pos = block * width + lax.broadcasted_iota(jnp.int32, (width, width), 0)
    query_pos = first_pos + lax.broadcasted_iota(jnp.int32, (width, width), 1)
    return (key_pos <= query_pos) & (key_pos >= starts)


NEAR = (0, 2, 1, 3)
TILE_ROWS = 256
TILE_COLS = 512


def near_at(step, size):
    return pl.ds(pl.multiple_of((lax.axis_index("wsh") ^ step) * size, 128), size)


def project_kernel(x_ref, *refs):
    *weights, out_ref = refs
    size = weights[0].shape[0]
    total = None
    for step, weight in zip(NEAR, weights):
        part = mat(x_ref[:, near_at(step, size)], weight[...])
        total = part if total is None else total + part
    out_ref[...] = total.astype(out_ref.dtype)


def project(x, weights, tile, kind=F32):
    tokens, depth = x.shape
    size, columns = weights[0].shape
    return pl.pallas_call(
        project_kernel,
        grid=(columns // tile,),
        in_specs=[pl.BlockSpec((tokens, depth), lambda i: (0, 0))]
        + [pl.BlockSpec((size, tile), lambda i: (0, i))] * 4,
        out_specs=pl.BlockSpec((tokens, tile), lambda i: (0, i)),
        out_shape=jax.ShapeDtypeStruct((tokens, columns), kind),
        compiler_params=pltpu.CompilerParams(vmem_limit_bytes=KERNEL_VMEM),
        cost_estimate=pl.CostEstimate(
            flops=2 * tokens * depth * columns,
            bytes_accessed=2 * depth * columns + 4 * tokens * columns,
            transcendentals=0,
        ),
        name="project",
    )(x, *weights)


def near_specs(own, tile, offset):
    size = own.shape[0]
    return [pl.BlockSpec((size, tile), lambda i: (0, i + offset))] + [
        pl.BlockSpec((None, size, tile), lambda i, place=place: (place, 0, i + offset))
        for place in range(3)
    ]


def unproject_kernel(base_ref, grad_ref, *refs):
    *weights, out_ref = refs
    size = weights[0].shape[0]

    @pl.when(pl.program_id(0) == 0)
    def _():
        out_ref[...] = base_ref[...]

    for step, weight in zip(NEAR, weights):
        out_ref[:, near_at(step, size)] += mat_right_t(grad_ref[...], weight[...])


def unproject(base, grad, weights, tile, specs=None):
    tokens, columns = grad.shape
    size = weights[0].shape[0]
    whole = pl.BlockSpec((tokens, 4 * size), lambda i: (0, 0))
    return pl.pallas_call(
        unproject_kernel,
        grid=(columns // tile,),
        in_specs=[whole, pl.BlockSpec((tokens, tile), lambda i: (0, i))]
        + (specs or [pl.BlockSpec((size, tile), lambda i: (0, i))] * 4),
        out_specs=whole,
        out_shape=jax.ShapeDtypeStruct((tokens, 4 * size), F32),
        compiler_params=pltpu.CompilerParams(vmem_limit_bytes=KERNEL_VMEM),
        cost_estimate=pl.CostEstimate(
            flops=8 * tokens * size * columns,
            bytes_accessed=8 * size * columns + 2 * tokens * columns,
            transcendentals=0,
        ),
        name="unproject",
    )(base, grad, *weights)


def out_proj_kernel(
    x_ref, mixed_ref, heads_ref, gain_ref, own_ref, others_ref, middle_ref, normed_ref
):
    weights = [own_ref] + [others_ref.at[place] for place in range(3)]
    wide = mixed_ref.shape[1] // 4
    narrow = heads_ref.shape[0] // 4
    middle_ref[...] = x_ref[...].astype(F32)
    for step, weight in zip(NEAR, weights):
        middle_ref[...] += mat(mixed_ref[:, near_at(step, wide)], weight[:wide]) + mat_left_t(
            heads_ref[near_at(step, narrow), :], weight[wide:]
        )
    middle = middle_ref[...]
    normed_ref[...] = (middle * inv_rms(middle) * gain_ref[...]).astype(BF16)


def out_project(x, mixed, heads_t, gain, weights):
    vmem = pl.BlockSpec(memory_space=pltpu.VMEM)
    return pl.pallas_call(
        out_proj_kernel,
        in_specs=[vmem] * 6,
        out_specs=[vmem, vmem],
        out_shape=[jax.ShapeDtypeStruct(x.shape, F32), jax.ShapeDtypeStruct(x.shape, BF16)],
        compiler_params=pltpu.CompilerParams(vmem_limit_bytes=KERNEL_VMEM),
        cost_estimate=pl.CostEstimate(
            flops=2 * x.size * 2048, bytes_accessed=12 * MIB, transcendentals=0
        ),
        name="out_project",
    )(x, mixed, heads_t, gain[None], *weights)


def out_back_kernel(branch_ref, own_ref, others_ref, mixed_ref, heads_ref):
    weights = [own_ref] + [others_ref.at[place] for place in range(3)]
    wide = mixed_ref.shape[1] // 4
    narrow = heads_ref.shape[0] // 4
    for step, weight in zip(NEAR, weights):
        mixed_ref[:, near_at(step, wide)] = mat_right_t(branch_ref[...], weight[:wide])
        heads_ref[near_at(step, narrow), :] = mat_right_t(weight[wide:], branch_ref[...]).astype(
            BF16
        )


def out_unproject(branch, weights, mixed_width, heads_width):
    vmem = pl.BlockSpec(memory_space=pltpu.VMEM)
    tokens = branch.shape[0]
    return pl.pallas_call(
        out_back_kernel,
        in_specs=[vmem] * 3,
        out_specs=[vmem, vmem],
        out_shape=[
            jax.ShapeDtypeStruct((tokens, mixed_width), F32),
            jax.ShapeDtypeStruct((heads_width, tokens), BF16),
        ],
        compiler_params=pltpu.CompilerParams(vmem_limit_bytes=KERNEL_VMEM),
        cost_estimate=pl.CostEstimate(
            flops=2 * branch.size * 2048, bytes_accessed=12 * MIB, transcendentals=0
        ),
        name="out_unproject",
    )(branch, *weights)


FF_TILE = 512


def mlp_kernel(
    place_ref, normed_ref, top_ref, middle_ref, gain_ref, *refs
):
    gates, ups, downs = refs[0:4], refs[4:8], refs[8:12]
    layer_ref, grad_ref, branch_ref, gain_grad_ref, hidden_ref, pair_ref = refs[12:18]
    down_tile, out_sum, back_sum = refs[18:]
    step_at = pl.program_id(0)
    per_piece = pl.num_programs(0) // 4
    size = gates[0].shape[0]
    for piece in range(4):

        @pl.when(step_at // per_piece == piece)
        def _():
            down_tile[...] = downs[piece][...]

    gate = up = None
    for step, gate_ref, up_ref in zip(NEAR, gates, ups):
        rows = normed_ref[:, near_at(step, size)]
        gate_part, up_part = mat(rows, gate_ref[...]), mat(rows, up_ref[...])
        gate = gate_part if gate is None else gate + gate_part
        up = up_part if up is None else up + up_part
    sig = 1.0 / (1.0 + jnp.exp(-gate))
    silu = gate * sig
    hidden = (silu * up).astype(BF16)
    hidden_ref[...] = hidden
    grad_hidden = mat_right_t(top_ref[...], down_tile[...])
    grad_gate = (grad_hidden * up * (sig + silu * (1.0 - sig))).astype(BF16)
    grad_up = (grad_hidden * silu).astype(BF16)
    pair_ref[0] = grad_gate
    pair_ref[1] = grad_up

    @pl.when(step_at == 0)
    def _():
        out_sum[...] = jnp.zeros(out_sum.shape, F32)
        back_sum[...] = jnp.zeros(back_sum.shape, F32)

    out_sum[...] += mat(hidden, down_tile[...])
    for step, gate_ref, up_ref in zip(NEAR, gates, ups):
        back_sum[:, near_at(step, size)] += mat_right_t(grad_gate, gate_ref[...]) + mat_right_t(
            grad_up, up_ref[...]
        )

    @pl.when(step_at == pl.num_programs(0) - 1)
    def _():
        middle = middle_ref[...]
        layer_ref[...] = (middle + out_sum[...]).astype(BF16)
        grad_rows, grad_gain = rms_pull(middle, inv_rms(middle), gain_ref[...], back_sum[...])
        grad = top_ref[...].astype(F32) + grad_rows
        grad_ref[...] = grad
        branch_ref[...] = grad.astype(BF16)
        gain_grad_ref[...] = grad_gain[None]


def mlp_both(place, normed, top, middle, gain, gu_weights, down_weights):
    tokens, features = middle.shape
    size, columns = gu_weights[0].shape
    width = columns // 2
    steps = width // FF_TILE
    per_piece = steps // 4

    def natural(i, p):
        piece = i // per_piece
        near = (piece % 2) * 2 + piece // 2
        return (near ^ p[0]) * per_piece + i % per_piece

    whole = pl.BlockSpec((tokens, features), lambda i, p: (0, 0))
    gain_spec = pl.BlockSpec((1, features), lambda i, p: (0, 0))

    def down_spec(piece):
        return pl.BlockSpec(
            (FF_TILE, features),
            lambda i, p: (jnp.clip(i - piece * per_piece, 0, per_piece - 1), 0),
        )

    return pl.pallas_call(
        mlp_kernel,
        grid_spec=pltpu.PrefetchScalarGridSpec(
            num_scalar_prefetch=1,
            grid=(steps,),
            in_specs=[whole, whole, whole, gain_spec]
            + [pl.BlockSpec((size, FF_TILE), lambda i, p: (0, natural(i, p)))] * 4
            + [pl.BlockSpec((size, FF_TILE), lambda i, p: (0, natural(i, p) + steps))] * 4
            + [down_spec(piece) for piece in range(4)],
            out_specs=[
                whole,
                whole,
                whole,
                gain_spec,
                pl.BlockSpec((tokens, FF_TILE), lambda i, p: (0, natural(i, p))),
                pl.BlockSpec((2, tokens, FF_TILE), lambda i, p: (0, 0, natural(i, p))),
            ],
            scratch_shapes=[
                pltpu.VMEM((FF_TILE, features), BF16),
                pltpu.VMEM((tokens, features), F32),
                pltpu.VMEM((tokens, features), F32),
            ],
        ),
        out_shape=[
            jax.ShapeDtypeStruct((tokens, features), BF16),
            jax.ShapeDtypeStruct((tokens, features), F32),
            jax.ShapeDtypeStruct((tokens, features), BF16),
            jax.ShapeDtypeStruct((1, features), F32),
            jax.ShapeDtypeStruct((tokens, width), BF16),
            jax.ShapeDtypeStruct((2, tokens, width), BF16),
        ],
        compiler_params=pltpu.CompilerParams(vmem_limit_bytes=KERNEL_VMEM),
        cost_estimate=pl.CostEstimate(
            flops=12 * tokens * features * width, bytes_accessed=30 * MIB, transcendentals=0
        ),
        name="mlp_both",
    )(
        place,
        normed,
        top,
        middle,
        gain[None],
        *gu_weights,
        *gu_weights,
        *down_weights,
    )


EDGE = 8
EARLY_TILE = 256


def conv_inputs(edge_rows, own_rows):
    return jnp.concatenate([edge_rows, own_rows], axis=0)


def conv_valid(rel_start, tap, taps):
    rows = rel_start.shape[0]
    place = lax.broadcasted_iota(jnp.int32, (rows, 1), 0)
    return place - (taps - 1) + tap >= rel_start


def conv_sums(extended, weights, bias, rel_start):
    taps = weights.shape[0]
    rows = rel_start.shape[0]
    shifted = []
    total = None
    for tap in range(taps):
        begin = EDGE - (taps - 1) + tap
        part = jnp.where(
            conv_valid(rel_start, tap, taps), extended[begin : begin + rows], 0.0
        )
        shifted.append(part)
        term = weights[tap : tap + 1] * part
        total = bias + term if total is None else total + term
    return total, shifted


def conv_tile_spec(rows, first, last, begin=0):
    return pl.BlockSpec(
        (rows, EARLY_TILE), lambda i: (0, jnp.clip(i - begin + first, first, last))
    )


def conv_back(extended, weights, bias, rel_start, grad_act):
    total, shifted = conv_sums(extended, weights, bias, rel_start)
    gate = sigmoid(total)
    return grad_act * gate * (1.0 + total * (1.0 - gate)), shifted


def edge_grad_kernel(
    dx_ref, db_ref, dc_ref, conv_ref, edge_ref, start_ref, weight_ref, bias_ref, out_ref
):
    taps = weight_ref.shape[0]
    grad_act = jnp.concatenate([dx_ref[...], db_ref[...], dc_ref[...]], axis=1)
    extended = conv_inputs(edge_ref[...], conv_ref[...])
    grad, _ = conv_back(extended, weight_ref[...], bias_ref[...], start_ref[...], grad_act)
    total = jnp.zeros(grad.shape, F32)
    for tap in range(taps):
        part = jnp.where(
            conv_valid(start_ref[...], tap, taps), grad * weight_ref[tap : tap + 1], 0.0
        )
        padded = jnp.concatenate([jnp.zeros(part.shape, F32), part], axis=0)
        total = total + padded[taps - 1 - tap : taps - 1 - tap + EDGE]
    out_ref[...] = total


def edge_grads(count, dx, db, dc, conv_rows, edge_rows, rel_start, conv_weight, conv_bias):
    rows = dx.shape[0] // count
    steps = rows // EDGE

    def first(array):
        return pl.BlockSpec((EDGE, array.shape[1]), lambda b: (b * steps, 0))

    channels = conv_weight.shape[1]
    return pl.pallas_call(
        edge_grad_kernel,
        grid=(count,),
        in_specs=[
            first(dx),
            first(db),
            first(dc),
            first(conv_rows),
            pl.BlockSpec((EDGE, channels), lambda b: (b, 0)),
            first(rel_start),
            pl.BlockSpec(conv_weight.shape, lambda b: (0, 0)),
            pl.BlockSpec((1, channels), lambda b: (0, 0)),
        ],
        out_specs=pl.BlockSpec((EDGE, channels), lambda b: (b, 0)),
        out_shape=jax.ShapeDtypeStruct((count * EDGE, channels), F32),
        compiler_params=pltpu.CompilerParams(vmem_limit_bytes=KERNEL_VMEM),
        cost_estimate=pl.CostEstimate(flops=MIB, bytes_accessed=MIB, transcendentals=0),
        name="edge_grads",
    )(dx, db, dc, conv_rows, edge_rows, rel_start, conv_weight, conv_bias[None])


def early_back_kernel(
    count,
    base_ref,
    kv_ref,
    dx_ref,
    db_ref,
    dc_ref,
    conv_ref,
    edge_ref,
    came_ref,
    dt_ref,
    start_ref,
    weight_ref,
    bias_ref,
    x_ref,
    gain_ref,
    middle_ref,
    *refs,
):
    *blocks, grad_ref, conv_grad_ref, input_ref, gain_grad_ref, total = refs
    size = blocks[0].shape[0]
    tile = pl.program_id(0)
    last = pl.num_programs(0) - 1
    taps = weight_ref.shape[0]

    @pl.when(tile == 0)
    def _():
        total[...] = base_ref[...]
        grad_ref[...] = kv_ref[...]

    @pl.when(tile == last)
    def _():
        grad_ref[...] = dt_ref[...]

    @pl.when((tile > 0) & (tile < last))
    def _():
        rows = dx_ref.shape[0] // count
        tail = jnp.concatenate([db_ref[...], dc_ref[...]], axis=1)
        grad_act = jnp.where(tile == last - 1, tail, dx_ref[...])
        sums = [None] * (taps + 1)
        for b in range(count):
            span = slice(b * rows, (b + 1) * rows)
            ends = slice(b * EDGE, (b + 1) * EDGE)
            extended = conv_inputs(edge_ref[ends], conv_ref[span])
            rel_start = start_ref[span]
            grad, shifted = conv_back(
                extended, weight_ref[...], bias_ref[...], rel_start, grad_act[span]
            )
            back = jnp.concatenate(
                [jnp.zeros((rows - EDGE, grad.shape[1]), F32), came_ref[ends]], axis=0
            )
            for tap in range(taps):
                part = jnp.where(
                    conv_valid(rel_start, tap, taps), grad * weight_ref[tap : tap + 1], 0.0
                )
                padded = jnp.concatenate([part, jnp.zeros((EDGE, part.shape[1]), F32)], axis=0)
                back = back + padded[taps - 1 - tap : taps - 1 - tap + rows]
                term = jnp.sum(grad * shifted[tap], axis=0, keepdims=True)
                sums[tap] = term if sums[tap] is None else sums[tap] + term
            term = jnp.sum(grad, axis=0, keepdims=True)
            sums[taps] = term if sums[taps] is None else sums[taps] + term
            grad_ref[span] = back.astype(BF16)
        conv_grad_ref[0 : taps + 1] = jnp.concatenate(sums, axis=0)
        conv_grad_ref[taps + 1 :] = jnp.zeros(
            (conv_grad_ref.shape[0] - taps - 1, grad_act.shape[1]), F32
        )

    for step, block in zip(NEAR, blocks):
        total[:, near_at(step, size)] += mat_right_t(grad_ref[...], block[...])

    @pl.when(tile == last)
    def _():
        x = x_ref[...].astype(F32)
        grad_rows, grad_gain = rms_pull(x, inv_rms(x), gain_ref[...], total[...])
        input_ref[...] = (middle_ref[...] + grad_rows).astype(BF16)
        gain_grad_ref[...] = grad_gain[None]


def early_back(
    count,
    base,
    grad_kv,
    dx,
    db,
    dc,
    conv_rows,
    edge_rows,
    came,
    dt_grad,
    rel_start,
    conv_weight,
    conv_bias,
    x,
    gain,
    grad_middle,
    own,
    others,
):
    tokens, depth = base.shape
    channels = conv_weight.shape[1]
    tiles = conv_weight.shape[1] // EARLY_TILE + 2
    conv_tiles = channels // EARLY_TILE

    def whole(array):
        return pl.BlockSpec(array.shape, lambda i: (0, 0))

    return pl.pallas_call(
        functools.partial(early_back_kernel, count),
        grid=(tiles,),
        in_specs=[
            whole(base),
            whole(grad_kv),
            conv_tile_spec(tokens, 0, conv_tiles - 2, 1),
            whole(db),
            whole(dc),
            conv_tile_spec(tokens, 0, conv_tiles - 1, 1),
            conv_tile_spec(edge_rows.shape[0], 0, conv_tiles - 1, 1),
            conv_tile_spec(edge_rows.shape[0], 0, conv_tiles - 1, 1),
            whole(dt_grad),
            whole(rel_start),
            conv_tile_spec(conv_weight.shape[0], 0, conv_tiles - 1, 1),
            conv_tile_spec(1, 0, conv_tiles - 1, 1),
            whole(x),
            pl.BlockSpec((1, depth), lambda i: (0, 0)),
            whole(grad_middle),
        ]
        + near_specs(own, EARLY_TILE, DSSM // EARLY_TILE),
        out_specs=[
            pl.BlockSpec((tokens, EARLY_TILE), lambda i: (0, i)),
            conv_tile_spec(8, 0, conv_tiles - 1, 1),
            whole(x),
            pl.BlockSpec((1, depth), lambda i: (0, 0)),
        ],
        out_shape=[
            jax.ShapeDtypeStruct((tokens, tiles * EARLY_TILE), BF16),
            jax.ShapeDtypeStruct((8, channels), F32),
            jax.ShapeDtypeStruct(x.shape, BF16),
            jax.ShapeDtypeStruct((1, depth), F32),
        ],
        scratch_shapes=[pltpu.VMEM((tokens, depth), F32)],
        compiler_params=pltpu.CompilerParams(vmem_limit_bytes=KERNEL_VMEM),
        cost_estimate=pl.CostEstimate(
            flops=2 * tokens * depth * tiles * EARLY_TILE, bytes_accessed=20 * MIB, transcendentals=0
        ),
        name="early_back",
    )(
        base,
        grad_kv,
        dx,
        db,
        dc,
        conv_rows,
        edge_rows,
        came,
        dt_grad,
        rel_start,
        conv_weight,
        conv_bias[None],
        x,
        gain[None],
        grad_middle,
        own,
        others,
        others,
        others,
    )


def block_grads_kernel(steps, left_ref, right_ref, *refs):
    came = refs[0] if len(refs) == 3 else None
    outs = refs[-2:] if came is not None else refs
    size = left_ref.shape[1] // 4
    for place, step in enumerate(steps):
        value = mat_left_t(left_ref[:, near_at(step, size)], right_ref[0])
        if came is None:
            outs[0][place * size : (place + 1) * size] = value.astype(BF16)
        else:
            value = value + came[place * size : (place + 1) * size].astype(F32)
            outs[place][...] = value.astype(BF16)


def block_grads(left, right, steps, came=None):
    tokens, depth = left.shape
    size = depth // 4
    parts, _, width = right.shape
    per_part = width // TILE_COLS
    columns = parts * width
    tall = pl.BlockSpec((2 * size, TILE_COLS), lambda i: (0, i))
    flat = pl.BlockSpec((size, TILE_COLS), lambda i: (0, i))
    operands = [left, right] + ([] if came is None else [came])
    return pl.pallas_call(
        functools.partial(block_grads_kernel, steps),
        grid=(columns // TILE_COLS,),
        in_specs=[
            pl.BlockSpec((tokens, depth), lambda i: (0, 0)),
            pl.BlockSpec((1, tokens, TILE_COLS), lambda i: (i // per_part, 0, i % per_part)),
        ]
        + ([] if came is None else [tall]),
        out_specs=[tall] if came is None else [flat, flat],
        out_shape=[jax.ShapeDtypeStruct((2 * size, columns), BF16)]
        if came is None
        else [jax.ShapeDtypeStruct((size, columns), BF16)] * 2,
        compiler_params=pltpu.CompilerParams(vmem_limit_bytes=KERNEL_VMEM),
        cost_estimate=pl.CostEstimate(
            flops=4 * tokens * size * columns, bytes_accessed=6 * MIB, transcendentals=0
        ),
        name="block_grads",
    )(*operands)


def finish_kernel(
    early_ref, gate_ref, mix_ref, q_low_ref, in_ref, q_ref, kv_ref, out_ref, o_ref
):
    kv_width = kv_ref.shape[1]
    gate = gate_ref.shape[1]
    in_ref[:, :gate] = gate_ref[...].astype(F32)
    in_ref[:, gate:] = early_ref[:, kv_width:].astype(F32)
    q_ref[...] = q_low_ref[...].astype(F32)
    kv_ref[...] = early_ref[:, :kv_width].astype(F32)
    split = out_ref.shape[0]
    out_ref[...] = mix_ref[:split].astype(F32)
    o_ref[...] = mix_ref[split:].astype(F32)


def finish(early, gate, mix, q, shapes):
    vmem = pl.BlockSpec(memory_space=pltpu.VMEM)
    return pl.pallas_call(
        finish_kernel,
        in_specs=[vmem] * 4,
        out_specs=[vmem] * 5,
        out_shape=[jax.ShapeDtypeStruct(shape, F32) for shape in shapes],
        compiler_params=pltpu.CompilerParams(vmem_limit_bytes=KERNEL_VMEM),
        cost_estimate=pl.CostEstimate(flops=MIB, bytes_accessed=10 * MIB, transcendentals=0),
        name="finish",
    )(early, gate, mix, q)


def passed_along(block, axis, distance):
    devices = range(lax.axis_size(axis))
    route = [(i - distance, i) for i in devices if i - distance in devices]
    return lax.ppermute(block, axis, route)


def swapped(block, axis, bit):
    return lax.ppermute(block, axis, [(i, i ^ bit) for i in range(lax.axis_size(axis))])


def bits_of(axis):
    return [1 << k for k in range(lax.axis_size(axis).bit_length() - 1)]


def after(value, earlier):
    return lax.optimization_barrier((value, earlier))[0]


def gathered_near(shard, earlier=None, held=None):
    if earlier is not None:
        shard = after(shard, earlier)
    across = swapped(shard, "wsh", 2)
    if held is not None:
        across = after(across, held)
    return [shard, across, swapped(shard, "wsh", 1), swapped(across, "wsh", 1)]


class Scattering:
    def __init__(self, table, bits):
        self.table = table
        self.bits = list(bits)
        self.start()

    def start(self):
        if self.bits:
            half = self.table.shape[0] // 2
            self.came = swapped(self.table[half:], "ctx", self.bits.pop(0))
        else:
            self.came = None

    def advance(self, held=None):
        if self.came is not None:
            came = self.came if held is None else after(self.came, held)
            half = self.table.shape[0] // 2
            self.table = (self.table[:half].astype(F32) + came.astype(F32)).astype(BF16)
            self.start()
        return self.table

    def finish(self):
        while self.came is not None:
            self.advance()
        return self.table[0]


def ctx_bits(count):
    return [1 << k for k in range(count.bit_length() - 1)]


def partner_wsh(step):
    return (lax.axis_index("ctx"), lax.axis_index("wsh") ^ step)


def partner_ctx(step):
    return (lax.axis_index("ctx") ^ step, lax.axis_index("wsh"))


def remote(source, target, send, recv, device):
    return pltpu.make_async_remote_copy(
        src_ref=source,
        dst_ref=target,
        send_sem=send,
        recv_sem=recv,
        device_id=device,
        device_id_type=pl.DeviceIdType.MESH,
    )


def grads_kernel(
    count,
    split,
    early_units,
    gate_units,
    q_units,
    one_ref,
    mix_ref,
    heads_ref,
    early_ref,
    gate_ref,
    q_ref,
    branch_ref,
    small_ref,
    early_out,
    gate_out,
    q_out,
    mix_out,
    small_out,
    core_out,
    work,
    y_in,
    ctx_in,
    final,
    small_in,
    core_sems,
    y_sems,
    rs_sems,
    ag_sems,
    small_sems,
    out_sems,
):
    bits = ctx_bits(count)
    here = lax.axis_index("ctx")
    units = work.shape[0]
    rows = work.shape[2]
    width = work.shape[3]
    wsh_steps = (1, 2)
    barrier = pltpu.get_barrier_semaphore()
    partners = [partner_wsh(step) for step in wsh_steps] + [partner_ctx(bit) for bit in bits]
    for device in partners:
        pl.semaphore_signal(
            barrier, inc=1, device_id=device, device_id_type=pl.DeviceIdType.MESH
        )
    pl.semaphore_wait(barrier, len(partners))

    sizes = [rows >> (k + 1) for k in range(len(bits))]
    starts = []
    others = []
    base = 0
    for bit, size in zip(bits, sizes):
        upper = (here // bit) % 2
        others.append(base + (1 - upper) * size)
        base = base + upper * size
        starts.append(base)

    def span(start, size):
        return pl.ds(pl.multiple_of(start, 16), size)

    def core_copy(u):
        return remote(
            core_out.at[u % 2],
            work.at[u],
            core_sems.at[0, u],
            core_sems.at[1, u],
            partner_wsh(1),
        )

    def y_copy(u):
        return remote(work.at[u, 1], y_in.at[u], y_sems.at[0, u], y_sems.at[1, u], partner_wsh(2))

    recv_base = [rows - (rows >> k) for k in range(len(bits))]

    def rs_copy(u, k):
        return remote(
            work.at[u, 0, span(others[k], sizes[k])],
            ctx_in.at[u, pl.ds(recv_base[k], sizes[k])],
            rs_sems.at[0, k, u],
            rs_sems.at[1, k, u],
            partner_ctx(bits[k]),
        )

    def ag_copy(u, k):
        return remote(
            final.at[u, span(starts[k], sizes[k])],
            final.at[u, span(starts[k], sizes[k])],
            ag_sems.at[0, k, u],
            ag_sems.at[1, k, u],
            partner_ctx(bits[k]),
        )

    limits = []
    first_unit = 0
    for size in (early_units, gate_units, q_units, 4):
        limits.append((first_unit, first_unit + size))
        first_unit += size
    outs = (early_out, gate_out, q_out, mix_out)

    def by_part(u, action):
        for part, (low, high) in enumerate(limits):
            pl.when((u >= low) & (u < high))(functools.partial(action, part, u - low))

    def each_out(u, act):
        def one(part, v):
            tall = part == 3
            for i in range(split):
                row = (v // 2) * TILE_ROWS if tall else 0
                column = ((v % 2) if tall else v) * TILE_COLS + i * width
                copy = pltpu.make_async_copy(
                    final.at[u, pl.ds(i * TILE_ROWS, TILE_ROWS)],
                    outs[part].at[
                        pl.ds(pl.multiple_of(row, TILE_ROWS), TILE_ROWS),
                        pl.ds(pl.multiple_of(column, 128), width),
                    ],
                    out_sems.at[u, i],
                )
                act(copy)

        by_part(u, one)

    def columns_at(v):
        return pl.ds(pl.multiple_of(v * TILE_COLS, 128), TILE_COLS)

    wide = mix_ref.shape[1] // 4
    narrow = heads_ref.shape[0] // 4

    def pieces(u, first, put):
        steps = NEAR[2 * first : 2 * first + 2]

        def one(part, v):
            for place, step in enumerate(steps):
                if part < 3:
                    left = one_ref[:, near_at(step, TILE_ROWS)]
                    value = mat_left_t(left, (early_ref, gate_ref, q_ref)[part][:, columns_at(v)])
                else:
                    right = branch_ref[:, columns_at(v % 2)]
                    other = lax.axis_index("wsh") ^ step
                    begin = pl.multiple_of(other * wide, 128)

                    @pl.when(v < 2)
                    def _():
                        put(place, mat_left_t(mix_ref[:, pl.ds(begin, TILE_ROWS)], right))

                    @pl.when(v >= 2)
                    def _():
                        tail_at = pl.multiple_of(begin + TILE_ROWS, 128)
                        tail = mat_left_t(mix_ref[:, pl.ds(tail_at, wide - TILE_ROWS)], right)
                        heads_at = pl.multiple_of(other * narrow, 128)
                        heads = mat(heads_ref[pl.ds(heads_at, narrow), :], right)
                        put(place, jnp.concatenate([tail, heads], axis=0))

                    continue
                put(place, value)

        by_part(u, one)

    def chunked(value):
        return [
            (slice(i * TILE_ROWS, (i + 1) * TILE_ROWS), value[:, i * width : (i + 1) * width])
            for i in range(split)
        ]

    def begin(u):
        def put(place, value):
            for where, part in chunked(value):
                core_out[u % 2, place, where] = part.astype(BF16)

        pieces(u, 1, put)
        core_copy(u).start()

    def after_core(u):
        core_copy(u).wait()

        def put(place, value):
            for where, part in chunked(value):
                work[u, place, where] = (work[u, place, where].astype(F32) + part).astype(BF16)

        pieces(u, 0, put)
        y_copy(u).start()

    def after_y(u):
        y_copy(u).wait()
        work[u, 0] = (work[u, 0].astype(F32) + y_in[u].astype(F32)).astype(BF16)
        rs_copy(u, 0).start()

    def after_rs(u, k):
        rs_copy(u, k).wait()
        mine = span(starts[k], sizes[k])
        total = work[u, 0, mine].astype(F32) + ctx_in[
            u, pl.ds(recv_base[k], sizes[k])
        ].astype(F32)
        if k + 1 < len(bits):
            work[u, 0, mine] = total.astype(BF16)
            rs_copy(u, k + 1).start()
        else:
            final[u, mine] = total.astype(BF16)
            ag_copy(u, k).start()

    def after_ag(u, k):
        ag_copy(u, k).wait()
        if k > 0:
            ag_copy(u, k - 1).start()
        else:
            each_out(u, lambda copy: copy.start())

    stages = [(0, begin), (1, after_core), (3, after_y)]
    delay = 3
    for k in range(len(bits)):
        delay += 1
        stages.append((delay, functools.partial(after_rs, k=k)))
    for k in range(len(bits) - 1, -1, -1):
        delay += 1
        stages.append((delay, functools.partial(after_ag, k=k)))

    small_out[...] = small_ref[...]
    hops = partners

    def small_copy(k):
        return remote(
            small_in.at[k, 0], small_in.at[k, 1], small_sems.at[0, k], small_sems.at[1, k], hops[k]
        )

    def small_step(k):
        if k > 0:
            small_copy(k - 1).wait()
            small_out[...] += small_in[k - 1, 1]
        if k < len(hops):
            small_in[k, 0] = small_out[...]
            small_copy(k).start()

    def one_step(t, carry):
        for k in range(len(hops) + 1):
            pl.when(t == 2 * k + 1)(functools.partial(small_step, k))
        for offset, stage in stages[::-1]:
            u = t - offset
            pl.when((u >= 0) & (u < units))(functools.partial(stage, u))
        return carry

    lax.fori_loop(0, units + delay, one_step, 0)

    def finish(u, carry):
        each_out(u, lambda copy: copy.wait())
        return carry

    lax.fori_loop(0, units, finish, 0)


def reduce_grads(
    count, early_width, one, mixed, heads_t, early, gate, q, branch, small
):
    bits = ctx_bits(count)
    hops = len(bits) + 2
    split = max(1, 16 * count // TILE_ROWS)
    early_units = early_width // TILE_COLS
    gate_units = gate.shape[1] // TILE_COLS
    q_units = q.shape[1] // TILE_COLS
    units = early_units + gate_units + q_units + 4
    rows, width = TILE_ROWS * split, TILE_COLS // split
    dma = pltpu.SemaphoreType.DMA
    vmem = pl.BlockSpec(memory_space=pltpu.VMEM)
    hbm = pl.BlockSpec(memory_space=pl.ANY)
    return pl.pallas_call(
        functools.partial(grads_kernel, count, split, early_units, gate_units, q_units),
        in_specs=[vmem] * 8,
        out_specs=[hbm] * 4 + [vmem],
        out_shape=[
            jax.ShapeDtypeStruct((TILE_ROWS, early_units * TILE_COLS), BF16),
            jax.ShapeDtypeStruct((TILE_ROWS, gate_units * TILE_COLS), BF16),
            jax.ShapeDtypeStruct((TILE_ROWS, q_units * TILE_COLS), BF16),
            jax.ShapeDtypeStruct((2 * TILE_ROWS, 2 * TILE_COLS), BF16),
            jax.ShapeDtypeStruct(small.shape, F32),
        ],
        scratch_shapes=[
            pltpu.VMEM((2, 2, rows, width), BF16),
            pltpu.VMEM((units, 2, rows, width), BF16),
            pltpu.VMEM((units, rows, width), BF16),
            pltpu.VMEM((units, rows, width), BF16),
            pltpu.VMEM((units, rows, width), BF16),
            pltpu.VMEM((hops, 2) + small.shape, F32),
            dma((2, units)),
            dma((2, units)),
            dma((2, len(bits), units)),
            dma((2, len(bits), units)),
            dma((2, hops)),
            dma((units, split)),
        ],
        compiler_params=pltpu.CompilerParams(
            collective_id=1, has_side_effects=True, vmem_limit_bytes=KERNEL_VMEM
        ),
        cost_estimate=pl.CostEstimate(
            flops=6_500_000_000, bytes_accessed=30 * MIB, transcendentals=0
        ),
        name="reduce_grads",
    )(one, mixed, heads_t, early, gate, q, branch, small)


def exchange_barrier(devices):
    barrier = pltpu.get_barrier_semaphore()
    for device in devices:
        pl.semaphore_signal(
            barrier, inc=1, device_id=device, device_id_type=pl.DeviceIdType.MESH
        )
    pl.semaphore_wait(barrier, len(devices))


def row_factors(totals, owner):
    rows = owner.shape[0]
    picks = (owner == lax.broadcasted_iota(jnp.int32, (rows, 128), 1)).astype(BF16)
    high = totals.astype(BF16)
    low = (totals - high.astype(F32)).astype(BF16)
    return mat_right_t(picks, high) + mat_right_t(picks, low)


STATE_GROUP = 4


class StateExchange:
    def __init__(self, count, forward, state_ref, totals, result, scratch):
        self.group = min(STATE_GROUP, count)
        self.groups = count // self.group
        self.forward = forward
        self.state_ref, self.totals, self.result = state_ref, totals, result
        (
            self.sent,
            self.came,
            self.before,
            self.back,
            self.whole,
            self.cross,
            self.sems,
            self.cross_sems,
        ) = scratch
        self.place = lax.axis_index("ctx") % self.group
        self.at = lax.axis_index("ctx") // self.group
        self.share = state_ref.shape[1] // self.group

    @staticmethod
    def scratch(count, state):
        group = min(STATE_GROUP, count)
        groups = count // group
        part = (state.shape[0], state.shape[1] // group, STATE)
        return [
            pltpu.VMEM(state.shape, BF16),
            pltpu.VMEM((group,) + part, BF16),
            pltpu.VMEM((group,) + part, F32),
            pltpu.VMEM((group,) + part, BF16),
            pltpu.VMEM(part, BF16),
            pltpu.VMEM((groups,) + part, BF16),
            pltpu.SemaphoreType.DMA((4, group)),
            pltpu.SemaphoreType.DMA((2, groups)),
        ]

    def rows_of(self, place):
        return pl.ds(pl.multiple_of(place * self.share, 16), self.share)

    def deal(self, k, slot):
        return remote(
            self.sent.at[:, self.rows_of(self.place ^ k)],
            self.came.at[slot],
            self.sems.at[0, k],
            self.sems.at[1, k],
            partner_ctx(k),
        )

    def give(self, m, slot):
        return remote(
            self.whole,
            self.cross.at[slot],
            self.cross_sems.at[0, m],
            self.cross_sems.at[1, m],
            partner_ctx(m * self.group),
        )

    def give_back(self, k, slot):
        return remote(
            self.back.at[self.place ^ k],
            self.result.at[:, self.rows_of(slot)],
            self.sems.at[2, k],
            self.sems.at[3, k],
            partner_ctx(k),
        )

    def order(self, count):
        return range(count) if self.forward else range(count - 1, -1, -1)

    def factors(self, blocks):
        part = self.totals[blocks]
        batch = part.shape[1]
        place = lax.broadcasted_iota(jnp.int32, (self.share, 128), 0) + self.place * self.share
        columns = row_factors(part.reshape(-1, 128), place // MDIM)

        def column(block, b):
            at = (block * batch + b) * 8
            return columns[:, at : at + 1]

        return column

    def own_blocks(self):
        return pl.ds(self.at * self.group, self.group)

    def begin(self):
        self.sent[...] = self.state_ref[...].astype(BF16)
        for k in range(1, self.group):
            self.deal(k, self.place).start()
        self.came[self.place] = self.state_ref[:, self.rows_of(self.place), :].astype(BF16)
        self.cross[self.at] = jnp.zeros(self.whole.shape, BF16)

    def middle(self):
        for k in range(1, self.group):
            self.deal(k, self.place).wait_send()
            self.deal(k, self.place ^ k).wait_recv()
        factor_of = self.factors(self.own_blocks())
        for b in range(self.whole.shape[0]):
            total = jnp.zeros((self.share, STATE), F32)
            for j in self.order(self.group):
                self.before[j, b] = total
                total = factor_of(j, b) * total + self.came[j, b].astype(F32)
            self.whole[b] = total.astype(BF16)
        for m in range(1, self.groups):
            self.give(m, self.at).start()

    def carry(self):
        for m in range(1, self.groups):
            self.give(m, self.at).wait_send()
            self.give(m, self.at ^ m).wait_recv()
        factor_of = self.factors(self.own_blocks())
        any_factor = self.factors(slice(None))
        for b in range(self.whole.shape[0]):
            reach = jnp.zeros((self.share, STATE), F32)
            for g in self.order(self.groups):
                decay = None
                for j in range(self.group):
                    one = any_factor(g * self.group + j, b)
                    decay = one if decay is None else decay * one
                earlier = (g < self.at) if self.forward else (g > self.at)
                reach = jnp.where(earlier, decay * reach + self.cross[g, b].astype(F32), reach)
            for j in self.order(self.group):
                self.back[j, b] = (self.before[j, b] + reach).astype(BF16)
                reach = reach * factor_of(j, b)
        for k in range(1, self.group):
            self.give_back(k, self.place).start()
        self.result[:, self.rows_of(self.place), :] = self.back[self.place]

    def end(self):
        for k in range(1, self.group):
            self.give_back(k, self.place).wait_send()
            self.give_back(k, self.place ^ k).wait_recv()


def mix_forward_kernel(
    count,
    start_ref,
    q_ref,
    near_ref,
    state_ref,
    total_ref,
    out_ref,
    log_ref,
    table_out,
    state_out,
    totals_out,
    q_wide,
    top,
    total,
    acc,
    far,
    totals,
    result,
    total_sems,
    table_sems,
    *state_scratch,
):
    here = lax.axis_index("ctx")
    batch = near_ref.shape[1]
    width = near_ref.shape[2]
    half = count // 2
    exchange_barrier([partner_ctx(k) for k in range(1, count)])
    totals[here] = total_ref[...]

    def total_copy(k, place):
        return remote(
            totals.at[here],
            totals.at[place],
            total_sems.at[0, k],
            total_sems.at[1, k],
            partner_ctx(k),
        )

    def table_copy(i):
        return remote(
            near_ref.at[i], far.at[i], table_sems.at[0, i], table_sems.at[1, i], partner_ctx(1)
        )

    for k in range(1, count):
        total_copy(k, here).start()
    states = StateExchange(count, True, state_ref, totals, result, state_scratch)
    states.begin()
    for i in range(half):
        table_copy(i).start()
    for b in range(batch):
        spread_heads(q_ref.at[:, b * width : (b + 1) * width], q_wide.at[b], HDIM**-0.5)
    top[...] = jnp.full(top.shape, MASKED_SCORE, F32)
    total[...] = jnp.zeros(total.shape, F32)
    acc[...] = jnp.zeros(acc.shape, F32)
    first_pos = here * width

    def attend(b, source, i, block):
        kv_rows = source[i, b]
        keys = kv_rows[:, : KVHEADS * HDIM]
        values_t = kv_rows[:, KVHEADS * HDIM :].T
        allowed = attend_allowed(block, first_pos, start_ref[b][:1], width)
        tops, totals_now = top[b], total[b]
        new_tops, new_totals = [], []
        for head in range(QHEADS):
            group = head // (QHEADS // KVHEADS)
            line = slice(head, head + 1)
            scores = mat(keys, q_wide[b, :, head * width : (head + 1) * width])
            scores = jnp.where(allowed, scores, MASKED_SCORE)
            old = tops[line]
            new = jnp.maximum(old, jnp.max(scores, axis=0, keepdims=True))
            terms = jnp.exp(scores - new)
            shrink = jnp.exp(old - new)
            new_tops.append(new)
            new_totals.append(
                totals_now[line] * shrink + jnp.sum(terms, axis=0, keepdims=True)
            )
            acc[b, head] = acc[b, head] * shrink + mat(
                values_t[group * HDIM : (group + 1) * HDIM, :], terms.astype(BF16)
            )
        top[b] = jnp.concatenate(new_tops, axis=0)
        total[b] = jnp.concatenate(new_totals, axis=0)

    bits = ctx_bits(count)
    high = len(bits) - 1

    def step_of(i):
        return sum(((i // (1 << p)) % 2) * (1 << (high - p)) for p in range(high))

    def pair(source, low, begin=0, end=half):
        def one(i, carry):
            if low:
                table_copy(i).wait()
            block = here ^ (step_of(i) + low)

            @pl.when(block <= here)
            def _():
                for b in range(batch):
                    attend(b, source, i, block)

            return carry

        lax.fori_loop(begin, end, one, 0)

    pair(near_ref, 0)
    for k in range(1, count):
        total_copy(k, here).wait_send()
        total_copy(k, here ^ k).wait_recv()
    states.middle()
    pair(far, 1, 0, half // 2)
    states.carry()
    pair(far, 1, half // 2)
    for b in range(batch):
        for head in range(QHEADS):
            out_ref[head * HDIM : (head + 1) * HDIM, b * width : (b + 1) * width] = (
                acc[b, head] / total[b, head : head + 1, :]
            ).astype(BF16)
        log_ref[b] = top[b] + jnp.log(total[b])
    table_out[:half] = near_ref[...]
    table_out[half:] = far[...]
    totals_out[...] = totals[...]
    states.end()
    state_out[...] = result[...]


def mix_forward(count, starts, queries_t, near, state, total):
    half, batch, width, kv_width = near.shape
    vmem = pl.BlockSpec(memory_space=pltpu.VMEM)
    dma = pltpu.SemaphoreType.DMA
    low = functools.partial(jax.ShapeDtypeStruct, dtype=BF16)
    wide = functools.partial(jax.ShapeDtypeStruct, dtype=F32)
    return pl.pallas_call(
        functools.partial(mix_forward_kernel, count),
        in_specs=[vmem] * 5,
        out_specs=[vmem] * 5,
        out_shape=[
            low(queries_t.shape),
            wide((batch, QHEADS, width)),
            low((count,) + near.shape[1:]),
            low(state.shape),
            wide((count,) + total.shape),
        ],
        scratch_shapes=[
            pltpu.VMEM((batch, KVHEADS * HDIM, QHEADS * width), BF16),
            pltpu.VMEM((batch, QHEADS, width), F32),
            pltpu.VMEM((batch, QHEADS, width), F32),
            pltpu.VMEM((batch, QHEADS, HDIM, width), F32),
            pltpu.VMEM(near.shape, BF16),
            pltpu.VMEM((count,) + total.shape, F32),
            pltpu.VMEM(state.shape, BF16),
            dma((2, count)),
            dma((2, half)),
        ]
        + StateExchange.scratch(count, state),
        compiler_params=pltpu.CompilerParams(
            collective_id=2, has_side_effects=True, vmem_limit_bytes=KERNEL_VMEM
        ),
        cost_estimate=pl.CostEstimate(
            flops=batch * count * width * width * 8 * 1000,
            bytes_accessed=4 * MIB,
            transcendentals=0,
        ),
        name="mix_forward",
    )(starts, queries_t, near, state, total)


def mix_backward_kernel(
    count,
    start_ref,
    q_ref,
    table_ref,
    attended_ref,
    grad_ref,
    log_ref,
    state_ref,
    totals_ref,
    dq_ref,
    dkv_ref,
    later_ref,
    q_wide,
    g_wide,
    q_tall,
    g_tall,
    delta,
    acc,
    mine,
    theirs,
    far,
    result,
    table_sems,
    *state_scratch,
):
    here = lax.axis_index("ctx")
    batch = table_ref.shape[1]
    width = table_ref.shape[2]
    half = count // 2
    kv_width = KVHEADS * HDIM
    exchange_barrier([partner_ctx(k) for k in range(1, count)])
    states = StateExchange(count, False, state_ref, totals_ref, result, state_scratch)
    states.begin()
    first_pos = here * width
    acc[...] = jnp.zeros(acc.shape, F32)
    mine[...] = jnp.zeros(mine.shape, BF16)
    theirs[...] = jnp.zeros(theirs.shape, BF16)
    for b in range(batch):
        columns = slice(b * width, (b + 1) * width)
        spread_heads(q_ref.at[:, columns], q_wide.at[b], HDIM**-0.5)
        spread_heads(grad_ref.at[:, columns], g_wide.at[b], 1.0)
        for head in range(QHEADS):
            lanes = slice(head * width, (head + 1) * width)
            q_tall[b, lanes, :] = q_wide[b, :, lanes].T
            g_tall[b, lanes, :] = g_wide[b, :, lanes].T
            span = slice(head * HDIM, (head + 1) * HDIM)
            delta[b, head : head + 1, :] = jnp.sum(
                attended_ref[span, columns].astype(F32) * grad_ref[span, columns].astype(F32),
                axis=0,
                keepdims=True,
            )

    def attend(b, place, block, target, i):
        kv_rows = table_ref[place, b]
        keys = kv_rows[:, :kv_width]
        values = kv_rows[:, kv_width:]
        keys_t = keys.T
        allowed = attend_allowed(block, first_pos, start_ref[b][:1], width)
        logs_now, deltas = log_ref[b], delta[b]
        dk = jnp.zeros((width, kv_width), F32)
        dv = jnp.zeros((width, kv_width), F32)
        for head in range(QHEADS):
            group = head // (QHEADS // KVHEADS)
            lanes = slice(head * width, (head + 1) * width)
            line = slice(head, head + 1)
            scores = mat(keys, q_wide[b, :, lanes])
            shifted = jnp.where(allowed, scores - logs_now[line], MASKED_SCORE)
            probs = jnp.exp(shifted)
            grad_probs = mat(values, g_wide[b, :, lanes])
            grad_scores = (probs * (grad_probs - deltas[line])).astype(BF16)
            dk = dk + mat(grad_scores, q_tall[b, lanes, :])
            dv = dv + mat(probs.astype(BF16), g_tall[b, lanes, :])
            acc[b, head] += mat(keys_t[group * HDIM : (group + 1) * HDIM, :], grad_scores)
        target[i, b] = jnp.concatenate([dk, dv], axis=1).astype(BF16)

    bits = ctx_bits(count)
    high = len(bits) - 1

    def step_of(i):
        return sum(((i // (1 << p)) % 2) * (1 << (high - p)) for p in range(high))

    def pair(target, low, begin=0, end=half):
        def one(i, carry):
            block = here ^ (step_of(i) + low)

            @pl.when(block <= here)
            def _():
                for b in range(batch):
                    attend(b, i + low * half, block, target, i)

            return carry

        lax.fori_loop(begin, end, one, 0)

    def table_copy(i):
        return remote(
            theirs.at[i], far.at[i], table_sems.at[0, i], table_sems.at[1, i], partner_ctx(1)
        )

    pair(theirs, 1, 0, half // 2)
    states.middle()
    pair(theirs, 1, half // 2)
    for i in range(half):
        table_copy(i).start()
    states.carry()
    pair(mine, 0)
    for b in range(batch):
        for head in range(QHEADS):
            dq_ref[head * HDIM : (head + 1) * HDIM, b * width : (b + 1) * width] = (
                acc[b, head] * HDIM**-0.5
            ).astype(BF16)
    for i in range(half):
        table_copy(i).wait()
    dkv_ref[...] = (mine[...].astype(F32) + far[...].astype(F32)).astype(BF16)
    states.end()
    later_ref[...] = result[...]


def mix_backward(count, starts, queries_t, table, attended_t, grad_t, logs, state, totals):
    _, batch, width, kv_width = table.shape
    half = count // 2
    vmem = pl.BlockSpec(memory_space=pltpu.VMEM)
    dma = pltpu.SemaphoreType.DMA
    low = functools.partial(jax.ShapeDtypeStruct, dtype=BF16)
    near = (half, batch, width, kv_width)
    wide = pltpu.VMEM((batch, KVHEADS * HDIM, QHEADS * width), BF16)
    tall = pltpu.VMEM((batch, QHEADS * width, KVHEADS * HDIM), BF16)
    return pl.pallas_call(
        functools.partial(mix_backward_kernel, count),
        in_specs=[vmem] * 8,
        out_specs=[vmem] * 3,
        out_shape=[low(queries_t.shape), low(near), low(state.shape)],
        scratch_shapes=[
            wide,
            wide,
            tall,
            tall,
            pltpu.VMEM((batch, QHEADS, width), F32),
            pltpu.VMEM((batch, QHEADS, HDIM, width), F32),
            pltpu.VMEM(near, BF16),
            pltpu.VMEM(near, BF16),
            pltpu.VMEM(near, BF16),
            pltpu.VMEM(state.shape, BF16),
            dma((2, half)),
        ]
        + StateExchange.scratch(count, state),
        compiler_params=pltpu.CompilerParams(
            collective_id=3, has_side_effects=True, vmem_limit_bytes=KERNEL_VMEM
        ),
        cost_estimate=pl.CostEstimate(
            flops=batch * count * width * width * 8 * 2000,
            bytes_accessed=8 * MIB,
            transcendentals=0,
        ),
        name="mix_backward",
    )(starts, queries_t, table, attended_t, grad_t, logs, state, totals)


def front_kernel(
    count,
    conv_tiles,
    gate_tiles,
    x_ref,
    gain_ref,
    start_ref,
    own_ref,
    tall_ref,
    weight_ref,
    bias_ref,
    normed_ref,
    others_ref,
    tall_others,
    conv_ref,
    edge_ref,
    act_ref,
    dt_ref,
    q_ref,
    gate_ref,
    table_ref,
    edge_x,
    near,
    tall_near,
    table,
    cross_sems,
    core_sems,
    side_sems,
    last_sems,
    tall_sems,
    table_sems,
    edge_sems,
):
    here = lax.axis_index("ctx")
    batch = table.shape[1]
    rows = table.shape[2]
    size = own_ref.shape[0]
    chunks = own_ref.shape[1] // EARLY_TILE
    half = count // 2
    exchange_barrier(
        [partner_wsh(1), partner_wsh(2)] + [partner_ctx(k) for k in range(1, count)]
    )
    right = (here + 1) % count

    def edge_copy(b):
        return remote(
            x_ref.at[pl.ds((b + 1) * rows - 16, 16)],
            edge_x.at[b],
            edge_sems.at[0, b],
            edge_sems.at[1, b],
            (right, lax.axis_index("wsh")),
        )

    my_half = pl.ds(pl.multiple_of((here % 2) * (size // 2), 16), size // 2)
    other_half = pl.ds(pl.multiple_of((1 - here % 2) * (size // 2), 16), size // 2)

    def tile(place):
        return pl.ds(pl.multiple_of(place * EARLY_TILE, EARLY_TILE), EARLY_TILE)

    def columns(k):
        return tile((k + gate_tiles) % chunks)

    gate_from = chunks - gate_tiles

    def cross_copy(k):
        return remote(
            own_ref.at[my_half, columns(k)],
            near.at[0, my_half, columns(k)],
            cross_sems.at[0, k],
            cross_sems.at[1, k],
            partner_wsh(2),
        )

    def side_copy(k):
        return remote(
            near.at[0, my_half, columns(k)],
            near.at[0, my_half, columns(k)],
            side_sems.at[0, k],
            side_sems.at[1, k],
            partner_ctx(1),
        )

    def side_in(k):
        return remote(
            near.at[0, other_half, columns(k)],
            near.at[0, other_half, columns(k)],
            side_sems.at[0, k],
            side_sems.at[1, k],
            partner_ctx(1),
        )

    def core_copy(k):
        return remote(
            own_ref.at[:, columns(k)],
            near.at[1, :, columns(k)],
            core_sems.at[0, k],
            core_sems.at[1, k],
            partner_wsh(1),
        )

    def last_copy(k):
        return remote(
            near.at[0, :, columns(k)],
            near.at[2, :, columns(k)],
            last_sems.at[0, k],
            last_sems.at[1, k],
            partner_wsh(1),
        )

    tall_size = tall_ref.shape[0]
    tall_chunks = tall_ref.shape[1] // EARLY_TILE
    tall_mine = pl.ds(pl.multiple_of((here % 2) * (tall_size // 2), 16), tall_size // 2)
    tall_theirs = pl.ds(pl.multiple_of((1 - here % 2) * (tall_size // 2), 16), tall_size // 2)

    def tall_copy(source, target, kind, k, device):
        return remote(
            source, target, tall_sems.at[kind, 0, k], tall_sems.at[kind, 1, k], device
        )

    def tall_cross(k):
        place = tall_near.at[0, tall_mine, tile(k)]
        return tall_copy(tall_ref.at[tall_mine, tile(k)], place, 0, k, partner_wsh(2))

    def tall_core(k):
        place = tall_near.at[1, :, tile(k)]
        return tall_copy(tall_ref.at[:, tile(k)], place, 1, k, partner_wsh(1))

    def tall_side(k, rows_at):
        place = tall_near.at[0, rows_at, tile(k)]
        return tall_copy(place, place, 2, k, partner_ctx(1))

    def tall_last(k):
        place = tall_near.at[2, :, tile(k)]
        return tall_copy(tall_near.at[0, :, tile(k)], place, 3, k, partner_wsh(1))

    def tall_step(j):
        @pl.when((j >= 0) & (j < tall_chunks))
        def _():
            tall_cross(j).wait()
            tall_side(j, tall_mine).start()

        @pl.when((j >= 2) & (j <= tall_chunks + 1))
        def _():
            tall_side(j - 2, tall_mine).wait_send()
            tall_side(j - 2, tall_theirs).wait_recv()
            tall_last(j - 2).start()

    bits = ctx_bits(count)
    high = len(bits) - 1

    def step_of(i):
        return sum(((i >> p) & 1) * (1 << (high - p)) for p in range(high))

    def table_copy(i):
        return remote(
            table.at[0],
            table.at[i],
            table_sems.at[0, i],
            table_sems.at[1, i],
            partner_ctx(step_of(i)),
        )

    def send_first(k, carry):
        cross_copy(k).start()
        core_copy(k).start()
        return carry

    def send_tall(k, carry):
        tall_cross(k).start()
        tall_core(k).start()
        return carry

    lax.fori_loop(0, gate_from, send_first, 0)
    lax.fori_loop(0, tall_chunks, send_tall, 0)
    lax.fori_loop(gate_from, chunks, send_first, 0)
    for b in range(batch):
        edge_copy(b).start()

    def normalized(low):
        wide = low.astype(F32)
        return (wide * inv_rms(wide) * gain_ref[...]).astype(BF16)

    normed_ref[...] = normalized(x_ref[...])
    for b in range(batch):
        edge_copy(b).wait()
    edge_normed = normalized(
        jnp.concatenate([edge_x[b] for b in range(batch)], axis=0)
    )
    edge_x[...] = edge_normed.reshape(edge_x.shape)

    def product(pick, k):
        total = None
        for place, step in enumerate(NEAR):
            block = own_ref[:, columns(k)] if place == 0 else near[place - 1, :, columns(k)]
            part = mat(pick(near_at(step, size)), block)
            total = part if total is None else total + part
        return total

    def compute(k):
        core_copy(k).wait()
        last_copy(k).wait()
        value = product(lambda at: normed_ref[:, at], k)

        @pl.when(k == 0)
        def _():
            table[0] = value.astype(BF16).reshape(table.shape[1:])
            for i in range(1, half):
                table_copy(i).start()

        @pl.when((k > 0) & (k <= conv_tiles))
        def _():
            place = tile(k - 1)
            conv_ref[:, place] = value
            taps = weight_ref[:, place]
            bias = bias_ref[:, place]
            for b in range(batch):
                edge = product(lambda at, b=b: edge_x[b, :, at], k)[16 - EDGE :]
                edge_ref[b * EDGE : (b + 1) * EDGE, place] = edge
                span = slice(b * rows, (b + 1) * rows)
                total, _ = conv_sums(
                    conv_inputs(edge, value[span]), taps, bias, start_ref[span]
                )
                act_ref[span, place] = total * sigmoid(total)

        @pl.when(k == conv_tiles + 1)
        def _():
            dt_ref[...] = value

        @pl.when((k > conv_tiles + 1) & (k < gate_from))
        def _():
            q_ref[tile(k - conv_tiles - 2), :] = value.T.astype(BF16)

        @pl.when(k >= gate_from)
        def _():
            gate_ref[:, tile(k - gate_from)] = value

    def one_step(t, carry):
        @pl.when(t < chunks)
        def _():
            cross_copy(t).wait()
            side_copy(t).start()

        @pl.when((t >= 2) & (t <= chunks + 1))
        def _():
            side_copy(t - 2).wait_send()
            side_in(t - 2).wait_recv()
            last_copy(t - 2).start()

        tall_step(t - gate_from)
        pl.when(t >= 4)(functools.partial(compute, t - 4))
        return carry

    lax.fori_loop(0, chunks + 4, one_step, 0)
    others_ref[...] = near[...]

    def end_tall(k, carry):
        tall_core(k).wait()
        tall_last(k).wait()
        return carry

    lax.fori_loop(0, tall_chunks, end_tall, 0)
    tall_others[...] = tall_near[...]
    for i in range(1, half):
        table_copy(i).wait()
    table_ref[...] = table[...]


def front(count, batch, x, gain, rel_start, own, tall, conv_weight, conv_bias, q_width):
    tokens, depth = x.shape
    size, columns = own.shape
    rows = tokens // batch
    channels = conv_weight.shape[1]
    chunks = columns // EARLY_TILE
    half = count // 2
    vmem = pl.BlockSpec(memory_space=pltpu.VMEM)
    dma = pltpu.SemaphoreType.DMA
    low = functools.partial(jax.ShapeDtypeStruct, dtype=BF16)
    wide = functools.partial(jax.ShapeDtypeStruct, dtype=F32)
    table = (half, batch, rows, EARLY_TILE)
    return pl.pallas_call(
        functools.partial(
            front_kernel, count, channels // EARLY_TILE, DSSM // EARLY_TILE
        ),
        in_specs=[vmem] * 7,
        out_specs=[vmem] * 10,
        out_shape=[
            low((tokens, depth)),
            low((3, size, columns)),
            low((3,) + tall.shape),
            wide((tokens, channels)),
            wide((batch * EDGE, channels)),
            wide((tokens, channels)),
            wide((tokens, EARLY_TILE)),
            low((q_width, tokens)),
            wide((tokens, DSSM)),
            low(table),
        ],
        scratch_shapes=[
            pltpu.VMEM((batch, 16, depth), BF16),
            pltpu.VMEM((3, size, columns), BF16),
            pltpu.VMEM((3,) + tall.shape, BF16),
            pltpu.VMEM(table, BF16),
            dma((2, chunks)),
            dma((2, chunks)),
            dma((2, chunks)),
            dma((2, chunks)),
            dma((4, 2, tall.shape[1] // EARLY_TILE)),
            dma((2, half)),
            dma((2, batch)),
        ],
        compiler_params=pltpu.CompilerParams(
            collective_id=4, has_side_effects=True, vmem_limit_bytes=KERNEL_VMEM
        ),
        cost_estimate=pl.CostEstimate(
            flops=2 * tokens * depth * columns, bytes_accessed=20 * MIB, transcendentals=0
        ),
        name="front",
    )(x, gain[None], rel_start, own, tall, conv_weight, conv_bias[None])


def local(
    inputs,
    cotangent,
    lengths,
    norm1_gain,
    in_weight,
    dt_weight,
    conv_weight,
    conv_bias,
    dt_bias,
    decay_rate,
    skip_gain,
    mamba_gain,
    out_weight,
    q_weight,
    kv_weight,
    o_weight,
    norm2_gain,
    gu_weight,
    down_weight,
):
    count, _, rows, features = inputs.shape
    here = lax.axis_index("ctx")
    ctx_count = lax.axis_size("ctx")
    tokens = count * rows
    first_pos = here * rows
    own_pos = first_pos + jnp.arange(rows, dtype=jnp.int32)
    starts = jax.vmap(lambda row: seq_starts(row, own_pos))(lengths[:, 0])
    rel_start = (starts - first_pos).reshape(tokens, 1)
    taps = conv_weight.shape[0]
    channels = conv_weight.shape[1]
    kv_width = kv_weight.shape[1]
    x_low = inputs.reshape(tokens, features)
    grad_top = cotangent.reshape(tokens, features)

    conv_tiles = channels // EARLY_TILE
    gate_tiles = DSSM // EARLY_TILE
    early_shard = jnp.concatenate(
        [
            in_weight[:, :DSSM],
            kv_weight,
            in_weight[:, DSSM:],
            jnp.pad(dt_weight, ((0, 0), (0, EARLY_TILE - dt_weight.shape[1]))),
            q_weight,
        ],
        axis=1,
    )

    outs_own = jnp.concatenate([out_weight, o_weight], axis=0)
    normed, early_others, outs_others, conv_rows, edge_rows, act, dt_rows, queries_t, gate_z, near_table = front(
        ctx_count,
        count,
        x_low,
        norm1_gain,
        rel_start,
        early_shard,
        outs_own,
        conv_weight,
        conv_bias,
        q_weight.shape[1],
    )
    high_bits = bits_of("ctx")[1:]
    later_shards = after(
        (
            gu_weight,
            down_weight,
        ),
        dt_rows,
    )
    crossing = [swapped(shard, "wsh", 2) for shard in later_shards]

    def head_row(values):
        return jnp.pad(values, (0, 128 - MHEADS))[None]

    bias_row, rate_row = head_row(dt_bias), head_row(decay_rate)
    steps, decay, decay_t, to_end, total, fresh = ssd_state(
        count, act, dt_rows, bias_row, rate_row, rel_start
    )
    starts_row = jnp.broadcast_to(starts[:, None, :], (count, 8, rows))
    attended_t, logs, key_table, state_in, totals = mix_forward(
        ctx_count, starts_row, queries_t, near_table, fresh, total
    )

    def near_blocks(which, held):
        shard, across = later_shards[which], after(crossing[which], held)
        return [shard, across, swapped(shard, "wsh", 1), swapped(across, "wsh", 1)]

    outs = (outs_own, outs_others)
    skip_row = jnp.repeat(skip_gain, MDIM)[None]
    scanned = ssd_forward(count, act, steps, decay, decay_t, rel_start, state_in, skip_row)
    gate_sig = jax.nn.sigmoid(gate_z)
    gated = scanned * gate_z * gate_sig
    scale_m = inv_rms(gated)
    mixed = (gated * scale_m * mamba_gain).astype(BF16)
    gu_full, down_full = near_blocks(0, mixed), near_blocks(1, mixed)
    middle, normed_two = out_project(x_low, mixed, attended_t, norm2_gain, outs)

    layer_out, grad_middle, branch, grad_norm2, hidden, grad_pair = mlp_both(
        lax.axis_index("wsh").astype(jnp.int32)[None],
        normed_two,
        grad_top,
        middle,
        norm2_gain,
        gu_full,
        down_full,
    )
    gu_send = block_grads(normed_two, grad_pair, NEAR[2:])[0]
    down_send = block_grads(hidden, grad_top[None], NEAR[2:])[0]
    gu_sent = swapped(gu_send, "wsh", 1)
    down_sent = swapped(down_send, "wsh", 1)
    branch = after(branch, (gu_send, down_send))
    grad_mixed, grad_attended_t = out_unproject(branch, outs, DSSM, QHEADS * HDIM)
    gu_left, down_left = after((normed_two, hidden), grad_attended_t)
    gu_kept, gu_other = block_grads(gu_left, grad_pair, NEAR[:2], gu_sent)
    down_kept, down_other = block_grads(down_left, grad_top[None], NEAR[:2], down_sent)
    gu_crossed = swapped(gu_other, "wsh", 2)
    down_crossed = swapped(down_other, "wsh", 2)

    grad_mixed = after(grad_mixed, (gu_other, down_other))
    grad_gated, grad_mamba = rms_pull(gated, scale_m, mamba_gain, grad_mixed)
    grad_gate_z = grad_gated * scanned * gate_sig * (1.0 + gate_z * (1.0 - gate_sig))
    grad_scanned = grad_gated * gate_z * gate_sig
    grad_state = state_grad(count, grad_scanned, act, decay, rel_start)
    dq_t, dkv_near, later = mix_backward(
        ctx_count,
        starts_row,
        queries_t,
        key_table,
        attended_t,
        grad_attended_t,
        logs,
        grad_state,
        totals,
    )
    key_grads = Scattering(dkv_near, high_bits)

    def total_of(kept, crossed):
        return (kept.astype(F32) + crossed.astype(F32)).astype(BF16)

    held = after((gu_crossed, down_crossed), dq_t)
    parts = total_of(gu_kept, held[0]), total_of(down_kept, held[1])
    grad_gate_z = after(grad_gate_z.astype(BF16), parts)
    dq_rows = dq_t.T
    grad_normed = unproject(
        jnp.zeros((tokens, features), F32),
        grad_gate_z,
        [early_shard] + [early_others] * 3,
        768,
        near_specs(early_shard, 768, 0),
    )
    grad_normed = unproject(
        grad_normed,
        dq_rows,
        [early_shard] + [early_others] * 3,
        EARLY_TILE,
        near_specs(early_shard, EARLY_TILE, gate_tiles + conv_tiles + 2),
    )
    later = after(later, key_grads.advance(grad_normed))
    dx, db, dc, dt_grad, small_ssd = ssd_backward(
        count,
        act,
        steps,
        decay,
        decay_t,
        rel_start,
        state_in,
        skip_row,
        scanned,
        grad_scanned,
        later,
        to_end,
        total,
        dt_rows,
        bias_row,
        rate_row,
    )
    key_grads.advance(dx)
    grad_kv_rows = key_grads.finish().reshape(tokens, -1)
    edge_back = passed_along(
        edge_grads(count, dx, db, dc, conv_rows, edge_rows, rel_start, conv_weight, conv_bias),
        "ctx",
        -1,
    )
    grad_early, conv_grads, input_grad, grad_norm1 = early_back(
        count,
        grad_normed,
        grad_kv_rows,
        dx,
        db,
        dc,
        conv_rows,
        edge_rows,
        edge_back,
        dt_grad,
        rel_start,
        conv_weight,
        conv_bias,
        x_low,
        norm1_gain,
        grad_middle,
        early_shard,
        early_others,
    )
    small_ssd = jnp.sum(small_ssd, axis=0)
    grad_dt_w = mat_left_t(normed, dt_grad[:, :MHEADS])

    gu_sum, down_sum = lax.psum(parts, "ctx")
    pieces = (
        grad_norm1[0],
        conv_grads[:taps],
        conv_grads[taps],
        small_ssd[0, :MHEADS],
        small_ssd[1, :MHEADS],
        small_ssd[2, :MHEADS],
        grad_mamba,
        grad_norm2[0],
        grad_dt_w,
    )
    packed = jnp.concatenate(
        [
            jnp.pad(piece.reshape(-1), (0, -piece.size % 1024)).reshape(-1, 128)
            for piece in pieces
        ],
        axis=0,
    )
    early_sum, gate_sum, q_sum, mix_sum, packed = reduce_grads(
        ctx_count,
        kv_width + channels,
        normed,
        mixed,
        attended_t,
        grad_early,
        grad_gate_z,
        dq_rows,
        branch,
        packed,
    )
    in_sum, q_sum, kv_sum, out_sum, o_sum = finish(
        early_sum,
        gate_sum,
        mix_sum,
        q_sum,
        [w.shape for w in (in_weight, q_weight, kv_weight, out_weight, o_weight)],
    )
    totals_w = [in_sum, out_sum, q_sum, kv_sum, o_sum, gu_sum.astype(F32), down_sum.astype(F32)]
    small = []
    place = 0
    for piece in pieces:
        lines = -(-piece.size // 1024) * 8
        small.append(packed[place : place + lines].reshape(-1)[: piece.size].reshape(piece.shape))
        place += lines
    dt_size = dt_weight.shape[0]
    dt_sum = lax.dynamic_slice_in_dim(small[8], lax.axis_index("wsh") * dt_size, dt_size, 0)
    shape = (count, 1, rows, features)
    return (
        layer_out.reshape(shape),
        input_grad.reshape(shape),
        small[0],
        totals_w[0],
        dt_sum,
        small[1],
        small[2],
        small[3],
        small[4],
        small[5],
        small[6],
        totals_w[1],
        totals_w[2],
        totals_w[3],
        totals_w[4],
        small[7],
        totals_w[5],
        totals_w[6],
    )


def solution(mesh):
    stream = P(None, "wsh", "ctx", None)
    shard = P("wsh", None)
    in_specs = (
        stream,
        stream,
        P(None, "wsh", None),
        P(),
        shard,
        shard,
        P(),
        P(),
        P(),
        P(),
        P(),
        P(),
        shard,
        shard,
        shard,
        shard,
        P(),
        shard,
        shard,
    )
    out_specs = (
        stream,
        stream,
        P(),
        shard,
        shard,
        P(),
        P(),
        P(),
        P(),
        P(),
        P(),
        shard,
        shard,
        shard,
        shard,
        P(),
        shard,
        shard,
    )
    return jax.shard_map(local, mesh=mesh, in_specs=in_specs, out_specs=out_specs, check_vma=False)
```

```python
import functools

import jax
import jax.numpy as jnp
from jax import lax
from jax.experimental import pallas as pl
from jax.experimental.pallas import tpu as pltpu
from jax.sharding import PartitionSpec as P

FF = 2048
MHEADS = 24
MDIM = 64
STATE = 128
QHEADS = 8
KVHEADS = 2
HDIM = 64
DSSM = 1536
HGROUP = 8
NGROUP = MHEADS // HGROUP
GWIDTH = HGROUP * MDIM
PAIR = 2 * MDIM

NORM_EPS = 1e-05
PRECISE = lax.Precision.HIGHEST
MASKED_SCORE = -1e30
MIB = 2**20
KERNEL_VMEM = 60 * MIB
F32 = jnp.float32
BF16 = jnp.bfloat16


def dot_as(left, right, left_dim, right_dim):
    return lax.dot_general(
        left, right, (((left_dim,), (right_dim,)), ((), ())), preferred_element_type=F32
    )


def mat(left, right):
    return dot_as(left, right, 1, 0)


def mat_left_t(left, right):
    return dot_as(left, right, 0, 0)


def mat_right_t(left, right):
    return dot_as(left, right, 1, 1)


def inv_rms(rows):
    return lax.rsqrt(jnp.mean(rows * rows, axis=-1, keepdims=True) + NORM_EPS)


def rms_pull(rows, scale, gain, grad):
    scaled = rows * scale
    grad_gain = jnp.sum(grad * scaled, axis=0)
    through = grad * gain
    inner = jnp.mean(through * scaled, axis=-1, keepdims=True)
    return scale * (through - scaled * inner), grad_gain


def seq_starts(lengths_row, positions):
    begins = jnp.cumsum(lengths_row, dtype=jnp.int32) - lengths_row
    picked = jnp.where(begins[None, :] <= positions[:, None], begins[None, :], 0)
    return jnp.max(picked, axis=1)


def head_lanes(rows):
    return lax.broadcasted_iota(jnp.int32, (rows, PAIR), 1) < MDIM


def masked_products(b_low, c_low, rel_start):
    rows = b_low.shape[0]
    at_row = lax.broadcasted_iota(jnp.int32, (rows, rows), 0)
    at_col = lax.broadcasted_iota(jnp.int32, (rows, rows), 1)
    allowed = (at_col <= at_row) & (at_col >= rel_start)
    return allowed, jnp.where(allowed, mat_right_t(c_low, b_low), 0.0)


def pair_columns(first_half, columns, head):
    return jnp.where(first_half, columns[:, head : head + 1], columns[:, head + 1 : head + 2])


def exact(left, right, left_dim, right_dim):
    return lax.dot_general(
        left,
        right,
        (((left_dim,), (right_dim,)), ((), ())),
        precision=PRECISE,
        preferred_element_type=F32,
    )


def sums_by(values, picks):
    high = values.astype(BF16)
    low = (values - high.astype(F32)).astype(BF16)
    return mat(high, picks) + mat(low, picks)


def lower_ones(rows):
    at_row = lax.broadcasted_iota(jnp.int32, (rows, rows), 0)
    at_col = lax.broadcasted_iota(jnp.int32, (rows, rows), 1)
    return (at_row >= at_col).astype(F32)


def sigmoid(value):
    return 1.0 / (1.0 + jnp.exp(-value))


def softplus(value):
    return jnp.maximum(value, 0.0) + jnp.log1p(jnp.exp(-jnp.abs(value)))


def scaled_rows(target, source_ref, factors):
    first_half = head_lanes(source_ref.shape[0])
    for head in range(0, MHEADS, 2):
        lanes = slice(head * MDIM, head * MDIM + PAIR)
        target[:, lanes] = (
            source_ref[:, lanes] * pair_columns(first_half, factors, head)
        ).astype(BF16)


def ssd_state_kernel(
    act_ref,
    dt_ref,
    bias_ref,
    rate_ref,
    start_ref,
    step_ref,
    decay_ref,
    decay_t_ref,
    end_ref,
    total_ref,
    state_ref,
    scaled,
):
    rows = act_ref.shape[0]
    steps = softplus(dt_ref[:, :128] + bias_ref[...])
    decay = exact(lower_ones(rows), -steps * rate_ref[...], 1, 0)
    rel_start = start_ref[...]
    last_start = rel_start[rows - 1 : rows, :]
    kept = lax.broadcasted_iota(jnp.int32, (rows, 1), 0) >= last_start
    end = decay[rows - 1 : rows, :]
    to_end = jnp.where(kept, jnp.exp(end - decay), 0.0)
    step_ref[...] = steps
    decay_ref[...] = decay
    decay_t_ref[0] = decay.T
    end_ref[...] = to_end
    total_ref[0] = jnp.broadcast_to(jnp.where(last_start < 0, jnp.exp(end), 0.0), (8, 128))
    scaled_rows(scaled, act_ref, to_end * steps)
    state_ref[0] = mat_left_t(scaled[...], act_ref[:, DSSM : DSSM + STATE].astype(BF16))


def row_spec(rows, width, place=0):
    return pl.BlockSpec((rows, width), lambda b: (b, place))


def ssd_state(count, act, dt_rows, bias, rate, rel_start):
    rows = act.shape[0] // count
    lanes = pl.BlockSpec((1, 128), lambda b: (0, 0))
    heads = jax.ShapeDtypeStruct((count * rows, 128), F32)
    return pl.pallas_call(
        ssd_state_kernel,
        grid=(count,),
        in_specs=[
            row_spec(rows, act.shape[1]),
            row_spec(rows, dt_rows.shape[1]),
            lanes,
            lanes,
            row_spec(rows, 1),
        ],
        out_specs=[
            row_spec(rows, 128),
            row_spec(rows, 128),
            pl.BlockSpec((1, 128, rows), lambda b: (b, 0, 0)),
            row_spec(rows, 128),
            pl.BlockSpec((1, 8, 128), lambda b: (b, 0, 0)),
            pl.BlockSpec((1, DSSM, STATE), lambda b: (b, 0, 0)),
        ],
        out_shape=[
            heads,
            heads,
            jax.ShapeDtypeStruct((count, 128, rows), F32),
            heads,
            jax.ShapeDtypeStruct((count, 8, 128), F32),
            jax.ShapeDtypeStruct((count, DSSM, STATE), F32),
        ],
        scratch_shapes=[pltpu.VMEM((rows, DSSM), BF16)],
        compiler_params=pltpu.CompilerParams(vmem_limit_bytes=KERNEL_VMEM),
        cost_estimate=pl.CostEstimate(
            flops=1_000_000_000, bytes_accessed=8 * MIB, transcendentals=0
        ),
        name="ssd_state",
    )(act, dt_rows, bias, rate, rel_start)


def state_grad_kernel(dy_ref, c_ref, decay_ref, start_ref, out_ref, scaled):
    reach = jnp.where(start_ref[...] < 0, jnp.exp(decay_ref[...]), 0.0)
    scaled_rows(scaled, dy_ref, reach)
    out_ref[0] = mat_left_t(scaled[...], c_ref[...].astype(BF16))


def state_grad(count, dy, act, decay, rel_start):
    rows = act.shape[0] // count
    return pl.pallas_call(
        state_grad_kernel,
        grid=(count,),
        in_specs=[
            row_spec(rows, DSSM),
            row_spec(rows, STATE, DSSM // STATE + 1),
            row_spec(rows, 128),
            row_spec(rows, 1),
        ],
        out_specs=pl.BlockSpec((1, DSSM, STATE), lambda b: (b, 0, 0)),
        out_shape=jax.ShapeDtypeStruct((count, DSSM, STATE), F32),
        scratch_shapes=[pltpu.VMEM((rows, DSSM), BF16)],
        compiler_params=pltpu.CompilerParams(vmem_limit_bytes=KERNEL_VMEM),
        cost_estimate=pl.CostEstimate(
            flops=1_000_000_000, bytes_accessed=8 * MIB, transcendentals=0
        ),
        name="state_grad",
    )(dy, act, decay, rel_start)


def group_heads(ref):
    return pltpu.roll(ref[...], (128 - HGROUP * pl.program_id(1)) % 128, 1)


def group_rows(decay_t_ref):
    return decay_t_ref[0, pl.ds(pl.multiple_of(HGROUP * pl.program_id(1), HGROUP), HGROUP), :]


def ssd_forward_kernel(
    x_ref, b_ref, c_ref, step_ref, decay_ref, decay_t_ref, start_ref, state_ref, skip_ref, y_ref
):
    rows = x_ref.shape[0]
    b_low = b_ref[...].astype(BF16)
    c_low = c_ref[...].astype(BF16)
    rel_start = start_ref[...]
    _, products = masked_products(b_low, c_low, rel_start)
    incoming = mat_right_t(c_low, state_ref[0].astype(BF16))
    first_half = head_lanes(rows)
    steps = group_heads(step_ref)
    decay = group_heads(decay_ref)
    decay_t = group_rows(decay_t_ref)
    reach = jnp.where(rel_start < 0, jnp.exp(decay), 0.0)
    for head in range(0, HGROUP, 2):
        lanes = slice(head * MDIM, head * MDIM + PAIR)
        x_pair = x_ref[:, lanes]
        scaled = (x_pair * pair_columns(first_half, steps, head)).astype(BF16)
        parts = []
        for one in (head, head + 1):
            gaps = decay[:, one : one + 1] - decay_t[one : one + 1, :]
            weights = (jnp.exp(jnp.minimum(gaps, 0.0)) * products).astype(BF16)
            parts.append(mat(weights, scaled))
        y_ref[:, lanes] = (
            jnp.where(first_half, parts[0], parts[1])
            + pair_columns(first_half, reach, head) * incoming[:, lanes]
            + skip_ref[:, lanes] * x_pair
        )


def ssd_backward_kernel(
    x_ref,
    b_ref,
    c_ref,
    step_ref,
    decay_ref,
    decay_t_ref,
    start_ref,
    state_ref,
    skip_ref,
    y_ref,
    dy_ref,
    later_ref,
    end_ref,
    total_ref,
    dt_ref,
    bias_ref,
    rate_ref,
    dx_ref,
    db_ref,
    dc_ref,
    dt_grad_ref,
    small_ref,
    one_sum,
    two_sum,
    three_sum,
    mixed_y,
    mixed_x,
    head_sums,
    row_sums,
):
    rows = x_ref.shape[0]
    b_low = b_ref[...].astype(BF16)
    c_low = c_ref[...].astype(BF16)
    rel_start = start_ref[...]
    allowed, products = masked_products(b_low, c_low, rel_start)
    state_low = state_ref[0].astype(BF16)
    later_low = later_ref[0].astype(BF16)
    spread = mat_right_t(b_low, later_low)
    first_half = head_lanes(rows)
    steps = group_heads(step_ref)
    decay = group_heads(decay_ref)
    decay_t = group_rows(decay_t_ref)
    reach = jnp.where(rel_start < 0, jnp.exp(decay), 0.0)
    to_end = group_heads(end_ref) * steps
    product_grad = jnp.zeros((rows, rows), F32)
    skip_parts = []
    for head in range(0, HGROUP, 2):
        lanes = slice(head * MDIM, head * MDIM + PAIR)
        x_pair = x_ref[:, lanes]
        dy_pair = dy_ref[:, lanes]
        step_pair = pair_columns(first_half, steps, head)
        scaled = (x_pair * step_pair).astype(BF16)
        dy_low = dy_pair.astype(BF16)
        parts = []
        for one in (head, head + 1):
            gaps = decay[:, one : one + 1] - decay_t[one : one + 1, :]
            decays = jnp.exp(jnp.minimum(gaps, 0.0))
            mine = first_half if one == head else ~first_half
            dy_mine = jnp.where(mine, dy_pair, 0.0).astype(BF16)
            weight_grad = mat_right_t(dy_mine, scaled)
            product_grad = product_grad + weight_grad * decays
            parts.append(mat_left_t((decays * products).astype(BF16), dy_low))
        dz_pair = jnp.where(first_half, parts[0], parts[1])
        skip_pair = skip_ref[:, lanes]
        end_pair = pair_columns(first_half, to_end, head)
        spread_pair = spread[:, lanes]
        dx_ref[:, lanes] = skip_pair * dy_pair + step_pair * dz_pair + end_pair * spread_pair
        one_sum[:, lanes] = dy_pair * (y_ref[:, lanes] - skip_pair * x_pair)
        two_sum[:, lanes] = x_pair * dz_pair
        three_sum[:, lanes] = x_pair * spread_pair
        mixed_y[:, lanes] = (dy_pair * pair_columns(first_half, reach, head)).astype(BF16)
        mixed_x[:, lanes] = (x_pair * end_pair).astype(BF16)
        skip_parts.append(jnp.sum(dy_pair * x_pair, axis=0, keepdims=True))
    grad_low = jnp.where(allowed, product_grad, 0.0).astype(BF16)
    dc = mat(grad_low, b_low) + mat(mixed_y[...], state_low)
    db = mat_left_t(grad_low, c_low) + mat(mixed_x[...], later_low)
    group = pl.program_id(1)

    @pl.when(group == 0)
    def _():
        dc_ref[...] = jnp.zeros(dc_ref.shape, F32)
        db_ref[...] = jnp.zeros(db_ref.shape, F32)
        head_sums[...] = jnp.zeros(head_sums.shape, F32)
        row_sums[...] = jnp.zeros(row_sums.shape, F32)

    dc_ref[...] += dc
    db_ref[...] += db
    owner = lax.broadcasted_iota(jnp.int32, (GWIDTH, 128), 0) // MDIM + group * HGROUP
    picks = (owner == lax.broadcasted_iota(jnp.int32, (GWIDTH, 128), 1)).astype(BF16)
    for place, source in enumerate((one_sum, two_sum, three_sum)):
        head_sums[place] += sums_by(source[...], picks)
    skips = jnp.broadcast_to(jnp.concatenate(skip_parts, axis=1), (8, GWIDTH))
    row_sums[0] += sums_by(skips, picks)
    meets = exact(
        jnp.ones((8, STATE), F32), later_ref[0].astype(F32) * state_ref[0].astype(F32), 1, 1
    )
    row_sums[1] += sums_by(meets, picks)

    @pl.when(group == pl.num_programs(1) - 1)
    def _():
        all_steps = step_ref[...]
        all_end = end_ref[...]
        rate = rate_ref[...]
        row_dot, u_dot, v_dot = head_sums[0], head_sums[1], head_sums[2]
        to_last = v_dot * all_end * all_steps
        grad_decay = row_dot - u_dot * all_steps - to_last
        at_end = jnp.sum(to_last, axis=0, keepdims=True) + row_sums[1, :1] * total_ref[0, :1]
        grad_drop = exact(lower_ones(rows), grad_decay, 0, 0) + at_end
        grad_steps = u_dot + v_dot * all_end - rate * grad_drop
        grad_dt = grad_steps * sigmoid(dt_ref[:, :128] + bias_ref[...])
        dt_grad_ref[:, :128] = grad_dt.astype(BF16)
        dt_grad_ref[:, 128:] = jnp.zeros((rows, dt_grad_ref.shape[1] - 128), BF16)
        small_ref[0, 0:1] = jnp.sum(grad_dt, axis=0, keepdims=True)
        small_ref[0, 1:2] = jnp.sum(-all_steps * grad_drop, axis=0, keepdims=True)
        small_ref[0, 2:8] = row_sums[0, :6]


def ssd_specs(rows):
    wide = pl.BlockSpec((rows, GWIDTH), lambda b, g: (b, g))
    b_spec = pl.BlockSpec((rows, STATE), lambda b, g: (b, DSSM // STATE))
    c_spec = pl.BlockSpec((rows, STATE), lambda b, g: (b, DSSM // STATE + 1))
    heads = pl.BlockSpec((rows, 128), lambda b, g: (b, 0))
    heads_t = pl.BlockSpec((1, 128, rows), lambda b, g: (b, 0, 0))
    column = pl.BlockSpec((rows, 1), lambda b, g: (b, 0))
    state = pl.BlockSpec((1, GWIDTH, STATE), lambda b, g: (b, g, 0))
    skip = pl.BlockSpec((1, GWIDTH), lambda b, g: (0, g))
    return [wide, b_spec, c_spec, heads, heads, heads_t, column, state, skip]


def ssd_forward(count, act, steps, decay, decay_t, rel_start, state_in, skip_row):
    rows = act.shape[0] // count
    specs = ssd_specs(rows)
    return pl.pallas_call(
        ssd_forward_kernel,
        grid=(count, NGROUP),
        in_specs=specs,
        out_specs=specs[0],
        out_shape=jax.ShapeDtypeStruct((count * rows, DSSM), F32),
        compiler_params=pltpu.CompilerParams(vmem_limit_bytes=KERNEL_VMEM),
        cost_estimate=pl.CostEstimate(
            flops=count * MHEADS * rows * rows * 400, bytes_accessed=8 * MIB, transcendentals=0
        ),
        name="ssd_forward",
    )(act, act, act, steps, decay, decay_t, rel_start, state_in, skip_row)


def ssd_backward(
    count,
    act,
    steps,
    decay,
    decay_t,
    rel_start,
    state_in,
    skip_row,
    scanned,
    grad_scanned,
    later,
    to_end,
    total,
    dt_rows,
    bias,
    rate,
):
    rows = act.shape[0] // count
    specs = ssd_specs(rows)
    wide, heads, state = specs[0], specs[3], specs[7]
    row = pl.BlockSpec((1, 128), lambda b, g: (0, 0))
    packed = pl.BlockSpec((1, 8, 128), lambda b, g: (b, 0, 0))
    narrow = pl.BlockSpec((rows, STATE), lambda b, g: (b, 0))
    dt_spec = pl.BlockSpec((rows, dt_rows.shape[1]), lambda b, g: (b, 0))
    tokens = count * rows
    return pl.pallas_call(
        ssd_backward_kernel,
        grid=(count, NGROUP),
        in_specs=specs + [wide, wide, state, heads, packed, dt_spec, row, row],
        out_specs=[wide, narrow, narrow, dt_spec, packed],
        out_shape=[
            jax.ShapeDtypeStruct((tokens, DSSM), F32),
            jax.ShapeDtypeStruct((tokens, STATE), F32),
            jax.ShapeDtypeStruct((tokens, STATE), F32),
            jax.ShapeDtypeStruct(dt_rows.shape, BF16),
            jax.ShapeDtypeStruct((count, 8, 128), F32),
        ],
        scratch_shapes=[pltpu.VMEM((rows, GWIDTH), F32)] * 3
        + [pltpu.VMEM((rows, GWIDTH), BF16)] * 2
        + [pltpu.VMEM((3, rows, 128), F32), pltpu.VMEM((2, 8, 128), F32)],
        compiler_params=pltpu.CompilerParams(vmem_limit_bytes=KERNEL_VMEM),
        cost_estimate=pl.CostEstimate(
            flops=count * MHEADS * rows * rows * 1000, bytes_accessed=16 * MIB, transcendentals=0
        ),
        name="ssd_backward",
    )(
        act,
        act,
        act,
        steps,
        decay,
        decay_t,
        rel_start,
        state_in,
        skip_row,
        scanned,
        grad_scanned,
        later,
        to_end,
        total,
        dt_rows,
        bias,
        rate,
    )


def spread_heads(source_ref, target, factor):
    width = source_ref.shape[1]
    target[...] = jnp.zeros(target.shape, target.dtype)
    for head in range(QHEADS):
        group = head // (QHEADS // KVHEADS)
        value = source_ref[head * HDIM : (head + 1) * HDIM, :]
        target[group * HDIM : (group + 1) * HDIM, head * width : (head + 1) * width] = (
            value * factor if factor != 1.0 else value
        )


def attend_allowed(block, first_pos, starts, width):
    key_pos = block * width + lax.broadcasted_iota(jnp.int32, (width, width), 0)
    query_pos = first_pos + lax.broadcasted_iota(jnp.int32, (width, width), 1)
    return (key_pos <= query_pos) & (key_pos >= starts)


NEAR = (0, 2, 1, 3)
TILE_ROWS = 256
TILE_COLS = 512


def near_at(step, size):
    return pl.ds(pl.multiple_of((lax.axis_index("wsh") ^ step) * size, 128), size)


def project_kernel(x_ref, *refs):
    *weights, out_ref = refs
    size = weights[0].shape[0]
    total = None
    for step, weight in zip(NEAR, weights):
        part = mat(x_ref[:, near_at(step, size)], weight[...])
        total = part if total is None else total + part
    out_ref[...] = total.astype(out_ref.dtype)


def project(x, weights, tile, kind=F32):
    tokens, depth = x.shape
    size, columns = weights[0].shape
    return pl.pallas_call(
        project_kernel,
        grid=(columns // tile,),
        in_specs=[pl.BlockSpec((tokens, depth), lambda i: (0, 0))]
        + [pl.BlockSpec((size, tile), lambda i: (0, i))] * 4,
        out_specs=pl.BlockSpec((tokens, tile), lambda i: (0, i)),
        out_shape=jax.ShapeDtypeStruct((tokens, columns), kind),
        compiler_params=pltpu.CompilerParams(vmem_limit_bytes=KERNEL_VMEM),
        cost_estimate=pl.CostEstimate(
            flops=2 * tokens * depth * columns,
            bytes_accessed=2 * depth * columns + 4 * tokens * columns,
            transcendentals=0,
        ),
        name="project",
    )(x, *weights)


def near_specs(own, tile, offset):
    size = own.shape[0]
    return [pl.BlockSpec((size, tile), lambda i: (0, i + offset))] + [
        pl.BlockSpec((None, size, tile), lambda i, place=place: (place, 0, i + offset))
        for place in range(3)
    ]


def unproject_kernel(base_ref, grad_ref, *refs):
    *weights, out_ref = refs
    size = weights[0].shape[0]

    @pl.when(pl.program_id(0) == 0)
    def _():
        out_ref[...] = base_ref[...]

    for step, weight in zip(NEAR, weights):
        out_ref[:, near_at(step, size)] += mat_right_t(grad_ref[...], weight[...])


def unproject(base, grad, weights, tile, specs=None):
    tokens, columns = grad.shape
    size = weights[0].shape[0]
    whole = pl.BlockSpec((tokens, 4 * size), lambda i: (0, 0))
    return pl.pallas_call(
        unproject_kernel,
        grid=(columns // tile,),
        in_specs=[whole, pl.BlockSpec((tokens, tile), lambda i: (0, i))]
        + (specs or [pl.BlockSpec((size, tile), lambda i: (0, i))] * 4),
        out_specs=whole,
        out_shape=jax.ShapeDtypeStruct((tokens, 4 * size), F32),
        compiler_params=pltpu.CompilerParams(vmem_limit_bytes=KERNEL_VMEM),
        cost_estimate=pl.CostEstimate(
            flops=8 * tokens * size * columns,
            bytes_accessed=8 * size * columns + 2 * tokens * columns,
            transcendentals=0,
        ),
        name="unproject",
    )(base, grad, *weights)


def out_proj_kernel(
    x_ref, mixed_ref, heads_ref, gain_ref, own_ref, others_ref, middle_ref, normed_ref
):
    weights = [own_ref] + [others_ref.at[place] for place in range(3)]
    wide = mixed_ref.shape[1] // 4
    narrow = heads_ref.shape[0] // 4
    middle_ref[...] = x_ref[...].astype(F32)
    for step, weight in zip(NEAR, weights):
        middle_ref[...] += mat(mixed_ref[:, near_at(step, wide)], weight[:wide]) + mat_left_t(
            heads_ref[near_at(step, narrow), :], weight[wide:]
        )
    middle = middle_ref[...]
    normed_ref[...] = (middle * inv_rms(middle) * gain_ref[...]).astype(BF16)


def out_project(x, mixed, heads_t, gain, weights):
    vmem = pl.BlockSpec(memory_space=pltpu.VMEM)
    return pl.pallas_call(
        out_proj_kernel,
        in_specs=[vmem] * 6,
        out_specs=[vmem, vmem],
        out_shape=[jax.ShapeDtypeStruct(x.shape, F32), jax.ShapeDtypeStruct(x.shape, BF16)],
        compiler_params=pltpu.CompilerParams(vmem_limit_bytes=KERNEL_VMEM),
        cost_estimate=pl.CostEstimate(
            flops=2 * x.size * 2048, bytes_accessed=12 * MIB, transcendentals=0
        ),
        name="out_project",
    )(x, mixed, heads_t, gain[None], *weights)


def out_back_kernel(branch_ref, own_ref, others_ref, mixed_ref, heads_ref):
    weights = [own_ref] + [others_ref.at[place] for place in range(3)]
    wide = mixed_ref.shape[1] // 4
    narrow = heads_ref.shape[0] // 4
    for step, weight in zip(NEAR, weights):
        mixed_ref[:, near_at(step, wide)] = mat_right_t(branch_ref[...], weight[:wide])
        heads_ref[near_at(step, narrow), :] = mat_right_t(weight[wide:], branch_ref[...]).astype(
            BF16
        )


def out_unproject(branch, weights, mixed_width, heads_width):
    vmem = pl.BlockSpec(memory_space=pltpu.VMEM)
    tokens = branch.shape[0]
    return pl.pallas_call(
        out_back_kernel,
        in_specs=[vmem] * 3,
        out_specs=[vmem, vmem],
        out_shape=[
            jax.ShapeDtypeStruct((tokens, mixed_width), F32),
            jax.ShapeDtypeStruct((heads_width, tokens), BF16),
        ],
        compiler_params=pltpu.CompilerParams(vmem_limit_bytes=KERNEL_VMEM),
        cost_estimate=pl.CostEstimate(
            flops=2 * branch.size * 2048, bytes_accessed=12 * MIB, transcendentals=0
        ),
        name="out_unproject",
    )(branch, *weights)


FF_TILE = 512


def mlp_kernel(
    place_ref, normed_ref, top_ref, middle_ref, gain_ref, *refs
):
    gates, ups, downs = refs[0:4], refs[4:8], refs[8:12]
    layer_ref, grad_ref, branch_ref, gain_grad_ref, hidden_ref, pair_ref = refs[12:18]
    down_tile, out_sum, back_sum = refs[18:]
    step_at = pl.program_id(0)
    per_piece = pl.num_programs(0) // 4
    size = gates[0].shape[0]
    for piece in range(4):

        @pl.when(step_at // per_piece == piece)
        def _():
            down_tile[...] = downs[piece][...]

    gate = up = None
    for step, gate_ref, up_ref in zip(NEAR, gates, ups):
        rows = normed_ref[:, near_at(step, size)]
        gate_part, up_part = mat(rows, gate_ref[...]), mat(rows, up_ref[...])
        gate = gate_part if gate is None else gate + gate_part
        up = up_part if up is None else up + up_part
    sig = 1.0 / (1.0 + jnp.exp(-gate))
    silu = gate * sig
    hidden = (silu * up).astype(BF16)
    hidden_ref[...] = hidden
    grad_hidden = mat_right_t(top_ref[...], down_tile[...])
    grad_gate = (grad_hidden * up * (sig + silu * (1.0 - sig))).astype(BF16)
    grad_up = (grad_hidden * silu).astype(BF16)
    pair_ref[0] = grad_gate
    pair_ref[1] = grad_up

    @pl.when(step_at == 0)
    def _():
        out_sum[...] = jnp.zeros(out_sum.shape, F32)
        back_sum[...] = jnp.zeros(back_sum.shape, F32)

    out_sum[...] += mat(hidden, down_tile[...])
    for step, gate_ref, up_ref in zip(NEAR, gates, ups):
        back_sum[:, near_at(step, size)] += mat_right_t(grad_gate, gate_ref[...]) + mat_right_t(
            grad_up, up_ref[...]
        )

    @pl.when(step_at == pl.num_programs(0) - 1)
    def _():
        middle = middle_ref[...]
        layer_ref[...] = (middle + out_sum[...]).astype(BF16)
        grad_rows, grad_gain = rms_pull(middle, inv_rms(middle), gain_ref[...], back_sum[...])
        grad = top_ref[...].astype(F32) + grad_rows
        grad_ref[...] = grad
        branch_ref[...] = grad.astype(BF16)
        gain_grad_ref[...] = grad_gain[None]


def mlp_both(place, normed, top, middle, gain, gu_weights, down_weights):
    tokens, features = middle.shape
    size, columns = gu_weights[0].shape
    width = columns // 2
    steps = width // FF_TILE
    per_piece = steps // 4

    def natural(i, p):
        piece = i // per_piece
        near = (piece % 2) * 2 + piece // 2
        return (near ^ p[0]) * per_piece + i % per_piece

    whole = pl.BlockSpec((tokens, features), lambda i, p: (0, 0))
    gain_spec = pl.BlockSpec((1, features), lambda i, p: (0, 0))

    def down_spec(piece):
        return pl.BlockSpec(
            (FF_TILE, features),
            lambda i, p: (jnp.clip(i - piece * per_piece, 0, per_piece - 1), 0),
        )

    return pl.pallas_call(
        mlp_kernel,
        grid_spec=pltpu.PrefetchScalarGridSpec(
            num_scalar_prefetch=1,
            grid=(steps,),
            in_specs=[whole, whole, whole, gain_spec]
            + [pl.BlockSpec((size, FF_TILE), lambda i, p: (0, natural(i, p)))] * 4
            + [pl.BlockSpec((size, FF_TILE), lambda i, p: (0, natural(i, p) + steps))] * 4
            + [down_spec(piece) for piece in range(4)],
            out_specs=[
                whole,
                whole,
                whole,
                gain_spec,
                pl.BlockSpec((tokens, FF_TILE), lambda i, p: (0, natural(i, p))),
                pl.BlockSpec((2, tokens, FF_TILE), lambda i, p: (0, 0, natural(i, p))),
            ],
            scratch_shapes=[
                pltpu.VMEM((FF_TILE, features), BF16),
                pltpu.VMEM((tokens, features), F32),
                pltpu.VMEM((tokens, features), F32),
            ],
        ),
        out_shape=[
            jax.ShapeDtypeStruct((tokens, features), BF16),
            jax.ShapeDtypeStruct((tokens, features), F32),
            jax.ShapeDtypeStruct((tokens, features), BF16),
            jax.ShapeDtypeStruct((1, features), F32),
            jax.ShapeDtypeStruct((tokens, width), BF16),
            jax.ShapeDtypeStruct((2, tokens, width), BF16),
        ],
        compiler_params=pltpu.CompilerParams(vmem_limit_bytes=KERNEL_VMEM),
        cost_estimate=pl.CostEstimate(
            flops=12 * tokens * features * width, bytes_accessed=30 * MIB, transcendentals=0
        ),
        name="mlp_both",
    )(
        place,
        normed,
        top,
        middle,
        gain[None],
        *gu_weights,
        *gu_weights,
        *down_weights,
    )


EDGE = 8
EARLY_TILE = 256


def conv_inputs(edge_rows, own_rows):
    return jnp.concatenate([edge_rows, own_rows], axis=0)


def conv_valid(rel_start, tap, taps):
    rows = rel_start.shape[0]
    place = lax.broadcasted_iota(jnp.int32, (rows, 1), 0)
    return place - (taps - 1) + tap >= rel_start


def conv_sums(extended, weights, bias, rel_start):
    taps = weights.shape[0]
    rows = rel_start.shape[0]
    shifted = []
    total = None
    for tap in range(taps):
        begin = EDGE - (taps - 1) + tap
        part = jnp.where(
            conv_valid(rel_start, tap, taps), extended[begin : begin + rows], 0.0
        )
        shifted.append(part)
        term = weights[tap : tap + 1] * part
        total = bias + term if total is None else total + term
    return total, shifted


def conv_tile_spec(rows, first, last, begin=0):
    return pl.BlockSpec(
        (rows, EARLY_TILE), lambda i: (0, jnp.clip(i - begin + first, first, last))
    )


def conv_back(extended, weights, bias, rel_start, grad_act):
    total, shifted = conv_sums(extended, weights, bias, rel_start)
    gate = sigmoid(total)
    return grad_act * gate * (1.0 + total * (1.0 - gate)), shifted


def edge_grad_kernel(
    dx_ref, db_ref, dc_ref, conv_ref, edge_ref, start_ref, weight_ref, bias_ref, out_ref
):
    taps = weight_ref.shape[0]
    grad_act = jnp.concatenate([dx_ref[...], db_ref[...], dc_ref[...]], axis=1)
    extended = conv_inputs(edge_ref[...], conv_ref[...])
    grad, _ = conv_back(extended, weight_ref[...], bias_ref[...], start_ref[...], grad_act)
    total = jnp.zeros(grad.shape, F32)
    for tap in range(taps):
        part = jnp.where(
            conv_valid(start_ref[...], tap, taps), grad * weight_ref[tap : tap + 1], 0.0
        )
        padded = jnp.concatenate([jnp.zeros(part.shape, F32), part], axis=0)
        total = total + padded[taps - 1 - tap : taps - 1 - tap + EDGE]
    out_ref[...] = total


def edge_grads(count, dx, db, dc, conv_rows, edge_rows, rel_start, conv_weight, conv_bias):
    rows = dx.shape[0] // count
    steps = rows // EDGE

    def first(array):
        return pl.BlockSpec((EDGE, array.shape[1]), lambda b: (b * steps, 0))

    channels = conv_weight.shape[1]
    return pl.pallas_call(
        edge_grad_kernel,
        grid=(count,),
        in_specs=[
            first(dx),
            first(db),
            first(dc),
            first(conv_rows),
            pl.BlockSpec((EDGE, channels), lambda b: (b, 0)),
            first(rel_start),
            pl.BlockSpec(conv_weight.shape, lambda b: (0, 0)),
            pl.BlockSpec((1, channels), lambda b: (0, 0)),
        ],
        out_specs=pl.BlockSpec((EDGE, channels), lambda b: (b, 0)),
        out_shape=jax.ShapeDtypeStruct((count * EDGE, channels), F32),
        compiler_params=pltpu.CompilerParams(vmem_limit_bytes=KERNEL_VMEM),
        cost_estimate=pl.CostEstimate(flops=MIB, bytes_accessed=MIB, transcendentals=0),
        name="edge_grads",
    )(dx, db, dc, conv_rows, edge_rows, rel_start, conv_weight, conv_bias[None])


def early_back_kernel(
    count,
    base_ref,
    kv_ref,
    dx_ref,
    db_ref,
    dc_ref,
    conv_ref,
    edge_ref,
    came_ref,
    dt_ref,
    start_ref,
    weight_ref,
    bias_ref,
    x_ref,
    gain_ref,
    middle_ref,
    *refs,
):
    *blocks, grad_ref, conv_grad_ref, input_ref, gain_grad_ref, total = refs
    size = blocks[0].shape[0]
    tile = pl.program_id(0)
    last = pl.num_programs(0) - 1
    taps = weight_ref.shape[0]

    @pl.when(tile == 0)
    def _():
        total[...] = base_ref[...]
        grad_ref[...] = kv_ref[...]

    @pl.when(tile == last)
    def _():
        grad_ref[...] = dt_ref[...]

    @pl.when((tile > 0) & (tile < last))
    def _():
        rows = dx_ref.shape[0] // count
        tail = jnp.concatenate([db_ref[...], dc_ref[...]], axis=1)
        grad_act = jnp.where(tile == last - 1, tail, dx_ref[...])
        sums = [None] * (taps + 1)
        for b in range(count):
            span = slice(b * rows, (b + 1) * rows)
            ends = slice(b * EDGE, (b + 1) * EDGE)
            extended = conv_inputs(edge_ref[ends], conv_ref[span])
            rel_start = start_ref[span]
            grad, shifted = conv_back(
                extended, weight_ref[...], bias_ref[...], rel_start, grad_act[span]
            )
            back = jnp.concatenate(
                [jnp.zeros((rows - EDGE, grad.shape[1]), F32), came_ref[ends]], axis=0
            )
            for tap in range(taps):
                part = jnp.where(
                    conv_valid(rel_start, tap, taps), grad * weight_ref[tap : tap + 1], 0.0
                )
                padded = jnp.concatenate([part, jnp.zeros((EDGE, part.shape[1]), F32)], axis=0)
                back = back + padded[taps - 1 - tap : taps - 1 - tap + rows]
                term = jnp.sum(grad * shifted[tap], axis=0, keepdims=True)
                sums[tap] = term if sums[tap] is None else sums[tap] + term
            term = jnp.sum(grad, axis=0, keepdims=True)
            sums[taps] = term if sums[taps] is None else sums[taps] + term
            grad_ref[span] = back.astype(BF16)
        conv_grad_ref[0 : taps + 1] = jnp.concatenate(sums, axis=0)
        conv_grad_ref[taps + 1 :] = jnp.zeros(
            (conv_grad_ref.shape[0] - taps - 1, grad_act.shape[1]), F32
        )

    for step, block in zip(NEAR, blocks):
        total[:, near_at(step, size)] += mat_right_t(grad_ref[...], block[...])

    @pl.when(tile == last)
    def _():
        x = x_ref[...].astype(F32)
        grad_rows, grad_gain = rms_pull(x, inv_rms(x), gain_ref[...], total[...])
        input_ref[...] = (middle_ref[...] + grad_rows).astype(BF16)
        gain_grad_ref[...] = grad_gain[None]


def early_back(
    count,
    base,
    grad_kv,
    dx,
    db,
    dc,
    conv_rows,
    edge_rows,
    came,
    dt_grad,
    rel_start,
    conv_weight,
    conv_bias,
    x,
    gain,
    grad_middle,
    own,
    others,
):
    tokens, depth = base.shape
    channels = conv_weight.shape[1]
    tiles = conv_weight.shape[1] // EARLY_TILE + 2
    conv_tiles = channels // EARLY_TILE

    def whole(array):
        return pl.BlockSpec(array.shape, lambda i: (0, 0))

    return pl.pallas_call(
        functools.partial(early_back_kernel, count),
        grid=(tiles,),
        in_specs=[
            whole(base),
            whole(grad_kv),
            conv_tile_spec(tokens, 0, conv_tiles - 2, 1),
            whole(db),
            whole(dc),
            conv_tile_spec(tokens, 0, conv_tiles - 1, 1),
            conv_tile_spec(edge_rows.shape[0], 0, conv_tiles - 1, 1),
            conv_tile_spec(edge_rows.shape[0], 0, conv_tiles - 1, 1),
            whole(dt_grad),
            whole(rel_start),
            conv_tile_spec(conv_weight.shape[0], 0, conv_tiles - 1, 1),
            conv_tile_spec(1, 0, conv_tiles - 1, 1),
            whole(x),
            pl.BlockSpec((1, depth), lambda i: (0, 0)),
            whole(grad_middle),
        ]
        + near_specs(own, EARLY_TILE, DSSM // EARLY_TILE),
        out_specs=[
            pl.BlockSpec((tokens, EARLY_TILE), lambda i: (0, i)),
            conv_tile_spec(8, 0, conv_tiles - 1, 1),
            whole(x),
            pl.BlockSpec((1, depth), lambda i: (0, 0)),
        ],
        out_shape=[
            jax.ShapeDtypeStruct((tokens, tiles * EARLY_TILE), BF16),
            jax.ShapeDtypeStruct((8, channels), F32),
            jax.ShapeDtypeStruct(x.shape, BF16),
            jax.ShapeDtypeStruct((1, depth), F32),
        ],
        scratch_shapes=[pltpu.VMEM((tokens, depth), F32)],
        compiler_params=pltpu.CompilerParams(vmem_limit_bytes=KERNEL_VMEM),
        cost_estimate=pl.CostEstimate(
            flops=2 * tokens * depth * tiles * EARLY_TILE, bytes_accessed=20 * MIB, transcendentals=0
        ),
        name="early_back",
    )(
        base,
        grad_kv,
        dx,
        db,
        dc,
        conv_rows,
        edge_rows,
        came,
        dt_grad,
        rel_start,
        conv_weight,
        conv_bias[None],
        x,
        gain[None],
        grad_middle,
        own,
        others,
        others,
        others,
    )


def block_grads_kernel(steps, left_ref, right_ref, *refs):
    came = refs[0] if len(refs) == 3 else None
    outs = refs[-2:] if came is not None else refs
    size = left_ref.shape[1] // 4
    for place, step in enumerate(steps):
        value = mat_left_t(left_ref[:, near_at(step, size)], right_ref[0])
        if came is None:
            outs[0][place * size : (place + 1) * size] = value.astype(BF16)
        else:
            value = value + came[place * size : (place + 1) * size].astype(F32)
            outs[place][...] = value.astype(BF16)


def block_grads(left, right, steps, came=None):
    tokens, depth = left.shape
    size = depth // 4
    parts, _, width = right.shape
    per_part = width // TILE_COLS
    columns = parts * width
    tall = pl.BlockSpec((2 * size, TILE_COLS), lambda i: (0, i))
    flat = pl.BlockSpec((size, TILE_COLS), lambda i: (0, i))
    operands = [left, right] + ([] if came is None else [came])
    return pl.pallas_call(
        functools.partial(block_grads_kernel, steps),
        grid=(columns // TILE_COLS,),
        in_specs=[
            pl.BlockSpec((tokens, depth), lambda i: (0, 0)),
            pl.BlockSpec((1, tokens, TILE_COLS), lambda i: (i // per_part, 0, i % per_part)),
        ]
        + ([] if came is None else [tall]),
        out_specs=[tall] if came is None else [flat, flat],
        out_shape=[jax.ShapeDtypeStruct((2 * size, columns), BF16)]
        if came is None
        else [jax.ShapeDtypeStruct((size, columns), BF16)] * 2,
        compiler_params=pltpu.CompilerParams(vmem_limit_bytes=KERNEL_VMEM),
        cost_estimate=pl.CostEstimate(
            flops=4 * tokens * size * columns, bytes_accessed=6 * MIB, transcendentals=0
        ),
        name="block_grads",
    )(*operands)


def finish_kernel(
    early_ref, gate_ref, mix_ref, q_low_ref, in_ref, q_ref, kv_ref, out_ref, o_ref
):
    kv_width = kv_ref.shape[1]
    gate = gate_ref.shape[1]
    in_ref[:, :gate] = gate_ref[...].astype(F32)
    in_ref[:, gate:] = early_ref[:, kv_width:].astype(F32)
    q_ref[...] = q_low_ref[...].astype(F32)
    kv_ref[...] = early_ref[:, :kv_width].astype(F32)
    split = out_ref.shape[0]
    out_ref[...] = mix_ref[:split].astype(F32)
    o_ref[...] = mix_ref[split:].astype(F32)


def finish(early, gate, mix, q, shapes):
    vmem = pl.BlockSpec(memory_space=pltpu.VMEM)
    return pl.pallas_call(
        finish_kernel,
        in_specs=[vmem] * 4,
        out_specs=[vmem] * 5,
        out_shape=[jax.ShapeDtypeStruct(shape, F32) for shape in shapes],
        compiler_params=pltpu.CompilerParams(vmem_limit_bytes=KERNEL_VMEM),
        cost_estimate=pl.CostEstimate(flops=MIB, bytes_accessed=10 * MIB, transcendentals=0),
        name="finish",
    )(early, gate, mix, q)


def passed_along(block, axis, distance):
    devices = range(lax.axis_size(axis))
    route = [(i - distance, i) for i in devices if i - distance in devices]
    return lax.ppermute(block, axis, route)


def swapped(block, axis, bit):
    return lax.ppermute(block, axis, [(i, i ^ bit) for i in range(lax.axis_size(axis))])


def bits_of(axis):
    return [1 << k for k in range(lax.axis_size(axis).bit_length() - 1)]


def after(value, earlier):
    return lax.optimization_barrier((value, earlier))[0]


def gathered_near(shard, earlier=None, held=None):
    if earlier is not None:
        shard = after(shard, earlier)
    across = swapped(shard, "wsh", 2)
    if held is not None:
        across = after(across, held)
    return [shard, across, swapped(shard, "wsh", 1), swapped(across, "wsh", 1)]


class Scattering:
    def __init__(self, table, bits):
        self.table = table
        self.bits = list(bits)
        self.start()

    def start(self):
        if self.bits:
            half = self.table.shape[0] // 2
            self.came = swapped(self.table[half:], "ctx", self.bits.pop(0))
        else:
            self.came = None

    def advance(self, held=None):
        if self.came is not None:
            came = self.came if held is None else after(self.came, held)
            half = self.table.shape[0] // 2
            self.table = (self.table[:half].astype(F32) + came.astype(F32)).astype(BF16)
            self.start()
        return self.table

    def finish(self):
        while self.came is not None:
            self.advance()
        return self.table[0]


def ctx_bits(count):
    return [1 << k for k in range(count.bit_length() - 1)]


def partner_wsh(step):
    return (lax.axis_index("ctx"), lax.axis_index("wsh") ^ step)


def partner_ctx(step):
    return (lax.axis_index("ctx") ^ step, lax.axis_index("wsh"))


def remote(source, target, send, recv, device):
    return pltpu.make_async_remote_copy(
        src_ref=source,
        dst_ref=target,
        send_sem=send,
        recv_sem=recv,
        device_id=device,
        device_id_type=pl.DeviceIdType.MESH,
    )


def grads_kernel(
    count,
    split,
    early_units,
    gate_units,
    q_units,
    one_ref,
    mix_ref,
    heads_ref,
    early_ref,
    gate_ref,
    q_ref,
    branch_ref,
    small_ref,
    early_out,
    gate_out,
    q_out,
    mix_out,
    small_out,
    core_out,
    work,
    y_in,
    ctx_in,
    final,
    small_in,
    core_sems,
    y_sems,
    rs_sems,
    ag_sems,
    small_sems,
    out_sems,
):
    bits = ctx_bits(count)
    here = lax.axis_index("ctx")
    units = work.shape[0]
    rows = work.shape[2]
    width = work.shape[3]
    wsh_steps = (1, 2)
    barrier = pltpu.get_barrier_semaphore()
    partners = [partner_wsh(step) for step in wsh_steps] + [partner_ctx(bit) for bit in bits]
    for device in partners:
        pl.semaphore_signal(
            barrier, inc=1, device_id=device, device_id_type=pl.DeviceIdType.MESH
        )
    pl.semaphore_wait(barrier, len(partners))

    sizes = [rows >> (k + 1) for k in range(len(bits))]
    starts = []
    others = []
    base = 0
    for bit, size in zip(bits, sizes):
        upper = (here // bit) % 2
        others.append(base + (1 - upper) * size)
        base = base + upper * size
        starts.append(base)

    def span(start, size):
        return pl.ds(pl.multiple_of(start, 16), size)

    def core_copy(u):
        return remote(
            core_out.at[u % 2],
            work.at[u],
            core_sems.at[0, u],
            core_sems.at[1, u],
            partner_wsh(1),
        )

    def y_copy(u):
        return remote(work.at[u, 1], y_in.at[u], y_sems.at[0, u], y_sems.at[1, u], partner_wsh(2))

    recv_base = [rows - (rows >> k) for k in range(len(bits))]

    def rs_copy(u, k):
        return remote(
            work.at[u, 0, span(others[k], sizes[k])],
            ctx_in.at[u, pl.ds(recv_base[k], sizes[k])],
            rs_sems.at[0, k, u],
            rs_sems.at[1, k, u],
            partner_ctx(bits[k]),
        )

    def ag_copy(u, k):
        return remote(
            final.at[u, span(starts[k], sizes[k])],
            final.at[u, span(starts[k], sizes[k])],
            ag_sems.at[0, k, u],
            ag_sems.at[1, k, u],
            partner_ctx(bits[k]),
        )

    limits = []
    first_unit = 0
    for size in (early_units, gate_units, q_units, 4):
        limits.append((first_unit, first_unit + size))
        first_unit += size
    outs = (early_out, gate_out, q_out, mix_out)

    def by_part(u, action):
        for part, (low, high) in enumerate(limits):
            pl.when((u >= low) & (u < high))(functools.partial(action, part, u - low))

    def each_out(u, act):
        def one(part, v):
            tall = part == 3
            for i in range(split):
                row = (v // 2) * TILE_ROWS if tall else 0
                column = ((v % 2) if tall else v) * TILE_COLS + i * width
                copy = pltpu.make_async_copy(
                    final.at[u, pl.ds(i * TILE_ROWS, TILE_ROWS)],
                    outs[part].at[
                        pl.ds(pl.multiple_of(row, TILE_ROWS), TILE_ROWS),
                        pl.ds(pl.multiple_of(column, 128), width),
                    ],
                    out_sems.at[u, i],
                )
                act(copy)

        by_part(u, one)

    def columns_at(v):
        return pl.ds(pl.multiple_of(v * TILE_COLS, 128), TILE_COLS)

    wide = mix_ref.shape[1] // 4
    narrow = heads_ref.shape[0] // 4

    def pieces(u, first, put):
        steps = NEAR[2 * first : 2 * first + 2]

        def one(part, v):
            for place, step in enumerate(steps):
                if part < 3:
                    left = one_ref[:, near_at(step, TILE_ROWS)]
                    value = mat_left_t(left, (early_ref, gate_ref, q_ref)[part][:, columns_at(v)])
                else:
                    right = branch_ref[:, columns_at(v % 2)]
                    other = lax.axis_index("wsh") ^ step
                    begin = pl.multiple_of(other * wide, 128)

                    @pl.when(v < 2)
                    def _():
                        put(place, mat_left_t(mix_ref[:, pl.ds(begin, TILE_ROWS)], right))

                    @pl.when(v >= 2)
                    def _():
                        tail_at = pl.multiple_of(begin + TILE_ROWS, 128)
                        tail = mat_left_t(mix_ref[:, pl.ds(tail_at, wide - TILE_ROWS)], right)
                        heads_at = pl.multiple_of(other * narrow, 128)
                        heads = mat(heads_ref[pl.ds(heads_at, narrow), :], right)
                        put(place, jnp.concatenate([tail, heads], axis=0))

                    continue
                put(place, value)

        by_part(u, one)

    def chunked(value):
        return [
            (slice(i * TILE_ROWS, (i + 1) * TILE_ROWS), value[:, i * width : (i + 1) * width])
            for i in range(split)
        ]

    def begin(u):
        def put(place, value):
            for where, part in chunked(value):
                core_out[u % 2, place, where] = part.astype(BF16)

        pieces(u, 1, put)
        core_copy(u).start()

    def after_core(u):
        core_copy(u).wait()

        def put(place, value):
            for where, part in chunked(value):
                work[u, place, where] = (work[u, place, where].astype(F32) + part).astype(BF16)

        pieces(u, 0, put)
        y_copy(u).start()

    def after_y(u):
        y_copy(u).wait()
        work[u, 0] = (work[u, 0].astype(F32) + y_in[u].astype(F32)).astype(BF16)
        rs_copy(u, 0).start()

    def after_rs(u, k):
        rs_copy(u, k).wait()
        mine = span(starts[k], sizes[k])
        total = work[u, 0, mine].astype(F32) + ctx_in[
            u, pl.ds(recv_base[k], sizes[k])
        ].astype(F32)
        if k + 1 < len(bits):
            work[u, 0, mine] = total.astype(BF16)
            rs_copy(u, k + 1).start()
        else:
            final[u, mine] = total.astype(BF16)
            ag_copy(u, k).start()

    def after_ag(u, k):
        ag_copy(u, k).wait()
        if k > 0:
            ag_copy(u, k - 1).start()
        else:
            each_out(u, lambda copy: copy.start())

    stages = [(0, begin), (1, after_core), (3, after_y)]
    delay = 3
    for k in range(len(bits)):
        delay += 1
        stages.append((delay, functools.partial(after_rs, k=k)))
    for k in range(len(bits) - 1, -1, -1):
        delay += 1
        stages.append((delay, functools.partial(after_ag, k=k)))

    small_out[...] = small_ref[...]
    hops = partners

    def small_copy(k):
        return remote(
            small_in.at[k, 0], small_in.at[k, 1], small_sems.at[0, k], small_sems.at[1, k], hops[k]
        )

    def small_step(k):
        if k > 0:
            small_copy(k - 1).wait()
            small_out[...] += small_in[k - 1, 1]
        if k < len(hops):
            small_in[k, 0] = small_out[...]
            small_copy(k).start()

    def one_step(t, carry):
        for k in range(len(hops) + 1):
            pl.when(t == 2 * k + 1)(functools.partial(small_step, k))
        for offset, stage in stages[::-1]:
            u = t - offset
            pl.when((u >= 0) & (u < units))(functools.partial(stage, u))
        return carry

    lax.fori_loop(0, units + delay, one_step, 0)

    def finish(u, carry):
        each_out(u, lambda copy: copy.wait())
        return carry

    lax.fori_loop(0, units, finish, 0)


def reduce_grads(
    count, early_width, one, mixed, heads_t, early, gate, q, branch, small
):
    bits = ctx_bits(count)
    hops = len(bits) + 2
    split = max(1, 16 * count // TILE_ROWS)
    early_units = early_width // TILE_COLS
    gate_units = gate.shape[1] // TILE_COLS
    q_units = q.shape[1] // TILE_COLS
    units = early_units + gate_units + q_units + 4
    rows, width = TILE_ROWS * split, TILE_COLS // split
    dma = pltpu.SemaphoreType.DMA
    vmem = pl.BlockSpec(memory_space=pltpu.VMEM)
    hbm = pl.BlockSpec(memory_space=pl.ANY)
    return pl.pallas_call(
        functools.partial(grads_kernel, count, split, early_units, gate_units, q_units),
        in_specs=[vmem] * 8,
        out_specs=[hbm] * 4 + [vmem],
        out_shape=[
            jax.ShapeDtypeStruct((TILE_ROWS, early_units * TILE_COLS), BF16),
            jax.ShapeDtypeStruct((TILE_ROWS, gate_units * TILE_COLS), BF16),
            jax.ShapeDtypeStruct((TILE_ROWS, q_units * TILE_COLS), BF16),
            jax.ShapeDtypeStruct((2 * TILE_ROWS, 2 * TILE_COLS), BF16),
            jax.ShapeDtypeStruct(small.shape, F32),
        ],
        scratch_shapes=[
            pltpu.VMEM((2, 2, rows, width), BF16),
            pltpu.VMEM((units, 2, rows, width), BF16),
            pltpu.VMEM((units, rows, width), BF16),
            pltpu.VMEM((units, rows, width), BF16),
            pltpu.VMEM((units, rows, width), BF16),
            pltpu.VMEM((hops, 2) + small.shape, F32),
            dma((2, units)),
            dma((2, units)),
            dma((2, len(bits), units)),
            dma((2, len(bits), units)),
            dma((2, hops)),
            dma((units, split)),
        ],
        compiler_params=pltpu.CompilerParams(
            collective_id=1, has_side_effects=True, vmem_limit_bytes=KERNEL_VMEM
        ),
        cost_estimate=pl.CostEstimate(
            flops=6_500_000_000, bytes_accessed=30 * MIB, transcendentals=0
        ),
        name="reduce_grads",
    )(one, mixed, heads_t, early, gate, q, branch, small)


def exchange_barrier(devices):
    barrier = pltpu.get_barrier_semaphore()
    for device in devices:
        pl.semaphore_signal(
            barrier, inc=1, device_id=device, device_id_type=pl.DeviceIdType.MESH
        )
    pl.semaphore_wait(barrier, len(devices))


def row_factors(totals, owner):
    rows = owner.shape[0]
    picks = (owner == lax.broadcasted_iota(jnp.int32, (rows, 128), 1)).astype(BF16)
    high = totals.astype(BF16)
    low = (totals - high.astype(F32)).astype(BF16)
    return mat_right_t(picks, high) + mat_right_t(picks, low)


STATE_GROUP = 4


class StateExchange:
    def __init__(self, count, forward, state_ref, totals, result, scratch):
        self.group = min(STATE_GROUP, count)
        self.groups = count // self.group
        self.forward = forward
        self.state_ref, self.totals, self.result = state_ref, totals, result
        (
            self.sent,
            self.came,
            self.before,
            self.back,
            self.whole,
            self.cross,
            self.sems,
            self.cross_sems,
        ) = scratch
        self.place = lax.axis_index("ctx") % self.group
        self.at = lax.axis_index("ctx") // self.group
        self.share = state_ref.shape[1] // self.group

    @staticmethod
    def scratch(count, state):
        group = min(STATE_GROUP, count)
        groups = count // group
        part = (state.shape[0], state.shape[1] // group, STATE)
        return [
            pltpu.VMEM(state.shape, BF16),
            pltpu.VMEM((group,) + part, BF16),
            pltpu.VMEM((group,) + part, F32),
            pltpu.VMEM((group,) + part, BF16),
            pltpu.VMEM(part, BF16),
            pltpu.VMEM((groups,) + part, BF16),
            pltpu.SemaphoreType.DMA((4, group)),
            pltpu.SemaphoreType.DMA((2, groups)),
        ]

    def rows_of(self, place):
        return pl.ds(pl.multiple_of(place * self.share, 16), self.share)

    def deal(self, k, slot):
        return remote(
            self.sent.at[:, self.rows_of(self.place ^ k)],
            self.came.at[slot],
            self.sems.at[0, k],
            self.sems.at[1, k],
            partner_ctx(k),
        )

    def give(self, m, slot):
        return remote(
            self.whole,
            self.cross.at[slot],
            self.cross_sems.at[0, m],
            self.cross_sems.at[1, m],
            partner_ctx(m * self.group),
        )

    def give_back(self, k, slot):
        return remote(
            self.back.at[self.place ^ k],
            self.result.at[:, self.rows_of(slot)],
            self.sems.at[2, k],
            self.sems.at[3, k],
            partner_ctx(k),
        )

    def order(self, count):
        return range(count) if self.forward else range(count - 1, -1, -1)

    def factors(self, blocks):
        part = self.totals[blocks]
        batch = part.shape[1]
        place = lax.broadcasted_iota(jnp.int32, (self.share, 128), 0) + self.place * self.share
        columns = row_factors(part.reshape(-1, 128), place // MDIM)

        def column(block, b):
            at = (block * batch + b) * 8
            return columns[:, at : at + 1]

        return column

    def own_blocks(self):
        return pl.ds(self.at * self.group, self.group)

    def begin(self):
        self.sent[...] = self.state_ref[...].astype(BF16)
        for k in range(1, self.group):
            self.deal(k, self.place).start()
        self.came[self.place] = self.state_ref[:, self.rows_of(self.place), :].astype(BF16)
        self.cross[self.at] = jnp.zeros(self.whole.shape, BF16)

    def middle(self):
        for k in range(1, self.group):
            self.deal(k, self.place).wait_send()
            self.deal(k, self.place ^ k).wait_recv()
        factor_of = self.factors(self.own_blocks())
        for b in range(self.whole.shape[0]):
            total = jnp.zeros((self.share, STATE), F32)
            for j in self.order(self.group):
                self.before[j, b] = total
                total = factor_of(j, b) * total + self.came[j, b].astype(F32)
            self.whole[b] = total.astype(BF16)
        for m in range(1, self.groups):
            self.give(m, self.at).start()

    def carry(self):
        for m in range(1, self.groups):
            self.give(m, self.at).wait_send()
            self.give(m, self.at ^ m).wait_recv()
        factor_of = self.factors(self.own_blocks())
        any_factor = self.factors(slice(None))
        for b in range(self.whole.shape[0]):
            reach = jnp.zeros((self.share, STATE), F32)
            for g in self.order(self.groups):
                decay = None
                for j in range(self.group):
                    one = any_factor(g * self.group + j, b)
                    decay = one if decay is None else decay * one
                earlier = (g < self.at) if self.forward else (g > self.at)
                reach = jnp.where(earlier, decay * reach + self.cross[g, b].astype(F32), reach)
            for j in self.order(self.group):
                self.back[j, b] = (self.before[j, b] + reach).astype(BF16)
                reach = reach * factor_of(j, b)
        for k in range(1, self.group):
            self.give_back(k, self.place).start()
        self.result[:, self.rows_of(self.place), :] = self.back[self.place]

    def end(self):
        for k in range(1, self.group):
            self.give_back(k, self.place).wait_send()
            self.give_back(k, self.place ^ k).wait_recv()


def mix_forward_kernel(
    count,
    start_ref,
    q_ref,
    near_ref,
    state_ref,
    total_ref,
    out_ref,
    log_ref,
    table_out,
    state_out,
    totals_out,
    q_wide,
    top,
    total,
    acc,
    far,
    totals,
    result,
    total_sems,
    table_sems,
    *state_scratch,
):
    here = lax.axis_index("ctx")
    batch = near_ref.shape[1]
    width = near_ref.shape[2]
    half = count // 2
    exchange_barrier([partner_ctx(k) for k in range(1, count)])
    totals[here] = total_ref[...]

    def total_copy(k, place):
        return remote(
            totals.at[here],
            totals.at[place],
            total_sems.at[0, k],
            total_sems.at[1, k],
            partner_ctx(k),
        )

    def table_copy(i):
        return remote(
            near_ref.at[i], far.at[i], table_sems.at[0, i], table_sems.at[1, i], partner_ctx(1)
        )

    for k in range(1, count):
        total_copy(k, here).start()
    states = StateExchange(count, True, state_ref, totals, result, state_scratch)
    states.begin()
    for i in range(half):
        table_copy(i).start()
    for b in range(batch):
        spread_heads(q_ref.at[:, b * width : (b + 1) * width], q_wide.at[b], HDIM**-0.5)
    top[...] = jnp.full(top.shape, MASKED_SCORE, F32)
    total[...] = jnp.zeros(total.shape, F32)
    acc[...] = jnp.zeros(acc.shape, F32)
    first_pos = here * width

    def attend(b, source, i, block):
        kv_rows = source[i, b]
        keys = kv_rows[:, : KVHEADS * HDIM]
        values_t = kv_rows[:, KVHEADS * HDIM :].T
        allowed = attend_allowed(block, first_pos, start_ref[b][:1], width)
        tops, totals_now = top[b], total[b]
        new_tops, new_totals = [], []
        for head in range(QHEADS):
            group = head // (QHEADS // KVHEADS)
            line = slice(head, head + 1)
            scores = mat(keys, q_wide[b, :, head * width : (head + 1) * width])
            scores = jnp.where(allowed, scores, MASKED_SCORE)
            old = tops[line]
            new = jnp.maximum(old, jnp.max(scores, axis=0, keepdims=True))
            terms = jnp.exp(scores - new)
            shrink = jnp.exp(old - new)
            new_tops.append(new)
            new_totals.append(
                totals_now[line] * shrink + jnp.sum(terms, axis=0, keepdims=True)
            )
            acc[b, head] = acc[b, head] * shrink + mat(
                values_t[group * HDIM : (group + 1) * HDIM, :], terms.astype(BF16)
            )
        top[b] = jnp.concatenate(new_tops, axis=0)
        total[b] = jnp.concatenate(new_totals, axis=0)

    bits = ctx_bits(count)
    high = len(bits) - 1

    def step_of(i):
        return sum(((i // (1 << p)) % 2) * (1 << (high - p)) for p in range(high))

    def pair(source, low, begin=0, end=half):
        def one(i, carry):
            if low:
                table_copy(i).wait()
            block = here ^ (step_of(i) + low)

            @pl.when(block <= here)
            def _():
                for b in range(batch):
                    attend(b, source, i, block)

            return carry

        lax.fori_loop(begin, end, one, 0)

    pair(near_ref, 0)
    for k in range(1, count):
        total_copy(k, here).wait_send()
        total_copy(k, here ^ k).wait_recv()
    states.middle()
    pair(far, 1, 0, half // 2)
    states.carry()
    pair(far, 1, half // 2)
    for b in range(batch):
        for head in range(QHEADS):
            out_ref[head * HDIM : (head + 1) * HDIM, b * width : (b + 1) * width] = (
                acc[b, head] / total[b, head : head + 1, :]
            ).astype(BF16)
        log_ref[b] = top[b] + jnp.log(total[b])
    table_out[:half] = near_ref[...]
    table_out[half:] = far[...]
    totals_out[...] = totals[...]
    states.end()
    state_out[...] = result[...]


def mix_forward(count, starts, queries_t, near, state, total):
    half, batch, width, kv_width = near.shape
    vmem = pl.BlockSpec(memory_space=pltpu.VMEM)
    dma = pltpu.SemaphoreType.DMA
    low = functools.partial(jax.ShapeDtypeStruct, dtype=BF16)
    wide = functools.partial(jax.ShapeDtypeStruct, dtype=F32)
    return pl.pallas_call(
        functools.partial(mix_forward_kernel, count),
        in_specs=[vmem] * 5,
        out_specs=[vmem] * 5,
        out_shape=[
            low(queries_t.shape),
            wide((batch, QHEADS, width)),
            low((count,) + near.shape[1:]),
            low(state.shape),
            wide((count,) + total.shape),
        ],
        scratch_shapes=[
            pltpu.VMEM((batch, KVHEADS * HDIM, QHEADS * width), BF16),
            pltpu.VMEM((batch, QHEADS, width), F32),
            pltpu.VMEM((batch, QHEADS, width), F32),
            pltpu.VMEM((batch, QHEADS, HDIM, width), F32),
            pltpu.VMEM(near.shape, BF16),
            pltpu.VMEM((count,) + total.shape, F32),
            pltpu.VMEM(state.shape, BF16),
            dma((2, count)),
            dma((2, half)),
        ]
        + StateExchange.scratch(count, state),
        compiler_params=pltpu.CompilerParams(
            collective_id=2, has_side_effects=True, vmem_limit_bytes=KERNEL_VMEM
        ),
        cost_estimate=pl.CostEstimate(
            flops=batch * count * width * width * 8 * 1000,
            bytes_accessed=4 * MIB,
            transcendentals=0,
        ),
        name="mix_forward",
    )(starts, queries_t, near, state, total)


def mix_backward_kernel(
    count,
    start_ref,
    q_ref,
    table_ref,
    attended_ref,
    grad_ref,
    log_ref,
    state_ref,
    totals_ref,
    dq_ref,
    dkv_ref,
    later_ref,
    q_wide,
    g_wide,
    q_tall,
    g_tall,
    delta,
    acc,
    mine,
    theirs,
    far,
    result,
    table_sems,
    *state_scratch,
):
    here = lax.axis_index("ctx")
    batch = table_ref.shape[1]
    width = table_ref.shape[2]
    half = count // 2
    kv_width = KVHEADS * HDIM
    exchange_barrier([partner_ctx(k) for k in range(1, count)])
    states = StateExchange(count, False, state_ref, totals_ref, result, state_scratch)
    states.begin()
    first_pos = here * width
    acc[...] = jnp.zeros(acc.shape, F32)
    mine[...] = jnp.zeros(mine.shape, BF16)
    theirs[...] = jnp.zeros(theirs.shape, BF16)
    for b in range(batch):
        columns = slice(b * width, (b + 1) * width)
        spread_heads(q_ref.at[:, columns], q_wide.at[b], HDIM**-0.5)
        spread_heads(grad_ref.at[:, columns], g_wide.at[b], 1.0)
        for head in range(QHEADS):
            lanes = slice(head * width, (head + 1) * width)
            q_tall[b, lanes, :] = q_wide[b, :, lanes].T
            g_tall[b, lanes, :] = g_wide[b, :, lanes].T
            span = slice(head * HDIM, (head + 1) * HDIM)
            delta[b, head : head + 1, :] = jnp.sum(
                attended_ref[span, columns].astype(F32) * grad_ref[span, columns].astype(F32),
                axis=0,
                keepdims=True,
            )

    def attend(b, place, block, target, i):
        kv_rows = table_ref[place, b]
        keys = kv_rows[:, :kv_width]
        values = kv_rows[:, kv_width:]
        keys_t = keys.T
        allowed = attend_allowed(block, first_pos, start_ref[b][:1], width)
        logs_now, deltas = log_ref[b], delta[b]
        dk = jnp.zeros((width, kv_width), F32)
        dv = jnp.zeros((width, kv_width), F32)
        for head in range(QHEADS):
            group = head // (QHEADS // KVHEADS)
            lanes = slice(head * width, (head + 1) * width)
            line = slice(head, head + 1)
            scores = mat(keys, q_wide[b, :, lanes])
            shifted = jnp.where(allowed, scores - logs_now[line], MASKED_SCORE)
            probs = jnp.exp(shifted)
            grad_probs = mat(values, g_wide[b, :, lanes])
            grad_scores = (probs * (grad_probs - deltas[line])).astype(BF16)
            dk = dk + mat(grad_scores, q_tall[b, lanes, :])
            dv = dv + mat(probs.astype(BF16), g_tall[b, lanes, :])
            acc[b, head] += mat(keys_t[group * HDIM : (group + 1) * HDIM, :], grad_scores)
        target[i, b] = jnp.concatenate([dk, dv], axis=1).astype(BF16)

    bits = ctx_bits(count)
    high = len(bits) - 1

    def step_of(i):
        return sum(((i // (1 << p)) % 2) * (1 << (high - p)) for p in range(high))

    def pair(target, low, begin=0, end=half):
        def one(i, carry):
            block = here ^ (step_of(i) + low)

            @pl.when(block <= here)
            def _():
                for b in range(batch):
                    attend(b, i + low * half, block, target, i)

            return carry

        lax.fori_loop(begin, end, one, 0)

    def table_copy(i):
        return remote(
            theirs.at[i], far.at[i], table_sems.at[0, i], table_sems.at[1, i], partner_ctx(1)
        )

    pair(theirs, 1, 0, half // 2)
    states.middle()
    pair(theirs, 1, half // 2)
    for i in range(half):
        table_copy(i).start()
    states.carry()
    pair(mine, 0)
    for b in range(batch):
        for head in range(QHEADS):
            dq_ref[head * HDIM : (head + 1) * HDIM, b * width : (b + 1) * width] = (
                acc[b, head] * HDIM**-0.5
            ).astype(BF16)
    for i in range(half):
        table_copy(i).wait()
    dkv_ref[...] = (mine[...].astype(F32) + far[...].astype(F32)).astype(BF16)
    states.end()
    later_ref[...] = result[...]


def mix_backward(count, starts, queries_t, table, attended_t, grad_t, logs, state, totals):
    _, batch, width, kv_width = table.shape
    half = count // 2
    vmem = pl.BlockSpec(memory_space=pltpu.VMEM)
    dma = pltpu.SemaphoreType.DMA
    low = functools.partial(jax.ShapeDtypeStruct, dtype=BF16)
    near = (half, batch, width, kv_width)
    wide = pltpu.VMEM((batch, KVHEADS * HDIM, QHEADS * width), BF16)
    tall = pltpu.VMEM((batch, QHEADS * width, KVHEADS * HDIM), BF16)
    return pl.pallas_call(
        functools.partial(mix_backward_kernel, count),
        in_specs=[vmem] * 8,
        out_specs=[vmem] * 3,
        out_shape=[low(queries_t.shape), low(near), low(state.shape)],
        scratch_shapes=[
            wide,
            wide,
            tall,
            tall,
            pltpu.VMEM((batch, QHEADS, width), F32),
            pltpu.VMEM((batch, QHEADS, HDIM, width), F32),
            pltpu.VMEM(near, BF16),
            pltpu.VMEM(near, BF16),
            pltpu.VMEM(near, BF16),
            pltpu.VMEM(state.shape, BF16),
            dma((2, half)),
        ]
        + StateExchange.scratch(count, state),
        compiler_params=pltpu.CompilerParams(
            collective_id=3, has_side_effects=True, vmem_limit_bytes=KERNEL_VMEM
        ),
        cost_estimate=pl.CostEstimate(
            flops=batch * count * width * width * 8 * 2000,
            bytes_accessed=8 * MIB,
            transcendentals=0,
        ),
        name="mix_backward",
    )(starts, queries_t, table, attended_t, grad_t, logs, state, totals)


def front_kernel(
    count,
    conv_tiles,
    gate_tiles,
    x_ref,
    gain_ref,
    start_ref,
    own_ref,
    tall_ref,
    weight_ref,
    bias_ref,
    normed_ref,
    others_out,
    tall_out,
    conv_out,
    edge_ref,
    act_out,
    dt_ref,
    q_ref,
    gate_out,
    table_ref,
    conv_ref,
    act_ref,
    gate_ref,
    edge_x,
    near,
    tall_near,
    table,
    cross_sems,
    core_sems,
    side_sems,
    last_sems,
    tall_sems,
    table_sems,
    edge_sems,
    out_sems,
):
    here = lax.axis_index("ctx")
    batch = table.shape[1]
    rows = table.shape[2]
    size = own_ref.shape[0]
    chunks = own_ref.shape[1] // EARLY_TILE
    half = count // 2
    exchange_barrier(
        [partner_wsh(1), partner_wsh(2)] + [partner_ctx(k) for k in range(1, count)]
    )
    right = (here + 1) % count

    def edge_copy(b):
        return remote(
            x_ref.at[pl.ds((b + 1) * rows - 16, 16)],
            edge_x.at[b],
            edge_sems.at[0, b],
            edge_sems.at[1, b],
            (right, lax.axis_index("wsh")),
        )

    my_half = pl.ds(pl.multiple_of((here % 2) * (size // 2), 16), size // 2)
    other_half = pl.ds(pl.multiple_of((1 - here % 2) * (size // 2), 16), size // 2)

    def tile(place):
        return pl.ds(pl.multiple_of(place * EARLY_TILE, EARLY_TILE), EARLY_TILE)

    def columns(k):
        return tile((k + gate_tiles) % chunks)

    gate_from = chunks - gate_tiles

    def cross_copy(k):
        return remote(
            own_ref.at[my_half, columns(k)],
            near.at[0, my_half, columns(k)],
            cross_sems.at[0, k],
            cross_sems.at[1, k],
            partner_wsh(2),
        )

    def side_copy(k):
        return remote(
            near.at[0, my_half, columns(k)],
            near.at[0, my_half, columns(k)],
            side_sems.at[0, k],
            side_sems.at[1, k],
            partner_ctx(1),
        )

    def side_in(k):
        return remote(
            near.at[0, other_half, columns(k)],
            near.at[0, other_half, columns(k)],
            side_sems.at[0, k],
            side_sems.at[1, k],
            partner_ctx(1),
        )

    def core_copy(k):
        return remote(
            own_ref.at[:, columns(k)],
            near.at[1, :, columns(k)],
            core_sems.at[0, k],
            core_sems.at[1, k],
            partner_wsh(1),
        )

    def last_copy(k):
        return remote(
            near.at[0, :, columns(k)],
            near.at[2, :, columns(k)],
            last_sems.at[0, k],
            last_sems.at[1, k],
            partner_wsh(1),
        )

    tall_size = tall_ref.shape[0]
    tall_chunks = tall_ref.shape[1] // EARLY_TILE
    tall_mine = pl.ds(pl.multiple_of((here % 2) * (tall_size // 2), 16), tall_size // 2)
    tall_theirs = pl.ds(pl.multiple_of((1 - here % 2) * (tall_size // 2), 16), tall_size // 2)

    def tall_copy(source, target, kind, k, device):
        return remote(
            source, target, tall_sems.at[kind, 0, k], tall_sems.at[kind, 1, k], device
        )

    def tall_cross(k):
        place = tall_near.at[0, tall_mine, tile(k)]
        return tall_copy(tall_ref.at[tall_mine, tile(k)], place, 0, k, partner_wsh(2))

    def tall_core(k):
        place = tall_near.at[1, :, tile(k)]
        return tall_copy(tall_ref.at[:, tile(k)], place, 1, k, partner_wsh(1))

    def tall_side(k, rows_at):
        place = tall_near.at[0, rows_at, tile(k)]
        return tall_copy(place, place, 2, k, partner_ctx(1))

    def tall_last(k):
        place = tall_near.at[2, :, tile(k)]
        return tall_copy(tall_near.at[0, :, tile(k)], place, 3, k, partner_wsh(1))

    def tall_step(j):
        @pl.when((j >= 0) & (j < tall_chunks))
        def _():
            tall_cross(j).wait()
            tall_side(j, tall_mine).start()

        @pl.when((j >= 2) & (j <= tall_chunks + 1))
        def _():
            tall_side(j - 2, tall_mine).wait_send()
            tall_side(j - 2, tall_theirs).wait_recv()
            tall_last(j - 2).start()

    bits = ctx_bits(count)
    high = len(bits) - 1

    def step_of(i):
        return sum(((i >> p) & 1) * (1 << (high - p)) for p in range(high))

    def table_copy(i):
        return remote(
            table.at[0],
            table.at[i],
            table_sems.at[0, i],
            table_sems.at[1, i],
            partner_ctx(step_of(i)),
        )

    def send_first(k, carry):
        cross_copy(k).start()
        core_copy(k).start()
        return carry

    def send_tall(k, carry):
        tall_cross(k).start()
        tall_core(k).start()
        return carry

    lax.fori_loop(0, gate_from, send_first, 0)
    lax.fori_loop(0, tall_chunks, send_tall, 0)
    lax.fori_loop(gate_from, chunks, send_first, 0)
    for b in range(batch):
        edge_copy(b).start()

    def normalized(low):
        wide = low.astype(F32)
        return (wide * inv_rms(wide) * gain_ref[...]).astype(BF16)

    normed_ref[...] = normalized(x_ref[...])
    for b in range(batch):
        edge_copy(b).wait()
    edge_normed = normalized(
        jnp.concatenate([edge_x[b] for b in range(batch)], axis=0)
    )
    edge_x[...] = edge_normed.reshape(edge_x.shape)

    def product(pick, k):
        total = None
        for place, step in enumerate(NEAR):
            block = own_ref[:, columns(k)] if place == 0 else near[place - 1, :, columns(k)]
            part = mat(pick(near_at(step, size)), block)
            total = part if total is None else total + part
        return total

    def others_copy(k):
        return pltpu.make_async_copy(
            near.at[:, :, columns(k)], others_out.at[:, :, columns(k)], out_sems.at[0, k]
        )

    def conv_copy(k):
        return pltpu.make_async_copy(
            conv_ref.at[:, tile(k - 1)], conv_out.at[:, tile(k - 1)], out_sems.at[1, k]
        )

    def act_copy(k):
        return pltpu.make_async_copy(
            act_ref.at[:, tile(k - 1)], act_out.at[:, tile(k - 1)], out_sems.at[2, k]
        )

    def gate_copy(k):
        return pltpu.make_async_copy(
            gate_ref.at[:, tile(k - gate_from)],
            gate_out.at[:, tile(k - gate_from)],
            out_sems.at[1, k],
        )

    def compute(k):
        core_copy(k).wait()
        last_copy(k).wait()
        others_copy(k).start()
        value = product(lambda at: normed_ref[:, at], k)

        @pl.when(k == 0)
        def _():
            table[0] = value.astype(BF16).reshape(table.shape[1:])
            for i in range(1, half):
                table_copy(i).start()

        @pl.when((k > 0) & (k <= conv_tiles))
        def _():
            place = tile(k - 1)
            conv_ref[:, place] = value
            taps = weight_ref[:, place]
            bias = bias_ref[:, place]
            edges = product(lambda at: edge_x[:, :, at].reshape(batch * 16, size), k)
            for b in range(batch):
                edge = edges[(b + 1) * 16 - EDGE : (b + 1) * 16]
                edge_ref[b * EDGE : (b + 1) * EDGE, place] = edge
                span = slice(b * rows, (b + 1) * rows)
                total, _ = conv_sums(
                    conv_inputs(edge, value[span]), taps, bias, start_ref[span]
                )
                act_ref[span, place] = total * sigmoid(total)
            conv_copy(k).start()
            act_copy(k).start()

        @pl.when(k == conv_tiles + 1)
        def _():
            dt_ref[...] = value

        @pl.when((k > conv_tiles + 1) & (k < gate_from))
        def _():
            q_ref[tile(k - conv_tiles - 2), :] = value.T.astype(BF16)

        @pl.when(k >= gate_from)
        def _():
            gate_ref[:, tile(k - gate_from)] = value
            gate_copy(k).start()

    def one_step(t, carry):
        @pl.when(t < chunks)
        def _():
            cross_copy(t).wait()
            side_copy(t).start()

        @pl.when((t >= 2) & (t <= chunks + 1))
        def _():
            side_copy(t - 2).wait_send()
            side_in(t - 2).wait_recv()
            last_copy(t - 2).start()

        tall_step(t - gate_from)
        pl.when(t >= 4)(functools.partial(compute, t - 4))
        return carry

    lax.fori_loop(0, chunks + 4, one_step, 0)
    def end_tall(k, carry):
        tall_core(k).wait()
        tall_last(k).wait()
        return carry

    lax.fori_loop(0, tall_chunks, end_tall, 0)
    whole_tall = pltpu.make_async_copy(tall_near, tall_out, out_sems.at[2, 0])
    whole_tall.start()

    def end_outs(k, carry):
        others_copy(k).wait()

        @pl.when((k > 0) & (k <= conv_tiles))
        def _():
            conv_copy(k).wait()
            act_copy(k).wait()

        @pl.when(k >= gate_from)
        def _():
            gate_copy(k).wait()

        return carry

    lax.fori_loop(0, chunks, end_outs, 0)
    whole_tall.wait()
    for i in range(1, half):
        table_copy(i).wait()
    table_ref[...] = table[...]


def front(count, batch, x, gain, rel_start, own, tall, conv_weight, conv_bias, q_width):
    tokens, depth = x.shape
    size, columns = own.shape
    rows = tokens // batch
    channels = conv_weight.shape[1]
    chunks = columns // EARLY_TILE
    half = count // 2
    vmem = pl.BlockSpec(memory_space=pltpu.VMEM)
    hbm = pl.BlockSpec(memory_space=pl.ANY)
    dma = pltpu.SemaphoreType.DMA
    low = functools.partial(jax.ShapeDtypeStruct, dtype=BF16)
    wide = functools.partial(jax.ShapeDtypeStruct, dtype=F32)
    table = (half, batch, rows, EARLY_TILE)
    return pl.pallas_call(
        functools.partial(
            front_kernel, count, channels // EARLY_TILE, DSSM // EARLY_TILE
        ),
        in_specs=[vmem] * 7,
        out_specs=[vmem, hbm, hbm, hbm, vmem, hbm, vmem, vmem, hbm, vmem],
        out_shape=[
            low((tokens, depth)),
            low((3, size, columns)),
            low((3,) + tall.shape),
            wide((tokens, channels)),
            wide((batch * EDGE, channels)),
            wide((tokens, channels)),
            wide((tokens, EARLY_TILE)),
            low((q_width, tokens)),
            wide((tokens, DSSM)),
            low(table),
        ],
        scratch_shapes=[
            pltpu.VMEM((tokens, channels), F32),
            pltpu.VMEM((tokens, channels), F32),
            pltpu.VMEM((tokens, DSSM), F32),
            pltpu.VMEM((batch, 16, depth), BF16),
            pltpu.VMEM((3, size, columns), BF16),
            pltpu.VMEM((3,) + tall.shape, BF16),
            pltpu.VMEM(table, BF16),
            dma((2, chunks)),
            dma((2, chunks)),
            dma((2, chunks)),
            dma((2, chunks)),
            dma((4, 2, tall.shape[1] // EARLY_TILE)),
            dma((2, half)),
            dma((2, batch)),
            dma((3, chunks)),
        ],
        compiler_params=pltpu.CompilerParams(
            collective_id=4, has_side_effects=True, vmem_limit_bytes=KERNEL_VMEM
        ),
        cost_estimate=pl.CostEstimate(
            flops=2 * tokens * depth * columns, bytes_accessed=20 * MIB, transcendentals=0
        ),
        name="front",
    )(x, gain[None], rel_start, own, tall, conv_weight, conv_bias[None])


def local(
    inputs,
    cotangent,
    lengths,
    norm1_gain,
    in_weight,
    dt_weight,
    conv_weight,
    conv_bias,
    dt_bias,
    decay_rate,
    skip_gain,
    mamba_gain,
    out_weight,
    q_weight,
    kv_weight,
    o_weight,
    norm2_gain,
    gu_weight,
    down_weight,
):
    count, _, rows, features = inputs.shape
    here = lax.axis_index("ctx")
    ctx_count = lax.axis_size("ctx")
    tokens = count * rows
    first_pos = here * rows
    own_pos = first_pos + jnp.arange(rows, dtype=jnp.int32)
    starts = jax.vmap(lambda row: seq_starts(row, own_pos))(lengths[:, 0])
    rel_start = (starts - first_pos).reshape(tokens, 1)
    taps = conv_weight.shape[0]
    channels = conv_weight.shape[1]
    kv_width = kv_weight.shape[1]
    x_low = inputs.reshape(tokens, features)
    grad_top = cotangent.reshape(tokens, features)

    conv_tiles = channels // EARLY_TILE
    gate_tiles = DSSM // EARLY_TILE
    early_shard = jnp.concatenate(
        [
            in_weight[:, :DSSM],
            kv_weight,
            in_weight[:, DSSM:],
            jnp.pad(dt_weight, ((0, 0), (0, EARLY_TILE - dt_weight.shape[1]))),
            q_weight,
        ],
        axis=1,
    )

    outs_own = jnp.concatenate([out_weight, o_weight], axis=0)
    normed, early_others, outs_others, conv_rows, edge_rows, act, dt_rows, queries_t, gate_z, near_table = front(
        ctx_count,
        count,
        x_low,
        norm1_gain,
        rel_start,
        early_shard,
        outs_own,
        conv_weight,
        conv_bias,
        q_weight.shape[1],
    )
    high_bits = bits_of("ctx")[1:]
    later_shards = after(
        (
            gu_weight,
            down_weight,
        ),
        dt_rows,
    )
    crossing = [swapped(shard, "wsh", 2) for shard in later_shards]

    def head_row(values):
        return jnp.pad(values, (0, 128 - MHEADS))[None]

    bias_row, rate_row = head_row(dt_bias), head_row(decay_rate)
    steps, decay, decay_t, to_end, total, fresh = ssd_state(
        count, act, dt_rows, bias_row, rate_row, rel_start
    )
    starts_row = jnp.broadcast_to(starts[:, None, :], (count, 8, rows))
    attended_t, logs, key_table, state_in, totals = mix_forward(
        ctx_count, starts_row, queries_t, near_table, fresh, total
    )

    def near_blocks(which, held):
        shard, across = later_shards[which], after(crossing[which], held)
        return [shard, across, swapped(shard, "wsh", 1), swapped(across, "wsh", 1)]

    outs = (outs_own, outs_others)
    skip_row = jnp.repeat(skip_gain, MDIM)[None]
    scanned = ssd_forward(count, act, steps, decay, decay_t, rel_start, state_in, skip_row)
    gate_sig = jax.nn.sigmoid(gate_z)
    gated = scanned * gate_z * gate_sig
    scale_m = inv_rms(gated)
    mixed = (gated * scale_m * mamba_gain).astype(BF16)
    gu_full, down_full = near_blocks(0, mixed), near_blocks(1, mixed)
    middle, normed_two = out_project(x_low, mixed, attended_t, norm2_gain, outs)

    layer_out, grad_middle, branch, grad_norm2, hidden, grad_pair = mlp_both(
        lax.axis_index("wsh").astype(jnp.int32)[None],
        normed_two,
        grad_top,
        middle,
        norm2_gain,
        gu_full,
        down_full,
    )
    gu_send = block_grads(normed_two, grad_pair, NEAR[2:])[0]
    down_send = block_grads(hidden, grad_top[None], NEAR[2:])[0]
    gu_sent = swapped(gu_send, "wsh", 1)
    down_sent = swapped(down_send, "wsh", 1)
    branch = after(branch, (gu_send, down_send))
    grad_mixed, grad_attended_t = out_unproject(branch, outs, DSSM, QHEADS * HDIM)
    gu_left, down_left = after((normed_two, hidden), grad_attended_t)
    gu_kept, gu_other = block_grads(gu_left, grad_pair, NEAR[:2], gu_sent)
    down_kept, down_other = block_grads(down_left, grad_top[None], NEAR[:2], down_sent)
    gu_crossed = swapped(gu_other, "wsh", 2)
    down_crossed = swapped(down_other, "wsh", 2)

    grad_mixed = after(grad_mixed, (gu_other, down_other))
    grad_gated, grad_mamba = rms_pull(gated, scale_m, mamba_gain, grad_mixed)
    grad_gate_z = grad_gated * scanned * gate_sig * (1.0 + gate_z * (1.0 - gate_sig))
    grad_scanned = grad_gated * gate_z * gate_sig
    grad_state = state_grad(count, grad_scanned, act, decay, rel_start)
    dq_t, dkv_near, later = mix_backward(
        ctx_count,
        starts_row,
        queries_t,
        key_table,
        attended_t,
        grad_attended_t,
        logs,
        grad_state,
        totals,
    )
    key_grads = Scattering(dkv_near, high_bits)

    def total_of(kept, crossed):
        return (kept.astype(F32) + crossed.astype(F32)).astype(BF16)

    held = after((gu_crossed, down_crossed), dq_t)
    parts = total_of(gu_kept, held[0]), total_of(down_kept, held[1])
    grad_gate_z = after(grad_gate_z.astype(BF16), parts)
    dq_rows = dq_t.T
    grad_normed = unproject(
        jnp.zeros((tokens, features), F32),
        grad_gate_z,
        [early_shard] + [early_others] * 3,
        768,
        near_specs(early_shard, 768, 0),
    )
    grad_normed = unproject(
        grad_normed,
        dq_rows,
        [early_shard] + [early_others] * 3,
        EARLY_TILE,
        near_specs(early_shard, EARLY_TILE, gate_tiles + conv_tiles + 2),
    )
    later = after(later, key_grads.advance(grad_normed))
    dx, db, dc, dt_grad, small_ssd = ssd_backward(
        count,
        act,
        steps,
        decay,
        decay_t,
        rel_start,
        state_in,
        skip_row,
        scanned,
        grad_scanned,
        later,
        to_end,
        total,
        dt_rows,
        bias_row,
        rate_row,
    )
    key_grads.advance(dx)
    grad_kv_rows = key_grads.finish().reshape(tokens, -1)
    edge_back = passed_along(
        edge_grads(count, dx, db, dc, conv_rows, edge_rows, rel_start, conv_weight, conv_bias),
        "ctx",
        -1,
    )
    grad_early, conv_grads, input_grad, grad_norm1 = early_back(
        count,
        grad_normed,
        grad_kv_rows,
        dx,
        db,
        dc,
        conv_rows,
        edge_rows,
        edge_back,
        dt_grad,
        rel_start,
        conv_weight,
        conv_bias,
        x_low,
        norm1_gain,
        grad_middle,
        early_shard,
        early_others,
    )
    small_ssd = jnp.sum(small_ssd, axis=0)
    grad_dt_w = mat_left_t(normed, dt_grad[:, :MHEADS])

    gu_sum, down_sum = lax.psum(parts, "ctx")
    pieces = (
        grad_norm1[0],
        conv_grads[:taps],
        conv_grads[taps],
        small_ssd[0, :MHEADS],
        small_ssd[1, :MHEADS],
        small_ssd[2, :MHEADS],
        grad_mamba,
        grad_norm2[0],
        grad_dt_w,
    )
    packed = jnp.concatenate(
        [
            jnp.pad(piece.reshape(-1), (0, -piece.size % 1024)).reshape(-1, 128)
            for piece in pieces
        ],
        axis=0,
    )
    early_sum, gate_sum, q_sum, mix_sum, packed = reduce_grads(
        ctx_count,
        kv_width + channels,
        normed,
        mixed,
        attended_t,
        grad_early,
        grad_gate_z,
        dq_rows,
        branch,
        packed,
    )
    in_sum, q_sum, kv_sum, out_sum, o_sum = finish(
        early_sum,
        gate_sum,
        mix_sum,
        q_sum,
        [w.shape for w in (in_weight, q_weight, kv_weight, out_weight, o_weight)],
    )
    totals_w = [in_sum, out_sum, q_sum, kv_sum, o_sum, gu_sum.astype(F32), down_sum.astype(F32)]
    small = []
    place = 0
    for piece in pieces:
        lines = -(-piece.size // 1024) * 8
        small.append(packed[place : place + lines].reshape(-1)[: piece.size].reshape(piece.shape))
        place += lines
    dt_size = dt_weight.shape[0]
    dt_sum = lax.dynamic_slice_in_dim(small[8], lax.axis_index("wsh") * dt_size, dt_size, 0)
    shape = (count, 1, rows, features)
    return (
        layer_out.reshape(shape),
        input_grad.reshape(shape),
        small[0],
        totals_w[0],
        dt_sum,
        small[1],
        small[2],
        small[3],
        small[4],
        small[5],
        small[6],
        totals_w[1],
        totals_w[2],
        totals_w[3],
        totals_w[4],
        small[7],
        totals_w[5],
        totals_w[6],
    )


def solution(mesh):
    stream = P(None, "wsh", "ctx", None)
    shard = P("wsh", None)
    in_specs = (
        stream,
        stream,
        P(None, "wsh", None),
        P(),
        shard,
        shard,
        P(),
        P(),
        P(),
        P(),
        P(),
        P(),
        shard,
        shard,
        shard,
        shard,
        P(),
        shard,
        shard,
    )
    out_specs = (
        stream,
        stream,
        P(),
        shard,
        shard,
        P(),
        P(),
        P(),
        P(),
        P(),
        P(),
        shard,
        shard,
        shard,
        shard,
        P(),
        shard,
        shard,
    )
    return jax.shard_map(local, mesh=mesh, in_specs=in_specs, out_specs=out_specs, check_vma=False)
```

```python
import functools

import jax
import jax.numpy as jnp
from jax import lax
from jax.experimental import pallas as pl
from jax.experimental.pallas import tpu as pltpu
from jax.sharding import PartitionSpec as P

FF = 2048
MHEADS = 24
MDIM = 64
STATE = 128
QHEADS = 8
KVHEADS = 2
HDIM = 64
DSSM = 1536
HGROUP = 8
NGROUP = MHEADS // HGROUP
GWIDTH = HGROUP * MDIM
PAIR = 2 * MDIM

NORM_EPS = 1e-05
PRECISE = lax.Precision.HIGHEST
MASKED_SCORE = -1e30
MIB = 2**20
KERNEL_VMEM = 60 * MIB
F32 = jnp.float32
BF16 = jnp.bfloat16


def dot_as(left, right, left_dim, right_dim):
    return lax.dot_general(
        left, right, (((left_dim,), (right_dim,)), ((), ())), preferred_element_type=F32
    )


def mat(left, right):
    return dot_as(left, right, 1, 0)


def mat_left_t(left, right):
    return dot_as(left, right, 0, 0)


def mat_right_t(left, right):
    return dot_as(left, right, 1, 1)


def inv_rms(rows):
    return lax.rsqrt(jnp.mean(rows * rows, axis=-1, keepdims=True) + NORM_EPS)


def rms_pull(rows, scale, gain, grad):
    scaled = rows * scale
    grad_gain = jnp.sum(grad * scaled, axis=0)
    through = grad * gain
    inner = jnp.mean(through * scaled, axis=-1, keepdims=True)
    return scale * (through - scaled * inner), grad_gain


def seq_starts(lengths_row, positions):
    begins = jnp.cumsum(lengths_row, dtype=jnp.int32) - lengths_row
    picked = jnp.where(begins[None, :] <= positions[:, None], begins[None, :], 0)
    return jnp.max(picked, axis=1)


def head_lanes(rows):
    return lax.broadcasted_iota(jnp.int32, (rows, PAIR), 1) < MDIM


def masked_products(b_low, c_low, rel_start):
    rows = b_low.shape[0]
    at_row = lax.broadcasted_iota(jnp.int32, (rows, rows), 0)
    at_col = lax.broadcasted_iota(jnp.int32, (rows, rows), 1)
    allowed = (at_col <= at_row) & (at_col >= rel_start)
    return allowed, jnp.where(allowed, mat_right_t(c_low, b_low), 0.0)


def pair_columns(first_half, columns, head):
    return jnp.where(first_half, columns[:, head : head + 1], columns[:, head + 1 : head + 2])


def exact(left, right, left_dim, right_dim):
    return lax.dot_general(
        left,
        right,
        (((left_dim,), (right_dim,)), ((), ())),
        precision=PRECISE,
        preferred_element_type=F32,
    )


def sums_by(values, picks):
    high = values.astype(BF16)
    low = (values - high.astype(F32)).astype(BF16)
    return mat(high, picks) + mat(low, picks)


def lower_ones(rows):
    at_row = lax.broadcasted_iota(jnp.int32, (rows, rows), 0)
    at_col = lax.broadcasted_iota(jnp.int32, (rows, rows), 1)
    return (at_row >= at_col).astype(F32)


def sigmoid(value):
    return 1.0 / (1.0 + jnp.exp(-value))


def softplus(value):
    return jnp.maximum(value, 0.0) + jnp.log1p(jnp.exp(-jnp.abs(value)))


def scaled_rows(target, source_ref, factors):
    first_half = head_lanes(source_ref.shape[0])
    for head in range(0, MHEADS, 2):
        lanes = slice(head * MDIM, head * MDIM + PAIR)
        target[:, lanes] = (
            source_ref[:, lanes] * pair_columns(first_half, factors, head)
        ).astype(BF16)


def ssd_state_kernel(
    act_ref,
    dt_ref,
    bias_ref,
    rate_ref,
    start_ref,
    step_ref,
    decay_ref,
    decay_t_ref,
    end_ref,
    total_ref,
    state_ref,
    scaled,
):
    rows = act_ref.shape[0]
    steps = softplus(dt_ref[:, :128] + bias_ref[...])
    decay = exact(lower_ones(rows), -steps * rate_ref[...], 1, 0)
    rel_start = start_ref[...]
    last_start = rel_start[rows - 1 : rows, :]
    kept = lax.broadcasted_iota(jnp.int32, (rows, 1), 0) >= last_start
    end = decay[rows - 1 : rows, :]
    to_end = jnp.where(kept, jnp.exp(end - decay), 0.0)
    step_ref[...] = steps
    decay_ref[...] = decay
    decay_t_ref[0] = decay.T
    end_ref[...] = to_end
    total_ref[0] = jnp.broadcast_to(jnp.where(last_start < 0, jnp.exp(end), 0.0), (8, 128))
    scaled_rows(scaled, act_ref, to_end * steps)
    state_ref[0] = mat_left_t(scaled[...], act_ref[:, DSSM : DSSM + STATE].astype(BF16))


def row_spec(rows, width, place=0):
    return pl.BlockSpec((rows, width), lambda b: (b, place))


def ssd_state(count, act, dt_rows, bias, rate, rel_start):
    rows = act.shape[0] // count
    lanes = pl.BlockSpec((1, 128), lambda b: (0, 0))
    heads = jax.ShapeDtypeStruct((count * rows, 128), F32)
    return pl.pallas_call(
        ssd_state_kernel,
        grid=(count,),
        in_specs=[
            row_spec(rows, act.shape[1]),
            row_spec(rows, dt_rows.shape[1]),
            lanes,
            lanes,
            row_spec(rows, 1),
        ],
        out_specs=[
            row_spec(rows, 128),
            row_spec(rows, 128),
            pl.BlockSpec((1, 128, rows), lambda b: (b, 0, 0)),
            row_spec(rows, 128),
            pl.BlockSpec((1, 8, 128), lambda b: (b, 0, 0)),
            pl.BlockSpec((1, DSSM, STATE), lambda b: (b, 0, 0)),
        ],
        out_shape=[
            heads,
            heads,
            jax.ShapeDtypeStruct((count, 128, rows), F32),
            heads,
            jax.ShapeDtypeStruct((count, 8, 128), F32),
            jax.ShapeDtypeStruct((count, DSSM, STATE), F32),
        ],
        scratch_shapes=[pltpu.VMEM((rows, DSSM), BF16)],
        compiler_params=pltpu.CompilerParams(vmem_limit_bytes=KERNEL_VMEM),
        cost_estimate=pl.CostEstimate(
            flops=1_000_000_000, bytes_accessed=8 * MIB, transcendentals=0
        ),
        name="ssd_state",
    )(act, dt_rows, bias, rate, rel_start)


def state_grad_kernel(dy_ref, c_ref, decay_ref, start_ref, out_ref, scaled):
    reach = jnp.where(start_ref[...] < 0, jnp.exp(decay_ref[...]), 0.0)
    scaled_rows(scaled, dy_ref, reach)
    out_ref[0] = mat_left_t(scaled[...], c_ref[...].astype(BF16))


def state_grad(count, dy, act, decay, rel_start):
    rows = act.shape[0] // count
    return pl.pallas_call(
        state_grad_kernel,
        grid=(count,),
        in_specs=[
            row_spec(rows, DSSM),
            row_spec(rows, STATE, DSSM // STATE + 1),
            row_spec(rows, 128),
            row_spec(rows, 1),
        ],
        out_specs=pl.BlockSpec((1, DSSM, STATE), lambda b: (b, 0, 0)),
        out_shape=jax.ShapeDtypeStruct((count, DSSM, STATE), F32),
        scratch_shapes=[pltpu.VMEM((rows, DSSM), BF16)],
        compiler_params=pltpu.CompilerParams(vmem_limit_bytes=KERNEL_VMEM),
        cost_estimate=pl.CostEstimate(
            flops=1_000_000_000, bytes_accessed=8 * MIB, transcendentals=0
        ),
        name="state_grad",
    )(dy, act, decay, rel_start)


def group_heads(ref):
    return pltpu.roll(ref[...], (128 - HGROUP * pl.program_id(1)) % 128, 1)


def group_rows(decay_t_ref):
    return decay_t_ref[0, pl.ds(pl.multiple_of(HGROUP * pl.program_id(1), HGROUP), HGROUP), :]


def ssd_forward_kernel(
    x_ref, b_ref, c_ref, step_ref, decay_ref, decay_t_ref, start_ref, state_ref, skip_ref, y_ref
):
    rows = x_ref.shape[0]
    b_low = b_ref[...].astype(BF16)
    c_low = c_ref[...].astype(BF16)
    rel_start = start_ref[...]
    _, products = masked_products(b_low, c_low, rel_start)
    incoming = mat_right_t(c_low, state_ref[0].astype(BF16))
    first_half = head_lanes(rows)
    steps = group_heads(step_ref)
    decay = group_heads(decay_ref)
    decay_t = group_rows(decay_t_ref)
    reach = jnp.where(rel_start < 0, jnp.exp(decay), 0.0)
    for head in range(0, HGROUP, 2):
        lanes = slice(head * MDIM, head * MDIM + PAIR)
        x_pair = x_ref[:, lanes]
        scaled = (x_pair * pair_columns(first_half, steps, head)).astype(BF16)
        parts = []
        for one in (head, head + 1):
            gaps = decay[:, one : one + 1] - decay_t[one : one + 1, :]
            weights = (jnp.exp(jnp.minimum(gaps, 0.0)) * products).astype(BF16)
            parts.append(mat(weights, scaled))
        y_ref[:, lanes] = (
            jnp.where(first_half, parts[0], parts[1])
            + pair_columns(first_half, reach, head) * incoming[:, lanes]
            + skip_ref[:, lanes] * x_pair
        )


def ssd_backward_kernel(
    x_ref,
    b_ref,
    c_ref,
    step_ref,
    decay_ref,
    decay_t_ref,
    start_ref,
    state_ref,
    skip_ref,
    y_ref,
    dy_ref,
    later_ref,
    end_ref,
    total_ref,
    dt_ref,
    bias_ref,
    rate_ref,
    dx_ref,
    db_ref,
    dc_ref,
    dt_grad_ref,
    small_ref,
    one_sum,
    two_sum,
    three_sum,
    mixed_y,
    mixed_x,
    head_sums,
    row_sums,
):
    rows = x_ref.shape[0]
    b_low = b_ref[...].astype(BF16)
    c_low = c_ref[...].astype(BF16)
    rel_start = start_ref[...]
    allowed, products = masked_products(b_low, c_low, rel_start)
    state_low = state_ref[0].astype(BF16)
    later_low = later_ref[0].astype(BF16)
    spread = mat_right_t(b_low, later_low)
    first_half = head_lanes(rows)
    steps = group_heads(step_ref)
    decay = group_heads(decay_ref)
    decay_t = group_rows(decay_t_ref)
    reach = jnp.where(rel_start < 0, jnp.exp(decay), 0.0)
    to_end = group_heads(end_ref) * steps
    product_grad = jnp.zeros((rows, rows), F32)
    skip_parts = []
    for head in range(0, HGROUP, 2):
        lanes = slice(head * MDIM, head * MDIM + PAIR)
        x_pair = x_ref[:, lanes]
        dy_pair = dy_ref[:, lanes]
        step_pair = pair_columns(first_half, steps, head)
        scaled = (x_pair * step_pair).astype(BF16)
        dy_low = dy_pair.astype(BF16)
        parts = []
        for one in (head, head + 1):
            gaps = decay[:, one : one + 1] - decay_t[one : one + 1, :]
            decays = jnp.exp(jnp.minimum(gaps, 0.0))
            mine = first_half if one == head else ~first_half
            dy_mine = jnp.where(mine, dy_pair, 0.0).astype(BF16)
            weight_grad = mat_right_t(dy_mine, scaled)
            product_grad = product_grad + weight_grad * decays
            parts.append(mat_left_t((decays * products).astype(BF16), dy_low))
        dz_pair = jnp.where(first_half, parts[0], parts[1])
        skip_pair = skip_ref[:, lanes]
        end_pair = pair_columns(first_half, to_end, head)
        spread_pair = spread[:, lanes]
        dx_ref[:, lanes] = skip_pair * dy_pair + step_pair * dz_pair + end_pair * spread_pair
        one_sum[:, lanes] = dy_pair * (y_ref[:, lanes] - skip_pair * x_pair)
        two_sum[:, lanes] = x_pair * dz_pair
        three_sum[:, lanes] = x_pair * spread_pair
        mixed_y[:, lanes] = (dy_pair * pair_columns(first_half, reach, head)).astype(BF16)
        mixed_x[:, lanes] = (x_pair * end_pair).astype(BF16)
        skip_parts.append(jnp.sum(dy_pair * x_pair, axis=0, keepdims=True))
    grad_low = jnp.where(allowed, product_grad, 0.0).astype(BF16)
    dc = mat(grad_low, b_low) + mat(mixed_y[...], state_low)
    db = mat_left_t(grad_low, c_low) + mat(mixed_x[...], later_low)
    group = pl.program_id(1)

    @pl.when(group == 0)
    def _():
        dc_ref[...] = jnp.zeros(dc_ref.shape, F32)
        db_ref[...] = jnp.zeros(db_ref.shape, F32)
        head_sums[...] = jnp.zeros(head_sums.shape, F32)
        row_sums[...] = jnp.zeros(row_sums.shape, F32)

    dc_ref[...] += dc
    db_ref[...] += db
    owner = lax.broadcasted_iota(jnp.int32, (GWIDTH, 128), 0) // MDIM + group * HGROUP
    picks = (owner == lax.broadcasted_iota(jnp.int32, (GWIDTH, 128), 1)).astype(BF16)
    for place, source in enumerate((one_sum, two_sum, three_sum)):
        head_sums[place] += sums_by(source[...], picks)
    skips = jnp.broadcast_to(jnp.concatenate(skip_parts, axis=1), (8, GWIDTH))
    row_sums[0] += sums_by(skips, picks)
    meets = exact(
        jnp.ones((8, STATE), F32), later_ref[0].astype(F32) * state_ref[0].astype(F32), 1, 1
    )
    row_sums[1] += sums_by(meets, picks)

    @pl.when(group == pl.num_programs(1) - 1)
    def _():
        all_steps = step_ref[...]
        all_end = end_ref[...]
        rate = rate_ref[...]
        row_dot, u_dot, v_dot = head_sums[0], head_sums[1], head_sums[2]
        to_last = v_dot * all_end * all_steps
        grad_decay = row_dot - u_dot * all_steps - to_last
        at_end = jnp.sum(to_last, axis=0, keepdims=True) + row_sums[1, :1] * total_ref[0, :1]
        grad_drop = exact(lower_ones(rows), grad_decay, 0, 0) + at_end
        grad_steps = u_dot + v_dot * all_end - rate * grad_drop
        grad_dt = grad_steps * sigmoid(dt_ref[:, :128] + bias_ref[...])
        dt_grad_ref[:, :128] = grad_dt.astype(BF16)
        dt_grad_ref[:, 128:] = jnp.zeros((rows, dt_grad_ref.shape[1] - 128), BF16)
        small_ref[0, 0:1] = jnp.sum(grad_dt, axis=0, keepdims=True)
        small_ref[0, 1:2] = jnp.sum(-all_steps * grad_drop, axis=0, keepdims=True)
        small_ref[0, 2:8] = row_sums[0, :6]


def ssd_specs(rows):
    wide = pl.BlockSpec((rows, GWIDTH), lambda b, g: (b, g))
    b_spec = pl.BlockSpec((rows, STATE), lambda b, g: (b, DSSM // STATE))
    c_spec = pl.BlockSpec((rows, STATE), lambda b, g: (b, DSSM // STATE + 1))
    heads = pl.BlockSpec((rows, 128), lambda b, g: (b, 0))
    heads_t = pl.BlockSpec((1, 128, rows), lambda b, g: (b, 0, 0))
    column = pl.BlockSpec((rows, 1), lambda b, g: (b, 0))
    state = pl.BlockSpec((1, GWIDTH, STATE), lambda b, g: (b, g, 0))
    skip = pl.BlockSpec((1, GWIDTH), lambda b, g: (0, g))
    return [wide, b_spec, c_spec, heads, heads, heads_t, column, state, skip]


def ssd_forward(count, act, steps, decay, decay_t, rel_start, state_in, skip_row):
    rows = act.shape[0] // count
    specs = ssd_specs(rows)
    return pl.pallas_call(
        ssd_forward_kernel,
        grid=(count, NGROUP),
        in_specs=specs,
        out_specs=specs[0],
        out_shape=jax.ShapeDtypeStruct((count * rows, DSSM), F32),
        compiler_params=pltpu.CompilerParams(vmem_limit_bytes=KERNEL_VMEM),
        cost_estimate=pl.CostEstimate(
            flops=count * MHEADS * rows * rows * 400, bytes_accessed=8 * MIB, transcendentals=0
        ),
        name="ssd_forward",
    )(act, act, act, steps, decay, decay_t, rel_start, state_in, skip_row)


def ssd_backward(
    count,
    act,
    steps,
    decay,
    decay_t,
    rel_start,
    state_in,
    skip_row,
    scanned,
    grad_scanned,
    later,
    to_end,
    total,
    dt_rows,
    bias,
    rate,
):
    rows = act.shape[0] // count
    specs = ssd_specs(rows)
    wide, heads, state = specs[0], specs[3], specs[7]
    row = pl.BlockSpec((1, 128), lambda b, g: (0, 0))
    packed = pl.BlockSpec((1, 8, 128), lambda b, g: (b, 0, 0))
    narrow = pl.BlockSpec((rows, STATE), lambda b, g: (b, 0))
    dt_spec = pl.BlockSpec((rows, dt_rows.shape[1]), lambda b, g: (b, 0))
    tokens = count * rows
    return pl.pallas_call(
        ssd_backward_kernel,
        grid=(count, NGROUP),
        in_specs=specs + [wide, wide, state, heads, packed, dt_spec, row, row],
        out_specs=[wide, narrow, narrow, dt_spec, packed],
        out_shape=[
            jax.ShapeDtypeStruct((tokens, DSSM), F32),
            jax.ShapeDtypeStruct((tokens, STATE), F32),
            jax.ShapeDtypeStruct((tokens, STATE), F32),
            jax.ShapeDtypeStruct(dt_rows.shape, BF16),
            jax.ShapeDtypeStruct((count, 8, 128), F32),
        ],
        scratch_shapes=[pltpu.VMEM((rows, GWIDTH), F32)] * 3
        + [pltpu.VMEM((rows, GWIDTH), BF16)] * 2
        + [pltpu.VMEM((3, rows, 128), F32), pltpu.VMEM((2, 8, 128), F32)],
        compiler_params=pltpu.CompilerParams(vmem_limit_bytes=KERNEL_VMEM),
        cost_estimate=pl.CostEstimate(
            flops=count * MHEADS * rows * rows * 1000, bytes_accessed=16 * MIB, transcendentals=0
        ),
        name="ssd_backward",
    )(
        act,
        act,
        act,
        steps,
        decay,
        decay_t,
        rel_start,
        state_in,
        skip_row,
        scanned,
        grad_scanned,
        later,
        to_end,
        total,
        dt_rows,
        bias,
        rate,
    )


def spread_heads(source_ref, target, factor):
    width = source_ref.shape[1]
    target[...] = jnp.zeros(target.shape, target.dtype)
    for head in range(QHEADS):
        group = head // (QHEADS // KVHEADS)
        value = source_ref[head * HDIM : (head + 1) * HDIM, :]
        target[group * HDIM : (group + 1) * HDIM, head * width : (head + 1) * width] = (
            value * factor if factor != 1.0 else value
        )


def attend_allowed(block, first_pos, starts, width):
    key_pos = block * width + lax.broadcasted_iota(jnp.int32, (width, width), 0)
    query_pos = first_pos + lax.broadcasted_iota(jnp.int32, (width, width), 1)
    return (key_pos <= query_pos) & (key_pos >= starts)


NEAR = (0, 2, 1, 3)
TILE_ROWS = 256
TILE_COLS = 512


def near_at(step, size):
    return pl.ds(pl.multiple_of((lax.axis_index("wsh") ^ step) * size, 128), size)


def project_kernel(x_ref, *refs):
    *weights, out_ref = refs
    size = weights[0].shape[0]
    total = None
    for step, weight in zip(NEAR, weights):
        part = mat(x_ref[:, near_at(step, size)], weight[...])
        total = part if total is None else total + part
    out_ref[...] = total.astype(out_ref.dtype)


def project(x, weights, tile, kind=F32):
    tokens, depth = x.shape
    size, columns = weights[0].shape
    return pl.pallas_call(
        project_kernel,
        grid=(columns // tile,),
        in_specs=[pl.BlockSpec((tokens, depth), lambda i: (0, 0))]
        + [pl.BlockSpec((size, tile), lambda i: (0, i))] * 4,
        out_specs=pl.BlockSpec((tokens, tile), lambda i: (0, i)),
        out_shape=jax.ShapeDtypeStruct((tokens, columns), kind),
        compiler_params=pltpu.CompilerParams(vmem_limit_bytes=KERNEL_VMEM),
        cost_estimate=pl.CostEstimate(
            flops=2 * tokens * depth * columns,
            bytes_accessed=2 * depth * columns + 4 * tokens * columns,
            transcendentals=0,
        ),
        name="project",
    )(x, *weights)


def near_specs(own, tile, offset):
    size = own.shape[0]
    return [pl.BlockSpec((size, tile), lambda i: (0, i + offset))] + [
        pl.BlockSpec((None, size, tile), lambda i, place=place: (place, 0, i + offset))
        for place in range(3)
    ]


def unproject_kernel(has_base, *refs):
    base_ref = refs[0] if has_base else None
    grad_ref, *weights, out_ref = refs[1:] if has_base else refs
    size = weights[0].shape[0]

    @pl.when(pl.program_id(0) == 0)
    def _():
        out_ref[...] = base_ref[...] if has_base else jnp.zeros(out_ref.shape, F32)

    for step, weight in zip(NEAR, weights):
        out_ref[:, near_at(step, size)] += mat_right_t(grad_ref[...], weight[...])


def unproject(base, grad, weights, tile, specs=None):
    tokens, columns = grad.shape
    size = weights[0].shape[0]
    whole = pl.BlockSpec((tokens, 4 * size), lambda i: (0, 0))
    return pl.pallas_call(
        functools.partial(unproject_kernel, base is not None),
        grid=(columns // tile,),
        in_specs=([] if base is None else [whole])
        + [pl.BlockSpec((tokens, tile), lambda i: (0, i))]
        + (specs or [pl.BlockSpec((size, tile), lambda i: (0, i))] * 4),
        out_specs=whole,
        out_shape=jax.ShapeDtypeStruct((tokens, 4 * size), F32),
        compiler_params=pltpu.CompilerParams(vmem_limit_bytes=KERNEL_VMEM),
        cost_estimate=pl.CostEstimate(
            flops=8 * tokens * size * columns,
            bytes_accessed=8 * size * columns + 2 * tokens * columns,
            transcendentals=0,
        ),
        name="unproject",
    )(*([] if base is None else [base]), grad, *weights)


def out_proj_kernel(
    x_ref, mixed_ref, heads_ref, gain_ref, own_ref, others_ref, middle_ref, normed_ref
):
    weights = [own_ref] + [others_ref.at[place] for place in range(3)]
    wide = mixed_ref.shape[1] // 4
    narrow = heads_ref.shape[0] // 4
    middle_ref[...] = x_ref[...].astype(F32)
    for step, weight in zip(NEAR, weights):
        middle_ref[...] += mat(mixed_ref[:, near_at(step, wide)], weight[:wide]) + mat_left_t(
            heads_ref[near_at(step, narrow), :], weight[wide:]
        )
    middle = middle_ref[...]
    normed_ref[...] = (middle * inv_rms(middle) * gain_ref[...]).astype(BF16)


def out_project(x, mixed, heads_t, gain, weights):
    vmem = pl.BlockSpec(memory_space=pltpu.VMEM)
    return pl.pallas_call(
        out_proj_kernel,
        in_specs=[vmem] * 6,
        out_specs=[vmem, vmem],
        out_shape=[jax.ShapeDtypeStruct(x.shape, F32), jax.ShapeDtypeStruct(x.shape, BF16)],
        compiler_params=pltpu.CompilerParams(vmem_limit_bytes=KERNEL_VMEM),
        cost_estimate=pl.CostEstimate(
            flops=2 * x.size * 2048, bytes_accessed=12 * MIB, transcendentals=0
        ),
        name="out_project",
    )(x, mixed, heads_t, gain[None], *weights)


def out_back_kernel(branch_ref, own_ref, others_ref, mixed_ref, heads_ref):
    weights = [own_ref] + [others_ref.at[place] for place in range(3)]
    wide = mixed_ref.shape[1] // 4
    narrow = heads_ref.shape[0] // 4
    for step, weight in zip(NEAR, weights):
        mixed_ref[:, near_at(step, wide)] = mat_right_t(branch_ref[...], weight[:wide])
        heads_ref[near_at(step, narrow), :] = mat_right_t(weight[wide:], branch_ref[...]).astype(
            BF16
        )


def out_unproject(branch, weights, mixed_width, heads_width):
    vmem = pl.BlockSpec(memory_space=pltpu.VMEM)
    tokens = branch.shape[0]
    return pl.pallas_call(
        out_back_kernel,
        in_specs=[vmem] * 3,
        out_specs=[vmem, vmem],
        out_shape=[
            jax.ShapeDtypeStruct((tokens, mixed_width), F32),
            jax.ShapeDtypeStruct((heads_width, tokens), BF16),
        ],
        compiler_params=pltpu.CompilerParams(vmem_limit_bytes=KERNEL_VMEM),
        cost_estimate=pl.CostEstimate(
            flops=2 * branch.size * 2048, bytes_accessed=12 * MIB, transcendentals=0
        ),
        name="out_unproject",
    )(branch, *weights)


FF_TILE = 512


def mlp_kernel(
    place_ref, normed_ref, top_ref, middle_ref, gain_ref, *refs
):
    gates, ups, downs = refs[0:4], refs[4:8], refs[8:12]
    layer_ref, grad_ref, branch_ref, gain_grad_ref, hidden_ref, pair_ref = refs[12:18]
    down_tile, out_sum, back_sum = refs[18:]
    step_at = pl.program_id(0)
    per_piece = pl.num_programs(0) // 4
    size = gates[0].shape[0]
    for piece in range(4):

        @pl.when(step_at // per_piece == piece)
        def _():
            down_tile[...] = downs[piece][...]

    gate = up = None
    for step, gate_ref, up_ref in zip(NEAR, gates, ups):
        rows = normed_ref[:, near_at(step, size)]
        gate_part, up_part = mat(rows, gate_ref[...]), mat(rows, up_ref[...])
        gate = gate_part if gate is None else gate + gate_part
        up = up_part if up is None else up + up_part
    sig = 1.0 / (1.0 + jnp.exp(-gate))
    silu = gate * sig
    hidden = (silu * up).astype(BF16)
    hidden_ref[...] = hidden
    grad_hidden = mat_right_t(top_ref[...], down_tile[...])
    grad_gate = (grad_hidden * up * (sig + silu * (1.0 - sig))).astype(BF16)
    grad_up = (grad_hidden * silu).astype(BF16)
    pair_ref[0] = grad_gate
    pair_ref[1] = grad_up

    @pl.when(step_at == 0)
    def _():
        out_sum[...] = jnp.zeros(out_sum.shape, F32)
        back_sum[...] = jnp.zeros(back_sum.shape, F32)

    out_sum[...] += mat(hidden, down_tile[...])
    for step, gate_ref, up_ref in zip(NEAR, gates, ups):
        back_sum[:, near_at(step, size)] += mat_right_t(grad_gate, gate_ref[...]) + mat_right_t(
            grad_up, up_ref[...]
        )

    @pl.when(step_at == pl.num_programs(0) - 1)
    def _():
        middle = middle_ref[...]
        layer_ref[...] = (middle + out_sum[...]).astype(BF16)
        grad_rows, grad_gain = rms_pull(middle, inv_rms(middle), gain_ref[...], back_sum[...])
        grad = top_ref[...].astype(F32) + grad_rows
        grad_ref[...] = grad
        branch_ref[...] = grad.astype(BF16)
        gain_grad_ref[...] = grad_gain[None]


def mlp_both(place, normed, top, middle, gain, gu_weights, down_weights):
    tokens, features = middle.shape
    size, columns = gu_weights[0].shape
    width = columns // 2
    steps = width // FF_TILE
    per_piece = steps // 4

    def natural(i, p):
        piece = i // per_piece
        near = (piece % 2) * 2 + piece // 2
        return (near ^ p[0]) * per_piece + i % per_piece

    whole = pl.BlockSpec((tokens, features), lambda i, p: (0, 0))
    gain_spec = pl.BlockSpec((1, features), lambda i, p: (0, 0))

    def down_spec(piece):
        return pl.BlockSpec(
            (FF_TILE, features),
            lambda i, p: (jnp.clip(i - piece * per_piece, 0, per_piece - 1), 0),
        )

    return pl.pallas_call(
        mlp_kernel,
        grid_spec=pltpu.PrefetchScalarGridSpec(
            num_scalar_prefetch=1,
            grid=(steps,),
            in_specs=[whole, whole, whole, gain_spec]
            + [pl.BlockSpec((size, FF_TILE), lambda i, p: (0, natural(i, p)))] * 4
            + [pl.BlockSpec((size, FF_TILE), lambda i, p: (0, natural(i, p) + steps))] * 4
            + [down_spec(piece) for piece in range(4)],
            out_specs=[
                whole,
                whole,
                whole,
                gain_spec,
                pl.BlockSpec((tokens, FF_TILE), lambda i, p: (0, natural(i, p))),
                pl.BlockSpec((2, tokens, FF_TILE), lambda i, p: (0, 0, natural(i, p))),
            ],
            scratch_shapes=[
                pltpu.VMEM((FF_TILE, features), BF16),
                pltpu.VMEM((tokens, features), F32),
                pltpu.VMEM((tokens, features), F32),
            ],
        ),
        out_shape=[
            jax.ShapeDtypeStruct((tokens, features), BF16),
            jax.ShapeDtypeStruct((tokens, features), F32),
            jax.ShapeDtypeStruct((tokens, features), BF16),
            jax.ShapeDtypeStruct((1, features), F32),
            jax.ShapeDtypeStruct((tokens, width), BF16),
            jax.ShapeDtypeStruct((2, tokens, width), BF16),
        ],
        compiler_params=pltpu.CompilerParams(vmem_limit_bytes=KERNEL_VMEM),
        cost_estimate=pl.CostEstimate(
            flops=12 * tokens * features * width, bytes_accessed=30 * MIB, transcendentals=0
        ),
        name="mlp_both",
    )(
        place,
        normed,
        top,
        middle,
        gain[None],
        *gu_weights,
        *gu_weights,
        *down_weights,
    )


EDGE = 8
EARLY_TILE = 256


def conv_inputs(edge_rows, own_rows):
    return jnp.concatenate([edge_rows, own_rows], axis=0)


def conv_valid(rel_start, tap, taps):
    rows = rel_start.shape[0]
    place = lax.broadcasted_iota(jnp.int32, (rows, 1), 0)
    return place - (taps - 1) + tap >= rel_start


def conv_sums(extended, weights, bias, rel_start):
    taps = weights.shape[0]
    rows = rel_start.shape[0]
    shifted = []
    total = None
    for tap in range(taps):
        begin = EDGE - (taps - 1) + tap
        part = jnp.where(
            conv_valid(rel_start, tap, taps), extended[begin : begin + rows], 0.0
        )
        shifted.append(part)
        term = weights[tap : tap + 1] * part
        total = bias + term if total is None else total + term
    return total, shifted


def conv_tile_spec(rows, first, last, begin=0):
    return pl.BlockSpec(
        (rows, EARLY_TILE), lambda i: (0, jnp.clip(i - begin + first, first, last))
    )


def conv_back(extended, weights, bias, rel_start, grad_act):
    total, shifted = conv_sums(extended, weights, bias, rel_start)
    gate = sigmoid(total)
    return grad_act * gate * (1.0 + total * (1.0 - gate)), shifted


def edge_grad_kernel(
    dx_ref, db_ref, dc_ref, conv_ref, edge_ref, start_ref, weight_ref, bias_ref, out_ref
):
    taps = weight_ref.shape[0]
    grad_act = jnp.concatenate([dx_ref[...], db_ref[...], dc_ref[...]], axis=1)
    extended = conv_inputs(edge_ref[...], conv_ref[...])
    grad, _ = conv_back(extended, weight_ref[...], bias_ref[...], start_ref[...], grad_act)
    total = jnp.zeros(grad.shape, F32)
    for tap in range(taps):
        part = jnp.where(
            conv_valid(start_ref[...], tap, taps), grad * weight_ref[tap : tap + 1], 0.0
        )
        padded = jnp.concatenate([jnp.zeros(part.shape, F32), part], axis=0)
        total = total + padded[taps - 1 - tap : taps - 1 - tap + EDGE]
    out_ref[...] = total


def edge_grads(count, dx, db, dc, conv_rows, edge_rows, rel_start, conv_weight, conv_bias):
    rows = dx.shape[0] // count
    steps = rows // EDGE

    def first(array):
        return pl.BlockSpec((EDGE, array.shape[1]), lambda b: (b * steps, 0))

    channels = conv_weight.shape[1]
    return pl.pallas_call(
        edge_grad_kernel,
        grid=(count,),
        in_specs=[
            first(dx),
            first(db),
            first(dc),
            first(conv_rows),
            pl.BlockSpec((EDGE, channels), lambda b: (b, 0)),
            first(rel_start),
            pl.BlockSpec(conv_weight.shape, lambda b: (0, 0)),
            pl.BlockSpec((1, channels), lambda b: (0, 0)),
        ],
        out_specs=pl.BlockSpec((EDGE, channels), lambda b: (b, 0)),
        out_shape=jax.ShapeDtypeStruct((count * EDGE, channels), F32),
        compiler_params=pltpu.CompilerParams(vmem_limit_bytes=KERNEL_VMEM),
        cost_estimate=pl.CostEstimate(flops=MIB, bytes_accessed=MIB, transcendentals=0),
        name="edge_grads",
    )(dx, db, dc, conv_rows, edge_rows, rel_start, conv_weight, conv_bias[None])


def early_back_kernel(
    count,
    base_ref,
    kv_ref,
    dx_ref,
    db_ref,
    dc_ref,
    conv_ref,
    edge_ref,
    came_ref,
    dt_ref,
    start_ref,
    weight_ref,
    bias_ref,
    x_ref,
    gain_ref,
    middle_ref,
    *refs,
):
    *blocks, grad_ref, conv_grad_ref, input_ref, gain_grad_ref, total = refs
    size = blocks[0].shape[0]
    tile = pl.program_id(0)
    last = pl.num_programs(0) - 1
    taps = weight_ref.shape[0]

    @pl.when(tile == 0)
    def _():
        total[...] = base_ref[...]
        grad_ref[...] = kv_ref[...]

    @pl.when(tile == last)
    def _():
        grad_ref[...] = dt_ref[...]

    @pl.when((tile > 0) & (tile < last))
    def _():
        rows = dx_ref.shape[0] // count
        tail = jnp.concatenate([db_ref[...], dc_ref[...]], axis=1)
        grad_act = jnp.where(tile == last - 1, tail, dx_ref[...])
        sums = [None] * (taps + 1)
        for b in range(count):
            span = slice(b * rows, (b + 1) * rows)
            ends = slice(b * EDGE, (b + 1) * EDGE)
            extended = conv_inputs(edge_ref[ends], conv_ref[span])
            rel_start = start_ref[span]
            grad, shifted = conv_back(
                extended, weight_ref[...], bias_ref[...], rel_start, grad_act[span]
            )
            back = jnp.concatenate(
                [jnp.zeros((rows - EDGE, grad.shape[1]), F32), came_ref[ends]], axis=0
            )
            for tap in range(taps):
                part = jnp.where(
                    conv_valid(rel_start, tap, taps), grad * weight_ref[tap : tap + 1], 0.0
                )
                padded = jnp.concatenate([part, jnp.zeros((EDGE, part.shape[1]), F32)], axis=0)
                back = back + padded[taps - 1 - tap : taps - 1 - tap + rows]
                term = jnp.sum(grad * shifted[tap], axis=0, keepdims=True)
                sums[tap] = term if sums[tap] is None else sums[tap] + term
            term = jnp.sum(grad, axis=0, keepdims=True)
            sums[taps] = term if sums[taps] is None else sums[taps] + term
            grad_ref[span] = back.astype(BF16)
        conv_grad_ref[0 : taps + 1] = jnp.concatenate(sums, axis=0)
        conv_grad_ref[taps + 1 :] = jnp.zeros(
            (conv_grad_ref.shape[0] - taps - 1, grad_act.shape[1]), F32
        )

    for step, block in zip(NEAR, blocks):
        total[:, near_at(step, size)] += mat_right_t(grad_ref[...], block[...])

    @pl.when(tile == last)
    def _():
        x = x_ref[...].astype(F32)
        grad_rows, grad_gain = rms_pull(x, inv_rms(x), gain_ref[...], total[...])
        input_ref[...] = (middle_ref[...] + grad_rows).astype(BF16)
        gain_grad_ref[...] = grad_gain[None]


def early_back(
    count,
    base,
    grad_kv,
    dx,
    db,
    dc,
    conv_rows,
    edge_rows,
    came,
    dt_grad,
    rel_start,
    conv_weight,
    conv_bias,
    x,
    gain,
    grad_middle,
    own,
    others,
):
    tokens, depth = base.shape
    channels = conv_weight.shape[1]
    tiles = conv_weight.shape[1] // EARLY_TILE + 2
    conv_tiles = channels // EARLY_TILE

    def whole(array):
        return pl.BlockSpec(array.shape, lambda i: (0, 0))

    return pl.pallas_call(
        functools.partial(early_back_kernel, count),
        grid=(tiles,),
        in_specs=[
            whole(base),
            whole(grad_kv),
            conv_tile_spec(tokens, 0, conv_tiles - 2, 1),
            whole(db),
            whole(dc),
            conv_tile_spec(tokens, 0, conv_tiles - 1, 1),
            conv_tile_spec(edge_rows.shape[0], 0, conv_tiles - 1, 1),
            conv_tile_spec(edge_rows.shape[0], 0, conv_tiles - 1, 1),
            whole(dt_grad),
            whole(rel_start),
            conv_tile_spec(conv_weight.shape[0], 0, conv_tiles - 1, 1),
            conv_tile_spec(1, 0, conv_tiles - 1, 1),
            whole(x),
            pl.BlockSpec((1, depth), lambda i: (0, 0)),
            whole(grad_middle),
        ]
        + near_specs(own, EARLY_TILE, DSSM // EARLY_TILE),
        out_specs=[
            pl.BlockSpec((tokens, EARLY_TILE), lambda i: (0, i)),
            conv_tile_spec(8, 0, conv_tiles - 1, 1),
            whole(x),
            pl.BlockSpec((1, depth), lambda i: (0, 0)),
        ],
        out_shape=[
            jax.ShapeDtypeStruct((tokens, tiles * EARLY_TILE), BF16),
            jax.ShapeDtypeStruct((8, channels), F32),
            jax.ShapeDtypeStruct(x.shape, BF16),
            jax.ShapeDtypeStruct((1, depth), F32),
        ],
        scratch_shapes=[pltpu.VMEM((tokens, depth), F32)],
        compiler_params=pltpu.CompilerParams(vmem_limit_bytes=KERNEL_VMEM),
        cost_estimate=pl.CostEstimate(
            flops=2 * tokens * depth * tiles * EARLY_TILE, bytes_accessed=20 * MIB, transcendentals=0
        ),
        name="early_back",
    )(
        base,
        grad_kv,
        dx,
        db,
        dc,
        conv_rows,
        edge_rows,
        came,
        dt_grad,
        rel_start,
        conv_weight,
        conv_bias[None],
        x,
        gain[None],
        grad_middle,
        own,
        others,
        others,
        others,
    )


def block_grads_kernel(steps, left_ref, right_ref, *refs):
    came = refs[0] if len(refs) == 3 else None
    outs = refs[-2:] if came is not None else refs
    size = left_ref.shape[1] // 4
    for place, step in enumerate(steps):
        value = mat_left_t(left_ref[:, near_at(step, size)], right_ref[0])
        if came is None:
            outs[0][place * size : (place + 1) * size] = value.astype(BF16)
        else:
            value = value + came[place * size : (place + 1) * size].astype(F32)
            outs[place][...] = value.astype(BF16)


def block_grads(left, right, steps, came=None):
    tokens, depth = left.shape
    size = depth // 4
    parts, _, width = right.shape
    per_part = width // TILE_COLS
    columns = parts * width
    tall = pl.BlockSpec((2 * size, TILE_COLS), lambda i: (0, i))
    flat = pl.BlockSpec((size, TILE_COLS), lambda i: (0, i))
    operands = [left, right] + ([] if came is None else [came])
    return pl.pallas_call(
        functools.partial(block_grads_kernel, steps),
        grid=(columns // TILE_COLS,),
        in_specs=[
            pl.BlockSpec((tokens, depth), lambda i: (0, 0)),
            pl.BlockSpec((1, tokens, TILE_COLS), lambda i: (i // per_part, 0, i % per_part)),
        ]
        + ([] if came is None else [tall]),
        out_specs=[tall] if came is None else [flat, flat],
        out_shape=[jax.ShapeDtypeStruct((2 * size, columns), BF16)]
        if came is None
        else [jax.ShapeDtypeStruct((size, columns), BF16)] * 2,
        compiler_params=pltpu.CompilerParams(vmem_limit_bytes=KERNEL_VMEM),
        cost_estimate=pl.CostEstimate(
            flops=4 * tokens * size * columns, bytes_accessed=6 * MIB, transcendentals=0
        ),
        name="block_grads",
    )(*operands)


def finish_kernel(
    early_ref,
    gate_ref,
    out_low,
    o_low,
    q_low,
    gu_low,
    down_low,
    in_ref,
    q_ref,
    kv_ref,
    out_ref,
    o_ref,
    gu_ref,
    down_ref,
):
    kv_width = kv_ref.shape[1]
    gate = gate_ref.shape[1]
    in_ref[:, :gate] = gate_ref[...].astype(F32)
    in_ref[:, gate:] = early_ref[:, kv_width:].astype(F32)
    kv_ref[...] = early_ref[:, :kv_width].astype(F32)
    for low, target in (
        (q_low, q_ref),
        (out_low, out_ref),
        (o_low, o_ref),
        (gu_low, gu_ref),
        (down_low, down_ref),
    ):
        target[...] = low[...].astype(F32)


FINISH_STEPS = 4


def finish(early, gate, mix, q, gu, down, shapes):
    def rows_of(shape, skip=0):
        size = shape[0] // FINISH_STEPS
        return pl.BlockSpec((size, shape[1]), lambda i: (skip // size + i, 0))

    out_shape, o_shape = shapes[3], shapes[4]
    return pl.pallas_call(
        finish_kernel,
        grid=(FINISH_STEPS,),
        in_specs=[
            rows_of(early.shape),
            rows_of(gate.shape),
            rows_of(out_shape),
            rows_of(o_shape, out_shape[0]),
            rows_of(q.shape),
            rows_of(gu.shape),
            rows_of(down.shape),
        ],
        out_specs=[rows_of(shape) for shape in shapes],
        out_shape=[jax.ShapeDtypeStruct(shape, F32) for shape in shapes],
        compiler_params=pltpu.CompilerParams(vmem_limit_bytes=KERNEL_VMEM),
        cost_estimate=pl.CostEstimate(flops=MIB, bytes_accessed=20 * MIB, transcendentals=0),
        name="finish",
    )(early, gate, mix, mix, q, gu, down)


def passed_along(block, axis, distance):
    devices = range(lax.axis_size(axis))
    route = [(i - distance, i) for i in devices if i - distance in devices]
    return lax.ppermute(block, axis, route)


def swapped(block, axis, bit):
    return lax.ppermute(block, axis, [(i, i ^ bit) for i in range(lax.axis_size(axis))])


def bits_of(axis):
    return [1 << k for k in range(lax.axis_size(axis).bit_length() - 1)]


def after(value, earlier):
    return lax.optimization_barrier((value, earlier))[0]


def gathered_near(shard, earlier=None, held=None):
    if earlier is not None:
        shard = after(shard, earlier)
    across = swapped(shard, "wsh", 2)
    if held is not None:
        across = after(across, held)
    return [shard, across, swapped(shard, "wsh", 1), swapped(across, "wsh", 1)]


class Scattering:
    def __init__(self, table, bits):
        self.table = table
        self.bits = list(bits)
        self.start()

    def start(self):
        if self.bits:
            half = self.table.shape[0] // 2
            self.came = swapped(self.table[half:], "ctx", self.bits.pop(0))
        else:
            self.came = None

    def advance(self, held=None):
        if self.came is not None:
            came = self.came if held is None else after(self.came, held)
            half = self.table.shape[0] // 2
            self.table = (self.table[:half].astype(F32) + came.astype(F32)).astype(BF16)
            self.start()
        return self.table

    def finish(self):
        while self.came is not None:
            self.advance()
        return self.table[0]


def ctx_bits(count):
    return [1 << k for k in range(count.bit_length() - 1)]


def partner_wsh(step):
    return (lax.axis_index("ctx"), lax.axis_index("wsh") ^ step)


def partner_ctx(step):
    return (lax.axis_index("ctx") ^ step, lax.axis_index("wsh"))


def remote(source, target, send, recv, device):
    return pltpu.make_async_remote_copy(
        src_ref=source,
        dst_ref=target,
        send_sem=send,
        recv_sem=recv,
        device_id=device,
        device_id_type=pl.DeviceIdType.MESH,
    )


def grads_kernel(
    count,
    split,
    early_units,
    gate_units,
    q_units,
    one_ref,
    mix_ref,
    heads_ref,
    early_ref,
    gate_ref,
    q_ref,
    branch_ref,
    small_ref,
    early_out,
    gate_out,
    q_out,
    mix_out,
    small_out,
    core_out,
    work,
    y_in,
    ctx_in,
    final,
    small_in,
    core_sems,
    y_sems,
    rs_sems,
    ag_sems,
    small_sems,
    out_sems,
):
    bits = ctx_bits(count)
    here = lax.axis_index("ctx")
    units = work.shape[0]
    rows = work.shape[2]
    width = work.shape[3]
    wsh_steps = (1, 2)
    barrier = pltpu.get_barrier_semaphore()
    partners = [partner_wsh(step) for step in wsh_steps] + [partner_ctx(bit) for bit in bits]
    for device in partners:
        pl.semaphore_signal(
            barrier, inc=1, device_id=device, device_id_type=pl.DeviceIdType.MESH
        )
    pl.semaphore_wait(barrier, len(partners))

    sizes = [rows >> (k + 1) for k in range(len(bits))]
    starts = []
    others = []
    base = 0
    for bit, size in zip(bits, sizes):
        upper = (here // bit) % 2
        others.append(base + (1 - upper) * size)
        base = base + upper * size
        starts.append(base)

    def span(start, size):
        return pl.ds(pl.multiple_of(start, 16), size)

    def core_copy(u):
        return remote(
            core_out.at[u % 2],
            work.at[u],
            core_sems.at[0, u],
            core_sems.at[1, u],
            partner_wsh(1),
        )

    def y_copy(u):
        return remote(work.at[u, 1], y_in.at[u], y_sems.at[0, u], y_sems.at[1, u], partner_wsh(2))

    recv_base = [rows - (rows >> k) for k in range(len(bits))]

    def rs_copy(u, k):
        return remote(
            work.at[u, 0, span(others[k], sizes[k])],
            ctx_in.at[u, pl.ds(recv_base[k], sizes[k])],
            rs_sems.at[0, k, u],
            rs_sems.at[1, k, u],
            partner_ctx(bits[k]),
        )

    def ag_copy(u, k):
        return remote(
            final.at[u, span(starts[k], sizes[k])],
            final.at[u, span(starts[k], sizes[k])],
            ag_sems.at[0, k, u],
            ag_sems.at[1, k, u],
            partner_ctx(bits[k]),
        )

    limits = []
    first_unit = 0
    for size in (early_units, gate_units, q_units, 4):
        limits.append((first_unit, first_unit + size))
        first_unit += size
    outs = (early_out, gate_out, q_out, mix_out)

    def by_part(u, action):
        for part, (low, high) in enumerate(limits):
            pl.when((u >= low) & (u < high))(functools.partial(action, part, u - low))

    def each_out(u, act):
        def one(part, v):
            tall = part == 3
            for i in range(split):
                row = (v // 2) * TILE_ROWS if tall else 0
                column = ((v % 2) if tall else v) * TILE_COLS + i * width
                copy = pltpu.make_async_copy(
                    final.at[u, pl.ds(i * TILE_ROWS, TILE_ROWS)],
                    outs[part].at[
                        pl.ds(pl.multiple_of(row, TILE_ROWS), TILE_ROWS),
                        pl.ds(pl.multiple_of(column, 128), width),
                    ],
                    out_sems.at[u, i],
                )
                act(copy)

        by_part(u, one)

    def columns_at(v):
        return pl.ds(pl.multiple_of(v * TILE_COLS, 128), TILE_COLS)

    wide = mix_ref.shape[1] // 4
    narrow = heads_ref.shape[0] // 4

    def pieces(u, first, put):
        steps = NEAR[2 * first : 2 * first + 2]

        def one(part, v):
            for place, step in enumerate(steps):
                if part < 3:
                    left = one_ref[:, near_at(step, TILE_ROWS)]
                    value = mat_left_t(left, (early_ref, gate_ref, q_ref)[part][:, columns_at(v)])
                else:
                    right = branch_ref[:, columns_at(v % 2)]
                    other = lax.axis_index("wsh") ^ step
                    begin = pl.multiple_of(other * wide, 128)

                    @pl.when(v < 2)
                    def _():
                        put(place, mat_left_t(mix_ref[:, pl.ds(begin, TILE_ROWS)], right))

                    @pl.when(v >= 2)
                    def _():
                        tail_at = pl.multiple_of(begin + TILE_ROWS, 128)
                        tail = mat_left_t(mix_ref[:, pl.ds(tail_at, wide - TILE_ROWS)], right)
                        heads_at = pl.multiple_of(other * narrow, 128)
                        heads = mat(heads_ref[pl.ds(heads_at, narrow), :], right)
                        put(place, jnp.concatenate([tail, heads], axis=0))

                    continue
                put(place, value)

        by_part(u, one)

    def chunked(value):
        return [
            (slice(i * TILE_ROWS, (i + 1) * TILE_ROWS), value[:, i * width : (i + 1) * width])
            for i in range(split)
        ]

    def begin(u):
        def put(place, value):
            for where, part in chunked(value):
                core_out[u % 2, place, where] = part.astype(BF16)

        pieces(u, 1, put)
        core_copy(u).start()

    def after_core(u):
        core_copy(u).wait()

        def put(place, value):
            for where, part in chunked(value):
                work[u, place, where] = (work[u, place, where].astype(F32) + part).astype(BF16)

        pieces(u, 0, put)
        y_copy(u).start()

    def after_y(u):
        y_copy(u).wait()
        work[u, 0] = (work[u, 0].astype(F32) + y_in[u].astype(F32)).astype(BF16)
        rs_copy(u, 0).start()

    def after_rs(u, k):
        rs_copy(u, k).wait()
        mine = span(starts[k], sizes[k])
        total = work[u, 0, mine].astype(F32) + ctx_in[
            u, pl.ds(recv_base[k], sizes[k])
        ].astype(F32)
        if k + 1 < len(bits):
            work[u, 0, mine] = total.astype(BF16)
            rs_copy(u, k + 1).start()
        else:
            final[u, mine] = total.astype(BF16)
            ag_copy(u, k).start()

    def after_ag(u, k):
        ag_copy(u, k).wait()
        if k > 0:
            ag_copy(u, k - 1).start()
        else:
            each_out(u, lambda copy: copy.start())

    stages = [(0, begin), (1, after_core), (3, after_y)]
    delay = 3
    for k in range(len(bits)):
        delay += 1
        stages.append((delay, functools.partial(after_rs, k=k)))
    for k in range(len(bits) - 1, -1, -1):
        delay += 1
        stages.append((delay, functools.partial(after_ag, k=k)))

    small_out[...] = small_ref[...]
    hops = partners

    def small_copy(k):
        return remote(
            small_in.at[k, 0], small_in.at[k, 1], small_sems.at[0, k], small_sems.at[1, k], hops[k]
        )

    def small_step(k):
        if k > 0:
            small_copy(k - 1).wait()
            small_out[...] += small_in[k - 1, 1]
        if k < len(hops):
            small_in[k, 0] = small_out[...]
            small_copy(k).start()

    def one_step(t, carry):
        for k in range(len(hops) + 1):
            pl.when(t == 2 * k + 1)(functools.partial(small_step, k))
        for offset, stage in stages[::-1]:
            u = t - offset
            pl.when((u >= 0) & (u < units))(functools.partial(stage, u))
        return carry

    lax.fori_loop(0, units + delay, one_step, 0)

    def finish(u, carry):
        each_out(u, lambda copy: copy.wait())
        return carry

    lax.fori_loop(0, units, finish, 0)


def reduce_grads(
    count, early_width, one, mixed, heads_t, early, gate, q, branch, small
):
    bits = ctx_bits(count)
    hops = len(bits) + 2
    split = max(1, 16 * count // TILE_ROWS)
    early_units = early_width // TILE_COLS
    gate_units = gate.shape[1] // TILE_COLS
    q_units = q.shape[1] // TILE_COLS
    units = early_units + gate_units + q_units + 4
    rows, width = TILE_ROWS * split, TILE_COLS // split
    dma = pltpu.SemaphoreType.DMA
    vmem = pl.BlockSpec(memory_space=pltpu.VMEM)
    hbm = pl.BlockSpec(memory_space=pl.ANY)
    return pl.pallas_call(
        functools.partial(grads_kernel, count, split, early_units, gate_units, q_units),
        in_specs=[vmem] * 8,
        out_specs=[hbm] * 4 + [vmem],
        out_shape=[
            jax.ShapeDtypeStruct((TILE_ROWS, early_units * TILE_COLS), BF16),
            jax.ShapeDtypeStruct((TILE_ROWS, gate_units * TILE_COLS), BF16),
            jax.ShapeDtypeStruct((TILE_ROWS, q_units * TILE_COLS), BF16),
            jax.ShapeDtypeStruct((2 * TILE_ROWS, 2 * TILE_COLS), BF16),
            jax.ShapeDtypeStruct(small.shape, F32),
        ],
        scratch_shapes=[
            pltpu.VMEM((2, 2, rows, width), BF16),
            pltpu.VMEM((units, 2, rows, width), BF16),
            pltpu.VMEM((units, rows, width), BF16),
            pltpu.VMEM((units, rows, width), BF16),
            pltpu.VMEM((units, rows, width), BF16),
            pltpu.VMEM((hops, 2) + small.shape, F32),
            dma((2, units)),
            dma((2, units)),
            dma((2, len(bits), units)),
            dma((2, len(bits), units)),
            dma((2, hops)),
            dma((units, split)),
        ],
        compiler_params=pltpu.CompilerParams(
            collective_id=1, has_side_effects=True, vmem_limit_bytes=KERNEL_VMEM
        ),
        cost_estimate=pl.CostEstimate(
            flops=6_500_000_000, bytes_accessed=30 * MIB, transcendentals=0
        ),
        name="reduce_grads",
    )(one, mixed, heads_t, early, gate, q, branch, small)


def exchange_barrier(devices):
    barrier = pltpu.get_barrier_semaphore()
    for device in devices:
        pl.semaphore_signal(
            barrier, inc=1, device_id=device, device_id_type=pl.DeviceIdType.MESH
        )
    pl.semaphore_wait(barrier, len(devices))


def row_factors(totals, owner):
    rows = owner.shape[0]
    picks = (owner == lax.broadcasted_iota(jnp.int32, (rows, 128), 1)).astype(BF16)
    high = totals.astype(BF16)
    low = (totals - high.astype(F32)).astype(BF16)
    return mat_right_t(picks, high) + mat_right_t(picks, low)


STATE_GROUP = 4


class StateExchange:
    def __init__(self, count, forward, state_ref, totals, result, scratch):
        self.group = min(STATE_GROUP, count)
        self.groups = count // self.group
        self.forward = forward
        self.state_ref, self.totals, self.result = state_ref, totals, result
        (
            self.sent,
            self.came,
            self.before,
            self.back,
            self.whole,
            self.cross,
            self.sems,
            self.cross_sems,
        ) = scratch
        self.place = lax.axis_index("ctx") % self.group
        self.at = lax.axis_index("ctx") // self.group
        self.share = state_ref.shape[1] // self.group

    @staticmethod
    def scratch(count, state):
        group = min(STATE_GROUP, count)
        groups = count // group
        part = (state.shape[0], state.shape[1] // group, STATE)
        return [
            pltpu.VMEM(state.shape, BF16),
            pltpu.VMEM((group,) + part, BF16),
            pltpu.VMEM((group,) + part, F32),
            pltpu.VMEM((group,) + part, BF16),
            pltpu.VMEM(part, BF16),
            pltpu.VMEM((groups,) + part, BF16),
            pltpu.SemaphoreType.DMA((4, group)),
            pltpu.SemaphoreType.DMA((2, groups)),
        ]

    def rows_of(self, place):
        return pl.ds(pl.multiple_of(place * self.share, 16), self.share)

    def deal(self, k, slot):
        return remote(
            self.sent.at[:, self.rows_of(self.place ^ k)],
            self.came.at[slot],
            self.sems.at[0, k],
            self.sems.at[1, k],
            partner_ctx(k),
        )

    def give(self, m, slot):
        return remote(
            self.whole,
            self.cross.at[slot],
            self.cross_sems.at[0, m],
            self.cross_sems.at[1, m],
            partner_ctx(m * self.group),
        )

    def give_back(self, k, slot):
        return remote(
            self.back.at[self.place ^ k],
            self.result.at[:, self.rows_of(slot)],
            self.sems.at[2, k],
            self.sems.at[3, k],
            partner_ctx(k),
        )

    def order(self, count):
        return range(count) if self.forward else range(count - 1, -1, -1)

    def factors(self, blocks):
        part = self.totals[blocks]
        batch = part.shape[1]
        place = lax.broadcasted_iota(jnp.int32, (self.share, 128), 0) + self.place * self.share
        columns = row_factors(part.reshape(-1, 128), place // MDIM)

        def column(block, b):
            at = (block * batch + b) * 8
            return columns[:, at : at + 1]

        return column

    def own_blocks(self):
        return pl.ds(self.at * self.group, self.group)

    def begin(self):
        self.sent[...] = self.state_ref[...].astype(BF16)
        for k in range(1, self.group):
            self.deal(k, self.place).start()
        self.came[self.place] = self.state_ref[:, self.rows_of(self.place), :].astype(BF16)
        self.cross[self.at] = jnp.zeros(self.whole.shape, BF16)

    def middle(self):
        for k in range(1, self.group):
            self.deal(k, self.place).wait_send()
            self.deal(k, self.place ^ k).wait_recv()
        factor_of = self.factors(self.own_blocks())
        for b in range(self.whole.shape[0]):
            total = jnp.zeros((self.share, STATE), F32)
            for j in self.order(self.group):
                self.before[j, b] = total
                total = factor_of(j, b) * total + self.came[j, b].astype(F32)
            self.whole[b] = total.astype(BF16)
        for m in range(1, self.groups):
            self.give(m, self.at).start()

    def carry(self):
        for m in range(1, self.groups):
            self.give(m, self.at).wait_send()
            self.give(m, self.at ^ m).wait_recv()
        factor_of = self.factors(self.own_blocks())
        any_factor = self.factors(slice(None))
        for b in range(self.whole.shape[0]):
            reach = jnp.zeros((self.share, STATE), F32)
            for g in self.order(self.groups):
                decay = None
                for j in range(self.group):
                    one = any_factor(g * self.group + j, b)
                    decay = one if decay is None else decay * one
                earlier = (g < self.at) if self.forward else (g > self.at)
                reach = jnp.where(earlier, decay * reach + self.cross[g, b].astype(F32), reach)
            for j in self.order(self.group):
                self.back[j, b] = (self.before[j, b] + reach).astype(BF16)
                reach = reach * factor_of(j, b)
        for k in range(1, self.group):
            self.give_back(k, self.place).start()
        self.result[:, self.rows_of(self.place), :] = self.back[self.place]

    def end(self):
        for k in range(1, self.group):
            self.give_back(k, self.place).wait_send()
            self.give_back(k, self.place ^ k).wait_recv()


def mix_forward_kernel(
    count,
    start_ref,
    q_ref,
    near_ref,
    state_ref,
    total_ref,
    out_ref,
    log_ref,
    table_out,
    state_out,
    totals_out,
    q_wide,
    top,
    total,
    acc,
    far,
    totals,
    result,
    total_sems,
    table_sems,
    *state_scratch,
):
    here = lax.axis_index("ctx")
    batch = near_ref.shape[1]
    width = near_ref.shape[2]
    half = count // 2
    exchange_barrier([partner_ctx(k) for k in range(1, count)])
    totals[here] = total_ref[...]

    def total_copy(k, place):
        return remote(
            totals.at[here],
            totals.at[place],
            total_sems.at[0, k],
            total_sems.at[1, k],
            partner_ctx(k),
        )

    def table_copy(i):
        return remote(
            near_ref.at[i], far.at[i], table_sems.at[0, i], table_sems.at[1, i], partner_ctx(1)
        )

    for k in range(1, count):
        total_copy(k, here).start()
    states = StateExchange(count, True, state_ref, totals, result, state_scratch)
    states.begin()
    for i in range(half):
        table_copy(i).start()
    for b in range(batch):
        spread_heads(q_ref.at[:, b * width : (b + 1) * width], q_wide.at[b], HDIM**-0.5)
    top[...] = jnp.full(top.shape, MASKED_SCORE, F32)
    total[...] = jnp.zeros(total.shape, F32)
    acc[...] = jnp.zeros(acc.shape, F32)
    first_pos = here * width

    def attend(b, source, i, block):
        kv_rows = source[i, b]
        keys = kv_rows[:, : KVHEADS * HDIM]
        values_t = kv_rows[:, KVHEADS * HDIM :].T
        allowed = attend_allowed(block, first_pos, start_ref[b][:1], width)
        tops, totals_now = top[b], total[b]
        new_tops, new_totals = [], []
        for head in range(QHEADS):
            group = head // (QHEADS // KVHEADS)
            line = slice(head, head + 1)
            scores = mat(keys, q_wide[b, :, head * width : (head + 1) * width])
            scores = jnp.where(allowed, scores, MASKED_SCORE)
            old = tops[line]
            new = jnp.maximum(old, jnp.max(scores, axis=0, keepdims=True))
            terms = jnp.exp(scores - new)
            shrink = jnp.exp(old - new)
            new_tops.append(new)
            new_totals.append(
                totals_now[line] * shrink + jnp.sum(terms, axis=0, keepdims=True)
            )
            acc[b, head] = acc[b, head] * shrink + mat(
                values_t[group * HDIM : (group + 1) * HDIM, :], terms.astype(BF16)
            )
        top[b] = jnp.concatenate(new_tops, axis=0)
        total[b] = jnp.concatenate(new_totals, axis=0)

    bits = ctx_bits(count)
    high = len(bits) - 1

    def step_of(i):
        return sum(((i // (1 << p)) % 2) * (1 << (high - p)) for p in range(high))

    def pair(source, low, begin=0, end=half):
        def one(i, carry):
            if low:
                table_copy(i).wait()
            block = here ^ (step_of(i) + low)

            @pl.when(block <= here)
            def _():
                for b in range(batch):
                    attend(b, source, i, block)

            return carry

        lax.fori_loop(begin, end, one, 0)

    pair(near_ref, 0)
    for k in range(1, count):
        total_copy(k, here).wait_send()
        total_copy(k, here ^ k).wait_recv()
    states.middle()
    pair(far, 1, 0, half // 2)
    states.carry()
    pair(far, 1, half // 2)
    for b in range(batch):
        for head in range(QHEADS):
            out_ref[head * HDIM : (head + 1) * HDIM, b * width : (b + 1) * width] = (
                acc[b, head] / total[b, head : head + 1, :]
            ).astype(BF16)
        log_ref[b] = top[b] + jnp.log(total[b])
    table_out[:half] = near_ref[...]
    table_out[half:] = far[...]
    totals_out[...] = totals[...]
    states.end()
    state_out[...] = result[...]


def mix_forward(count, starts, queries_t, near, state, total):
    half, batch, width, kv_width = near.shape
    vmem = pl.BlockSpec(memory_space=pltpu.VMEM)
    dma = pltpu.SemaphoreType.DMA
    low = functools.partial(jax.ShapeDtypeStruct, dtype=BF16)
    wide = functools.partial(jax.ShapeDtypeStruct, dtype=F32)
    return pl.pallas_call(
        functools.partial(mix_forward_kernel, count),
        in_specs=[vmem] * 5,
        out_specs=[vmem] * 5,
        out_shape=[
            low(queries_t.shape),
            wide((batch, QHEADS, width)),
            low((count,) + near.shape[1:]),
            low(state.shape),
            wide((count,) + total.shape),
        ],
        scratch_shapes=[
            pltpu.VMEM((batch, KVHEADS * HDIM, QHEADS * width), BF16),
            pltpu.VMEM((batch, QHEADS, width), F32),
            pltpu.VMEM((batch, QHEADS, width), F32),
            pltpu.VMEM((batch, QHEADS, HDIM, width), F32),
            pltpu.VMEM(near.shape, BF16),
            pltpu.VMEM((count,) + total.shape, F32),
            pltpu.VMEM(state.shape, BF16),
            dma((2, count)),
            dma((2, half)),
        ]
        + StateExchange.scratch(count, state),
        compiler_params=pltpu.CompilerParams(
            collective_id=2, has_side_effects=True, vmem_limit_bytes=KERNEL_VMEM
        ),
        cost_estimate=pl.CostEstimate(
            flops=batch * count * width * width * 8 * 1000,
            bytes_accessed=4 * MIB,
            transcendentals=0,
        ),
        name="mix_forward",
    )(starts, queries_t, near, state, total)


def mix_backward_kernel(
    count,
    start_ref,
    q_ref,
    table_ref,
    attended_ref,
    grad_ref,
    log_ref,
    state_ref,
    totals_ref,
    dq_ref,
    dkv_ref,
    later_ref,
    q_wide,
    g_wide,
    q_tall,
    g_tall,
    delta,
    acc,
    mine,
    theirs,
    far,
    result,
    table_sems,
    *state_scratch,
):
    here = lax.axis_index("ctx")
    batch = table_ref.shape[1]
    width = table_ref.shape[2]
    half = count // 2
    kv_width = KVHEADS * HDIM
    exchange_barrier([partner_ctx(k) for k in range(1, count)])
    states = StateExchange(count, False, state_ref, totals_ref, result, state_scratch)
    states.begin()
    first_pos = here * width
    acc[...] = jnp.zeros(acc.shape, F32)
    mine[...] = jnp.zeros(mine.shape, BF16)
    theirs[...] = jnp.zeros(theirs.shape, BF16)
    for b in range(batch):
        columns = slice(b * width, (b + 1) * width)
        spread_heads(q_ref.at[:, columns], q_wide.at[b], HDIM**-0.5)
        spread_heads(grad_ref.at[:, columns], g_wide.at[b], 1.0)
        for head in range(QHEADS):
            lanes = slice(head * width, (head + 1) * width)
            q_tall[b, lanes, :] = q_wide[b, :, lanes].T
            g_tall[b, lanes, :] = g_wide[b, :, lanes].T
            span = slice(head * HDIM, (head + 1) * HDIM)
            delta[b, head : head + 1, :] = jnp.sum(
                attended_ref[span, columns].astype(F32) * grad_ref[span, columns].astype(F32),
                axis=0,
                keepdims=True,
            )

    def attend(b, place, block, target, i):
        kv_rows = table_ref[place, b]
        keys = kv_rows[:, :kv_width]
        values = kv_rows[:, kv_width:]
        keys_t = keys.T
        allowed = attend_allowed(block, first_pos, start_ref[b][:1], width)
        logs_now, deltas = log_ref[b], delta[b]
        dk = jnp.zeros((width, kv_width), F32)
        dv = jnp.zeros((width, kv_width), F32)
        for head in range(QHEADS):
            group = head // (QHEADS // KVHEADS)
            lanes = slice(head * width, (head + 1) * width)
            line = slice(head, head + 1)
            scores = mat(keys, q_wide[b, :, lanes])
            shifted = jnp.where(allowed, scores - logs_now[line], MASKED_SCORE)
            probs = jnp.exp(shifted)
            grad_probs = mat(values, g_wide[b, :, lanes])
            grad_scores = (probs * (grad_probs - deltas[line])).astype(BF16)
            dk = dk + mat(grad_scores, q_tall[b, lanes, :])
            dv = dv + mat(probs.astype(BF16), g_tall[b, lanes, :])
            acc[b, head] += mat(keys_t[group * HDIM : (group + 1) * HDIM, :], grad_scores)
        target[i, b] = jnp.concatenate([dk, dv], axis=1).astype(BF16)

    bits = ctx_bits(count)
    high = len(bits) - 1

    def step_of(i):
        return sum(((i // (1 << p)) % 2) * (1 << (high - p)) for p in range(high))

    def pair(target, low, begin=0, end=half):
        def one(i, carry):
            block = here ^ (step_of(i) + low)

            @pl.when(block <= here)
            def _():
                for b in range(batch):
                    attend(b, i + low * half, block, target, i)

            return carry

        lax.fori_loop(begin, end, one, 0)

    def table_copy(i):
        return remote(
            theirs.at[i], far.at[i], table_sems.at[0, i], table_sems.at[1, i], partner_ctx(1)
        )

    pair(theirs, 1, 0, half // 2)
    states.middle()
    pair(theirs, 1, half // 2)
    for i in range(half):
        table_copy(i).start()
    states.carry()
    pair(mine, 0)
    for b in range(batch):
        for head in range(QHEADS):
            dq_ref[head * HDIM : (head + 1) * HDIM, b * width : (b + 1) * width] = (
                acc[b, head] * HDIM**-0.5
            ).astype(BF16)
    for i in range(half):
        table_copy(i).wait()
    dkv_ref[...] = (mine[...].astype(F32) + far[...].astype(F32)).astype(BF16)
    states.end()
    later_ref[...] = result[...]


def mix_backward(count, starts, queries_t, table, attended_t, grad_t, logs, state, totals):
    _, batch, width, kv_width = table.shape
    half = count // 2
    vmem = pl.BlockSpec(memory_space=pltpu.VMEM)
    dma = pltpu.SemaphoreType.DMA
    low = functools.partial(jax.ShapeDtypeStruct, dtype=BF16)
    near = (half, batch, width, kv_width)
    wide = pltpu.VMEM((batch, KVHEADS * HDIM, QHEADS * width), BF16)
    tall = pltpu.VMEM((batch, QHEADS * width, KVHEADS * HDIM), BF16)
    return pl.pallas_call(
        functools.partial(mix_backward_kernel, count),
        in_specs=[vmem] * 8,
        out_specs=[vmem] * 3,
        out_shape=[low(queries_t.shape), low(near), low(state.shape)],
        scratch_shapes=[
            wide,
            wide,
            tall,
            tall,
            pltpu.VMEM((batch, QHEADS, width), F32),
            pltpu.VMEM((batch, QHEADS, HDIM, width), F32),
            pltpu.VMEM(near, BF16),
            pltpu.VMEM(near, BF16),
            pltpu.VMEM(near, BF16),
            pltpu.VMEM(state.shape, BF16),
            dma((2, half)),
        ]
        + StateExchange.scratch(count, state),
        compiler_params=pltpu.CompilerParams(
            collective_id=3, has_side_effects=True, vmem_limit_bytes=KERNEL_VMEM
        ),
        cost_estimate=pl.CostEstimate(
            flops=batch * count * width * width * 8 * 2000,
            bytes_accessed=8 * MIB,
            transcendentals=0,
        ),
        name="mix_backward",
    )(starts, queries_t, table, attended_t, grad_t, logs, state, totals)


def front_kernel(
    count,
    conv_tiles,
    gate_tiles,
    x_ref,
    gain_ref,
    start_ref,
    own_ref,
    tall_ref,
    weight_ref,
    bias_ref,
    normed_ref,
    others_out,
    tall_out,
    conv_out,
    edge_ref,
    act_out,
    dt_ref,
    q_ref,
    gate_out,
    table_ref,
    conv_ref,
    act_ref,
    gate_ref,
    edge_x,
    near,
    tall_near,
    table,
    cross_sems,
    core_sems,
    side_sems,
    last_sems,
    tall_sems,
    table_sems,
    edge_sems,
    out_sems,
):
    here = lax.axis_index("ctx")
    batch = table.shape[1]
    rows = table.shape[2]
    size = own_ref.shape[0]
    chunks = own_ref.shape[1] // EARLY_TILE
    half = count // 2
    exchange_barrier(
        [partner_wsh(1), partner_wsh(2)] + [partner_ctx(k) for k in range(1, count)]
    )
    right = (here + 1) % count

    def edge_copy(b):
        return remote(
            x_ref.at[pl.ds((b + 1) * rows - 16, 16)],
            edge_x.at[b],
            edge_sems.at[0, b],
            edge_sems.at[1, b],
            (right, lax.axis_index("wsh")),
        )

    my_half = pl.ds(pl.multiple_of((here % 2) * (size // 2), 16), size // 2)
    other_half = pl.ds(pl.multiple_of((1 - here % 2) * (size // 2), 16), size // 2)

    def tile(place):
        return pl.ds(pl.multiple_of(place * EARLY_TILE, EARLY_TILE), EARLY_TILE)

    def columns(k):
        return tile((k + gate_tiles) % chunks)

    gate_from = chunks - gate_tiles

    def cross_copy(k):
        return remote(
            own_ref.at[my_half, columns(k)],
            near.at[0, my_half, columns(k)],
            cross_sems.at[0, k],
            cross_sems.at[1, k],
            partner_wsh(2),
        )

    def side_copy(k):
        return remote(
            near.at[0, my_half, columns(k)],
            near.at[0, my_half, columns(k)],
            side_sems.at[0, k],
            side_sems.at[1, k],
            partner_ctx(1),
        )

    def side_in(k):
        return remote(
            near.at[0, other_half, columns(k)],
            near.at[0, other_half, columns(k)],
            side_sems.at[0, k],
            side_sems.at[1, k],
            partner_ctx(1),
        )

    def core_copy(k):
        return remote(
            own_ref.at[:, columns(k)],
            near.at[1, :, columns(k)],
            core_sems.at[0, k],
            core_sems.at[1, k],
            partner_wsh(1),
        )

    def last_copy(k):
        return remote(
            near.at[0, :, columns(k)],
            near.at[2, :, columns(k)],
            last_sems.at[0, k],
            last_sems.at[1, k],
            partner_wsh(1),
        )

    tall_size = tall_ref.shape[0]
    tall_chunks = tall_ref.shape[1] // EARLY_TILE
    tall_mine = pl.ds(pl.multiple_of((here % 2) * (tall_size // 2), 16), tall_size // 2)
    tall_theirs = pl.ds(pl.multiple_of((1 - here % 2) * (tall_size // 2), 16), tall_size // 2)

    def tall_copy(source, target, kind, k, device):
        return remote(
            source, target, tall_sems.at[kind, 0, k], tall_sems.at[kind, 1, k], device
        )

    def tall_cross(k):
        place = tall_near.at[0, tall_mine, tile(k)]
        return tall_copy(tall_ref.at[tall_mine, tile(k)], place, 0, k, partner_wsh(2))

    def tall_core(k):
        place = tall_near.at[1, :, tile(k)]
        return tall_copy(tall_ref.at[:, tile(k)], place, 1, k, partner_wsh(1))

    def tall_side(k, rows_at):
        place = tall_near.at[0, rows_at, tile(k)]
        return tall_copy(place, place, 2, k, partner_ctx(1))

    def tall_last(k):
        place = tall_near.at[2, :, tile(k)]
        return tall_copy(tall_near.at[0, :, tile(k)], place, 3, k, partner_wsh(1))

    def tall_step(j):
        @pl.when((j >= 0) & (j < tall_chunks))
        def _():
            tall_cross(j).wait()
            tall_side(j, tall_mine).start()

        @pl.when((j >= 2) & (j <= tall_chunks + 1))
        def _():
            tall_side(j - 2, tall_mine).wait_send()
            tall_side(j - 2, tall_theirs).wait_recv()
            tall_last(j - 2).start()

    bits = ctx_bits(count)
    high = len(bits) - 1

    def step_of(i):
        return sum(((i >> p) & 1) * (1 << (high - p)) for p in range(high))

    def table_copy(i):
        return remote(
            table.at[0],
            table.at[i],
            table_sems.at[0, i],
            table_sems.at[1, i],
            partner_ctx(step_of(i)),
        )

    def send_first(k, carry):
        cross_copy(k).start()
        core_copy(k).start()
        return carry

    def send_tall(k, carry):
        tall_cross(k).start()
        tall_core(k).start()
        return carry

    lax.fori_loop(0, gate_from, send_first, 0)
    lax.fori_loop(0, tall_chunks, send_tall, 0)
    lax.fori_loop(gate_from, chunks, send_first, 0)
    for b in range(batch):
        edge_copy(b).start()

    def normalized(low):
        wide = low.astype(F32)
        return (wide * inv_rms(wide) * gain_ref[...]).astype(BF16)

    normed_ref[...] = normalized(x_ref[...])
    for b in range(batch):
        edge_copy(b).wait()
    edge_normed = normalized(
        jnp.concatenate([edge_x[b] for b in range(batch)], axis=0)
    )
    edge_x[...] = edge_normed.reshape(edge_x.shape)

    def product(pick, k):
        total = None
        for place, step in enumerate(NEAR):
            block = own_ref[:, columns(k)] if place == 0 else near[place - 1, :, columns(k)]
            part = mat(pick(near_at(step, size)), block)
            total = part if total is None else total + part
        return total

    def others_copy(k):
        return pltpu.make_async_copy(
            near.at[:, :, columns(k)], others_out.at[:, :, columns(k)], out_sems.at[0, k]
        )

    def conv_copy(k):
        return pltpu.make_async_copy(
            conv_ref.at[:, tile(k - 1)], conv_out.at[:, tile(k - 1)], out_sems.at[1, k]
        )

    def act_copy(k):
        return pltpu.make_async_copy(
            act_ref.at[:, tile(k - 1)], act_out.at[:, tile(k - 1)], out_sems.at[2, k]
        )

    def gate_copy(k):
        return pltpu.make_async_copy(
            gate_ref.at[:, tile(k - gate_from)],
            gate_out.at[:, tile(k - gate_from)],
            out_sems.at[1, k],
        )

    def compute(k):
        core_copy(k).wait()
        last_copy(k).wait()
        others_copy(k).start()
        value = product(lambda at: normed_ref[:, at], k)

        @pl.when(k == 0)
        def _():
            table[0] = value.astype(BF16).reshape(table.shape[1:])
            for i in range(1, half):
                table_copy(i).start()

        @pl.when((k > 0) & (k <= conv_tiles))
        def _():
            place = tile(k - 1)
            conv_ref[:, place] = value
            taps = weight_ref[:, place]
            bias = bias_ref[:, place]
            edges = product(lambda at: edge_x[:, :, at].reshape(batch * 16, size), k)
            for b in range(batch):
                edge = edges[(b + 1) * 16 - EDGE : (b + 1) * 16]
                edge_ref[b * EDGE : (b + 1) * EDGE, place] = edge
                span = slice(b * rows, (b + 1) * rows)
                total, _ = conv_sums(
                    conv_inputs(edge, value[span]), taps, bias, start_ref[span]
                )
                act_ref[span, place] = total * sigmoid(total)
            conv_copy(k).start()
            act_copy(k).start()

        @pl.when(k == conv_tiles + 1)
        def _():
            dt_ref[...] = value

        @pl.when((k > conv_tiles + 1) & (k < gate_from))
        def _():
            q_ref[tile(k - conv_tiles - 2), :] = value.T.astype(BF16)

        @pl.when(k >= gate_from)
        def _():
            gate_ref[:, tile(k - gate_from)] = value
            gate_copy(k).start()

    def one_step(t, carry):
        @pl.when(t < chunks)
        def _():
            cross_copy(t).wait()
            side_copy(t).start()

        @pl.when((t >= 2) & (t <= chunks + 1))
        def _():
            side_copy(t - 2).wait_send()
            side_in(t - 2).wait_recv()
            last_copy(t - 2).start()

        tall_step(t - gate_from)
        pl.when(t >= 4)(functools.partial(compute, t - 4))
        return carry

    lax.fori_loop(0, chunks + 4, one_step, 0)
    def end_tall(k, carry):
        tall_core(k).wait()
        tall_last(k).wait()
        return carry

    lax.fori_loop(0, tall_chunks, end_tall, 0)
    whole_tall = pltpu.make_async_copy(tall_near, tall_out, out_sems.at[2, 0])
    whole_tall.start()

    def end_outs(k, carry):
        others_copy(k).wait()

        @pl.when((k > 0) & (k <= conv_tiles))
        def _():
            conv_copy(k).wait()
            act_copy(k).wait()

        @pl.when(k >= gate_from)
        def _():
            gate_copy(k).wait()

        return carry

    lax.fori_loop(0, chunks, end_outs, 0)
    whole_tall.wait()
    for i in range(1, half):
        table_copy(i).wait()
    table_ref[...] = table[...]


def front(count, batch, x, gain, rel_start, own, tall, conv_weight, conv_bias, q_width):
    tokens, depth = x.shape
    size, columns = own.shape
    rows = tokens // batch
    channels = conv_weight.shape[1]
    chunks = columns // EARLY_TILE
    half = count // 2
    vmem = pl.BlockSpec(memory_space=pltpu.VMEM)
    hbm = pl.BlockSpec(memory_space=pl.ANY)
    dma = pltpu.SemaphoreType.DMA
    low = functools.partial(jax.ShapeDtypeStruct, dtype=BF16)
    wide = functools.partial(jax.ShapeDtypeStruct, dtype=F32)
    table = (half, batch, rows, EARLY_TILE)
    return pl.pallas_call(
        functools.partial(
            front_kernel, count, channels // EARLY_TILE, DSSM // EARLY_TILE
        ),
        in_specs=[vmem] * 7,
        out_specs=[vmem, hbm, hbm, hbm, vmem, hbm, vmem, vmem, hbm, vmem],
        out_shape=[
            low((tokens, depth)),
            low((3, size, columns)),
            low((3,) + tall.shape),
            wide((tokens, channels)),
            wide((batch * EDGE, channels)),
            wide((tokens, channels)),
            wide((tokens, EARLY_TILE)),
            low((q_width, tokens)),
            wide((tokens, DSSM)),
            low(table),
        ],
        scratch_shapes=[
            pltpu.VMEM((tokens, channels), F32),
            pltpu.VMEM((tokens, channels), F32),
            pltpu.VMEM((tokens, DSSM), F32),
            pltpu.VMEM((batch, 16, depth), BF16),
            pltpu.VMEM((3, size, columns), BF16),
            pltpu.VMEM((3,) + tall.shape, BF16),
            pltpu.VMEM(table, BF16),
            dma((2, chunks)),
            dma((2, chunks)),
            dma((2, chunks)),
            dma((2, chunks)),
            dma((4, 2, tall.shape[1] // EARLY_TILE)),
            dma((2, half)),
            dma((2, batch)),
            dma((3, chunks)),
        ],
        compiler_params=pltpu.CompilerParams(
            collective_id=4, has_side_effects=True, vmem_limit_bytes=KERNEL_VMEM
        ),
        cost_estimate=pl.CostEstimate(
            flops=2 * tokens * depth * columns, bytes_accessed=20 * MIB, transcendentals=0
        ),
        name="front",
    )(x, gain[None], rel_start, own, tall, conv_weight, conv_bias[None])


def local(
    inputs,
    cotangent,
    lengths,
    norm1_gain,
    in_weight,
    dt_weight,
    conv_weight,
    conv_bias,
    dt_bias,
    decay_rate,
    skip_gain,
    mamba_gain,
    out_weight,
    q_weight,
    kv_weight,
    o_weight,
    norm2_gain,
    gu_weight,
    down_weight,
):
    count, _, rows, features = inputs.shape
    here = lax.axis_index("ctx")
    ctx_count = lax.axis_size("ctx")
    tokens = count * rows
    first_pos = here * rows
    own_pos = first_pos + jnp.arange(rows, dtype=jnp.int32)
    starts = jax.vmap(lambda row: seq_starts(row, own_pos))(lengths[:, 0])
    rel_start = (starts - first_pos).reshape(tokens, 1)
    taps = conv_weight.shape[0]
    channels = conv_weight.shape[1]
    kv_width = kv_weight.shape[1]
    x_low = inputs.reshape(tokens, features)
    grad_top = cotangent.reshape(tokens, features)

    conv_tiles = channels // EARLY_TILE
    gate_tiles = DSSM // EARLY_TILE
    early_shard = jnp.concatenate(
        [
            in_weight[:, :DSSM],
            kv_weight,
            in_weight[:, DSSM:],
            jnp.pad(dt_weight, ((0, 0), (0, EARLY_TILE - dt_weight.shape[1]))),
            q_weight,
        ],
        axis=1,
    )

    outs_own = jnp.concatenate([out_weight, o_weight], axis=0)
    normed, early_others, outs_others, conv_rows, edge_rows, act, dt_rows, queries_t, gate_z, near_table = front(
        ctx_count,
        count,
        x_low,
        norm1_gain,
        rel_start,
        early_shard,
        outs_own,
        conv_weight,
        conv_bias,
        q_weight.shape[1],
    )
    high_bits = bits_of("ctx")[1:]
    later_shards = after(
        (
            gu_weight,
            down_weight,
        ),
        dt_rows,
    )
    crossing = [swapped(shard, "wsh", 2) for shard in later_shards]

    def head_row(values):
        return jnp.pad(values, (0, 128 - MHEADS))[None]

    bias_row, rate_row = head_row(dt_bias), head_row(decay_rate)
    steps, decay, decay_t, to_end, total, fresh = ssd_state(
        count, act, dt_rows, bias_row, rate_row, rel_start
    )
    starts_row = jnp.broadcast_to(starts[:, None, :], (count, 8, rows))
    attended_t, logs, key_table, state_in, totals = mix_forward(
        ctx_count, starts_row, queries_t, near_table, fresh, total
    )

    def near_blocks(which, held):
        shard, across = later_shards[which], after(crossing[which], held)
        return [shard, across, swapped(shard, "wsh", 1), swapped(across, "wsh", 1)]

    outs = (outs_own, outs_others)
    skip_row = jnp.repeat(skip_gain, MDIM)[None]
    scanned = ssd_forward(count, act, steps, decay, decay_t, rel_start, state_in, skip_row)
    gate_sig = jax.nn.sigmoid(gate_z)
    gated = scanned * gate_z * gate_sig
    scale_m = inv_rms(gated)
    mixed = (gated * scale_m * mamba_gain).astype(BF16)
    gu_full, down_full = near_blocks(0, mixed), near_blocks(1, mixed)
    middle, normed_two = out_project(x_low, mixed, attended_t, norm2_gain, outs)

    layer_out, grad_middle, branch, grad_norm2, hidden, grad_pair = mlp_both(
        lax.axis_index("wsh").astype(jnp.int32)[None],
        normed_two,
        grad_top,
        middle,
        norm2_gain,
        gu_full,
        down_full,
    )
    gu_send = block_grads(normed_two, grad_pair, NEAR[2:])[0]
    down_send = block_grads(hidden, grad_top[None], NEAR[2:])[0]
    gu_sent = swapped(gu_send, "wsh", 1)
    down_sent = swapped(down_send, "wsh", 1)
    branch = after(branch, (gu_send, down_send))
    grad_mixed, grad_attended_t = out_unproject(branch, outs, DSSM, QHEADS * HDIM)
    gu_left, down_left = after((normed_two, hidden), grad_attended_t)
    gu_kept, gu_other = block_grads(gu_left, grad_pair, NEAR[:2], gu_sent)
    down_kept, down_other = block_grads(down_left, grad_top[None], NEAR[:2], down_sent)
    gu_crossed = swapped(gu_other, "wsh", 2)
    down_crossed = swapped(down_other, "wsh", 2)

    grad_mixed = after(grad_mixed, (gu_other, down_other))
    grad_gated, grad_mamba = rms_pull(gated, scale_m, mamba_gain, grad_mixed)
    grad_gate_z = grad_gated * scanned * gate_sig * (1.0 + gate_z * (1.0 - gate_sig))
    grad_scanned = grad_gated * gate_z * gate_sig
    grad_state = state_grad(count, grad_scanned, act, decay, rel_start)
    dq_t, dkv_near, later = mix_backward(
        ctx_count,
        starts_row,
        queries_t,
        key_table,
        attended_t,
        grad_attended_t,
        logs,
        grad_state,
        totals,
    )
    key_grads = Scattering(dkv_near, high_bits)

    def total_of(kept, crossed):
        return (kept.astype(F32) + crossed.astype(F32)).astype(BF16)

    held = after((gu_crossed, down_crossed), dq_t)
    parts = total_of(gu_kept, held[0]), total_of(down_kept, held[1])
    grad_gate_z = after(grad_gate_z.astype(BF16), parts)
    dq_rows = dq_t.T
    grad_normed = unproject(
        None,
        grad_gate_z,
        [early_shard] + [early_others] * 3,
        768,
        near_specs(early_shard, 768, 0),
    )
    grad_normed = unproject(
        grad_normed,
        dq_rows,
        [early_shard] + [early_others] * 3,
        EARLY_TILE,
        near_specs(early_shard, EARLY_TILE, gate_tiles + conv_tiles + 2),
    )
    later = after(later, key_grads.advance(grad_normed))
    dx, db, dc, dt_grad, small_ssd = ssd_backward(
        count,
        act,
        steps,
        decay,
        decay_t,
        rel_start,
        state_in,
        skip_row,
        scanned,
        grad_scanned,
        later,
        to_end,
        total,
        dt_rows,
        bias_row,
        rate_row,
    )
    key_grads.advance(dx)
    grad_kv_rows = key_grads.finish().reshape(tokens, -1)
    edge_back = passed_along(
        edge_grads(count, dx, db, dc, conv_rows, edge_rows, rel_start, conv_weight, conv_bias),
        "ctx",
        -1,
    )
    grad_early, conv_grads, input_grad, grad_norm1 = early_back(
        count,
        grad_normed,
        grad_kv_rows,
        dx,
        db,
        dc,
        conv_rows,
        edge_rows,
        edge_back,
        dt_grad,
        rel_start,
        conv_weight,
        conv_bias,
        x_low,
        norm1_gain,
        grad_middle,
        early_shard,
        early_others,
    )
    small_ssd = jnp.sum(small_ssd, axis=0)
    grad_dt_w = mat_left_t(normed, dt_grad[:, :MHEADS])

    gu_sum, down_sum = lax.psum(parts, "ctx")
    pieces = (
        grad_norm1[0],
        conv_grads[:taps],
        conv_grads[taps],
        small_ssd[0, :MHEADS],
        small_ssd[1, :MHEADS],
        small_ssd[2, :MHEADS],
        grad_mamba,
        grad_norm2[0],
        grad_dt_w,
    )
    packed = jnp.concatenate(
        [
            jnp.pad(piece.reshape(-1), (0, -piece.size % 1024)).reshape(-1, 128)
            for piece in pieces
        ],
        axis=0,
    )
    early_sum, gate_sum, q_sum, mix_sum, packed = reduce_grads(
        ctx_count,
        kv_width + channels,
        normed,
        mixed,
        attended_t,
        grad_early,
        grad_gate_z,
        dq_rows,
        branch,
        packed,
    )
    in_sum, q_sum, kv_sum, out_sum, o_sum, gu_sum, down_sum = finish(
        early_sum,
        gate_sum,
        mix_sum,
        q_sum,
        gu_sum,
        down_sum,
        [
            w.shape
            for w in (
                in_weight,
                q_weight,
                kv_weight,
                out_weight,
                o_weight,
                gu_weight,
                down_weight,
            )
        ],
    )
    totals_w = [in_sum, out_sum, q_sum, kv_sum, o_sum, gu_sum, down_sum]
    small = []
    place = 0
    for piece in pieces:
        lines = -(-piece.size // 1024) * 8
        small.append(packed[place : place + lines].reshape(-1)[: piece.size].reshape(piece.shape))
        place += lines
    dt_size = dt_weight.shape[0]
    dt_sum = lax.dynamic_slice_in_dim(small[8], lax.axis_index("wsh") * dt_size, dt_size, 0)
    shape = (count, 1, rows, features)
    return (
        layer_out.reshape(shape),
        input_grad.reshape(shape),
        small[0],
        totals_w[0],
        dt_sum,
        small[1],
        small[2],
        small[3],
        small[4],
        small[5],
        small[6],
        totals_w[1],
        totals_w[2],
        totals_w[3],
        totals_w[4],
        small[7],
        totals_w[5],
        totals_w[6],
    )


def solution(mesh):
    stream = P(None, "wsh", "ctx", None)
    shard = P("wsh", None)
    in_specs = (
        stream,
        stream,
        P(None, "wsh", None),
        P(),
        shard,
        shard,
        P(),
        P(),
        P(),
        P(),
        P(),
        P(),
        shard,
        shard,
        shard,
        shard,
        P(),
        shard,
        shard,
    )
    out_specs = (
        stream,
        stream,
        P(),
        shard,
        shard,
        P(),
        P(),
        P(),
        P(),
        P(),
        P(),
        shard,
        shard,
        shard,
        shard,
        P(),
        shard,
        shard,
    )
    return jax.shard_map(local, mesh=mesh, in_specs=in_specs, out_specs=out_specs, check_vma=False)
```
